32 devices in a mesh: ctx: 8 (over z, x), head: 4 (over y, core).
Axes of the slice: x: 2, y: 2, z: 4, core: 2. Of those that a mesh axis runs over, the one named last changes fastest.
Arguments:
- values: bfloat16 [8192, 5120], P(('ctx', 'head')), may hold values from -6 to 6
- state_in: bfloat16 [8192, 128], P('ctx'), may hold values from -0.5 to 0.5
- state_out: bfloat16 [8192, 128], P('ctx'), may hold values from -6 to 6
- log_decay: float32 [8192, 80], P('ctx', 'head'), may hold values from -1 to 0
- level_class: int32 [8192], P('ctx'), may hold values from 0 to 31
- level_table: float32 [32, 8, 80], P(None, None, 'head'), may hold values from 0.2 to 2
- skip_gain: float32 [80], P('head'), may hold values from 0.5 to 2
- norm_gain: float32 [5120], P('head'), may hold values from 0.1 to 1.9
- out_weight: bfloat16 [5120, 2560], P('head', 'ctx'), may hold values from -0.078125 to 0.078125
Outputs:
- projected: bfloat16 [8192, 2560], P(('ctx', 'head'))
The draws below stay inside these ranges and needn't reach their ends.
All inputs are finite; a program needn't handle non-finite values.
Results may differ from the reference program's by a relative error of at most 0.0049.
Values may be sent and summed in bfloat16 or wider, within the bound.
No kernel may reach another device: no remote copies, remote signals or barrier semaphores. Data moves between devices by JAX's collectives and lax.ppermute only.
A program may use at most 128 MiB of HBM per device.

```python
import math
import jax
import jax.numpy as jnp
from jax import lax

D = 2560
HEADS = 80
P_SIZE = 64
N_STATE = 128
CH = 64
CLASSES = 32
STRETCHES_DEV = 16
TOK_DEV = 1024
SEQUENCE_TOKENS = 8192
D_INNER = 5120
LEVELS = 8


def draw_log_decay(key, part):
    split_random_keys = jax.random.split(key, 7)
    picked = jax.random.uniform(split_random_keys[0], (HEADS,))
    fast_share = 0.5
    rough_low = 0.5
    rough_high = 1.5
    fast_head = picked < fast_share
    fast_rate = jnp.exp(jax.random.uniform(split_random_keys[1], (HEADS,), minval=jnp.log(1.0 / 50.0), maxval=jnp.log(1.0 / 30.0)))
    slow_total = jnp.exp(jax.random.uniform(split_random_keys[2], (HEADS,), minval=jnp.log(0.05), maxval=jnp.log(0.3)))
    baseline_rate = jnp.where(fast_head, fast_rate, slow_total / SEQUENCE_TOKENS)
    partition_factor = jnp.exp(jax.random.uniform(split_random_keys[3], (SEQUENCE_TOKENS // TOK_DEV, HEADS), minval=jnp.log(0.5), maxval=jnp.log(2.0)))
    partition_factor = jnp.repeat(partition_factor, TOK_DEV, axis=0)
    coarseness_level = jax.random.uniform(split_random_keys[4], (SEQUENCE_TOKENS, HEADS), minval=rough_low, maxval=rough_high)
    surge_position = jax.random.randint(split_random_keys[5], (2,), 0, SEQUENCE_TOKENS)
    surge_length = jax.random.uniform(split_random_keys[6], (2,), minval=0.22, maxval=0.69)
    surge_struck = jnp.arange(SEQUENCE_TOKENS)[:, None] == surge_position[None, :]
    surge_penalty = jnp.sum(jnp.where(surge_struck, surge_length[None, :], 0.0), axis=1)
    return -(baseline_rate[None, :] * partition_factor * coarseness_level + surge_penalty[:, None])


def place_ends(entries, key, least, top_value):
    shape = entries.shape
    index_at = [jax.random.randint(jax.random.fold_in(key, axis), (), 0, shape[axis]) for axis in range(len(shape))]
    entries = entries.at[tuple(index_at)].set(least)
    longest = shape.index(max(shape))
    index_at[longest] = (index_at[longest] + 1) % shape[longest]
    return entries.at[tuple(index_at)].set(top_value)


def block_levels(own_key, extent, cuts, low, high):
    def one(position, blocks):
        steps = jax.random.uniform(jax.random.fold_in(jax.random.fold_in(own_key, 6), position), (blocks,), jnp.float32, low / len(cuts), high / len(cuts))
        return jnp.repeat(jnp.exp(steps), extent[position] // blocks).reshape((-1,) + (1,) * (len(extent) - position - 1))

    loudness = one(*cuts[0])
    for cut in cuts[1:]:
        loudness = loudness * one(*cut)
    return loudness


def normal_values(stream_key, extent, scale, limit, cuts=(), kind=jnp.bfloat16):
    array = jax.random.normal(stream_key, extent, jnp.float32) * scale
    if len(cuts) > 0:
        array = block_levels(stream_key, extent, cuts, -0.22, 0.18) * array
    return jnp.clip(array, min=-limit, max=limit).astype(kind)


def setup_inputs(seed: int = 0) -> dict:
    key_of = jax.random.split(jax.random.key(seed), 10)
    return {
        "values": normal_values(key_of[0], (SEQUENCE_TOKENS, D_INNER), 1.0, 6.0, ((0, 32),)),
        "state_in": normal_values(key_of[1], (SEQUENCE_TOKENS, N_STATE), (N_STATE ** -0.5), 0.5, ((0, 8),)),
        "state_out": normal_values(key_of[2], (SEQUENCE_TOKENS, N_STATE), 1.0, 6.0, ((0, 8),)),
        "log_decay": draw_log_decay(jax.random.fold_in(key_of[9], 71), 0),
        "level_class": place_ends(jax.random.randint(key_of[4], (SEQUENCE_TOKENS,), 0, CLASSES), jax.random.fold_in(key_of[4], 1), 0, CLASSES - 1).astype(jnp.int32),
        "level_table": jnp.clip(jnp.exp(math.log(2.0) - 2.3025851 * jax.random.uniform(key_of[5], (CLASSES, LEVELS, HEADS), jnp.float32) ** block_levels(key_of[5], (CLASSES, LEVELS, HEADS), ((2, 4),), -0.2, 0.2)), 0.2, 2.0),
        "skip_gain": jnp.clip(0.5 + 1.5 * jax.random.uniform(key_of[6], (HEADS,), jnp.float32) ** block_levels(key_of[6], (HEADS,), ((0, 4),), -0.2, 0.2), 0.5, 2.0),
        "norm_gain": jnp.clip(1.0 + 0.18 * jax.random.normal(key_of[7], (D_INNER,), jnp.float32), 0.1, 1.9),
        "out_weight": normal_values(key_of[8], (D_INNER, D), D_INNER ** -0.5, 0.078125, ((0, 4), (1, 8))),
    }


PRECISE = lax.Precision.HIGHEST
EPSILON = 1e-05

def expand_heads(factor, head_width):
    return jnp.repeat(factor, head_width, axis=-1)

def local_levels(inputs, state_in, state_out, log_decay, weights, stretch_size, head_width, readout):
    tokens_dev = inputs.shape[0]
    features = inputs.shape[1]
    state_size = state_in.shape[1]
    head_count = log_decay.shape[1]
    stretch_count = tokens_dev // stretch_size
    height_count = stretch_count.bit_length() - 1
    within = jnp.cumsum(log_decay.reshape(stretch_count, stretch_size, head_count), axis=1)
    stretch_sum = within[:, -1]
    block_end = jnp.cumsum(stretch_sum, axis=0)
    cumul = (block_end - stretch_sum)[:, None, :] + within
    flat_cumul = cumul.reshape(tokens_dev, head_count)
    in_pieces = state_in.reshape(stretch_count, stretch_size, state_size)
    input_pieces = inputs.reshape(stretch_count, stretch_size, features)
    to_end = expand_heads(jnp.exp(stretch_sum[:, None, :] - within), head_width) * input_pieces
    merged = jnp.einsum('csn,csf->cnf', in_pieces, to_end, precision=PRECISE)
    output = None
    if readout:
        out_pieces = state_out.reshape(stretch_count, stretch_size, state_size)
        scores = jnp.einsum('ctn,csn->cts', out_pieces, in_pieces, precision=PRECISE)
        causal = jnp.arange(stretch_size)[:, None] >= jnp.arange(stretch_size)[None, :]
        scores = jnp.where(causal[None], scores, 0.0)
        lifted = expand_heads(jnp.exp(-within), head_width) * input_pieces
        direct = jnp.einsum('cts,csf->ctf', scores, lifted, precision=PRECISE)
        level_zero = weights[:, 0].reshape(stretch_count, stretch_size, head_count)
        output = (expand_heads(jnp.exp(within) * level_zero, head_width) * direct).reshape(tokens_dev, features)
    for height in range(1, height_count + 1):
        group_count = merged.shape[0] // 2
        paired = merged.reshape(group_count, 2, state_size, features)
        end_pair = block_end.reshape(group_count, 2, head_count)
        if readout:
            half_rows = tokens_dev // group_count // 2
            reader = state_out.reshape(group_count, 2, half_rows, state_size)[:, 1]
            upper_cumul = flat_cumul.reshape(group_count, 2, half_rows, head_count)[:, 1]
            upper_weight = weights[:, height].reshape(group_count, 2, half_rows, head_count)[:, 1]
            fading = jnp.exp(upper_cumul - end_pair[:, 0][:, None, :])
            gained = expand_heads(fading * upper_weight, head_width) * jnp.einsum('grn,gnf->grf', reader, paired[:, 0], precision=PRECISE)
            padded = jnp.stack([jnp.zeros_like(gained), gained], axis=1)
            output = output + padded.reshape(tokens_dev, features)
        carried = expand_heads(jnp.exp(end_pair[:, 1] - end_pair[:, 0]), head_width)
        merged = carried[:, None, :] * paired[:, 0] + paired[:, 1]
        block_end = end_pair[:, 1]
    return (output, merged[0], block_end[0], flat_cumul)

def cross_levels(output, state_out, flat_cumul, weights, every_state, every_total, block_index, local_bits, head_width):
    device_count = every_total.shape[0]
    device = jnp.arange(device_count, dtype=jnp.int32)
    between = (device[:, None] < device[None, :]) & (device[None, :] < block_index)
    span_decay = jnp.dot(between.astype(jnp.float32), every_total, precision=PRECISE)
    for bit_index in range(device_count.bit_length() - 1):
        stride = 2 ** (bit_index + 1)
        half_stride = 2 ** bit_index
        member = (device // stride == block_index // stride) & (device // half_stride % 2 == 0) & (block_index // half_stride % 2 == 1)
        factor = jnp.where(member[:, None], jnp.exp(jnp.where(member[:, None], span_decay, 0.0)), 0.0)
        bucket = jnp.einsum('df,dnf->nf', expand_heads(factor, head_width), every_state, precision=PRECISE)
        scaling = expand_heads(jnp.exp(flat_cumul) * weights[:, local_bits + 1 + bit_index], head_width)
        output = output + scaling * jnp.dot(state_out, bucket, precision=PRECISE)
    return output

def finish(output, inputs, skip_gain, norm_gain, head_width):
    output = output + expand_heads(skip_gain, head_width)[None, :] * inputs
    grouped = output.reshape(output.shape[0], -1, head_width)
    mean_square = lax.optimization_barrier(jnp.mean(grouped * grouped, axis=-1, keepdims=True))
    normed = grouped * lax.rsqrt(mean_square + EPSILON)
    return (normed.reshape(output.shape) * norm_gain[None, :]).astype(jnp.bfloat16)

def reference(values, state_in, state_out, log_decay, level_class, level_table, skip_gain, norm_gain, out_weight):
    blocks = SEQUENCE_TOKENS // TOK_DEV
    local_bits = STRETCHES_DEV.bit_length() - 1

    def block_rows(source, block_index):
        return lax.dynamic_slice_in_dim(source, (block_index * TOK_DEV).astype(jnp.int32), TOK_DEV, 0)

    def first_pass(block_index):
        outcome = local_levels(block_rows(values, block_index).astype(jnp.float32), block_rows(state_in, block_index).astype(jnp.float32), None, block_rows(log_decay, block_index), None, CH, P_SIZE, False)
        return (outcome[1], outcome[2])
    every_state, every_total = lax.map(first_pass, jnp.arange(blocks, dtype=jnp.int32))

    def second_pass(block_index):
        inputs = block_rows(values, block_index).astype(jnp.float32)
        readers = block_rows(state_out, block_index).astype(jnp.float32)
        weights = level_table[block_rows(level_class, block_index)]
        output, unused_state, unused_total, flat_cumul = local_levels(inputs, block_rows(state_in, block_index).astype(jnp.float32), readers, block_rows(log_decay, block_index), weights, CH, P_SIZE, True)
        output = cross_levels(output, readers, flat_cumul, weights, every_state, every_total, block_index, local_bits, P_SIZE)
        normed = finish(output, inputs, skip_gain, norm_gain, P_SIZE)
        return jnp.dot(normed, out_weight, preferred_element_type=jnp.float32).astype(jnp.bfloat16)
    projected = lax.map(second_pass, jnp.arange(blocks, dtype=jnp.int32))
    return projected.reshape(SEQUENCE_TOKENS, D)
```

```python
import jax
import jax.numpy as jnp
from jax import lax
from jax.experimental import pallas as pl
from jax.experimental.pallas import tpu as pltpu
from jax.sharding import PartitionSpec as P

CH = 64
EPSILON = 1e-05
F32 = jnp.float32
BF16 = jnp.bfloat16
VMEM_LIMIT = 56 * 1024 * 1024


def dot(a, b):
    return lax.dot_general(a, b, (((1,), (0,)), ((), ())), preferred_element_type=F32)


def dot_t(a, b):
    return lax.dot_general(a, b, (((0,), (0,)), ((), ())), preferred_element_type=F32)


def dot_nt(a, b):
    return lax.dot_general(a, b, (((1,), (1,)), ((), ())), preferred_element_type=F32)


def swap(value, axis, distance):
    pairs = [(source, source ^ distance) for source in range(lax.axis_size(axis))]
    return lax.ppermute(value, axis, pairs)


def three_parts(x):
    high = x.astype(BF16)
    rest = x - high.astype(F32)
    middle = rest.astype(BF16)
    low = (rest - middle.astype(F32)).astype(BF16)
    return high, middle, low


def two_parts(x):
    high = x.astype(BF16)
    return high, (x - high.astype(F32)).astype(BF16)


def halves(x, head_count):
    high = x.astype(BF16).astype(F32)
    lane = lax.broadcasted_iota(jnp.int32, x.shape, x.ndim - 1)
    return jnp.where(lane < head_count, high, x - high).astype(BF16)


def merge_rows(stretches):
    rows = [("own", c, 0) for c in range(stretches - 1)]
    for c in range(stretches - 1):
        k = 0
        while (c >> k) & 1:
            rows.append(("merge", c, k))
            k += 1
    return rows


def factors_kernel(
    decay_ref, class_ref, table_ref, fade_ref, lift_ref, read_ref, cross_ref, merge_ref, total_ref
):
    tokens, width = decay_ref.shape
    head_count = width // 2
    stretches = tokens // CH
    levels, classes, _ = table_ref.shape
    local = read_ref.shape[0] - 1
    row = lax.broadcasted_iota(jnp.int32, (CH, CH), 0)
    col = lax.broadcasted_iota(jnp.int32, (CH, CH), 1)
    lower = jnp.where(row >= col, 1.0, 0.0).astype(BF16)
    lower = jnp.concatenate([lower] * 3, axis=1)
    tables = [jnp.concatenate(three_parts(table_ref[level]), axis=0) for level in range(levels)]
    within, starts = [], [jnp.zeros((1, width), F32)]
    for c in range(stretches):
        parts = jnp.concatenate(three_parts(decay_ref[c * CH : (c + 1) * CH, :]), axis=0)
        summed = dot(lower, parts)
        within.append(summed)
        starts.append(starts[-1] + summed[CH - 1 : CH, :])
    total = starts[-1]
    total_ref[...] = total
    class_iota = lax.broadcasted_iota(jnp.int32, (CH, 3 * classes), 1) % classes
    for c in range(stretches):
        rows = slice(c * CH, (c + 1) * CH)
        fade_ref[rows, :] = halves(jnp.exp(total - starts[c] - within[c]), head_count)
        lift_ref[rows, :] = halves(jnp.exp(-within[c]), head_count)
        onehot = jnp.where(class_ref[rows, :] == class_iota, 1.0, 0.0).astype(BF16)
        read_ref[0, rows, :] = halves(jnp.exp(within[c]) * dot(onehot, tables[0]), head_count)
        for level in range(1, local + 1):
            if (c >> (level - 1)) & 1:
                begin = starts[c] - starts[(c >> (level - 1)) << (level - 1)]
                factor = jnp.exp(within[c] + begin) * dot(onehot, tables[level])
                read_ref[level, rows, :] = halves(factor, head_count)
            else:
                read_ref[level, rows, :] = jnp.zeros((CH, width), BF16)
        far = jnp.exp(within[c] + starts[c])
        for level in range(local + 1, levels):
            cross_ref[level - local - 1, rows, :] = far * dot(onehot, tables[level])
    kinds = merge_rows(stretches)
    exps = []
    for kind, c, k in kinds:
        first = c if kind == "own" else c + 1 - 2**k
        exps.append(jnp.exp(starts[c + 1] - starts[first]))
    exps += [jnp.zeros((1, width), F32)] * (merge_ref.shape[0] - len(exps))
    merge_ref[...] = halves(jnp.concatenate(exps, axis=0), head_count)


def partial_state_kernel(
    me_ref, even_ref, odd_ref, even_fade_ref, odd_fade_ref, in_ref, spread_ref, keep_ref, send_ref
):
    features = spread_ref.shape[1]
    tile = feature_tile(features)
    for f in range(0, features, tile):
        cols = slice(f, f + tile)
        spread = spread_ref[:, cols]
        odd = (dot(odd_fade_ref[0], spread) * odd_ref[:, cols].astype(F32)).astype(BF16)
        send_ref[0, :, cols] = dot_t(in_ref[...], odd).astype(BF16)
        even = (dot(even_fade_ref[0], spread) * even_ref[:, cols].astype(F32)).astype(BF16)
        keep_ref[0, :, cols] = dot_t(in_ref[...], even)


def local_kernel(
    me_ref, value_ref, in_ref, out_ref, lift_ref, read_ref, merge_ref, spread_ref, skip_ref,
    pre_ref, sums, operand
):
    tokens = in_ref.shape[0]
    rows_dev = value_ref.shape[1]
    me = me_ref[0]
    stretches = tokens // CH
    spread = spread_ref[...]
    merges = dot(merge_ref[...], spread)
    place = {kind: i for i, kind in enumerate(merge_rows(stretches))}
    row = lax.broadcasted_iota(jnp.int32, (CH, CH), 0)
    col = lax.broadcasted_iota(jnp.int32, (CH, CH), 1)
    causal = row >= col
    skip = skip_ref[...]
    for c in range(stretches):
        rows = slice(c * CH, (c + 1) * CH)
        block, first = divmod(c * CH, rows_dev)
        value = value_ref[me ^ block, first : first + CH, :].astype(F32)
        lifted = dot(lift_ref[rows, :], spread) * value
        high, low = two_parts(lifted)
        own_in, own_out = in_ref[rows, :], out_ref[rows, :]
        scores = jnp.where(causal, dot_nt(own_out, own_in), 0.0)
        s_high, s_low = two_parts(scores)
        direct = dot(
            jnp.concatenate([s_high, s_low, s_high], axis=1),
            jnp.concatenate([high, high, low], axis=0),
        )
        total = dot(read_ref[0, rows, :], spread) * direct + skip * value
        twice = jnp.concatenate([own_out, own_out], axis=1)
        level = 1
        while 2 ** (level - 1) < stretches:
            if (c >> (level - 1)) & 1:
                gained = dot(twice, operand[level - 1])
                total = total + dot(read_ref[level, rows, :], spread) * gained
            level += 1
        pre_ref[rows, :] = total
        if c + 1 < stretches:
            node = dot_t(
                jnp.concatenate([own_in, own_in], axis=0), jnp.concatenate([high, low], axis=0)
            )
            at = place[("own", c, 0)]
            node = node * merges[at : at + 1, :]
            k = 0
            while (c >> k) & 1:
                at = place[("merge", c, k)]
                node = node + merges[at : at + 1, :] * sums[k]
                k += 1
            sums[k] = node
            n_high, n_low = two_parts(node)
            operand[k] = jnp.concatenate([n_high, n_low], axis=0)


def finish_kernel(
    me_ref, pre_ref, out_ref, cross_ref, state_ref, spread_ref, same_ref, gain_ref, keep_ref, send_ref
):
    parts = pre_ref.shape[0]
    me = me_ref[0]
    spread = spread_ref[...]
    same = same_ref[...]
    gain = gain_ref[...]
    for r in range(parts):
        at = me ^ r
        total = pre_ref[at]
        readers = out_ref[at]
        for level in range(cross_ref.shape[0]):
            total = total + dot(cross_ref[level, at], spread) * dot(readers, state_ref[level])
        mean_square = dot((total * total).astype(BF16), same) * (1.0 / CH)
        normed = (total * lax.rsqrt(mean_square + EPSILON) * gain).astype(BF16)
        if r % 2 == 0:
            keep_ref[r // 2] = normed
        else:
            send_ref[r // 2] = normed


def assemble_kernel(me_ref, own_ref, far_ref, out_ref):
    blocks = own_ref.shape[0]
    width = own_ref.shape[2]
    me = me_ref[0]
    for j in range(blocks):
        at = me ^ j
        total = own_ref[at]
        for i in range(far_ref.shape[0]):
            total = total + far_ref[i, at].astype(F32)
        out_ref[:, j * width : (j + 1) * width] = total.astype(BF16)


def feature_tile(features):
    for tile in (256, 128):
        if features % tile == 0:
            return tile
    return features


def whole(shape):
    return pl.BlockSpec(shape, lambda *_: (0,) * len(shape))


def on_device(
    values,
    state_in,
    state_out,
    log_decay,
    level_class,
    level_table,
    skip_gain,
    norm_gain,
    out_weight,
):
    heads_size = lax.axis_size("head")
    ctx_size = lax.axis_size("ctx")
    ctx_bits = ctx_size.bit_length() - 1
    me = lax.axis_index("head")
    me1 = me.reshape(1).astype(jnp.int32)
    position = lax.axis_index("ctx")
    tokens = state_in.shape[0]
    rows_dev = values.shape[0]
    head_count = log_decay.shape[1]
    features = values.shape[1] // heads_size
    head_width = features // head_count
    state_size = state_in.shape[1]
    stretches = tokens // CH
    local = stretches.bit_length() - 1
    levels = level_table.shape[1]
    wide = 2 * head_count
    tile = feature_tile(features)
    tiles = features // tile
    half = heads_size // 2
    params = pltpu.CompilerParams(vmem_limit_bytes=VMEM_LIMIT)

    spread = (
        jnp.arange(wide)[:, None] % head_count == (jnp.arange(features) // head_width)[None, :]
    ).astype(BF16)
    same = (
        jnp.arange(tile)[:, None] // head_width == jnp.arange(tile)[None, :] // head_width
    ).astype(BF16)

    merge_count = -(-len(merge_rows(stretches)) // 16) * 16
    double = jnp.concatenate([log_decay, log_decay], axis=1)
    table = jnp.transpose(level_table, (1, 0, 2))
    table = jnp.concatenate([table, table], axis=2)
    fade, lift, read, cross, merge, total = pl.pallas_call(
        factors_kernel,
        out_shape=(
            jax.ShapeDtypeStruct((tokens, wide), BF16),
            jax.ShapeDtypeStruct((tokens, wide), BF16),
            jax.ShapeDtypeStruct((local + 1, tokens, wide), BF16),
            jax.ShapeDtypeStruct((levels - local - 1, tokens, wide), F32),
            jax.ShapeDtypeStruct((merge_count, wide), BF16),
            jax.ShapeDtypeStruct((1, wide), F32),
        ),
        compiler_params=params,
        name="factors",
    )(double, level_class.reshape(tokens, 1), table)

    def own_rows(array, owner):
        return lax.dynamic_slice_in_dim(array, owner * rows_dev, rows_dev, 0)

    fades = [own_rows(fade, me)]
    for r in range(1, heads_size):
        fades.append(swap(own_rows(fade, me ^ r), "head", r))
    even_fade = jnp.stack(fades[0::2])
    odd_fade = jnp.stack(fades[1::2])

    def head_columns(owner):
        return lax.dynamic_slice_in_dim(values, owner * features, features, 1)

    gathered = [head_columns(me)]
    for r in range(1, heads_size):
        gathered.append(swap(head_columns(me ^ r), "head", r))

    blocks = [out_weight] + [None] * (ctx_size - 1)
    for r in range(1, ctx_size):
        low = r & -r
        blocks[r] = swap(blocks[r ^ low], "ctx", low)
    partner_blocks = [swap(block, "head", 1) for block in blocks]

    keep, send = pl.pallas_call(
        partial_state_kernel,
        grid_spec=pltpu.PrefetchScalarGridSpec(
            num_scalar_prefetch=1,
            grid=(half,),
            in_specs=[
                pl.BlockSpec((rows_dev, features), lambda i, m: (0, m[0] ^ (2 * i))),
                pl.BlockSpec((rows_dev, features), lambda i, m: (0, m[0] ^ (2 * i + 1))),
                pl.BlockSpec((1, rows_dev, wide), lambda i, m: (i, 0, 0)),
                pl.BlockSpec((1, rows_dev, wide), lambda i, m: (i, 0, 0)),
                pl.BlockSpec((rows_dev, state_size), lambda i, m: (m[0], 0)),
                whole((wide, features)),
            ],
            out_specs=[
                pl.BlockSpec((1, state_size, features), lambda i, m: (i, 0, 0)),
                pl.BlockSpec((1, state_size, features), lambda i, m: (i, 0, 0)),
            ],
        ),
        out_shape=(
            jax.ShapeDtypeStruct((half, state_size, features), F32),
            jax.ShapeDtypeStruct((half, state_size, features), BF16),
        ),
        compiler_params=params,
        name="partial_states",
    )(me1, values, values, even_fade, odd_fade, state_in, spread)
    summed = keep + swap(send, "head", 1).astype(F32)
    running = summed[0]
    for i in range(1, half):
        running = running + swap(summed[i].astype(BF16), "head", 2 * i).astype(F32)

    totals = total
    for bit in range(ctx_bits):
        totals = jnp.concatenate([totals, swap(totals, "ctx", 2**bit)], axis=0)

    offset = jnp.zeros((wide,), F32)
    scaled = []
    states = []
    for bit in range(ctx_bits):
        upper = position // 2**bit % 2 == 1
        own_total = jnp.sum(totals[: 2**bit], axis=0)
        partner_total = jnp.sum(totals[2**bit : 2 ** (bit + 1)], axis=0)
        factor = jnp.where(upper, jnp.exp(offset), 0.0)
        scaled.append(halves(cross[bit] * factor[None, :], head_count))
        offset = jnp.where(upper, offset + partner_total, offset)
        sent = running.astype(BF16)
        partner = swap(sent, "ctx", 2**bit)
        states.append(partner)
        if bit + 1 < ctx_bits:
            on_partner = jnp.repeat(
                jnp.where(upper, jnp.exp(own_total), 1.0)[:head_count], head_width
            )
            on_own = jnp.repeat(
                jnp.where(upper, 1.0, jnp.exp(partner_total))[:head_count], head_width
            )
            running = on_own[None, :] * running + on_partner[None, :] * partner.astype(F32)
    crossed = jnp.stack(scaled).reshape(ctx_bits, heads_size, rows_dev, wide)
    all_states = jnp.stack(states)

    skip_row = jnp.repeat(skip_gain, head_width)[None, :]
    pre = pl.pallas_call(
        local_kernel,
        grid_spec=pltpu.PrefetchScalarGridSpec(
            num_scalar_prefetch=1,
            grid=(tiles,),
            in_specs=[
                pl.BlockSpec((heads_size, rows_dev, tile), lambda f, m: (0, 0, f)),
                whole((tokens, state_size)),
                whole((tokens, state_size)),
                whole((tokens, wide)),
                whole((local + 1, tokens, wide)),
                whole((merge_count, wide)),
                pl.BlockSpec((wide, tile), lambda f, m: (0, f)),
                pl.BlockSpec((1, tile), lambda f, m: (0, f)),
            ],
            out_specs=pl.BlockSpec((tokens, tile), lambda f, m: (0, f)),
            scratch_shapes=[
                pltpu.VMEM((max(local, 1), state_size, tile), F32),
                pltpu.VMEM((max(local, 1), 2 * state_size, tile), BF16),
            ],
        ),
        out_shape=jax.ShapeDtypeStruct((tokens, features), F32),
        compiler_params=params,
        name="local_levels",
    )(me1, jnp.stack(gathered), state_in, state_out, lift, read, merge, spread, skip_row)

    kept, sent = pl.pallas_call(
        finish_kernel,
        grid_spec=pltpu.PrefetchScalarGridSpec(
            num_scalar_prefetch=1,
            grid=(tiles,),
            in_specs=[
                pl.BlockSpec((heads_size, rows_dev, tile), lambda f, m: (0, 0, f)),
                whole((heads_size, rows_dev, state_size)),
                whole((ctx_bits, heads_size, rows_dev, wide)),
                pl.BlockSpec((ctx_bits, state_size, tile), lambda f, m: (0, 0, f)),
                pl.BlockSpec((wide, tile), lambda f, m: (0, f)),
                whole((tile, tile)),
                pl.BlockSpec((1, tile), lambda f, m: (0, f)),
            ],
            out_specs=[
                pl.BlockSpec((half, rows_dev, tile), lambda f, m: (0, 0, f)),
                pl.BlockSpec((half, rows_dev, tile), lambda f, m: (0, 0, f)),
            ],
        ),
        out_shape=(
            jax.ShapeDtypeStruct((half, rows_dev, features), BF16),
            jax.ShapeDtypeStruct((half, rows_dev, features), BF16),
        ),
        compiler_params=params,
        name="finish",
    )(
        me1,
        pre.reshape(heads_size, rows_dev, features),
        state_out.reshape(heads_size, rows_dev, state_size),
        crossed,
        all_states,
        spread,
        same,
        norm_gain[None, :],
    )
    other = swap(sent, "head", 1)

    own_sums = []
    far_sums = [[] for _ in range(1, half)]
    for r in range(ctx_size):
        for i in range(1, half):
            product = dot(kept[i], blocks[r]) + dot(other[i], partner_blocks[r])
            far_sums[i - 1].append(swap(product.astype(BF16), "head", 2 * i))
        own_sums.append(dot(kept[0], blocks[r]) + dot(other[0], partner_blocks[r]))
    columns = out_weight.shape[1]
    return pl.pallas_call(
        assemble_kernel,
        in_specs=[
            pl.BlockSpec(memory_space=pltpu.SMEM),
            pl.BlockSpec(memory_space=pltpu.VMEM),
            pl.BlockSpec(memory_space=pltpu.VMEM),
        ],
        out_shape=jax.ShapeDtypeStruct((rows_dev, ctx_size * columns), BF16),
        compiler_params=params,
        name="assemble",
    )(
        position.reshape(1).astype(jnp.int32),
        jnp.stack(own_sums),
        jnp.stack([jnp.stack(far) for far in far_sums]),
    )


def solution(mesh):
    return jax.shard_map(
        on_device,
        mesh=mesh,
        in_specs=(
            P(("ctx", "head"), None),
            P("ctx", None),
            P("ctx", None),
            P("ctx", "head"),
            P("ctx"),
            P(None, None, "head"),
            P("head"),
            P("head"),
            P("head", "ctx"),
        ),
        out_specs=P(("ctx", "head"), None),
        check_vma=False,
    )
```

```python
import jax
import jax.numpy as jnp
from jax import lax
from jax.experimental import pallas as pl
from jax.experimental.pallas import tpu as pltpu
from jax.sharding import PartitionSpec as P

CH = 64
EPSILON = 1e-05
F32 = jnp.float32
BF16 = jnp.bfloat16
VMEM_LIMIT = 32 * 1024 * 1024


def dot(a, b):
    return lax.dot_general(a, b, (((1,), (0,)), ((), ())), preferred_element_type=F32)


def dot_t(a, b):
    return lax.dot_general(a, b, (((0,), (0,)), ((), ())), preferred_element_type=F32)


def dot_nt(a, b):
    return lax.dot_general(a, b, (((1,), (1,)), ((), ())), preferred_element_type=F32)


def swap(value, axis, distance):
    pairs = [(source, source ^ distance) for source in range(lax.axis_size(axis))]
    return lax.ppermute(value, axis, pairs)


def tie(value, *after):
    return lax.optimization_barrier((value,) + after)[0]


def three_parts(x):
    high = x.astype(BF16)
    rest = x - high.astype(F32)
    middle = rest.astype(BF16)
    low = (rest - middle.astype(F32)).astype(BF16)
    return high, middle, low


def two_parts(x):
    high = x.astype(BF16)
    return high, (x - high.astype(F32)).astype(BF16)


def halves(x, head_count):
    high = x.astype(BF16).astype(F32)
    lane = lax.broadcasted_iota(jnp.int32, x.shape, x.ndim - 1)
    return jnp.where(lane < head_count, high, x - high).astype(BF16)


def merge_rows(stretches):
    rows = [("own", c, 0) for c in range(stretches - 1)]
    for c in range(stretches - 1):
        k = 0
        while (c >> k) & 1:
            rows.append(("merge", c, k))
            k += 1
    return rows


def stretch_sums(decay_ref):
    tokens, width = decay_ref.shape
    row = lax.broadcasted_iota(jnp.int32, (CH, CH), 0)
    col = lax.broadcasted_iota(jnp.int32, (CH, CH), 1)
    lower = jnp.where(row >= col, 1.0, 0.0).astype(BF16)
    lower = jnp.concatenate([lower] * 3, axis=1)
    within, starts = [], [jnp.zeros((1, width), F32)]
    for c in range(tokens // CH):
        parts = jnp.concatenate(three_parts(decay_ref[c * CH : (c + 1) * CH, :]), axis=0)
        summed = dot(lower, parts)
        within.append(summed)
        starts.append(starts[-1] + summed[CH - 1 : CH, :])
    return within, starts


def fade_kernel(decay_ref, fade_ref, total_ref):
    head_count = decay_ref.shape[1] // 2
    within, starts = stretch_sums(decay_ref)
    total_ref[...] = starts[-1]
    for c, summed in enumerate(within):
        left = starts[-1] - starts[c] - summed
        fade_ref[c * CH : (c + 1) * CH, :] = halves(jnp.exp(left), head_count)


def factors_kernel(
    decay_ref, class_ref, table_ref, in_ref, out_ref,
    lift_ref, read_ref, cross_ref, merge_ref, score_ref, masked_ref,
):
    tokens, width = decay_ref.shape
    head_count = width // 2
    stretches = tokens // CH
    levels, classes, _ = table_ref.shape
    local = read_ref.shape[0] - 1
    tables = [jnp.concatenate(three_parts(table_ref[level]), axis=0) for level in range(levels)]
    within, starts = stretch_sums(decay_ref)
    class_iota = lax.broadcasted_iota(jnp.int32, (CH, 3 * classes), 1) % classes
    for c in range(stretches):
        rows = slice(c * CH, (c + 1) * CH)
        lift_ref[rows, :] = halves(jnp.exp(-within[c]), head_count)
        onehot = jnp.where(class_ref[rows, :] == class_iota, 1.0, 0.0).astype(BF16)
        read_ref[0, rows, :] = halves(jnp.exp(within[c]) * dot(onehot, tables[0]), head_count)
        for level in range(1, local + 1):
            if (c >> (level - 1)) & 1:
                begin = starts[c] - starts[(c >> (level - 1)) << (level - 1)]
                factor = jnp.exp(within[c] + begin) * dot(onehot, tables[level])
                read_ref[level, rows, :] = halves(factor, head_count)
            else:
                read_ref[level, rows, :] = jnp.zeros((CH, width), BF16)
        far = jnp.exp(within[c] + starts[c])
        for level in range(local + 1, levels):
            cross_ref[level - local - 1, rows, :] = far * dot(onehot, tables[level])
    exps = []
    for kind, c, k in merge_rows(stretches):
        first = c if kind == "own" else c + 1 - 2**k
        exps.append(jnp.exp(starts[c + 1] - starts[first]))
    exps += [jnp.zeros((1, width), F32)] * (merge_ref.shape[0] - len(exps))
    merge_ref[...] = halves(jnp.concatenate(exps, axis=0), head_count)
    groups, _, group_rows, _ = score_ref.shape
    row = lax.broadcasted_iota(jnp.int32, (group_rows, group_rows), 0)
    col = lax.broadcasted_iota(jnp.int32, (group_rows, group_rows), 1)
    inside = (row // CH == col // CH) & (row >= col)
    state_size = in_ref.shape[1]
    lane = lax.broadcasted_iota(jnp.int32, (state_size, group_rows), 1) // CH
    for g in range(groups):
        rows = slice(g * group_rows, (g + 1) * group_rows)
        scores = jnp.where(inside, dot_nt(out_ref[rows, :], in_ref[rows, :]), 0.0)
        score_ref[g, 0], score_ref[g, 1] = two_parts(scores)
        turned = jnp.transpose(in_ref[rows, :].astype(F32))
        for s in range(group_rows // CH):
            at = slice(s * state_size, (s + 1) * state_size)
            masked_ref[g, at, :] = jnp.where(lane == s, turned, 0.0).astype(BF16)


def partial_state_kernel(
    me_ref, even_ref, odd_ref, even_fade_ref, odd_fade_ref, in_ref, spread_ref, keep_ref, send_ref
):
    spread = spread_ref[...]
    turned = in_ref[...]
    odd = (dot(odd_fade_ref[0], spread) * odd_ref[...].astype(F32)).astype(BF16)
    send_ref[0] = dot(turned, odd).astype(BF16)
    even = (dot(even_fade_ref[0], spread) * even_ref[...].astype(F32)).astype(BF16)
    keep_ref[0] = dot(turned, even)


def local_kernel(
    me_ref, value_ref, out_ref, lift_ref, read_ref, merge_ref, score_ref, masked_ref, spread_ref,
    skip_ref, cross_ref, state_ref, pre_ref, sums, operand
):
    groups, group_rows, _ = value_ref.shape
    me = me_ref[0]
    per_group = group_rows // CH
    stretches = groups * per_group
    state_size = out_ref.shape[1]
    spread = spread_ref[...]
    merges = dot(merge_ref[...], spread)
    place = {kind: i for i, kind in enumerate(merge_rows(stretches))}
    skip = skip_ref[...]
    for g in range(groups):
        rows = slice(g * group_rows, (g + 1) * group_rows)
        value = value_ref[me ^ g].astype(F32)
        high, low = two_parts(dot(lift_ref[rows, :], spread) * value)
        direct = dot(score_ref[g, 0], high) + dot(score_ref[g, 0], low) + dot(score_ref[g, 1], high)
        total = dot(read_ref[0, rows, :], spread) * direct + skip * value
        for level in range(state_ref.shape[0]):
            gained = dot(out_ref[rows, :], state_ref[level])
            total = total + dot(cross_ref[level, rows, :], spread) * gained
        pre_ref[rows, :] = total
        nodes = dot(masked_ref[g], high) + dot(masked_ref[g], low)
        level = 1
        while 2 ** (level - 1) < stretches:
            span = 2 ** (level - 1)
            for first in range(g * per_group, (g + 1) * per_group, max(span, 1)):
                count = min(span, per_group)
                if (first >> (level - 1)) & 1 and span >= per_group:
                    at = slice(first * CH, (first + count) * CH)
                    readers = out_ref[at, :]
                    twice = jnp.concatenate([readers, readers], axis=1)
                    gained = dot(twice, operand[level - 1])
                    pre_ref[at, :] += dot(read_ref[level, at, :], spread) * gained
            level += 1
        for s in range(per_group):
            c = g * per_group + s
            at = slice(c * CH, (c + 1) * CH)
            level = 1
            while 2 ** (level - 1) < per_group:
                span = 2 ** (level - 1)
                if c % (2 * span) == span:
                    where = slice(c * CH, (c + span) * CH)
                    readers = out_ref[where, :]
                    twice = jnp.concatenate([readers, readers], axis=1)
                    gained = dot(twice, operand[level - 1])
                    pre_ref[where, :] += dot(read_ref[level, where, :], spread) * gained
                level += 1
            if c + 1 < stretches:
                row = place[("own", c, 0)]
                node = nodes[s * state_size : (s + 1) * state_size, :] * merges[row : row + 1, :]
                k = 0
                while (c >> k) & 1:
                    row = place[("merge", c, k)]
                    node = node + merges[row : row + 1, :] * sums[k]
                    k += 1
                sums[k] = node
                n_high, n_low = two_parts(node)
                operand[k, :state_size, :] = n_high
                operand[k, state_size:, :] = n_low


def finish_kernel(
    me_ref, pre_ref, out_ref, cross_ref, state_ref, spread_ref, same_ref, gain_ref, keep_ref, send_ref
):
    parts = pre_ref.shape[0]
    me = me_ref[0]
    spread = spread_ref[...]
    same = same_ref[...]
    gain = gain_ref[...]
    state = state_ref[...]
    for r in range(parts):
        at = me ^ r
        total = pre_ref[at] + dot(cross_ref[at], spread) * dot(out_ref[at], state)
        mean_square = dot((total * total).astype(BF16), same)
        normed = (total * lax.rsqrt(mean_square + EPSILON) * gain).astype(BF16)
        if r % 2 == 0:
            keep_ref[r // 2] = normed
        else:
            send_ref[r // 2] = normed


def project_kernel(place_ref, kept_ref, other_ref, *refs):
    far_ref, own_ref = refs[-2:]
    count = (len(refs) - 2) // 2
    weights, partners = refs[:count], refs[count:-2]
    half = kept_ref.shape[0]
    width = weights[0].shape[0]
    for i in list(range(1, half)) + [0]:
        kept, other = kept_ref[i], other_ref[i]
        found = [
            dot_nt(kept, weight[...]) + dot_nt(other, partner[...])
            for weight, partner in zip(weights, partners)
        ]
        for bit in range(count.bit_length() - 1):
            turn = place_ref[0] // 2**bit % 2 == 1
            found = [jnp.where(turn, found[j ^ 2**bit], found[j]) for j in range(count)]
        for j, result in enumerate(found):
            if i > 0:
                far_ref[i - 1, :, j * width : (j + 1) * width] = result.astype(BF16)
            else:
                own_ref[:, j * width : (j + 1) * width] = result


def assemble_kernel(place_ref, *refs):
    out_ref = refs[-1]
    width = refs[0].shape[1]
    groups = out_ref.shape[1] // width
    each = (len(refs) - 1) // groups
    for p in range(groups):
        own_ref, *far_refs = refs[p * each : (p + 1) * each]
        total = own_ref[...]
        for far_ref in far_refs:
            total = total + far_ref[...].astype(F32)
        start = pl.multiple_of((place_ref[0] ^ p) * width, width)
        out_ref[:, pl.ds(start, width)] = total.astype(BF16)


def feature_tile(features):
    for tile in (256, 128):
        if features % tile == 0:
            return tile
    return features


def whole(shape):
    return pl.BlockSpec(shape, lambda *_: (0,) * len(shape))


def on_device(
    values,
    state_in,
    state_out,
    log_decay,
    level_class,
    level_table,
    skip_gain,
    norm_gain,
    out_weight,
):
    heads_size = lax.axis_size("head")
    ctx_size = lax.axis_size("ctx")
    ctx_bits = ctx_size.bit_length() - 1
    me = lax.axis_index("head")
    me1 = me.reshape(1).astype(jnp.int32)
    position = lax.axis_index("ctx")
    tokens = state_in.shape[0]
    rows_dev = values.shape[0]
    head_count = log_decay.shape[1]
    features = values.shape[1] // heads_size
    head_width = features // head_count
    state_size = state_in.shape[1]
    stretches = tokens // CH
    local = stretches.bit_length() - 1
    levels = level_table.shape[1]
    wide = 2 * head_count
    tile = feature_tile(features)
    tiles = features // tile
    half = heads_size // 2
    params = pltpu.CompilerParams(vmem_limit_bytes=VMEM_LIMIT)
    cheap = pl.CostEstimate(flops=0, bytes_accessed=0, transcendentals=0)

    spread = (
        jnp.arange(wide)[:, None] % head_count == (jnp.arange(features) // head_width)[None, :]
    ).astype(BF16)
    same = (
        (jnp.arange(tile)[:, None] // head_width == jnp.arange(tile)[None, :] // head_width)
        / head_width
    ).astype(BF16)

    blocks = [out_weight.T] + [None] * (ctx_size - 1)
    for bit in range(ctx_bits):
        blocks[2**bit] = swap(blocks[0], "ctx", 2**bit)

    def head_columns(owner):
        return lax.dynamic_slice_in_dim(values, owner * features, features, 1)

    def value_swap(r, after=None):
        sent = head_columns(me ^ r)
        return swap(sent if after is None else tie(sent, after), "head", r)

    gathered = [head_columns(me)] + [None] * (heads_size - 1)
    early = [r for r in range(1, heads_size) if r <= half]
    for r in early:
        gathered[r] = value_swap(r)

    merge_count = -(-len(merge_rows(stretches)) // 16) * 16
    double = jnp.concatenate([log_decay, log_decay], axis=1)
    fade, total = pl.pallas_call(
        fade_kernel,
        out_shape=(
            jax.ShapeDtypeStruct((tokens, wide), BF16),
            jax.ShapeDtypeStruct((1, wide), F32),
        ),
        compiler_params=params,
        cost_estimate=cheap,
        name="fade",
    )(double)

    def own_rows(array, owner):
        return lax.dynamic_slice_in_dim(array, owner * rows_dev, rows_dev, 0)

    fades = [own_rows(fade, me)]
    for r in range(1, heads_size):
        fades.append(swap(own_rows(fade, me ^ r), "head", r))
    even_fade = jnp.stack(fades[0::2])
    odd_fade = jnp.stack(fades[1::2])
    in_turned = own_rows(state_in, me).T

    keep, send = pl.pallas_call(
        partial_state_kernel,
        grid_spec=pltpu.PrefetchScalarGridSpec(
            num_scalar_prefetch=1,
            grid=(half,),
            in_specs=[
                pl.BlockSpec((rows_dev, features), lambda i, m: (0, m[0] ^ (2 * i))),
                pl.BlockSpec((rows_dev, features), lambda i, m: (0, m[0] ^ (2 * i + 1))),
                pl.BlockSpec((1, rows_dev, wide), lambda i, m: (i, 0, 0)),
                pl.BlockSpec((1, rows_dev, wide), lambda i, m: (i, 0, 0)),
                whole((state_size, rows_dev)),
                whole((wide, features)),
            ],
            out_specs=[
                pl.BlockSpec((1, state_size, features), lambda i, m: (i, 0, 0)),
                pl.BlockSpec((1, state_size, features), lambda i, m: (i, 0, 0)),
            ],
        ),
        out_shape=(
            jax.ShapeDtypeStruct((half, state_size, features), F32),
            jax.ShapeDtypeStruct((half, state_size, features), BF16),
        ),
        compiler_params=params,
        cost_estimate=cheap,
        name="partial_states",
    )(me1, values, values, even_fade, odd_fade, in_turned, spread)
    summed = keep + swap(send, "head", 1).astype(F32)
    running = summed[0]
    for i in range(1, half):
        running = running + swap(summed[i].astype(BF16), "head", 2 * i).astype(F32)

    table = jnp.transpose(level_table, (1, 0, 2))
    table = jnp.concatenate([table, table], axis=2)
    lift, read, cross, merge, scores, masked = pl.pallas_call(
        factors_kernel,
        out_shape=(
            jax.ShapeDtypeStruct((tokens, wide), BF16),
            jax.ShapeDtypeStruct((local + 1, tokens, wide), BF16),
            jax.ShapeDtypeStruct((levels - local - 1, tokens, wide), F32),
            jax.ShapeDtypeStruct((merge_count, wide), BF16),
            jax.ShapeDtypeStruct((heads_size, 2, rows_dev, rows_dev), BF16),
            jax.ShapeDtypeStruct((heads_size, rows_dev // CH * state_size, rows_dev), BF16),
        ),
        compiler_params=params,
        cost_estimate=cheap,
        name="factors",
    )(double, level_class.reshape(tokens, 1), table, state_in, state_out)

    totals = total
    for bit in range(ctx_bits):
        totals = jnp.concatenate([totals, swap(totals, "ctx", 2**bit)], axis=0)

    for r in range(1, heads_size):
        if r not in early:
            gathered[r] = value_swap(r, running)

    offset = jnp.zeros((wide,), F32)
    scaled = []
    states = []
    for bit in range(ctx_bits):
        upper = position // 2**bit % 2 == 1
        own_total = jnp.sum(totals[: 2**bit], axis=0)
        partner_total = jnp.sum(totals[2**bit : 2 ** (bit + 1)], axis=0)
        factor = jnp.where(upper, jnp.exp(offset), 0.0)
        scaled.append(halves(cross[bit] * factor[None, :], head_count))
        offset = jnp.where(upper, offset + partner_total, offset)
        sent = running.astype(BF16)
        if bit + 1 < ctx_bits:
            sent = tie(sent, blocks[2**bit])
        partner = swap(sent, "ctx", 2**bit)
        states.append(partner)
        if bit + 1 < ctx_bits:
            on_partner = jnp.repeat(
                jnp.where(upper, jnp.exp(own_total), 1.0)[:head_count], head_width
            )
            on_own = jnp.repeat(
                jnp.where(upper, 1.0, jnp.exp(partner_total))[:head_count], head_width
            )
            running = on_own[None, :] * running + on_partner[None, :] * partner.astype(F32)

    for r in range(1, ctx_size):
        if blocks[r] is None:
            low = r & -r
            held = blocks[r ^ low]
            step = low.bit_length() - 1
            held = tie(held, states[step]) if step + 1 < ctx_bits else held
            blocks[r] = swap(held, "ctx", low)
    partner_blocks = [swap(block, "head", 1) for block in blocks]

    skip_row = jnp.repeat(skip_gain, head_width)[None, :]
    near = ctx_bits - 1
    pre = pl.pallas_call(
        local_kernel,
        grid_spec=pltpu.PrefetchScalarGridSpec(
            num_scalar_prefetch=1,
            grid=(tiles,),
            in_specs=[
                pl.BlockSpec((heads_size, rows_dev, tile), lambda f, m: (0, 0, f)),
                whole((tokens, state_size)),
                whole((tokens, wide)),
                whole((local + 1, tokens, wide)),
                whole((merge_count, wide)),
                whole(scores.shape),
                whole(masked.shape),
                pl.BlockSpec((wide, tile), lambda f, m: (0, f)),
                pl.BlockSpec((1, tile), lambda f, m: (0, f)),
                whole((near, tokens, wide)),
                pl.BlockSpec((near, state_size, tile), lambda f, m: (0, 0, f)),
            ],
            out_specs=pl.BlockSpec((tokens, tile), lambda f, m: (0, f)),
            scratch_shapes=[
                pltpu.VMEM((max(local, 1), state_size, tile), F32),
                pltpu.VMEM((max(local, 1), 2 * state_size, tile), BF16),
            ],
        ),
        out_shape=jax.ShapeDtypeStruct((tokens, features), F32),
        compiler_params=params,
        cost_estimate=cheap,
        name="local_levels",
    )(
        me1, jnp.stack(gathered), state_out, lift, read, merge, scores, masked, spread, skip_row,
        jnp.stack(scaled[:near]), jnp.stack(states[:near]),
    )

    kept, sent = pl.pallas_call(
        finish_kernel,
        grid_spec=pltpu.PrefetchScalarGridSpec(
            num_scalar_prefetch=1,
            grid=(tiles,),
            in_specs=[
                pl.BlockSpec((heads_size, rows_dev, tile), lambda f, m: (0, 0, f)),
                whole((heads_size, rows_dev, state_size)),
                whole((heads_size, rows_dev, wide)),
                pl.BlockSpec((state_size, tile), lambda f, m: (0, f)),
                pl.BlockSpec((wide, tile), lambda f, m: (0, f)),
                whole((tile, tile)),
                pl.BlockSpec((1, tile), lambda f, m: (0, f)),
            ],
            out_specs=[
                pl.BlockSpec((half, rows_dev, tile), lambda f, m: (0, 0, f)),
                pl.BlockSpec((half, rows_dev, tile), lambda f, m: (0, 0, f)),
            ],
        ),
        out_shape=(
            jax.ShapeDtypeStruct((half, rows_dev, features), BF16),
            jax.ShapeDtypeStruct((half, rows_dev, features), BF16),
        ),
        compiler_params=params,
        cost_estimate=cheap,
        name="finish",
    )(
        me1,
        pre.reshape(heads_size, rows_dev, features),
        state_out.reshape(heads_size, rows_dev, state_size),
        scaled[-1].reshape(heads_size, rows_dev, wide),
        states[-1],
        spread,
        same,
        norm_gain[None, :],
    )
    other = swap(sent, "head", 1)

    columns = out_weight.shape[1]
    count = 1
    while count * columns % 128 and 2 * count <= ctx_size:
        count *= 2
    place1 = position.reshape(1).astype(jnp.int32)
    smem = pl.BlockSpec(memory_space=pltpu.SMEM)
    vmem = pl.BlockSpec(memory_space=pltpu.VMEM)
    pieces = []
    for r in range(0, ctx_size, count):
        far, own = pl.pallas_call(
            project_kernel,
            in_specs=[smem] + [vmem] * (2 + 2 * count),
            out_shape=(
                jax.ShapeDtypeStruct((half - 1, rows_dev, count * columns), BF16),
                jax.ShapeDtypeStruct((rows_dev, count * columns), F32),
            ),
            compiler_params=params,
            cost_estimate=cheap,
            name="project",
        )(place1, kept, other, *blocks[r : r + count], *partner_blocks[r : r + count])
        pieces.append(own)
        pieces += [swap(far[i - 1], "head", 2 * i) for i in range(1, half)]
    return pl.pallas_call(
        assemble_kernel,
        in_specs=[smem] + [vmem] * len(pieces),
        out_shape=jax.ShapeDtypeStruct((rows_dev, ctx_size * columns), BF16),
        compiler_params=params,
        cost_estimate=cheap,
        name="assemble",
    )(place1 // count, *pieces)


def solution(mesh):
    return jax.shard_map(
        on_device,
        mesh=mesh,
        in_specs=(
            P(("ctx", "head"), None),
            P("ctx", None),
            P("ctx", None),
            P("ctx", "head"),
            P("ctx"),
            P(None, None, "head"),
            P("head"),
            P("head"),
            P("head", "ctx"),
        ),
        out_specs=P(("ctx", "head"), None),
        check_vma=False,
    )
```

```python
import functools

import jax
import jax.numpy as jnp
from jax import lax
from jax.experimental import pallas as pl
from jax.experimental.pallas import tpu as pltpu
from jax.sharding import PartitionSpec as P

CH = 64
EPSILON = 1e-05
EXTRA = 16
F32 = jnp.float32
BF16 = jnp.bfloat16
VMEM_LIMIT = 32 * 1024 * 1024


def dot(a, b):
    return lax.dot_general(a, b, (((1,), (0,)), ((), ())), preferred_element_type=F32)


def dot_t(a, b):
    return lax.dot_general(a, b, (((0,), (0,)), ((), ())), preferred_element_type=F32)


def dot_nt(a, b):
    return lax.dot_general(a, b, (((1,), (1,)), ((), ())), preferred_element_type=F32)


def swap(value, axis, distance):
    pairs = [(source, source ^ distance) for source in range(lax.axis_size(axis))]
    return lax.ppermute(value, axis, pairs)


def tie(value, *after):
    return lax.optimization_barrier((value,) + after)[0]


def three_parts(x):
    high = x.astype(BF16)
    rest = x - high.astype(F32)
    middle = rest.astype(BF16)
    low = (rest - middle.astype(F32)).astype(BF16)
    return high, middle, low


def two_parts(x):
    high = x.astype(BF16)
    return high, (x - high.astype(F32)).astype(BF16)


def halves(x, head_count):
    high = x.astype(BF16).astype(F32)
    lane = lax.broadcasted_iota(jnp.int32, x.shape, x.ndim - 1)
    return jnp.where(lane < head_count, high, x - high).astype(BF16)


def merge_rows(stretches):
    rows = [("own", c, 0) for c in range(stretches - 1)]
    for c in range(stretches - 1):
        k = 0
        while (c >> k) & 1:
            rows.append(("merge", c, k))
            k += 1
    return rows


def stretch_sums(decay_ref):
    tokens, width = decay_ref.shape
    row = lax.broadcasted_iota(jnp.int32, (CH, CH), 0)
    col = lax.broadcasted_iota(jnp.int32, (CH, CH), 1)
    lower = jnp.where(row >= col, 1.0, 0.0).astype(BF16)
    lower = jnp.concatenate([lower] * 3, axis=1)
    within, starts = [], [jnp.zeros((1, width), F32)]
    for c in range(tokens // CH):
        parts = jnp.concatenate(three_parts(decay_ref[c * CH : (c + 1) * CH, :]), axis=0)
        summed = dot(lower, parts)
        within.append(summed)
        starts.append(starts[-1] + summed[CH - 1 : CH, :])
    return within, starts


def fade_kernel(me_ref, decay_ref, *refs):
    fade_refs, total_ref = refs[:-1], refs[-1]
    head_count = decay_ref.shape[1]
    rows_dev = fade_refs[0].shape[0]
    within, starts = stretch_sums(decay_ref)
    total = starts[-1]
    total_ref[...] = jnp.concatenate([total, total], axis=1)
    blocks = len(fade_refs)
    per_block = rows_dev // CH
    me = me_ref[0]
    for block in range(blocks):
        parts = []
        for c in range(block * per_block, (block + 1) * per_block):
            factor = jnp.exp(total - starts[c] - within[c])
            parts.append(halves(jnp.concatenate([factor, factor], axis=1), head_count))
        fade = jnp.concatenate(parts, axis=0)
        for r, fade_ref in enumerate(fade_refs):

            @pl.when((me ^ r) == block)
            def _():
                fade_ref[...] = fade


def factors_kernel(
    decay_ref, class_ref, table_ref, in_ref, out_ref,
    lift_ref, read_ref, cross_ref, merge_ref, score_ref, masked_ref,
):
    tokens, head_count = decay_ref.shape
    width = 2 * head_count
    stretches = tokens // CH
    levels, classes, _ = table_ref.shape
    local = read_ref.shape[0] - 1
    tables = [jnp.concatenate(three_parts(table_ref[level]), axis=0) for level in range(levels)]
    within, starts = stretch_sums(decay_ref)
    within = [jnp.concatenate([x, x], axis=1) for x in within]
    starts = [jnp.concatenate([x, x], axis=1) for x in starts]
    class_iota = lax.broadcasted_iota(jnp.int32, (CH, 3 * classes), 1) % classes
    for c in range(stretches):
        rows = slice(c * CH, (c + 1) * CH)
        lift_ref[rows, :] = halves(jnp.exp(-within[c]), head_count)
        onehot = jnp.where(class_ref[rows, :] == class_iota, 1.0, 0.0).astype(BF16)
        read_ref[0, rows, :] = halves(jnp.exp(within[c]) * dot(onehot, tables[0]), head_count)
        for level in range(1, local + 1):
            if (c >> (level - 1)) & 1:
                begin = starts[c] - starts[(c >> (level - 1)) << (level - 1)]
                factor = jnp.exp(within[c] + begin) * dot(onehot, tables[level])
                read_ref[level, rows, :] = halves(factor, head_count)
            else:
                read_ref[level, rows, :] = jnp.zeros((CH, width), BF16)
        far = jnp.exp(within[c] + starts[c])
        for level in range(local + 1, levels):
            far_factor = far * dot(onehot, tables[level])
            cross_ref[level - local - 1, rows, :] = halves(far_factor, head_count)
    exps = []
    for kind, c, k in merge_rows(stretches):
        first = c if kind == "own" else c + 1 - 2**k
        exps.append(jnp.exp(starts[c + 1] - starts[first]))
    exps += [jnp.zeros((1, width), F32)] * (merge_ref.shape[0] - len(exps))
    merge_ref[...] = halves(jnp.concatenate(exps, axis=0), head_count)
    groups, _, group_rows, _ = score_ref.shape
    row = lax.broadcasted_iota(jnp.int32, (group_rows, group_rows), 0)
    col = lax.broadcasted_iota(jnp.int32, (group_rows, group_rows), 1)
    inside = (row // CH == col // CH) & (row >= col)
    state_size = in_ref.shape[1]
    lane = lax.broadcasted_iota(jnp.int32, (state_size, group_rows), 1) // CH
    for g in range(groups):
        rows = slice(g * group_rows, (g + 1) * group_rows)
        scores = jnp.where(inside, dot_nt(out_ref[rows, :], in_ref[rows, :]), 0.0)
        score_ref[g, 0], score_ref[g, 1] = two_parts(scores)
        turned = jnp.transpose(in_ref[rows, :].astype(F32))
        for s in range(group_rows // CH):
            at = slice(s * state_size, (s + 1) * state_size)
            masked_ref[g, at, :] = jnp.where(lane == s, turned, 0.0).astype(BF16)


def partial_state_kernel(me_ref, *refs):
    even_ref, odd_ref, *fade_refs = refs[:-4]
    in_ref, spread_ref, keep_ref, send_ref = refs[-4:]
    spread = spread_ref[...]
    turned = in_ref[...]
    for i in range(len(fade_refs) // 2):

        @pl.when(pl.program_id(0) == i)
        def _():
            odd = (dot(fade_refs[2 * i + 1][...], spread) * odd_ref[...].astype(F32)).astype(BF16)
            send_ref[0] = dot(turned, odd).astype(BF16)
            even = (dot(fade_refs[2 * i][...], spread) * even_ref[...].astype(F32)).astype(BF16)
            keep_ref[0] = dot(turned, even)


def fold_kernel(keep_ref, got_ref, own_ref, *far_refs):
    own_ref[...] = keep_ref[0] + got_ref[0].astype(F32)
    for i, far_ref in enumerate(far_refs):
        far_ref[...] = (keep_ref[i + 1] + got_ref[i + 1].astype(F32)).astype(BF16)


def pack_state(sent_ref, state, total):
    rows, width = state.shape[0], total.shape[1]
    sent_ref[:rows, :] = state.astype(BF16)
    sent_ref[rows:, :] = jnp.zeros((EXTRA, state.shape[1]), BF16)
    parts = list(three_parts(total))
    parts.append(jnp.zeros((EXTRA - len(parts), width), BF16))
    sent_ref[rows:, :width] = jnp.concatenate(parts, axis=0)


def first_kernel(own_ref, total_ref, *refs):
    *far_refs, running_ref, sent_ref = refs
    running = own_ref[...]
    for far_ref in far_refs:
        running = running + far_ref[...].astype(F32)
    running_ref[...] = running
    pack_state(sent_ref, running, total_ref[...])


def merge_kernel(
    bit, place_ref, running_ref, total_ref, offset_ref, got_ref, spread_ref,
    next_running_ref, next_total_ref, next_offset_ref, factor_ref, sent_ref,
):
    rows, width = running_ref.shape[0], total_ref.shape[1]
    head_count = width // 2
    place = place_ref[0]
    upper = place // 2**bit % 2 == 1
    total = total_ref[...]
    parts = got_ref[rows:, :width].astype(F32)
    partner = parts[0:1] + parts[1:2] + parts[2:3]
    fading = jnp.exp(jnp.where(upper, total, partner))
    fading = halves(jnp.broadcast_to(fading, (EXTRA, width)), head_count)
    fading = dot(fading, spread_ref[...])[0:1, :]
    got, running = got_ref[:rows, :].astype(F32), running_ref[...]
    merged = fading * jnp.where(upper, got, running) + jnp.where(upper, running, got)
    next_running_ref[...] = merged
    joined = total + partner
    next_total_ref[...] = joined
    offset = jnp.where(upper, offset_ref[...] + partner, offset_ref[...])
    next_offset_ref[...] = offset
    next_upper = place // 2 ** (bit + 1) % 2 == 1
    factor = jnp.where(next_upper, jnp.exp(offset), 0.0)
    factor_ref[...] = halves(jnp.broadcast_to(factor, (EXTRA, width)), head_count)
    pack_state(sent_ref, merged, joined)


def local_kernel(me_ref, near, parts, *refs):
    value_refs, refs = refs[:parts], refs[parts:]
    out_ref, lift_ref, read_ref, merge_ref, score_ref, masked_ref, spread_ref = refs[:7]
    skip_ref, cross_ref, *refs = refs[7:]
    factor_refs, state_refs, refs = refs[:near], refs[near : 2 * near], refs[2 * near :]
    pre_ref, nodes, sums, operand = refs
    group_rows = value_refs[0].shape[0]
    groups = len(value_refs)
    me = me_ref[0]
    per_group = group_rows // CH
    stretches = groups * per_group
    state_size = out_ref.shape[2]
    spread = spread_ref[...]
    merges = dot(merge_ref[...], spread)
    place = {kind: i for i, kind in enumerate(merge_rows(stretches))}
    skip = skip_ref[...]
    states = [
        (state_ref[:state_size, :], dot(factor_ref[...], spread)[0:1, :])
        for state_ref, factor_ref in zip(state_refs, factor_refs)
    ]
    for r, value_ref in enumerate(value_refs):
        g = me ^ r
        value = value_ref[...].astype(F32)
        high, low = two_parts(dot(lift_ref[g], spread) * value)
        direct = dot(score_ref[g, 0], high) + dot(score_ref[g, 0], low) + dot(score_ref[g, 1], high)
        total = dot(read_ref[0, g], spread) * direct + skip * value
        for level, (state, row) in enumerate(states):
            total = total + dot(cross_ref[level, g], spread) * (dot(out_ref[g], state) * row)
        pre_ref[g] = total
        nodes[g] = dot(masked_ref[g], high) + dot(masked_ref[g], low)

    def gain(level, g, first, count):
        at = slice(first * CH, (first + count) * CH)
        readers = out_ref[g, at, :]
        twice = jnp.concatenate([readers, readers], axis=1)
        gained = dot(twice, operand[level - 1])
        pre_ref[g, at, :] += dot(read_ref[level, g, at, :], spread) * gained

    for c in range(stretches):
        g, s = divmod(c, per_group)
        level = 1
        while 2 ** (level - 1) < stretches:
            span = 2 ** (level - 1)
            if c % (2 * span) == span:
                for other in range(c, c + span, per_group):
                    gain(level, other // per_group, other % per_group, min(span, per_group))
            level += 1
        if c + 1 < stretches:
            row = place[("own", c, 0)]
            node = nodes[g, s * state_size : (s + 1) * state_size, :] * merges[row : row + 1, :]
            k = 0
            while (c >> k) & 1:
                row = place[("merge", c, k)]
                node = node + merges[row : row + 1, :] * sums[k]
                k += 1
            sums[k] = node
            n_high, n_low = two_parts(node)
            operand[k, :state_size, :] = n_high
            operand[k, state_size:, :] = n_low


def finish_kernel(
    me_ref, pre_ref, out_ref, cross_ref, factor_ref, state_ref, spread_ref, same_ref, gain_ref, *refs
):
    keep_ref, send_refs = refs[0], refs[1:]
    parts = pre_ref.shape[0]
    me = me_ref[0]
    spread = spread_ref[...]
    same = same_ref[...]
    gain = gain_ref[...]
    state = state_ref[: out_ref.shape[2], :]
    row = dot(factor_ref[...], spread)[0:1, :]
    for r in range(parts):
        at = me ^ r
        total = pre_ref[at] + dot(cross_ref[at], spread) * (dot(out_ref[at], state) * row)
        mean_square = dot((total * total).astype(BF16), same)
        normed = (total * lax.rsqrt(mean_square + EPSILON) * gain).astype(BF16)
        if r % 2 == 0:
            keep_ref[r // 2] = normed
        else:
            send_refs[r // 2][...] = normed


def project_kernel(place_ref, kept_ref, *refs):
    far_ref, own_ref = refs[-2:]
    half = kept_ref.shape[0]
    other_refs, refs = refs[:half], refs[half:-2]
    count = len(refs) // 2
    weights, partners = refs[:count], refs[count:]
    width = weights[0].shape[0]
    for i in list(range(1, half)) + [0]:
        kept, other = kept_ref[i], other_refs[i][...]
        found = [
            dot_nt(kept, weight[...]) + dot_nt(other, partner[...])
            for weight, partner in zip(weights, partners)
        ]
        for bit in range(count.bit_length() - 1):
            turn = place_ref[0] // 2**bit % 2 == 1
            found = [jnp.where(turn, found[j ^ 2**bit], found[j]) for j in range(count)]
        for j, result in enumerate(found):
            if i > 0:
                far_ref[i - 1, :, j * width : (j + 1) * width] = result.astype(BF16)
            else:
                own_ref[:, j * width : (j + 1) * width] = result


def assemble_kernel(place_ref, *refs):
    out_ref = refs[-1]
    width = refs[0].shape[1]
    groups = out_ref.shape[1] // width
    each = (len(refs) - 1) // groups
    for p in range(groups):
        own_ref, *far_refs = refs[p * each : (p + 1) * each]
        total = own_ref[...]
        for far_ref in far_refs:
            total = total + far_ref[...].astype(F32)
        start = pl.multiple_of((place_ref[0] ^ p) * width, width)
        out_ref[:, pl.ds(start, width)] = total.astype(BF16)


def feature_tile(features):
    for tile in (256, 128):
        if features % tile == 0:
            return tile
    return features


def whole(shape):
    return pl.BlockSpec(shape, lambda *_: (0,) * len(shape))


def on_device(
    values,
    state_in,
    state_out,
    log_decay,
    level_class,
    level_table,
    skip_gain,
    norm_gain,
    out_weight,
):
    heads_size = lax.axis_size("head")
    ctx_size = lax.axis_size("ctx")
    ctx_bits = ctx_size.bit_length() - 1
    me = lax.axis_index("head")
    me1 = me.reshape(1).astype(jnp.int32)
    position = lax.axis_index("ctx")
    tokens = state_in.shape[0]
    rows_dev = values.shape[0]
    head_count = log_decay.shape[1]
    features = values.shape[1] // heads_size
    head_width = features // head_count
    state_size = state_in.shape[1]
    stretches = tokens // CH
    local = stretches.bit_length() - 1
    levels = level_table.shape[1]
    wide = 2 * head_count
    tile = feature_tile(features)
    tiles = features // tile
    half = heads_size // 2
    params = pltpu.CompilerParams(vmem_limit_bytes=VMEM_LIMIT)
    cheap = pl.CostEstimate(flops=0, bytes_accessed=0, transcendentals=0)

    spread = (
        jnp.arange(wide)[:, None] % head_count == (jnp.arange(features) // head_width)[None, :]
    ).astype(BF16)
    same = (
        (jnp.arange(tile)[:, None] // head_width == jnp.arange(tile)[None, :] // head_width)
        / head_width
    ).astype(BF16)

    def kernel_call(body, name, out_shape, **kwargs):
        return pl.pallas_call(
            body, out_shape=out_shape, compiler_params=params, cost_estimate=cheap, name=name, **kwargs
        )

    def shape(dims, kind=BF16):
        return jax.ShapeDtypeStruct(dims, kind)

    smem = pl.BlockSpec(memory_space=pltpu.SMEM)
    vmem = pl.BlockSpec(memory_space=pltpu.VMEM)
    place1 = position.reshape(1).astype(jnp.int32)

    *fades, total = kernel_call(
        fade_kernel,
        "fade",
        tuple([shape((rows_dev, wide))] * heads_size + [shape((1, wide), F32)]),
        in_specs=[smem, vmem],
    )(me1, log_decay)
    fades = [fades[0]] + [swap(fades[r], "head", r) for r in range(1, heads_size)]

    held = {0: out_weight.T}
    for bit in range(ctx_bits):
        held[2**bit] = swap(held[0], "ctx", 2**bit)

    def value_swap(r, after=None):
        sent = lax.dynamic_slice_in_dim(values, (me ^ r) * features, features, 1)
        return swap(sent if after is None else tie(sent, after), "head", r)

    early = {r: value_swap(r) for r in range(1, heads_size) if r <= half}

    in_turned = lax.dynamic_slice_in_dim(state_in, me * rows_dev, rows_dev, 0).T
    keep, send = kernel_call(
        partial_state_kernel,
        "partial_states",
        (shape((half, state_size, features), F32), shape((half, state_size, features))),
        grid_spec=pltpu.PrefetchScalarGridSpec(
            num_scalar_prefetch=1,
            grid=(half,),
            in_specs=[
                pl.BlockSpec((rows_dev, features), lambda i, m: (0, m[0] ^ (2 * i))),
                pl.BlockSpec((rows_dev, features), lambda i, m: (0, m[0] ^ (2 * i + 1))),
            ]
            + [whole((rows_dev, wide))] * heads_size
            + [whole((state_size, rows_dev)), whole((wide, features))],
            out_specs=[
                pl.BlockSpec((1, state_size, features), lambda i, m: (i, 0, 0)),
                pl.BlockSpec((1, state_size, features), lambda i, m: (i, 0, 0)),
            ],
        ),
    )(me1, values, values, *fades, in_turned, spread)
    own_state, *far_states = kernel_call(
        fold_kernel,
        "fold",
        tuple(
            [shape((state_size, features), F32)] + [shape((state_size, features))] * (half - 1)
        ),
    )(keep, swap(send, "head", 1))
    got_states = [
        swap(tie(far, *early.values()), "head", 2 * (i + 1)) for i, far in enumerate(far_states)
    ]

    merge_count = -(-len(merge_rows(stretches)) // 16) * 16
    table = jnp.transpose(level_table, (1, 0, 2))
    table = jnp.concatenate([table, table], axis=2)
    lift, read, cross, merge, scores, masked = kernel_call(
        factors_kernel,
        "factors",
        (
            shape((tokens, wide)),
            shape((local + 1, tokens, wide)),
            shape((levels - local - 1, tokens, wide)),
            shape((merge_count, wide)),
            shape((heads_size, 2, rows_dev, rows_dev)),
            shape((heads_size, rows_dev // CH * state_size, rows_dev)),
        ),
    )(
        tie(log_decay, own_state), level_class.reshape(tokens, 1), table, state_in, state_out
    )

    running, sent = kernel_call(
        first_kernel,
        "first_state",
        (shape((state_size, features), F32), shape((state_size + EXTRA, features))),
    )(own_state, total, *got_states)
    late = {r: value_swap(r, got_states[-1]) for r in range(1, heads_size) if r not in early}
    offset = jnp.zeros((1, wide), F32)
    factors = [jnp.broadcast_to((position % 2).astype(BF16), (EXTRA, wide))]
    factors[0] = jnp.where(jnp.arange(wide)[None, :] < head_count, factors[0], 0)
    states = []
    for bit in range(ctx_bits):
        if bit == 0:
            sent = tie(sent, held[1], held[2])
        if bit == ctx_bits - 1:
            sent = tie(sent, *late.values())
        states.append(swap(sent, "ctx", 2**bit))
        if bit + 1 < ctx_bits:
            running, total, offset, factor, sent = kernel_call(
                functools.partial(merge_kernel, bit),
                "merge",
                (
                    shape((state_size, features), F32),
                    shape((1, wide), F32),
                    shape((1, wide), F32),
                    shape((EXTRA, wide)),
                    shape((state_size + EXTRA, features)),
                ),
                in_specs=[smem] + [vmem] * 5,
            )(place1, running, total, offset, states[-1], spread)
            factors.append(factor)

    columns = out_weight.shape[1]
    near = ctx_bits - 1
    for r in range(2, ctx_size):
        low = r & -r
        if r not in held and low > 1:
            held[r] = swap(tie(held[r ^ low], states[min(low.bit_length() - 1, near - 1)]), "ctx", low)
    for bit in range(1, ctx_bits):
        r = 2**bit
        held[r + 1] = swap(tie(held[r], states[min(bit - 1, near - 1)]), "ctx", 1)

    skip_row = jnp.repeat(skip_gain, head_width)[None, :]
    grouped = (heads_size, rows_dev)
    pre = kernel_call(
        lambda me_ref, *refs: local_kernel(me_ref, near, heads_size, *refs),
        "local_levels",
        shape((heads_size, rows_dev, features), F32),
        grid_spec=pltpu.PrefetchScalarGridSpec(
            num_scalar_prefetch=1,
            grid=(tiles,),
            in_specs=[pl.BlockSpec((rows_dev, tile), lambda f, m: (0, m[0] * tiles + f))]
            + [pl.BlockSpec((rows_dev, tile), lambda f, m: (0, f))] * (heads_size - 1)
            + [
                whole(grouped + (state_size,)),
                whole(grouped + (wide,)),
                whole((local + 1,) + grouped + (wide,)),
                whole((merge_count, wide)),
                whole(scores.shape),
                whole(masked.shape),
                pl.BlockSpec((wide, tile), lambda f, m: (0, f)),
                pl.BlockSpec((1, tile), lambda f, m: (0, f)),
                whole((ctx_bits,) + grouped + (wide,)),
            ]
            + [whole((EXTRA, wide))] * near
            + [pl.BlockSpec((state_size + EXTRA, tile), lambda f, m: (0, f))] * near,
            out_specs=pl.BlockSpec(grouped + (tile,), lambda f, m: (0, 0, f)),
            scratch_shapes=[
                pltpu.VMEM((heads_size, rows_dev // CH * state_size, tile), F32),
                pltpu.VMEM((max(local, 1), state_size, tile), F32),
                pltpu.VMEM((max(local, 1), 2 * state_size, tile), BF16),
            ],
        ),
    )(
        me1,
        values,
        *[early[r] if r in early else late[r] for r in range(1, heads_size)],
        state_out.reshape(grouped + (state_size,)),
        lift.reshape(grouped + (wide,)),
        read.reshape((local + 1,) + grouped + (wide,)),
        merge,
        scores,
        masked,
        spread,
        skip_row,
        cross.reshape((ctx_bits,) + grouped + (wide,)),
        *factors[:near],
        *states[:near],
    )

    kept, *sends = kernel_call(
        finish_kernel,
        "finish",
        tuple([shape((half, rows_dev, features))] + [shape((rows_dev, features))] * half),
        grid_spec=pltpu.PrefetchScalarGridSpec(
            num_scalar_prefetch=1,
            grid=(tiles,),
            in_specs=[
                pl.BlockSpec(grouped + (tile,), lambda f, m: (0, 0, f)),
                whole(grouped + (state_size,)),
                whole(grouped + (wide,)),
                whole((EXTRA, wide)),
                pl.BlockSpec((state_size + EXTRA, tile), lambda f, m: (0, f)),
                pl.BlockSpec((wide, tile), lambda f, m: (0, f)),
                whole((tile, tile)),
                pl.BlockSpec((1, tile), lambda f, m: (0, f)),
            ],
            out_specs=[pl.BlockSpec((half, rows_dev, tile), lambda f, m: (0, 0, f))]
            + [pl.BlockSpec((rows_dev, tile), lambda f, m: (0, f))] * half,
        ),
    )(
        me1,
        pre,
        state_out.reshape(grouped + (state_size,)),
        cross[-1].reshape(grouped + (wide,)),
        tie(factors[-1], *[held[r] for r in range(2, ctx_size // 2 + 1) if r in held]),
        states[-1],
        spread,
        same,
        norm_gain[None, :],
    )
    others = [swap(array, "head", 1) for array in sends]

    count = 1
    while count * columns % 128 and 2 * count <= ctx_size:
        count *= 2
    partners = {r: swap(held[r], "head", 1) for r in range(count)}
    pieces = []
    for first in range(0, ctx_size, count):
        group = range(first, first + count)
        for r in group:
            if r not in held:
                side = (r ^ 1) & -(r ^ 1)
                top = lax.slice_in_dim(tie(held[r ^ 1], pieces[0]), 0, columns // 2, axis=0)
                rest = lax.slice_in_dim(tie(held[r ^ side], pieces[0]), columns // 2, columns, axis=0)
                held[r] = jnp.concatenate([swap(top, "ctx", 1), swap(rest, "ctx", side)], axis=0)
            if r not in partners:
                partners[r] = swap(tie(held[r], pieces[0]), "head", 1)
        far, own = kernel_call(
            project_kernel,
            "project",
            (
                shape((half - 1, rows_dev, count * columns)),
                shape((rows_dev, count * columns), F32),
            ),
            in_specs=[smem] + [vmem] * (1 + half + 2 * count),
        )(place1, kept, *others, *[held[r] for r in group], *[partners[r] for r in group])
        pieces.append(own)
        pieces += [swap(far[i - 1], "head", 2 * i) for i in range(1, half)]
    return kernel_call(
        assemble_kernel,
        "assemble",
        shape((rows_dev, ctx_size * columns)),
        in_specs=[smem] + [vmem] * len(pieces),
    )(place1 // count, *pieces)


def solution(mesh):
    return jax.shard_map(
        on_device,
        mesh=mesh,
        in_specs=(
            P(("ctx", "head"), None),
            P("ctx", None),
            P("ctx", None),
            P("ctx", "head"),
            P("ctx"),
            P(None, None, "head"),
            P("head"),
            P("head"),
            P("head", "ctx"),
        ),
        out_specs=P(("ctx", "head"), None),
        check_vma=False,
    )
```

```python
import functools

import jax
import jax.numpy as jnp
from jax import lax
from jax.experimental import pallas as pl
from jax.experimental.pallas import tpu as pltpu
from jax.sharding import PartitionSpec as P

CH = 64
EPSILON = 1e-05
EXTRA = 16
F32 = jnp.float32
BF16 = jnp.bfloat16
VMEM_LIMIT = 32 * 1024 * 1024


def dot(a, b):
    return lax.dot_general(a, b, (((1,), (0,)), ((), ())), preferred_element_type=F32)


def dot_t(a, b):
    return lax.dot_general(a, b, (((0,), (0,)), ((), ())), preferred_element_type=F32)


def dot_nt(a, b):
    return lax.dot_general(a, b, (((1,), (1,)), ((), ())), preferred_element_type=F32)


def swap(value, axis, distance):
    pairs = [(source, source ^ distance) for source in range(lax.axis_size(axis))]
    return lax.ppermute(value, axis, pairs)


def tie(value, *after):
    return lax.optimization_barrier((value,) + after)[0]


def three_parts(x):
    high = x.astype(BF16)
    rest = x - high.astype(F32)
    middle = rest.astype(BF16)
    low = (rest - middle.astype(F32)).astype(BF16)
    return high, middle, low


def two_parts(x):
    high = x.astype(BF16)
    return high, (x - high.astype(F32)).astype(BF16)


def halves(x, head_count):
    high = x.astype(BF16).astype(F32)
    lane = lax.broadcasted_iota(jnp.int32, x.shape, x.ndim - 1)
    return jnp.where(lane < head_count, high, x - high).astype(BF16)


def merge_rows(stretches):
    rows = [("own", c, 0) for c in range(stretches - 1)]
    for c in range(stretches - 1):
        k = 0
        while (c >> k) & 1:
            rows.append(("merge", c, k))
            k += 1
    return rows


def stretch_sums(decay_ref):
    tokens, width = decay_ref.shape
    row = lax.broadcasted_iota(jnp.int32, (CH, CH), 0)
    col = lax.broadcasted_iota(jnp.int32, (CH, CH), 1)
    lower = jnp.where(row >= col, 1.0, 0.0).astype(BF16)
    lower = jnp.concatenate([lower] * 3, axis=1)
    within, starts = [], [jnp.zeros((1, width), F32)]
    for c in range(tokens // CH):
        parts = jnp.concatenate(three_parts(decay_ref[c * CH : (c + 1) * CH, :]), axis=0)
        summed = dot(lower, parts)
        within.append(summed)
        starts.append(starts[-1] + summed[CH - 1 : CH, :])
    return within, starts


def fade_kernel(me_ref, decay_ref, fade_ref, total_ref):
    blocks, rows_dev, _ = fade_ref.shape
    head_count = decay_ref.shape[1]
    within, starts = stretch_sums(decay_ref)
    total = starts[-1]
    total_ref[...] = jnp.concatenate([total, total], axis=1)
    per_block = rows_dev // CH
    me = me_ref[0]
    for block in range(blocks):
        for c in range(block * per_block, (block + 1) * per_block):
            factor = jnp.exp(total - starts[c] - within[c])
            factor = halves(jnp.concatenate([factor, factor], axis=1), head_count)
            first = (c - block * per_block) * CH
            fade_ref[me ^ block, first : first + CH, :] = factor


def factors_kernel(
    decay_ref, class_ref, table_ref, in_ref, out_ref,
    lift_ref, read_ref, cross_ref, merge_ref, score_ref, masked_ref,
):
    tokens, head_count = decay_ref.shape
    width = 2 * head_count
    stretches = tokens // CH
    levels, classes, _ = table_ref.shape
    local = read_ref.shape[0] - 1
    tables = [jnp.concatenate(three_parts(table_ref[level]), axis=0) for level in range(levels)]
    within, starts = stretch_sums(decay_ref)
    within = [jnp.concatenate([x, x], axis=1) for x in within]
    starts = [jnp.concatenate([x, x], axis=1) for x in starts]
    class_iota = lax.broadcasted_iota(jnp.int32, (CH, 3 * classes), 1) % classes
    for c in range(stretches):
        rows = slice(c * CH, (c + 1) * CH)
        lift_ref[rows, :] = halves(jnp.exp(-within[c]), head_count)
        onehot = jnp.where(class_ref[rows, :] == class_iota, 1.0, 0.0).astype(BF16)
        read_ref[0, rows, :] = halves(jnp.exp(within[c]) * dot(onehot, tables[0]), head_count)
        for level in range(1, local + 1):
            if (c >> (level - 1)) & 1:
                begin = starts[c] - starts[(c >> (level - 1)) << (level - 1)]
                factor = jnp.exp(within[c] + begin) * dot(onehot, tables[level])
                read_ref[level, rows, :] = halves(factor, head_count)
            else:
                read_ref[level, rows, :] = jnp.zeros((CH, width), BF16)
        far = jnp.exp(within[c] + starts[c])
        for level in range(local + 1, levels):
            far_factor = far * dot(onehot, tables[level])
            cross_ref[level - local - 1, rows, :] = halves(far_factor, head_count)
    exps = []
    for kind, c, k in merge_rows(stretches):
        first = c if kind == "own" else c + 1 - 2**k
        exps.append(jnp.exp(starts[c + 1] - starts[first]))
    exps += [jnp.zeros((1, width), F32)] * (merge_ref.shape[0] - len(exps))
    merge_ref[...] = halves(jnp.concatenate(exps, axis=0), head_count)
    groups, _, group_rows, _ = score_ref.shape
    row = lax.broadcasted_iota(jnp.int32, (group_rows, group_rows), 0)
    col = lax.broadcasted_iota(jnp.int32, (group_rows, group_rows), 1)
    inside = (row // CH == col // CH) & (row >= col)
    state_size = in_ref.shape[1]
    lane = lax.broadcasted_iota(jnp.int32, (state_size, group_rows), 1) // CH
    for g in range(groups):
        rows = slice(g * group_rows, (g + 1) * group_rows)
        scores = jnp.where(inside, dot_nt(out_ref[rows, :], in_ref[rows, :]), 0.0)
        score_ref[g, 0], score_ref[g, 1] = two_parts(scores)
        turned = jnp.transpose(in_ref[rows, :].astype(F32))
        for s in range(group_rows // CH):
            at = slice(s * state_size, (s + 1) * state_size)
            masked_ref[g, at, :] = jnp.where(lane == s, turned, 0.0).astype(BF16)


def partial_state_kernel(me_ref, *refs):
    even_ref, odd_ref, *fade_refs = refs[:-4]
    in_ref, spread_ref, keep_ref, send_ref = refs[-4:]
    spread = spread_ref[...]
    turned = in_ref[...]
    for i in range(len(fade_refs) // 2):

        @pl.when(pl.program_id(0) == i)
        def _():
            odd = (dot(fade_refs[2 * i + 1][...], spread) * odd_ref[...].astype(F32)).astype(BF16)
            send_ref[0] = dot(turned, odd).astype(BF16)
            even = (dot(fade_refs[2 * i][...], spread) * even_ref[...].astype(F32)).astype(BF16)
            keep_ref[0] = dot(turned, even)


def fold_kernel(keep_ref, got_ref, own_ref, *far_refs):
    own_ref[...] = keep_ref[0] + got_ref[0].astype(F32)
    for i, far_ref in enumerate(far_refs):
        far_ref[...] = (keep_ref[i + 1] + got_ref[i + 1].astype(F32)).astype(BF16)


def pack_state(sent_ref, state, total):
    rows, width = state.shape[0], total.shape[1]
    sent_ref[:rows, :] = state.astype(BF16)
    sent_ref[rows:, :] = jnp.zeros((EXTRA, state.shape[1]), BF16)
    parts = list(three_parts(total))
    parts.append(jnp.zeros((EXTRA - len(parts), width), BF16))
    sent_ref[rows:, :width] = jnp.concatenate(parts, axis=0)


def first_kernel(own_ref, total_ref, *refs):
    *far_refs, running_ref, sent_ref = refs
    running = own_ref[...]
    for far_ref in far_refs:
        running = running + far_ref[...].astype(F32)
    running_ref[...] = running
    pack_state(sent_ref, running, total_ref[...])


def merge_kernel(
    bit, place_ref, running_ref, total_ref, offset_ref, got_ref, spread_ref,
    next_running_ref, next_total_ref, next_offset_ref, factor_ref, sent_ref,
):
    rows, width = running_ref.shape[0], total_ref.shape[1]
    head_count = width // 2
    place = place_ref[0]
    upper = place // 2**bit % 2 == 1
    total = total_ref[...]
    parts = got_ref[rows:, :width].astype(F32)
    partner = parts[0:1] + parts[1:2] + parts[2:3]
    fading = jnp.exp(jnp.where(upper, total, partner))
    fading = halves(jnp.broadcast_to(fading, (EXTRA, width)), head_count)
    fading = dot(fading, spread_ref[...])[0:1, :]
    got, running = got_ref[:rows, :].astype(F32), running_ref[...]
    merged = fading * jnp.where(upper, got, running) + jnp.where(upper, running, got)
    next_running_ref[...] = merged
    joined = total + partner
    next_total_ref[...] = joined
    offset = jnp.where(upper, offset_ref[...] + partner, offset_ref[...])
    next_offset_ref[...] = offset
    next_upper = place // 2 ** (bit + 1) % 2 == 1
    factor = jnp.where(next_upper, jnp.exp(offset), 0.0)
    factor_ref[...] = halves(jnp.broadcast_to(factor, (EXTRA, width)), head_count)
    pack_state(sent_ref, merged, joined)


def local_kernel(me_ref, near, parts, *refs):
    count = 1 + max(at for pieces in parts for at, _, _ in pieces)
    value_refs, refs = refs[:count], refs[count:]
    out_ref, lift_ref, read_ref, merge_ref, score_ref, masked_ref, spread_ref = refs[:7]
    skip_ref, cross_ref, *refs = refs[7:]
    factor_refs, state_refs, refs = refs[:near], refs[near : 2 * near], refs[2 * near :]
    pre_ref, nodes, sums, operand = refs
    group_rows = value_refs[0].shape[0]
    groups = len(parts)
    me = me_ref[0]
    per_group = group_rows // CH
    stretches = groups * per_group
    state_size = out_ref.shape[2]
    spread = spread_ref[...]
    merges = dot(merge_ref[...], spread)
    place = {kind: i for i, kind in enumerate(merge_rows(stretches))}
    skip = skip_ref[...]
    states = [
        (state_ref[:state_size, :], dot(factor_ref[...], spread)[0:1, :])
        for state_ref, factor_ref in zip(state_refs, factor_refs)
    ]
    for r, pieces in enumerate(parts):
        g = me ^ r
        value = [value_refs[at][first : first + rows, :] for at, first, rows in pieces]
        value = jnp.concatenate(value, axis=0).astype(F32)
        high, low = two_parts(dot(lift_ref[g], spread) * value)
        direct = dot(score_ref[g, 0], high) + dot(score_ref[g, 0], low) + dot(score_ref[g, 1], high)
        total = dot(read_ref[0, g], spread) * direct + skip * value
        for level, (state, row) in enumerate(states):
            total = total + dot(cross_ref[level, g], spread) * (dot(out_ref[g], state) * row)
        pre_ref[g] = total
        nodes[g] = dot(masked_ref[g], high) + dot(masked_ref[g], low)

    def gain(level, g, first, count):
        at = slice(first * CH, (first + count) * CH)
        readers = out_ref[g, at, :]
        twice = jnp.concatenate([readers, readers], axis=1)
        gained = dot(twice, operand[level - 1])
        pre_ref[g, at, :] += dot(read_ref[level, g, at, :], spread) * gained

    for c in range(stretches):
        g, s = divmod(c, per_group)
        level = 1
        while 2 ** (level - 1) < stretches:
            span = 2 ** (level - 1)
            if c % (2 * span) == span:
                for other in range(c, c + span, per_group):
                    gain(level, other // per_group, other % per_group, min(span, per_group))
            level += 1
        if c + 1 < stretches:
            row = place[("own", c, 0)]
            node = nodes[g, s * state_size : (s + 1) * state_size, :] * merges[row : row + 1, :]
            k = 0
            while (c >> k) & 1:
                row = place[("merge", c, k)]
                node = node + merges[row : row + 1, :] * sums[k]
                k += 1
            sums[k] = node
            n_high, n_low = two_parts(node)
            operand[k, :state_size, :] = n_high
            operand[k, state_size:, :] = n_low


def finish_kernel(
    me_ref, pre_ref, out_ref, cross_ref, factor_ref, state_ref, spread_ref, same_ref, gain_ref, *refs
):
    parts = pre_ref.shape[0]
    me = me_ref[0]
    spread = spread_ref[...]
    same = same_ref[...]
    gain = gain_ref[...]
    state = state_ref[: out_ref.shape[2], :]
    row = dot(factor_ref[...], spread)[0:1, :]
    for r in range(parts):
        at = me ^ r
        total = pre_ref[at] + dot(cross_ref[at], spread) * (dot(out_ref[at], state) * row)
        mean_square = dot((total * total).astype(BF16), same)
        normed = (total * lax.rsqrt(mean_square + EPSILON) * gain).astype(BF16)
        refs[r][...] = normed


def project_kernel(place_ref, *refs):
    *refs, out_ref = refs
    rows = out_ref.shape[0]
    kept_refs, other_refs, refs = refs[:rows], refs[rows : 2 * rows], refs[2 * rows :]
    count = len(refs) // 2
    weights, partners = refs[:count], refs[count:]
    width = weights[0].shape[0]
    for i, (kept_ref, other_ref) in enumerate(zip(kept_refs, other_refs)):
        found = [
            dot_nt(kept_ref[...], weight[...]) + dot_nt(other_ref[...], partner[...])
            for weight, partner in zip(weights, partners)
        ]
        for bit in range(count.bit_length() - 1):
            turn = place_ref[0] // 2**bit % 2 == 1
            found = [jnp.where(turn, found[j ^ 2**bit], found[j]) for j in range(count)]
        for j, result in enumerate(found):
            out_ref[i, :, j * width : (j + 1) * width] = result.astype(out_ref.dtype)


def assemble_kernel(place_ref, *refs):
    out_ref = refs[-1]
    width = refs[0].shape[1]
    groups = out_ref.shape[1] // width
    each = (len(refs) - 1) // groups
    for p in range(groups):
        own_ref, *far_refs = refs[p * each : (p + 1) * each]
        total = own_ref[...]
        for far_ref in far_refs:
            total = total + far_ref[...].astype(F32)
        start = pl.multiple_of((place_ref[0] ^ p) * width, width)
        out_ref[:, pl.ds(start, width)] = total.astype(BF16)


def feature_tile(features):
    for tile in (256, 128):
        if features % tile == 0:
            return tile
    return features


def whole(shape):
    return pl.BlockSpec(shape, lambda *_: (0,) * len(shape))


def on_device(
    values,
    state_in,
    state_out,
    log_decay,
    level_class,
    level_table,
    skip_gain,
    norm_gain,
    out_weight,
):
    heads_size = lax.axis_size("head")
    ctx_size = lax.axis_size("ctx")
    ctx_bits = ctx_size.bit_length() - 1
    me = lax.axis_index("head")
    me1 = me.reshape(1).astype(jnp.int32)
    position = lax.axis_index("ctx")
    tokens = state_in.shape[0]
    rows_dev = values.shape[0]
    head_count = log_decay.shape[1]
    features = values.shape[1] // heads_size
    head_width = features // head_count
    state_size = state_in.shape[1]
    stretches = tokens // CH
    local = stretches.bit_length() - 1
    levels = level_table.shape[1]
    wide = 2 * head_count
    tile = feature_tile(features)
    tiles = features // tile
    half = heads_size // 2
    params = pltpu.CompilerParams(vmem_limit_bytes=VMEM_LIMIT)
    cheap = pl.CostEstimate(flops=0, bytes_accessed=0, transcendentals=0)

    def kernel_call(body, name, out_shape, **kwargs):
        return pl.pallas_call(
            body, out_shape=out_shape, compiler_params=params, cost_estimate=cheap, name=name, **kwargs
        )

    def shape(dims, kind=BF16):
        return jax.ShapeDtypeStruct(dims, kind)

    smem = pl.BlockSpec(memory_space=pltpu.SMEM)
    vmem = pl.BlockSpec(memory_space=pltpu.VMEM)
    place1 = position.reshape(1).astype(jnp.int32)

    def fenced(body, *operands):
        shapes = jax.eval_shape(body, *operands)
        zeros = lambda *_: jax.tree.map(lambda leaf: jnp.zeros(leaf.shape, leaf.dtype), shapes)
        return lax.cond(position < ctx_size, body, zeros, *operands)

    def spread_heads():
        return (
            jnp.arange(wide)[:, None] % head_count == (jnp.arange(features) // head_width)[None, :]
        ).astype(BF16)

    held = {0: out_weight.T}
    for bit in range(ctx_bits):
        held[2**bit] = swap(held[0], "ctx", 2**bit)

    def merge_step(bit, running, total, offset, got, spread):
        return kernel_call(
            functools.partial(merge_kernel, bit),
            "merge",
            (
                shape((state_size, features), F32),
                shape((1, wide), F32),
                shape((1, wide), F32),
                shape((EXTRA, wide)),
                shape((state_size + EXTRA, features)),
            ),
            in_specs=[smem] + [vmem] * 5,
        )(place1, running, total, offset, got, spread)

    merge_count = -(-len(merge_rows(stretches)) // 16) * 16

    def near_steps(running, total, sent, log_decay, level_class, level_table, state_in, state_out):
        table = jnp.transpose(level_table, (1, 0, 2))
        table = jnp.concatenate([table, table], axis=2)
        tables = kernel_call(
            factors_kernel,
            "factors",
            (
                shape((tokens, wide)),
                shape((local + 1, tokens, wide)),
                shape((levels - local - 1, tokens, wide)),
                shape((merge_count, wide)),
                shape((heads_size, 2, rows_dev, rows_dev)),
                shape((heads_size, rows_dev // CH * state_size, rows_dev)),
            ),
        )(log_decay, level_class.reshape(tokens, 1), table, state_in, state_out)
        spread = spread_heads()
        factor = jnp.broadcast_to((position % 2).astype(BF16), (EXTRA, wide))
        factor = jnp.where(jnp.arange(wide)[None, :] < head_count, factor, 0)
        offset = jnp.zeros((1, wide), F32)
        states, factors = [], [factor]
        for bit in range(ctx_bits - 1):
            states.append(swap(sent, "ctx", 2**bit))
            running, total, offset, factor, sent = merge_step(
                bit, running, total, offset, states[-1], spread
            )
            factors.append(factor)
        return states, factors, sent, tables, spread

    def value_columns(values, r, first, count):
        return lax.dynamic_slice(values, (first, (me ^ r) * features), (count, features))

    early_rows = rows_dev // 2

    def state_chain(values, log_decay, level_class, level_table, state_in, state_out):
        fade, total = kernel_call(
            fade_kernel,
            "fade",
            (shape((heads_size, rows_dev, wide)), shape((1, wide), F32)),
            in_specs=[smem, vmem],
        )(me1, log_decay)
        near_fades, side_fades = [fade[0]], [fade[1]]
        for d in range(2, heads_size, 2):
            got = swap(tie(fade[d : d + 2], near_fades[-1]), "head", d)
            near_fades.append(got[0])
            side_fades.append(got[1])
        sides = swap(jnp.stack(side_fades), "head", 1)
        fades = []
        for d in range(half):
            fades += [near_fades[d], sides[d]]
        in_turned = lax.dynamic_slice_in_dim(state_in, me * rows_dev, rows_dev, 0).T
        across = jnp.stack([value_columns(values, d + 1, 0, rows_dev) for d in range(0, heads_size, 2)])
        across = swap(across, "head", 1)
        value_head = swap(tie(value_columns(values, 2, 0, early_rows), across), "head", 2)
        keep, send = kernel_call(
            partial_state_kernel,
            "partial_states",
            (shape((half, state_size, features), F32), shape((half, state_size, features))),
            grid_spec=pltpu.PrefetchScalarGridSpec(
                num_scalar_prefetch=1,
                grid=(half,),
                in_specs=[
                    pl.BlockSpec((rows_dev, features), lambda i, m: (0, m[0] ^ (2 * i))),
                    pl.BlockSpec((rows_dev, features), lambda i, m: (0, m[0] ^ (2 * i + 1))),
                ]
                + [whole((rows_dev, wide))] * heads_size
                + [whole((state_size, rows_dev)), whole((wide, features))],
                out_specs=[
                    pl.BlockSpec((1, state_size, features), lambda i, m: (i, 0, 0)),
                    pl.BlockSpec((1, state_size, features), lambda i, m: (i, 0, 0)),
                ],
            ),
        )(me1, values, values, *fades, in_turned, spread_heads())
        own_state, *far_states = kernel_call(
            fold_kernel,
            "fold",
            tuple(
                [shape((state_size, features), F32)] + [shape((state_size, features))] * (half - 1)
            ),
        )(keep, swap(tie(send, across), "head", 1))
        got_states = []
        for i, far in enumerate(far_states):
            got_states.append(swap(tie(far, value_head, *got_states), "head", 2 * (i + 1)))
        running, sent = kernel_call(
            first_kernel,
            "first_state",
            (shape((state_size, features), F32), shape((state_size + EXTRA, features))),
        )(own_state, total, *got_states)
        others = []
        for d in range(2, heads_size, 2):
            first = early_rows if d == 2 else 0
            own = value_columns(values, d, first, rows_dev - first)
            both = jnp.concatenate([own, across[d // 2]], axis=0)
            others.append(swap(tie(both, running, *others), "head", d))
        states, factors, sent, tables, spread = fenced(
            near_steps, running, total, sent, log_decay, level_class, level_table, state_in, state_out
        )
        return states, factors, sent, tables, spread, across[0], value_head, others

    states, factors, sent, tables, spread, beside, value_head, other_values = fenced(
        state_chain, values, log_decay, level_class, level_table, state_in, state_out
    )
    lift, read, cross, merge, scores, masked = tables
    states = list(states)
    sent = tie(sent, *[held[2**bit] for bit in range(ctx_bits)])
    states.append(swap(sent, "ctx", 2 ** (ctx_bits - 1)))

    columns = out_weight.shape[1]
    near = ctx_bits - 1
    for r in range(2, ctx_size):
        low = r & -r
        if r not in held and low > 1:
            held[r] = swap(tie(held[r ^ low], states[near - 1]), "ctx", low)
    for bit in range(1, ctx_bits):
        r = 2**bit
        held[r + 1] = swap(tie(held[r], states[near - 1]), "ctx", 1)
    same = (
        (jnp.arange(tile)[:, None] // head_width == jnp.arange(tile)[None, :] // head_width)
        / head_width
    ).astype(BF16)

    arrays = [values, beside, value_head] + list(other_values)
    parts = [[(0, 0, rows_dev)], [(1, 0, rows_dev)]]
    for i in range(half - 1):
        if i == 0:
            mine = [(2, 0, early_rows), (3, 0, rows_dev - early_rows)]
        else:
            mine = [(3 + i, 0, rows_dev)]
        parts += [mine, [(3 + i, mine[-1][2], rows_dev)]]

    skip_row = jnp.repeat(skip_gain, head_width)[None, :]
    grouped = (heads_size, rows_dev)
    pre = kernel_call(
        lambda me_ref, *refs: local_kernel(me_ref, near, parts, *refs),
        "local_levels",
        shape((heads_size, rows_dev, features), F32),
        grid_spec=pltpu.PrefetchScalarGridSpec(
            num_scalar_prefetch=1,
            grid=(tiles,),
            in_specs=[pl.BlockSpec((rows_dev, tile), lambda f, m: (0, m[0] * tiles + f))]
            + [
                pl.BlockSpec((array.shape[0], tile), lambda f, m: (0, f)) for array in arrays[1:]
            ]
            + [
                whole(grouped + (state_size,)),
                whole(grouped + (wide,)),
                whole((local + 1,) + grouped + (wide,)),
                whole((merge_count, wide)),
                whole(scores.shape),
                whole(masked.shape),
                pl.BlockSpec((wide, tile), lambda f, m: (0, f)),
                pl.BlockSpec((1, tile), lambda f, m: (0, f)),
                whole((ctx_bits,) + grouped + (wide,)),
            ]
            + [whole((EXTRA, wide))] * near
            + [pl.BlockSpec((state_size + EXTRA, tile), lambda f, m: (0, f))] * near,
            out_specs=pl.BlockSpec(grouped + (tile,), lambda f, m: (0, 0, f)),
            scratch_shapes=[
                pltpu.VMEM((heads_size, rows_dev // CH * state_size, tile), F32),
                pltpu.VMEM((max(local, 1), state_size, tile), F32),
                pltpu.VMEM((max(local, 1), 2 * state_size, tile), BF16),
            ],
        ),
    )(
        me1,
        *arrays,
        state_out.reshape(grouped + (state_size,)),
        lift.reshape(grouped + (wide,)),
        read.reshape((local + 1,) + grouped + (wide,)),
        merge,
        scores,
        masked,
        spread,
        skip_row,
        cross.reshape((ctx_bits,) + grouped + (wide,)),
        *factors[:near],
        *states[:near],
    )

    normed = kernel_call(
        finish_kernel,
        "finish",
        tuple([shape((rows_dev, features))] * heads_size),
        grid_spec=pltpu.PrefetchScalarGridSpec(
            num_scalar_prefetch=1,
            grid=(tiles,),
            in_specs=[
                pl.BlockSpec(grouped + (tile,), lambda f, m: (0, 0, f)),
                whole(grouped + (state_size,)),
                whole(grouped + (wide,)),
                whole((EXTRA, wide)),
                pl.BlockSpec((state_size + EXTRA, tile), lambda f, m: (0, f)),
                pl.BlockSpec((wide, tile), lambda f, m: (0, f)),
                whole((tile, tile)),
                pl.BlockSpec((1, tile), lambda f, m: (0, f)),
            ],
            out_specs=[pl.BlockSpec((rows_dev, tile), lambda f, m: (0, f))] * heads_size,
        ),
    )(
        me1,
        pre,
        state_out.reshape(grouped + (state_size,)),
        cross[-1].reshape(grouped + (wide,)),
        factors[-1],
        states[-1],
        spread,
        same,
        norm_gain[None, :],
    )
    kept = normed[0::2]
    others = [swap(array, "head", 1) for array in normed[1::2]]

    count = 1
    while count * columns % 128 and 2 * count <= ctx_size:
        count *= 2
    def project(name, kept, others, blocks, partners, kind):
        return kernel_call(
            project_kernel,
            name,
            shape((len(kept), rows_dev, count * columns), kind),
            in_specs=[smem] + [vmem] * (2 * len(kept) + 2 * count),
        )(place1, *kept, *others, *blocks, *partners)

    def far_part(kept, others, blocks):
        partners = [swap(block, "head", 1) for block in blocks]
        return project("project_far", kept, others, blocks, partners, BF16), partners

    fars, arrived, owns = [], [], []
    for first in range(0, ctx_size, count):
        group = range(first, first + count)
        for r in group:
            if r not in held:
                side = (r ^ 1) & -(r ^ 1)
                ready = arrived[max(len(fars) - 3, 0)] + fars[max(len(fars) - 2, 0) :][:1]
                top = lax.slice_in_dim(tie(held[r ^ 1], *ready), 0, columns // 2, axis=0)
                rest = lax.slice_in_dim(tie(held[r ^ side], *ready), columns // 2, columns, axis=0)
                held[r] = jnp.concatenate([swap(top, "ctx", 1), swap(rest, "ctx", side)], axis=0)
        blocks = [held[r] for r in group]
        if first == 0:
            far, partners = far_part(kept[1:], others[1:], blocks)
        else:
            if len(owns) >= 3:
                blocks[0] = tie(blocks[0], *owns[:-1])
            far, partners = fenced(far_part, kept[1:], others[1:], blocks)
        fars.append(far)
        if len(arrived) >= 1:
            far = tie(far, *arrived[-1])
        arrived.append([swap(far[i - 1], "head", 2 * i) for i in range(1, half)])
        owns.append(project("project_own", kept[:1], others[:1], blocks, partners, F32))
    pieces = []
    for own, got in zip(owns, arrived):
        pieces += [own[0]] + got
    return kernel_call(
        assemble_kernel,
        "assemble",
        shape((rows_dev, ctx_size * columns)),
        in_specs=[smem] + [vmem] * len(pieces),
    )(place1 // count, *pieces)


def solution(mesh):
    return jax.shard_map(
        on_device,
        mesh=mesh,
        in_specs=(
            P(("ctx", "head"), None),
            P("ctx", None),
            P("ctx", None),
            P("ctx", "head"),
            P("ctx"),
            P(None, None, "head"),
            P("head"),
            P("head"),
            P("head", "ctx"),
        ),
        out_specs=P(("ctx", "head"), None),
        check_vma=False,
    )
```

```python
import functools

import jax
import jax.numpy as jnp
from jax import lax
from jax.experimental import pallas as pl
from jax.experimental.pallas import tpu as pltpu
from jax.sharding import PartitionSpec as P

CH = 64
EPSILON = 1e-05
EXTRA = 16
F32 = jnp.float32
BF16 = jnp.bfloat16
VMEM_LIMIT = 32 * 1024 * 1024


def dot(a, b):
    return lax.dot_general(a, b, (((1,), (0,)), ((), ())), preferred_element_type=F32)


def dot_t(a, b):
    return lax.dot_general(a, b, (((0,), (0,)), ((), ())), preferred_element_type=F32)


def dot_nt(a, b):
    return lax.dot_general(a, b, (((1,), (1,)), ((), ())), preferred_element_type=F32)


def swap(value, axis, distance):
    pairs = [(source, source ^ distance) for source in range(lax.axis_size(axis))]
    return lax.ppermute(value, axis, pairs)


def tie(value, *after):
    return lax.optimization_barrier((value,) + after)[0]


def three_parts(x):
    high = x.astype(BF16)
    rest = x - high.astype(F32)
    middle = rest.astype(BF16)
    low = (rest - middle.astype(F32)).astype(BF16)
    return high, middle, low


def two_parts(x):
    high = x.astype(BF16)
    return high, (x - high.astype(F32)).astype(BF16)


def halves(x, head_count):
    high = x.astype(BF16).astype(F32)
    lane = lax.broadcasted_iota(jnp.int32, x.shape, x.ndim - 1)
    return jnp.where(lane < head_count, high, x - high).astype(BF16)


def merge_rows(stretches):
    rows = [("own", c, 0) for c in range(stretches - 1)]
    for c in range(stretches - 1):
        k = 0
        while (c >> k) & 1:
            rows.append(("merge", c, k))
            k += 1
    return rows


def stretch_sums(decay_ref):
    tokens, width = decay_ref.shape
    row = lax.broadcasted_iota(jnp.int32, (CH, CH), 0)
    col = lax.broadcasted_iota(jnp.int32, (CH, CH), 1)
    lower = jnp.where(row >= col, 1.0, 0.0).astype(BF16)
    lower = jnp.concatenate([lower] * 3, axis=1)
    within, starts = [], [jnp.zeros((1, width), F32)]
    for c in range(tokens // CH):
        parts = jnp.concatenate(three_parts(decay_ref[c * CH : (c + 1) * CH, :]), axis=0)
        summed = dot(lower, parts)
        within.append(summed)
        starts.append(starts[-1] + summed[CH - 1 : CH, :])
    return within, starts


def fade_kernel(me_ref, decay_ref, fade_ref, total_ref):
    blocks, rows_dev, _ = fade_ref.shape
    head_count = decay_ref.shape[1]
    within, starts = stretch_sums(decay_ref)
    total = starts[-1]
    total_ref[...] = jnp.concatenate([total, total], axis=1)
    per_block = rows_dev // CH
    me = me_ref[0]
    for block in range(blocks):
        for c in range(block * per_block, (block + 1) * per_block):
            factor = jnp.exp(total - starts[c] - within[c])
            factor = halves(jnp.concatenate([factor, factor], axis=1), head_count)
            first = (c - block * per_block) * CH
            fade_ref[me ^ block, first : first + CH, :] = factor


def factors_kernel(
    decay_ref, class_ref, table_ref, in_ref, out_ref,
    lift_ref, read_ref, cross_ref, merge_ref, score_ref, masked_ref,
):
    tokens, head_count = decay_ref.shape
    width = 2 * head_count
    stretches = tokens // CH
    levels, classes, _ = table_ref.shape
    local = read_ref.shape[0] - 1
    tables = [jnp.concatenate(three_parts(table_ref[level]), axis=0) for level in range(levels)]
    within, starts = stretch_sums(decay_ref)
    within = [jnp.concatenate([x, x], axis=1) for x in within]
    starts = [jnp.concatenate([x, x], axis=1) for x in starts]
    class_iota = lax.broadcasted_iota(jnp.int32, (CH, 3 * classes), 1) % classes
    for c in range(stretches):
        rows = slice(c * CH, (c + 1) * CH)
        lift_ref[rows, :] = halves(jnp.exp(-within[c]), head_count)
        onehot = jnp.where(class_ref[rows, :] == class_iota, 1.0, 0.0).astype(BF16)
        read_ref[0, rows, :] = halves(jnp.exp(within[c]) * dot(onehot, tables[0]), head_count)
        for level in range(1, local + 1):
            if (c >> (level - 1)) & 1:
                begin = starts[c] - starts[(c >> (level - 1)) << (level - 1)]
                factor = jnp.exp(within[c] + begin) * dot(onehot, tables[level])
                read_ref[level, rows, :] = halves(factor, head_count)
            else:
                read_ref[level, rows, :] = jnp.zeros((CH, width), BF16)
        far = jnp.exp(within[c] + starts[c])
        for level in range(local + 1, levels):
            far_factor = far * dot(onehot, tables[level])
            cross_ref[level - local - 1, rows, :] = halves(far_factor, head_count)
    exps = []
    for kind, c, k in merge_rows(stretches):
        first = c if kind == "own" else c + 1 - 2**k
        exps.append(jnp.exp(starts[c + 1] - starts[first]))
    exps += [jnp.zeros((1, width), F32)] * (merge_ref.shape[0] - len(exps))
    merge_ref[...] = halves(jnp.concatenate(exps, axis=0), head_count)
    groups, _, group_rows, _ = score_ref.shape
    row = lax.broadcasted_iota(jnp.int32, (group_rows, group_rows), 0)
    col = lax.broadcasted_iota(jnp.int32, (group_rows, group_rows), 1)
    inside = (row // CH == col // CH) & (row >= col)
    state_size = in_ref.shape[1]
    lane = lax.broadcasted_iota(jnp.int32, (state_size, group_rows), 1) // CH
    for g in range(groups):
        rows = slice(g * group_rows, (g + 1) * group_rows)
        scores = jnp.where(inside, dot_nt(out_ref[rows, :], in_ref[rows, :]), 0.0)
        score_ref[g, 0], score_ref[g, 1] = two_parts(scores)
        turned = jnp.transpose(in_ref[rows, :].astype(F32))
        for s in range(group_rows // CH):
            at = slice(s * state_size, (s + 1) * state_size)
            masked_ref[g, at, :] = jnp.where(lane == s, turned, 0.0).astype(BF16)


def partial_state_kernel(me_ref, *refs):
    even_ref, odd_ref, *fade_refs = refs[:-4]
    in_ref, spread_ref, keep_ref, send_ref = refs[-4:]
    spread = spread_ref[...]
    turned = in_ref[...]
    for i in range(len(fade_refs) // 2):

        @pl.when(pl.program_id(0) == i)
        def _():
            odd = (dot(fade_refs[2 * i + 1][...], spread) * odd_ref[...].astype(F32)).astype(BF16)
            send_ref[0] = dot(turned, odd).astype(BF16)
            even = (dot(fade_refs[2 * i][...], spread) * even_ref[...].astype(F32)).astype(BF16)
            keep_ref[0] = dot(turned, even)


def fold_kernel(keep_ref, got_ref, own_ref, *far_refs):
    own_ref[...] = keep_ref[0] + got_ref[0].astype(F32)
    for i, far_ref in enumerate(far_refs):
        far_ref[...] = (keep_ref[i + 1] + got_ref[i + 1].astype(F32)).astype(BF16)


def pack_state(sent_ref, state, total):
    rows, width = state.shape[0], total.shape[1]
    sent_ref[:rows, :] = state.astype(BF16)
    sent_ref[rows:, :] = jnp.zeros((EXTRA, state.shape[1]), BF16)
    parts = list(three_parts(total))
    parts.append(jnp.zeros((EXTRA - len(parts), width), BF16))
    sent_ref[rows:, :width] = jnp.concatenate(parts, axis=0)


def first_kernel(own_ref, total_ref, *refs):
    *far_refs, running_ref, sent_ref = refs
    running = own_ref[...]
    for far_ref in far_refs:
        running = running + far_ref[...].astype(F32)
    running_ref[...] = running
    pack_state(sent_ref, running, total_ref[...])


def merge_kernel(
    bit, place_ref, running_ref, total_ref, offset_ref, got_ref, spread_ref,
    next_running_ref, next_total_ref, next_offset_ref, factor_ref, sent_ref,
):
    rows, width = running_ref.shape[0], total_ref.shape[1]
    head_count = width // 2
    place = place_ref[0]
    upper = place // 2**bit % 2 == 1
    total = total_ref[...]
    parts = got_ref[rows:, :width].astype(F32)
    partner = parts[0:1] + parts[1:2] + parts[2:3]
    fading = jnp.exp(jnp.where(upper, total, partner))
    fading = halves(jnp.broadcast_to(fading, (EXTRA, width)), head_count)
    fading = dot(fading, spread_ref[...])[0:1, :]
    got, running = got_ref[:rows, :].astype(F32), running_ref[...]
    merged = fading * jnp.where(upper, got, running) + jnp.where(upper, running, got)
    next_running_ref[...] = merged
    joined = total + partner
    next_total_ref[...] = joined
    offset = jnp.where(upper, offset_ref[...] + partner, offset_ref[...])
    next_offset_ref[...] = offset
    next_upper = place // 2 ** (bit + 1) % 2 == 1
    factor = jnp.where(next_upper, jnp.exp(offset), 0.0)
    factor_ref[...] = halves(jnp.broadcast_to(factor, (EXTRA, width)), head_count)
    pack_state(sent_ref, merged, joined)


def local_kernel(me_ref, near, parts, *refs):
    count = 1 + max(at for pieces in parts for at, _, _ in pieces)
    value_refs, refs = refs[:count], refs[count:]
    out_ref, lift_ref, read_ref, merge_ref, score_ref, masked_ref, spread_ref = refs[:7]
    skip_ref, cross_ref, *refs = refs[7:]
    factor_refs, state_refs, refs = refs[:near], refs[near : 2 * near], refs[2 * near :]
    pre_ref, nodes, sums, operand = refs
    group_rows = value_refs[0].shape[0]
    groups = len(parts)
    me = me_ref[0]
    per_group = group_rows // CH
    stretches = groups * per_group
    state_size = out_ref.shape[2]
    spread = spread_ref[...]
    merges = dot(merge_ref[...], spread)
    place = {kind: i for i, kind in enumerate(merge_rows(stretches))}
    skip = skip_ref[...]
    states = [
        (state_ref[:state_size, :], dot(factor_ref[...], spread)[0:1, :])
        for state_ref, factor_ref in zip(state_refs, factor_refs)
    ]
    for r, pieces in enumerate(parts):
        g = me ^ r
        value = [value_refs[at][first : first + rows, :] for at, first, rows in pieces]
        value = jnp.concatenate(value, axis=0).astype(F32)
        high, low = two_parts(dot(lift_ref[g], spread) * value)
        direct = dot(score_ref[g, 0], high) + dot(score_ref[g, 0], low) + dot(score_ref[g, 1], high)
        total = dot(read_ref[0, g], spread) * direct + skip * value
        for level, (state, row) in enumerate(states):
            total = total + dot(cross_ref[level, g], spread) * (dot(out_ref[g], state) * row)
        pre_ref[g] = total
        nodes[g] = dot(masked_ref[g], high) + dot(masked_ref[g], low)

    def gain(level, g, first, count):
        at = slice(first * CH, (first + count) * CH)
        readers = out_ref[g, at, :]
        twice = jnp.concatenate([readers, readers], axis=1)
        gained = dot(twice, operand[level - 1])
        pre_ref[g, at, :] += dot(read_ref[level, g, at, :], spread) * gained

    for c in range(stretches):
        g, s = divmod(c, per_group)
        level = 1
        while 2 ** (level - 1) < stretches:
            span = 2 ** (level - 1)
            if c % (2 * span) == span:
                for other in range(c, c + span, per_group):
                    gain(level, other // per_group, other % per_group, min(span, per_group))
            level += 1
        if c + 1 < stretches:
            row = place[("own", c, 0)]
            node = nodes[g, s * state_size : (s + 1) * state_size, :] * merges[row : row + 1, :]
            k = 0
            while (c >> k) & 1:
                row = place[("merge", c, k)]
                node = node + merges[row : row + 1, :] * sums[k]
                k += 1
            sums[k] = node
            n_high, n_low = two_parts(node)
            operand[k, :state_size, :] = n_high
            operand[k, state_size:, :] = n_low


def finish_kernel(
    me_ref, pre_ref, out_ref, cross_ref, factor_ref, state_ref, spread_ref, same_ref, gain_ref, *refs
):
    parts = pre_ref.shape[0]
    me = me_ref[0]
    spread = spread_ref[...]
    same = same_ref[...]
    gain = gain_ref[...]
    state = state_ref[: out_ref.shape[2], :]
    row = dot(factor_ref[...], spread)[0:1, :]
    for r in range(parts):
        at = me ^ r
        total = pre_ref[at] + dot(cross_ref[0, at], spread) * (dot(out_ref[at], state) * row)
        mean_square = dot((total * total).astype(BF16), same)
        normed = (total * lax.rsqrt(mean_square + EPSILON) * gain).astype(BF16)
        refs[r][...] = normed


def project_kernel(place_ref, *refs):
    *refs, out_ref = refs
    rows = out_ref.shape[0]
    kept_refs, other_refs, refs = refs[:rows], refs[rows : 2 * rows], refs[2 * rows :]
    count = len(refs) // 2
    weights, partners = refs[:count], refs[count:]
    width = weights[0].shape[0]
    for i, (kept_ref, other_ref) in enumerate(zip(kept_refs, other_refs)):
        found = [
            dot_nt(kept_ref[...], weight[...]) + dot_nt(other_ref[...], partner[...])
            for weight, partner in zip(weights, partners)
        ]
        for bit in range(count.bit_length() - 1):
            turn = place_ref[0] // 2**bit % 2 == 1
            found = [jnp.where(turn, found[j ^ 2**bit], found[j]) for j in range(count)]
        for j, result in enumerate(found):
            out_ref[i, :, j * width : (j + 1) * width] = result.astype(out_ref.dtype)


def assemble_kernel(place_ref, *refs):
    out_ref = refs[-1]
    width = refs[0].shape[1]
    groups = out_ref.shape[1] // width
    each = (len(refs) - 1) // groups
    for p in range(groups):
        own_ref, *far_refs = refs[p * each : (p + 1) * each]
        total = own_ref[...]
        for far_ref in far_refs:
            total = total + far_ref[...].astype(F32)
        start = pl.multiple_of((place_ref[0] ^ p) * width, width)
        out_ref[:, pl.ds(start, width)] = total.astype(BF16)


def feature_tile(features):
    for tile in (256, 128):
        if features % tile == 0:
            return tile
    return features


def whole(shape):
    return pl.BlockSpec(shape, lambda *_: (0,) * len(shape))


def on_device(
    values,
    state_in,
    state_out,
    log_decay,
    level_class,
    level_table,
    skip_gain,
    norm_gain,
    out_weight,
):
    heads_size = lax.axis_size("head")
    ctx_size = lax.axis_size("ctx")
    ctx_bits = ctx_size.bit_length() - 1
    me = lax.axis_index("head")
    me1 = me.reshape(1).astype(jnp.int32)
    position = lax.axis_index("ctx")
    tokens = state_in.shape[0]
    rows_dev = values.shape[0]
    head_count = log_decay.shape[1]
    features = values.shape[1] // heads_size
    head_width = features // head_count
    state_size = state_in.shape[1]
    stretches = tokens // CH
    local = stretches.bit_length() - 1
    levels = level_table.shape[1]
    wide = 2 * head_count
    tile = feature_tile(features)
    tiles = features // tile
    half = heads_size // 2
    params = pltpu.CompilerParams(vmem_limit_bytes=VMEM_LIMIT)
    cheap = pl.CostEstimate(flops=0, bytes_accessed=0, transcendentals=0)

    def kernel_call(body, name, out_shape, **kwargs):
        return pl.pallas_call(
            body, out_shape=out_shape, compiler_params=params, cost_estimate=cheap, name=name, **kwargs
        )

    def shape(dims, kind=BF16):
        return jax.ShapeDtypeStruct(dims, kind)

    smem = pl.BlockSpec(memory_space=pltpu.SMEM)
    vmem = pl.BlockSpec(memory_space=pltpu.VMEM)
    place1 = position.reshape(1).astype(jnp.int32)

    def fenced(body, *operands):
        shapes = jax.eval_shape(body, *operands)
        zeros = lambda *_: jax.tree.map(lambda leaf: jnp.zeros(leaf.shape, leaf.dtype), shapes)
        return lax.cond(position < ctx_size, body, zeros, *operands)

    columns = out_weight.shape[1]
    near = ctx_bits - 1
    grouped = (heads_size, rows_dev)
    spread = (
        jnp.arange(wide)[:, None] % head_count == (jnp.arange(features) // head_width)[None, :]
    ).astype(BF16)
    same = (
        (jnp.arange(tile)[:, None] // head_width == jnp.arange(tile)[None, :] // head_width)
        / head_width
    ).astype(BF16)

    held, partners = {0: out_weight.T}, {}
    for bit in range(ctx_bits):
        held[2**bit] = swap(held[0], "ctx", 2**bit)

    def value_columns(values, r):
        return lax.dynamic_slice_in_dim(values, (me ^ r) * features, features, 1)

    value_head = swap(value_columns(values, 2), "head", 2)

    fade, total = kernel_call(
        fade_kernel,
        "fade",
        (shape(grouped + (wide,)), shape((1, wide), F32)),
        in_specs=[smem, vmem],
    )(me1, log_decay)
    near_fades, side_fades = [fade[0]], [fade[1]]
    for d in range(2, heads_size, 2):
        got = swap(tie(fade[d : d + 2], near_fades[-1]), "head", d)
        near_fades.append(got[0])
        side_fades.append(got[1])
    sides = swap(jnp.stack(side_fades), "head", 1)
    fades = []
    for d in range(half):
        fades += [near_fades[d], sides[d]]

    in_turned = lax.dynamic_slice_in_dim(state_in, me * rows_dev, rows_dev, 0).T
    keep, send = kernel_call(
        partial_state_kernel,
        "partial_states",
        (shape((half, state_size, features), F32), shape((half, state_size, features))),
        grid_spec=pltpu.PrefetchScalarGridSpec(
            num_scalar_prefetch=1,
            grid=(half,),
            in_specs=[
                pl.BlockSpec((rows_dev, features), lambda i, m: (0, m[0] ^ (2 * i))),
                pl.BlockSpec((rows_dev, features), lambda i, m: (0, m[0] ^ (2 * i + 1))),
            ]
            + [whole((rows_dev, wide))] * heads_size
            + [whole((state_size, rows_dev)), whole((wide, features))],
            out_specs=[
                pl.BlockSpec((1, state_size, features), lambda i, m: (i, 0, 0)),
                pl.BlockSpec((1, state_size, features), lambda i, m: (i, 0, 0)),
            ],
        ),
    )(me1, values, values, *fades, in_turned, spread)

    def core_sum(keep, send):
        own_state, *far_states = kernel_call(
            fold_kernel,
            "fold",
            tuple(
                [shape((state_size, features), F32)] + [shape((state_size, features))] * (half - 1)
            ),
        )(keep, swap(send, "head", 1))
        return own_state, far_states

    own_state, far_states = fenced(core_sum, keep, send)

    merge_count = -(-len(merge_rows(stretches)) // 16) * 16

    def chip_sum(
        own_state, far_states, total, log_decay, level_class, level_table, state_in, state_out, values
    ):
        across = jnp.stack([value_columns(values, d + 1) for d in range(0, heads_size, 2)])
        across = swap(across, "head", 1)
        table = jnp.transpose(level_table, (1, 0, 2))
        table = jnp.concatenate([table, table], axis=2)
        tables = kernel_call(
            factors_kernel,
            "factors",
            (
                shape((tokens, wide)),
                shape((local + 1, tokens, wide)),
                shape((levels - local - 1, tokens, wide)),
                shape((merge_count, wide)),
                shape((heads_size, 2, rows_dev, rows_dev)),
                shape((heads_size, rows_dev // CH * state_size, rows_dev)),
            ),
        )(log_decay, level_class.reshape(tokens, 1), table, state_in, state_out)
        got_states = []
        for i, far in enumerate(far_states):
            got_states.append(swap(tie(far, *got_states), "head", 2 * (i + 1)))
        running, sent = kernel_call(
            first_kernel,
            "first_state",
            (shape((state_size, features), F32), shape((state_size + EXTRA, features))),
        )(own_state, total, *got_states)
        return running, sent, tables, across

    running, sent, tables, across = fenced(
        chip_sum, own_state, tie(far_states, value_head), total, log_decay, level_class, level_table,
        state_in, state_out, values,
    )
    lift, read, cross, merge, scores, masked = tables

    def step(bit, running, total, offset, sent, spread, passing):
        passed = [swap(array, "head", d) for array, d in zip(passing, distances[bit])]
        got = swap(sent, "ctx", 2**bit)
        merged = kernel_call(
            functools.partial(merge_kernel, bit),
            "merge",
            (
                shape((state_size, features), F32),
                shape((1, wide), F32),
                shape((1, wide), F32),
                shape((EXTRA, wide)),
                shape((state_size + EXTRA, features)),
            ),
            in_specs=[smem] + [vmem] * 5,
        )(place1, running, total, offset, got, spread)
        return got, merged, passed

    pending = [(d, across[d // 2]) for d in range(2, heads_size, 2)]
    pending += [(d, value_columns(values, d)) for d in range(4, heads_size, 2)]
    pieces = max(near, 1)
    cut = rows_dev // pieces // 16 * 16
    cuts = [(i * cut, rows_dev if i + 1 == pieces else (i + 1) * cut) for i in range(pieces)]
    distances = [[d for d, _ in pending]] * pieces
    factor = jnp.broadcast_to((position % 2).astype(BF16), (EXTRA, wide))
    factors = [jnp.where(jnp.arange(wide)[None, :] < head_count, factor, 0)]
    offset = jnp.zeros((1, wide), F32)
    states, passed = [], []
    for bit in range(near):
        if bit == 0:
            sent = tie(sent, held[1])
        if bit == 1:
            sent = tie(sent, held[2])
        passing = [array[cuts[bit][0] : cuts[bit][1]] for _, array in pending]
        got, merged, moved = fenced(
            functools.partial(step, bit), running, total, offset, sent, spread, passing
        )
        running, total, offset, factor, sent = merged
        states.append(got)
        factors.append(factor)
        passed.append(moved)

    sent = tie(sent, *[held[2**bit] for bit in range(1, ctx_bits)])
    for r in range(2, ctx_size):
        low = r & -r
        if r not in held and low > 1:
            held[r] = swap(tie(held[r ^ low], sent), "ctx", low)
    for bit in range(2, ctx_bits):
        held[2**bit + 1] = swap(tie(held[2**bit], sent), "ctx", 1)
    for r in (0, 1):
        partners[r] = swap(tie(held[r], sent), "head", 1)

    arrays = [values, across[0], value_head]
    parts = [[(0, 0, rows_dev)], [(1, 0, rows_dev)], [(2, 0, rows_dev)]]
    order = {}
    for i, (d, _) in enumerate(pending):
        r = d + 1 if i < half - 1 else d
        order[r] = []
        for step_index, (start, end) in enumerate(cuts):
            order[r].append((len(arrays), 0, end - start))
            arrays.append(passed[step_index][i])
    parts += [order[r] for r in range(3, heads_size)]

    skip_row = jnp.repeat(skip_gain, head_width)[None, :]

    def read_levels(sent, state_out, tables, factors, states, arrays, spread, same, skip_row, norm_row):
        lift, read, cross, merge, scores, masked = tables
        state = swap(sent, "ctx", 2**near)
        readers = state_out.reshape(grouped + (state_size,))
        cross = cross.reshape((ctx_bits,) + grouped + (wide,))
        pre = kernel_call(
            lambda me_ref, *refs: local_kernel(me_ref, near, parts, *refs),
            "local_levels",
            shape(grouped + (features,), F32),
            grid_spec=pltpu.PrefetchScalarGridSpec(
                num_scalar_prefetch=1,
                grid=(tiles,),
                in_specs=[pl.BlockSpec((rows_dev, tile), lambda f, m: (0, m[0] * tiles + f))]
                + [pl.BlockSpec((array.shape[0], tile), lambda f, m: (0, f)) for array in arrays[1:]]
                + [
                    whole(readers.shape),
                    whole(grouped + (wide,)),
                    whole((local + 1,) + grouped + (wide,)),
                    whole((merge_count, wide)),
                    whole(scores.shape),
                    whole(masked.shape),
                    pl.BlockSpec((wide, tile), lambda f, m: (0, f)),
                    pl.BlockSpec((1, tile), lambda f, m: (0, f)),
                    whole(cross.shape),
                ]
                + [whole((EXTRA, wide))] * near
                + [pl.BlockSpec((state_size + EXTRA, tile), lambda f, m: (0, f))] * near,
                out_specs=pl.BlockSpec(grouped + (tile,), lambda f, m: (0, 0, f)),
                scratch_shapes=[
                    pltpu.VMEM((heads_size, rows_dev // CH * state_size, tile), F32),
                    pltpu.VMEM((max(local, 1), state_size, tile), F32),
                    pltpu.VMEM((max(local, 1), 2 * state_size, tile), BF16),
                ],
            ),
        )(
            me1,
            *arrays,
            readers,
            lift.reshape(grouped + (wide,)),
            read.reshape((local + 1,) + grouped + (wide,)),
            merge,
            scores,
            masked,
            spread,
            skip_row,
            cross,
            *factors[:near],
            *states,
        )
        return kernel_call(
            finish_kernel,
            "finish",
            tuple([shape((rows_dev, features))] * heads_size),
            grid_spec=pltpu.PrefetchScalarGridSpec(
                num_scalar_prefetch=1,
                grid=(tiles,),
                in_specs=[
                    pl.BlockSpec(grouped + (tile,), lambda f, m: (0, 0, f)),
                    whole(readers.shape),
                    pl.BlockSpec((1,) + grouped + (wide,), lambda f, m: (near, 0, 0, 0)),
                    whole((EXTRA, wide)),
                    pl.BlockSpec((state_size + EXTRA, tile), lambda f, m: (0, f)),
                    pl.BlockSpec((wide, tile), lambda f, m: (0, f)),
                    whole((tile, tile)),
                    pl.BlockSpec((1, tile), lambda f, m: (0, f)),
                ],
                out_specs=[pl.BlockSpec((rows_dev, tile), lambda f, m: (0, f))] * heads_size,
            ),
        )(me1, pre, readers, cross, factors[near], state, spread, same, norm_row)

    normed = fenced(
        read_levels, sent, state_out, tables, factors, states, arrays, spread, same, skip_row,
        norm_gain[None, :],
    )
    early_blocks = set(held)
    done = [held[r] for r in held if r not in (0, 1)] + list(normed)
    held[3] = swap(tie(held[1], *done), "ctx", 2)
    for r in range(5, ctx_size, 2):
        if r not in held:
            held[r] = swap(tie(held[r ^ 1], *done), "ctx", 1)

    count = 1
    while count * columns % 128 and 2 * count <= ctx_size:
        count *= 2

    def project(name, kept, others, blocks, partners, kind):
        return kernel_call(
            project_kernel,
            name,
            shape((len(kept), rows_dev, count * columns), kind),
            in_specs=[smem] + [vmem] * (2 * len(kept) + 2 * count),
        )(place1, *kept, *others, *blocks, *partners)

    kept = list(normed[0::2])
    sides = list(normed[1::2])
    group_of = lambda first: range(first, first + count)

    def project_groups(firsts, kept, others, blocks, partners, arrived):
        partners, results = dict(partners), {}
        for first in firsts:
            for r in group_of(first):
                if r not in partners:
                    partners[r] = swap(blocks[r], "head", 1)
            weights = [blocks[r] for r in group_of(first)]
            given = [partners[r] for r in group_of(first)]
            far = project("project_far", kept[1:], others[1:], weights, given, BF16)
            if arrived:
                far = tie(far, arrived[-1])
            got = [swap(far[i - 1], "head", 2 * i) for i in range(1, half)]
            own = project("project_own", kept[:1], others[:1], weights, given, F32)
            results[first] = [own[0]] + got
            arrived = arrived + got[-1:]
        return results

    def first_groups(kept, sides, blocks, partners):
        others = [swap(side, "head", 1) for side in sides[1:]]
        partners = dict(partners)
        for r in first_blocks:
            if r not in partners:
                partners[r] = swap(blocks[r], "head", 1)
        others = [swap(tie(sides[0], *others, partners[first_blocks[-1]]), "head", 1)] + others
        return project_groups(early_groups, kept, others, blocks, partners, []), others

    def last_groups(kept, others, blocks, partners):
        return project_groups(late_groups, kept, others, blocks, partners, [])

    firsts = list(range(0, ctx_size, count))
    early_groups = [f for f in firsts if all(r in early_blocks for r in group_of(f))]
    early_groups = early_groups or firsts[:1]
    late_groups = [f for f in firsts if f not in early_groups]
    first_blocks = [r for f in early_groups for r in group_of(f)]
    last_blocks = [r for f in late_groups for r in group_of(f)]
    results, others = fenced(
        first_groups, kept, sides, {r: held[r] for r in first_blocks}, partners
    )
    if late_groups:
        results.update(
            fenced(last_groups, kept, others, {r: held[r] for r in last_blocks}, {})
        )
    pieces = [piece for first in firsts for piece in results[first]]
    return kernel_call(
        assemble_kernel,
        "assemble",
        shape((rows_dev, ctx_size * columns)),
        in_specs=[smem] + [vmem] * len(pieces),
    )(place1 // count, *pieces)


def solution(mesh):
    return jax.shard_map(
        on_device,
        mesh=mesh,
        in_specs=(
            P(("ctx", "head"), None),
            P("ctx", None),
            P("ctx", None),
            P("ctx", "head"),
            P("ctx"),
            P(None, None, "head"),
            P("head"),
            P("head"),
            P("head", "ctx"),
        ),
        out_specs=P(("ctx", "head"), None),
        check_vma=False,
    )
```

```python
import functools

import jax
import jax.numpy as jnp
from jax import lax
from jax.experimental import pallas as pl
from jax.experimental.pallas import tpu as pltpu
from jax.sharding import PartitionSpec as P

CH = 64
EPSILON = 1e-05
EXTRA = 16
F32 = jnp.float32
BF16 = jnp.bfloat16
VMEM_LIMIT = 32 * 1024 * 1024


def dot(a, b):
    return lax.dot_general(a, b, (((1,), (0,)), ((), ())), preferred_element_type=F32)


def dot_t(a, b):
    return lax.dot_general(a, b, (((0,), (0,)), ((), ())), preferred_element_type=F32)


def dot_nt(a, b):
    return lax.dot_general(a, b, (((1,), (1,)), ((), ())), preferred_element_type=F32)


def swap(value, axis, distance):
    pairs = [(source, source ^ distance) for source in range(lax.axis_size(axis))]
    return lax.ppermute(value, axis, pairs)


def tie(value, *after):
    return lax.optimization_barrier((value,) + after)[0]


def three_parts(x):
    high = x.astype(BF16)
    rest = x - high.astype(F32)
    middle = rest.astype(BF16)
    low = (rest - middle.astype(F32)).astype(BF16)
    return high, middle, low


def two_parts(x):
    high = x.astype(BF16)
    return high, (x - high.astype(F32)).astype(BF16)


def halves(x, head_count):
    high = x.astype(BF16).astype(F32)
    lane = lax.broadcasted_iota(jnp.int32, x.shape, x.ndim - 1)
    return jnp.where(lane < head_count, high, x - high).astype(BF16)


def merge_rows(stretches):
    rows = [("own", c, 0) for c in range(stretches - 1)]
    for c in range(stretches - 1):
        k = 0
        while (c >> k) & 1:
            rows.append(("merge", c, k))
            k += 1
    return rows


def stretch_sums(decay_ref):
    tokens, width = decay_ref.shape
    row = lax.broadcasted_iota(jnp.int32, (CH, CH), 0)
    col = lax.broadcasted_iota(jnp.int32, (CH, CH), 1)
    lower = jnp.where(row >= col, 1.0, 0.0).astype(BF16)
    lower = jnp.concatenate([lower] * 3, axis=1)
    within, starts = [], [jnp.zeros((1, width), F32)]
    for c in range(tokens // CH):
        parts = jnp.concatenate(three_parts(decay_ref[c * CH : (c + 1) * CH, :]), axis=0)
        summed = dot(lower, parts)
        within.append(summed)
        starts.append(starts[-1] + summed[CH - 1 : CH, :])
    return within, starts


def fade_kernel(me_ref, decay_ref, fade_ref, total_ref):
    blocks, rows_dev, _ = fade_ref.shape
    head_count = decay_ref.shape[1]
    within, starts = stretch_sums(decay_ref)
    total = starts[-1]
    total_ref[...] = jnp.concatenate([total, total], axis=1)
    per_block = rows_dev // CH
    me = me_ref[0]
    for block in range(blocks):
        for c in range(block * per_block, (block + 1) * per_block):
            factor = jnp.exp(total - starts[c] - within[c])
            factor = halves(jnp.concatenate([factor, factor], axis=1), head_count)
            first = (c - block * per_block) * CH
            fade_ref[me ^ block, first : first + CH, :] = factor


def factors_kernel(
    decay_ref, class_ref, table_ref, in_ref, out_ref,
    lift_ref, read_ref, cross_ref, merge_ref, score_ref, masked_ref,
):
    tokens, head_count = decay_ref.shape
    width = 2 * head_count
    stretches = tokens // CH
    levels, classes, _ = table_ref.shape
    local = read_ref.shape[0] - 1
    tables = [jnp.concatenate(three_parts(table_ref[level]), axis=0) for level in range(levels)]
    within, starts = stretch_sums(decay_ref)
    within = [jnp.concatenate([x, x], axis=1) for x in within]
    starts = [jnp.concatenate([x, x], axis=1) for x in starts]
    class_iota = lax.broadcasted_iota(jnp.int32, (CH, 3 * classes), 1) % classes
    for c in range(stretches):
        rows = slice(c * CH, (c + 1) * CH)
        lift_ref[rows, :] = halves(jnp.exp(-within[c]), head_count)
        onehot = jnp.where(class_ref[rows, :] == class_iota, 1.0, 0.0).astype(BF16)
        read_ref[0, rows, :] = halves(jnp.exp(within[c]) * dot(onehot, tables[0]), head_count)
        for level in range(1, local + 1):
            if (c >> (level - 1)) & 1:
                begin = starts[c] - starts[(c >> (level - 1)) << (level - 1)]
                factor = jnp.exp(within[c] + begin) * dot(onehot, tables[level])
                read_ref[level, rows, :] = halves(factor, head_count)
            else:
                read_ref[level, rows, :] = jnp.zeros((CH, width), BF16)
        far = jnp.exp(within[c] + starts[c])
        for level in range(local + 1, levels):
            far_factor = far * dot(onehot, tables[level])
            cross_ref[level - local - 1, rows, :] = halves(far_factor, head_count)
    exps = []
    for kind, c, k in merge_rows(stretches):
        first = c if kind == "own" else c + 1 - 2**k
        exps.append(jnp.exp(starts[c + 1] - starts[first]))
    exps += [jnp.zeros((1, width), F32)] * (merge_ref.shape[0] - len(exps))
    merge_ref[...] = halves(jnp.concatenate(exps, axis=0), head_count)
    groups, _, group_rows, _ = score_ref.shape
    row = lax.broadcasted_iota(jnp.int32, (group_rows, group_rows), 0)
    col = lax.broadcasted_iota(jnp.int32, (group_rows, group_rows), 1)
    inside = (row // CH == col // CH) & (row >= col)
    state_size = in_ref.shape[1]
    lane = lax.broadcasted_iota(jnp.int32, (state_size, group_rows), 1) // CH
    for g in range(groups):
        rows = slice(g * group_rows, (g + 1) * group_rows)
        scores = jnp.where(inside, dot_nt(out_ref[rows, :], in_ref[rows, :]), 0.0)
        score_ref[g, 0], score_ref[g, 1] = two_parts(scores)
        turned = jnp.transpose(in_ref[rows, :].astype(F32))
        for s in range(group_rows // CH):
            at = slice(s * state_size, (s + 1) * state_size)
            masked_ref[g, at, :] = jnp.where(lane == s, turned, 0.0).astype(BF16)


def partial_state_kernel(me_ref, *refs):
    even_ref, odd_ref, *fade_refs = refs[:-4]
    in_ref, spread_ref, keep_ref, send_ref = refs[-4:]
    spread = spread_ref[...]
    turned = in_ref[...]
    for i in range(len(fade_refs) // 2):

        @pl.when(pl.program_id(0) == i)
        def _():
            odd = (dot(fade_refs[2 * i + 1][...], spread) * odd_ref[...].astype(F32)).astype(BF16)
            send_ref[0] = dot(turned, odd).astype(BF16)
            even = (dot(fade_refs[2 * i][...], spread) * even_ref[...].astype(F32)).astype(BF16)
            keep_ref[0] = dot(turned, even)


def split_kernel(me_ref, *refs):
    half = len(refs) // 2
    for value_ref, part_ref in zip(refs[:half], refs[half:]):
        part_ref[...] = value_ref[...]


def fold_kernel(*refs):
    count = len(refs) // 3
    for keep_ref, got_ref, far_ref in zip(refs[:count], refs[count : 2 * count], refs[2 * count :]):
        far_ref[...] = (keep_ref[0] + got_ref[0].astype(F32)).astype(BF16)


def pack_state(sent_ref, state, total):
    rows, width = state.shape[0], total.shape[1]
    sent_ref[:rows, :] = state.astype(BF16)
    sent_ref[rows:, :] = jnp.zeros((EXTRA, state.shape[1]), BF16)
    parts = list(three_parts(total))
    parts.append(jnp.zeros((EXTRA - len(parts), width), BF16))
    sent_ref[rows:, :width] = jnp.concatenate(parts, axis=0)


def first_kernel(own_ref, core_ref, total_ref, *refs):
    *far_refs, running_ref, sent_ref = refs
    running = own_ref[0] + core_ref[0].astype(F32)
    for far_ref in far_refs:
        running = running + far_ref[...].astype(F32)
    running_ref[...] = running
    pack_state(sent_ref, running, total_ref[...])


def merge_kernel(
    bit, place_ref, running_ref, total_ref, offset_ref, got_ref, spread_ref,
    next_running_ref, next_total_ref, next_offset_ref, factor_ref, sent_ref,
):
    rows, width = running_ref.shape[0], total_ref.shape[1]
    head_count = width // 2
    place = place_ref[0]
    upper = place // 2**bit % 2 == 1
    total = total_ref[...]
    parts = got_ref[rows:, :width].astype(F32)
    partner = parts[0:1] + parts[1:2] + parts[2:3]
    fading = jnp.exp(jnp.where(upper, total, partner))
    fading = halves(jnp.broadcast_to(fading, (EXTRA, width)), head_count)
    fading = dot(fading, spread_ref[...])[0:1, :]
    got, running = got_ref[:rows, :].astype(F32), running_ref[...]
    merged = fading * jnp.where(upper, got, running) + jnp.where(upper, running, got)
    next_running_ref[...] = merged
    joined = total + partner
    next_total_ref[...] = joined
    offset = jnp.where(upper, offset_ref[...] + partner, offset_ref[...])
    next_offset_ref[...] = offset
    next_upper = place // 2 ** (bit + 1) % 2 == 1
    factor = jnp.where(next_upper, jnp.exp(offset), 0.0)
    factor_ref[...] = halves(jnp.broadcast_to(factor, (EXTRA, width)), head_count)
    pack_state(sent_ref, merged, joined)


def local_kernel(me_ref, near, parts, *refs):
    value_refs, refs = refs[:parts], refs[parts:]
    out_ref, lift_ref, read_ref, merge_ref, score_ref, masked_ref, spread_ref = refs[:7]
    skip_ref, cross_ref, *refs = refs[7:]
    factor_refs, state_refs, refs = refs[:near], refs[near : 2 * near], refs[2 * near :]
    pre_ref, nodes, sums, operand = refs
    group_rows = value_refs[0].shape[0]
    groups = parts
    me = me_ref[0]
    per_group = group_rows // CH
    stretches = groups * per_group
    state_size = out_ref.shape[2]
    spread = spread_ref[...]
    merges = dot(merge_ref[...], spread)
    place = {kind: i for i, kind in enumerate(merge_rows(stretches))}
    skip = skip_ref[...]
    states = [
        (state_ref[:state_size, :], dot(factor_ref[...], spread)[0:1, :])
        for state_ref, factor_ref in zip(state_refs, factor_refs)
    ]
    for r, value_ref in enumerate(value_refs):
        g = me ^ r
        value = value_ref[...].astype(F32)
        high, low = two_parts(dot(lift_ref[g], spread) * value)
        direct = dot(score_ref[g, 0], high) + dot(score_ref[g, 0], low) + dot(score_ref[g, 1], high)
        total = dot(read_ref[0, g], spread) * direct + skip * value
        for level, (state, row) in enumerate(states):
            total = total + dot(cross_ref[level, g], spread) * (dot(out_ref[g], state) * row)
        pre_ref[g] = total
        nodes[g] = dot(masked_ref[g], high) + dot(masked_ref[g], low)

    def gain(level, g, first, count):
        at = slice(first * CH, (first + count) * CH)
        readers = out_ref[g, at, :]
        twice = jnp.concatenate([readers, readers], axis=1)
        gained = dot(twice, operand[level - 1])
        pre_ref[g, at, :] += dot(read_ref[level, g, at, :], spread) * gained

    for c in range(stretches):
        g, s = divmod(c, per_group)
        level = 1
        while 2 ** (level - 1) < stretches:
            span = 2 ** (level - 1)
            if c % (2 * span) == span:
                for other in range(c, c + span, per_group):
                    gain(level, other // per_group, other % per_group, min(span, per_group))
            level += 1
        if c + 1 < stretches:
            row = place[("own", c, 0)]
            node = nodes[g, s * state_size : (s + 1) * state_size, :] * merges[row : row + 1, :]
            k = 0
            while (c >> k) & 1:
                row = place[("merge", c, k)]
                node = node + merges[row : row + 1, :] * sums[k]
                k += 1
            sums[k] = node
            n_high, n_low = two_parts(node)
            operand[k, :state_size, :] = n_high
            operand[k, state_size:, :] = n_low


def finish_kernel(
    me_ref, pre_ref, out_ref, cross_ref, factor_ref, state_ref, spread_ref, same_ref, gain_ref, *refs
):
    *keep_refs, send_ref = refs
    parts = pre_ref.shape[0]
    me = me_ref[0]
    spread = spread_ref[...]
    same = same_ref[...]
    gain = gain_ref[...]
    state = state_ref[: out_ref.shape[2], :]
    row = dot(factor_ref[...], spread)[0:1, :]
    for r in range(parts):
        at = me ^ r
        total = pre_ref[at] + dot(cross_ref[0, at], spread) * (dot(out_ref[at], state) * row)
        mean_square = dot((total * total).astype(BF16), same)
        normed = (total * lax.rsqrt(mean_square + EPSILON) * gain).astype(BF16)
        if r % 2 == 0:
            keep_refs[r // 2][...] = normed
        else:
            send_ref[r // 2] = normed


def project_kernel(place_ref, *refs):
    *refs, out_ref = refs
    rows = out_ref.shape[0]
    kept_refs, other_refs, refs = refs[:rows], refs[rows : 2 * rows], refs[2 * rows :]
    count = len(refs) // 2
    weights, partners = refs[:count], refs[count:]
    width = weights[0].shape[0]
    for i, (kept_ref, other_ref) in enumerate(zip(kept_refs, other_refs)):
        found = [
            dot_nt(kept_ref[...], weight[...]) + dot_nt(other_ref[0], partner[...])
            for weight, partner in zip(weights, partners)
        ]
        for bit in range(count.bit_length() - 1):
            turn = place_ref[0] // 2**bit % 2 == 1
            found = [jnp.where(turn, found[j ^ 2**bit], found[j]) for j in range(count)]
        for j, result in enumerate(found):
            out_ref[i, :, j * width : (j + 1) * width] = result.astype(out_ref.dtype)


def assemble_kernel(place_ref, *refs):
    out_ref = refs[-1]
    width = refs[0].shape[1]
    groups = out_ref.shape[1] // width
    each = (len(refs) - 1) // groups
    for p in range(groups):
        own_ref, *far_refs = refs[p * each : (p + 1) * each]
        total = own_ref[...]
        for far_ref in far_refs:
            total = total + far_ref[...].astype(F32)
        start = pl.multiple_of((place_ref[0] ^ p) * width, width)
        out_ref[:, pl.ds(start, width)] = total.astype(BF16)


def feature_tile(features):
    for tile in (256, 128):
        if features % tile == 0:
            return tile
    return features


def whole(shape):
    return pl.BlockSpec(shape, lambda *_: (0,) * len(shape))


def on_device(
    values,
    state_in,
    state_out,
    log_decay,
    level_class,
    level_table,
    skip_gain,
    norm_gain,
    out_weight,
):
    heads_size = lax.axis_size("head")
    ctx_size = lax.axis_size("ctx")
    ctx_bits = ctx_size.bit_length() - 1
    me = lax.axis_index("head")
    me1 = me.reshape(1).astype(jnp.int32)
    position = lax.axis_index("ctx")
    tokens = state_in.shape[0]
    rows_dev = values.shape[0]
    head_count = log_decay.shape[1]
    features = values.shape[1] // heads_size
    head_width = features // head_count
    state_size = state_in.shape[1]
    stretches = tokens // CH
    local = stretches.bit_length() - 1
    levels = level_table.shape[1]
    wide = 2 * head_count
    tile = feature_tile(features)
    tiles = features // tile
    half = heads_size // 2
    params = pltpu.CompilerParams(vmem_limit_bytes=VMEM_LIMIT)
    cheap = pl.CostEstimate(flops=0, bytes_accessed=0, transcendentals=0)

    def kernel_call(body, name, out_shape, **kwargs):
        return pl.pallas_call(
            body, out_shape=out_shape, compiler_params=params, cost_estimate=cheap, name=name, **kwargs
        )

    def shape(dims, kind=BF16):
        return jax.ShapeDtypeStruct(dims, kind)

    smem = pl.BlockSpec(memory_space=pltpu.SMEM)
    vmem = pl.BlockSpec(memory_space=pltpu.VMEM)
    place1 = position.reshape(1).astype(jnp.int32)

    def fenced(body, *operands):
        shapes = jax.eval_shape(body, *operands)
        zeros = lambda *_: jax.tree.map(lambda leaf: jnp.zeros(leaf.shape, leaf.dtype), shapes)
        return lax.cond(position < ctx_size, body, zeros, *operands)

    columns = out_weight.shape[1]
    near = ctx_bits - 1
    grouped = (heads_size, rows_dev)
    spread = (
        jnp.arange(wide)[:, None] % head_count == (jnp.arange(features) // head_width)[None, :]
    ).astype(BF16)
    same = (
        (jnp.arange(tile)[:, None] // head_width == jnp.arange(tile)[None, :] // head_width)
        / head_width
    ).astype(BF16)

    held, partners = {0: out_weight.T}, {}
    for bit in range(ctx_bits):
        held[2**bit] = swap(held[0], "ctx", 2**bit)

    portions = kernel_call(
        split_kernel,
        "split_values",
        tuple([shape((rows_dev, features))] * (heads_size - 1)),
        grid_spec=pltpu.PrefetchScalarGridSpec(
            num_scalar_prefetch=1,
            grid=(1,),
            in_specs=[
                pl.BlockSpec((rows_dev, features), lambda i, m, r=r: (0, m[0] ^ r))
                for r in range(1, heads_size)
            ],
            out_specs=[whole((rows_dev, features))] * (heads_size - 1),
        ),
    )(me1, *[values] * (heads_size - 1))
    portion = dict(zip(range(1, heads_size), portions))
    value_head = swap(portion[2], "head", 2)

    fade, total = kernel_call(
        fade_kernel,
        "fade",
        (shape(grouped + (wide,)), shape((1, wide), F32)),
        in_specs=[smem, vmem],
    )(me1, log_decay)
    near_fades, side_fades = [fade[0]], [fade[1]]
    for d in range(2, heads_size, 2):
        got = swap(tie(fade[d : d + 2], near_fades[-1]), "head", d)
        near_fades.append(got[0])
        side_fades.append(got[1])
    sides = swap(jnp.stack(side_fades), "head", 1)
    fades = []
    for d in range(half):
        fades += [near_fades[d], sides[d]]

    in_turned = lax.dynamic_slice_in_dim(state_in, me * rows_dev, rows_dev, 0).T
    keep, send = kernel_call(
        partial_state_kernel,
        "partial_states",
        (shape((half, state_size, features), F32), shape((half, state_size, features))),
        grid_spec=pltpu.PrefetchScalarGridSpec(
            num_scalar_prefetch=1,
            grid=(half,),
            in_specs=[
                pl.BlockSpec((rows_dev, features), lambda i, m: (0, m[0] ^ (2 * i))),
                pl.BlockSpec((rows_dev, features), lambda i, m: (0, m[0] ^ (2 * i + 1))),
            ]
            + [whole((rows_dev, wide))] * heads_size
            + [whole((state_size, rows_dev)), whole((wide, features))],
            out_specs=[
                pl.BlockSpec((1, state_size, features), lambda i, m: (i, 0, 0)),
                pl.BlockSpec((1, state_size, features), lambda i, m: (i, 0, 0)),
            ],
        ),
    )(me1, values, values, *fades, in_turned, spread)

    def core_sum(keep, send):
        got = swap(send, "head", 1)
        far = kernel_call(
            fold_kernel,
            "fold",
            tuple([shape((state_size, features))] * (half - 1)),
            in_specs=[
                pl.BlockSpec((1, state_size, features), lambda _, i=i: (i, 0, 0))
                for i in range(1, half)
            ]
            * 2,
            out_specs=tuple([whole((state_size, features))] * (half - 1)),
            grid=(1,),
        )(*[keep] * (half - 1), *[got] * (half - 1))
        return got, far

    core_states, far_states = fenced(core_sum, keep, send)

    merge_count = -(-len(merge_rows(stretches)) // 16) * 16

    def step(bit, running, total, offset, got):
        return kernel_call(
            functools.partial(merge_kernel, bit),
            "merge",
            (
                shape((state_size, features), F32),
                shape((1, wide), F32),
                shape((1, wide), F32),
                shape((EXTRA, wide)),
                shape((state_size + EXTRA, features)),
            ),
            in_specs=[smem] + [vmem] * 5,
        )(place1, running, total, offset, got, spread)

    def near_chain(
        keep, core_states, far_states, total, log_decay, level_class, level_table, state_in, state_out, portion
    ):
        table = jnp.transpose(level_table, (1, 0, 2))
        table = jnp.concatenate([table, table], axis=2)
        tables_call = kernel_call(
            factors_kernel,
            "factors",
            (
                shape((tokens, wide)),
                shape((local + 1, tokens, wide)),
                shape((levels - local - 1, tokens, wide)),
                shape((merge_count, wide)),
                shape((heads_size, 2, rows_dev, rows_dev)),
                shape((heads_size, rows_dev // CH * state_size, rows_dev)),
            ),
        )
        got_states, latest = [], []
        for i, far in enumerate(far_states):
            latest = [swap(tie(far, *latest), "head", 2 * (i + 1))]
            got_states += latest
        running, sent = kernel_call(
            first_kernel,
            "first_state",
            (shape((state_size, features), F32), shape((state_size + EXTRA, features))),
            grid_spec=pl.GridSpec(
                grid=(1,),
                in_specs=[pl.BlockSpec((1, state_size, features), lambda i: (0, 0, 0))] * 2
                + [whole((1, wide))]
                + [whole((state_size, features))] * len(got_states),
                out_specs=(whole((state_size, features)), whole((state_size + EXTRA, features))),
            ),
        )(keep, core_states, total, *got_states)
        moved, passed, after = {}, {}, []
        for r, array in portion.items():
            moved[r] = swap(tie(array, *after), "head", 1)
            after = [moved[r]]
        after = [running]
        for r, array in moved.items():
            passed[r] = swap(tie(array, *after), "head", r - 1)
            after = [passed[r]]
        tables = tables_call(
            tie(log_decay, running), level_class.reshape(tokens, 1), table, state_in, state_out
        )
        factor = jnp.broadcast_to((position % 2).astype(BF16), (EXTRA, wide))
        factors = [jnp.where(jnp.arange(wide)[None, :] < head_count, factor, 0)]
        offset = jnp.zeros((1, wide), F32)
        states = []
        for bit in range(near):
            got = swap(sent, "ctx", 2**bit)
            states.append(tie(got, tables[0]) if bit == 0 else got)
            running, total, offset, factor, sent = step(bit, running, total, offset, states[-1])
            factors.append(factor)
        return states, factors, sent, tables, passed

    states, factors, sent, tables, passed = fenced(
        near_chain, keep, core_states, tie(far_states, value_head), total, log_decay, level_class,
        level_table, state_in, state_out, {r: portion[r] for r in range(3, heads_size, 2)},
    )
    states, passed = list(states), dict(passed)
    passed[2] = value_head
    sent = tie(sent, *[held[2**bit] for bit in range(ctx_bits)])
    for r in range(4, heads_size, 2):
        passed[r] = swap(tie(portion[r], sent), "head", r)

    for r in range(2, ctx_size):
        low = r & -r
        if r not in held and low > 1:
            held[r] = swap(tie(held[r ^ low], sent), "ctx", low)
    for bit in range(2, ctx_bits):
        held[2**bit + 1] = swap(tie(held[2**bit], sent), "ctx", 1)
    for r in (0, 1):
        partners[r] = swap(tie(held[r], sent), "head", 1)

    arrays = [values, portion[1]] + [passed[r] for r in range(2, heads_size)]

    skip_row = jnp.repeat(skip_gain, head_width)[None, :]

    def read_levels(sent, state_out, tables, factors, states, arrays, spread, same, skip_row, norm_row):
        lift, read, cross, merge, scores, masked = tables
        state = swap(sent, "ctx", 2**near)
        arrays = [arrays[0], swap(arrays[1], "head", 1)] + arrays[2:]
        readers = state_out.reshape(grouped + (state_size,))
        cross = cross.reshape((ctx_bits,) + grouped + (wide,))
        pre = kernel_call(
            lambda me_ref, *refs: local_kernel(me_ref, near, heads_size, *refs),
            "local_levels",
            shape(grouped + (features,), F32),
            grid_spec=pltpu.PrefetchScalarGridSpec(
                num_scalar_prefetch=1,
                grid=(tiles,),
                in_specs=[pl.BlockSpec((rows_dev, tile), lambda f, m: (0, m[0] * tiles + f))]
                + [pl.BlockSpec((array.shape[0], tile), lambda f, m: (0, f)) for array in arrays[1:]]
                + [
                    whole(readers.shape),
                    whole(grouped + (wide,)),
                    whole((local + 1,) + grouped + (wide,)),
                    whole((merge_count, wide)),
                    whole(scores.shape),
                    whole(masked.shape),
                    pl.BlockSpec((wide, tile), lambda f, m: (0, f)),
                    pl.BlockSpec((1, tile), lambda f, m: (0, f)),
                    whole(cross.shape),
                ]
                + [whole((EXTRA, wide))] * near
                + [pl.BlockSpec((state_size + EXTRA, tile), lambda f, m: (0, f))] * near,
                out_specs=pl.BlockSpec(grouped + (tile,), lambda f, m: (0, 0, f)),
                scratch_shapes=[
                    pltpu.VMEM((heads_size, rows_dev // CH * state_size, tile), F32),
                    pltpu.VMEM((max(local, 1), state_size, tile), F32),
                    pltpu.VMEM((max(local, 1), 2 * state_size, tile), BF16),
                ],
            ),
        )(
            me1,
            *arrays,
            readers,
            lift.reshape(grouped + (wide,)),
            read.reshape((local + 1,) + grouped + (wide,)),
            merge,
            scores,
            masked,
            spread,
            skip_row,
            cross,
            *factors[:near],
            *states,
        )
        return kernel_call(
            finish_kernel,
            "finish",
            tuple([shape((rows_dev, features))] * half + [shape((half, rows_dev, features))]),
            grid_spec=pltpu.PrefetchScalarGridSpec(
                num_scalar_prefetch=1,
                grid=(tiles,),
                in_specs=[
                    pl.BlockSpec(grouped + (tile,), lambda f, m: (0, 0, f)),
                    whole(readers.shape),
                    pl.BlockSpec((1,) + grouped + (wide,), lambda f, m: (near, 0, 0, 0)),
                    whole((EXTRA, wide)),
                    pl.BlockSpec((state_size + EXTRA, tile), lambda f, m: (0, f)),
                    pl.BlockSpec((wide, tile), lambda f, m: (0, f)),
                    whole((tile, tile)),
                    pl.BlockSpec((1, tile), lambda f, m: (0, f)),
                ],
                out_specs=[pl.BlockSpec((rows_dev, tile), lambda f, m: (0, f))] * half
                + [pl.BlockSpec((half, rows_dev, tile), lambda f, m: (0, 0, f))],
            ),
        )(me1, pre, readers, cross, factors[near], state, spread, same, norm_row)

    *kept, sides = fenced(
        read_levels, sent, state_out, tables, factors, states, arrays, spread, same, skip_row,
        norm_gain[None, :],
    )
    early_blocks = set(held)
    done = [held[r] for r in held if r not in (0, 1)] + [kept[0]]
    held[3] = swap(tie(held[1], *done), "ctx", 2)
    for r in range(5, ctx_size, 2):
        if r not in held:
            held[r] = swap(tie(held[r ^ 1], *done), "ctx", 1)

    count = 1
    while count * columns % 128 and 2 * count <= ctx_size:
        count *= 2

    others = swap(sides, "head", 1)
    firsts = list(range(0, ctx_size, count))
    group_of = lambda first: range(first, first + count)

    def project(name, first, kept, others, blocks, partners, kind):
        rows = len(kept)
        return kernel_call(
            project_kernel,
            name,
            shape((rows, rows_dev, count * columns), kind),
            in_specs=[smem] + [vmem] * rows
            + [
                pl.BlockSpec((1,) + others.shape[1:], lambda _, i=i: (first + i, 0, 0))
                for i in range(rows)
            ]
            + [whole((columns, features))] * (2 * count),
            out_specs=whole((rows, rows_dev, count * columns)),
            grid=(1,),
        )(place1, *kept, *[others] * rows, *blocks, *partners)

    def far_rows(first, kept, others, blocks, partners):
        return project(
            "project_far", 1, kept[1:], others,
            [blocks[r] for r in group_of(first)], [partners[r] for r in group_of(first)], BF16,
        )

    def own_rows(first, kept, others, blocks, partners):
        return project(
            "project_own", 0, kept[:1], others,
            [blocks[r] for r in group_of(first)], [partners[r] for r in group_of(first)], F32,
        )[0]

    def send_rows(far, *after):
        far = tie(far, *after)
        return [swap(far[i - 1], "head", 2 * i) for i in range(1, half)]

    def first_groups(kept, others, blocks, partners):
        more = {r: swap(blocks[r], "head", 1) for r in blocks if r not in partners}
        partners = {**partners, **more}
        fars = [far_rows(first, kept, others, blocks, partners) for first in early_groups]
        return fars[1:], send_rows(fars[0]), more

    def last_groups(kept, others, blocks, partners, early):
        partners, results, arrived = dict(partners), {}, []
        for first in late_groups:
            for r in group_of(first):
                if r not in partners:
                    partners[r] = swap(blocks[r], "head", 1)
            got = send_rows(far_rows(first, kept, others, blocks, partners), *arrived)
            results[first] = [own_rows(first, kept, others, blocks, partners)] + got
            arrived = got
        owns = [own_rows(first, kept, others, early, partners) for first in early_groups[1:]]
        return results, owns

    early_groups = [f for f in firsts if all(r in early_blocks for r in group_of(f))] or firsts[:1]
    late_groups = [f for f in firsts if f not in early_groups]
    early = {r: held[r] for f in early_groups for r in group_of(f)}
    late = {r: held[r] for f in late_groups for r in group_of(f)}
    fars, got, more = fenced(first_groups, kept, others, early, partners)
    partners = {**partners, **more}
    sent_groups = [got]
    for far in fars:
        sent_groups.append(send_rows(far, *sent_groups[-1]))
    own = own_rows(early_groups[0], [tie(kept[0], *fars)], others, early, partners)
    if late_groups:
        late[late_groups[0]] = tie(late[late_groups[0]], own)
    results, owns = fenced(last_groups, kept, others, late, partners, early)
    for first, own, got in zip(early_groups, [own] + owns, sent_groups):
        results[first] = [own] + got
    pieces = [piece for first in firsts for piece in results[first]]
    return kernel_call(
        assemble_kernel,
        "assemble",
        shape((rows_dev, ctx_size * columns)),
        in_specs=[smem] + [vmem] * len(pieces),
    )(place1 // count, *pieces)


def solution(mesh):
    return jax.shard_map(
        on_device,
        mesh=mesh,
        in_specs=(
            P(("ctx", "head"), None),
            P("ctx", None),
            P("ctx", None),
            P("ctx", "head"),
            P("ctx"),
            P(None, None, "head"),
            P("head"),
            P("head"),
            P("head", "ctx"),
        ),
        out_specs=P(("ctx", "head"), None),
        check_vma=False,
    )
```

```python
import functools

import jax
import jax.numpy as jnp
from jax import lax
from jax.experimental import pallas as pl
from jax.experimental.pallas import tpu as pltpu
from jax.sharding import PartitionSpec as P

CH = 64
EPSILON = 1e-05
LANES = 128
F32 = jnp.float32
BF16 = jnp.bfloat16
VMEM_LIMIT = 40 * 1024 * 1024


def dot(a, b):
    return lax.dot_general(a, b, (((1,), (0,)), ((), ())), preferred_element_type=F32)


def dot_nt(a, b):
    return lax.dot_general(a, b, (((1,), (1,)), ((), ())), preferred_element_type=F32)


def swap(value, axis, distance):
    pairs = [(source, source ^ distance) for source in range(lax.axis_size(axis))]
    return lax.ppermute(value, axis, pairs)


def tie(value, *after):
    return lax.optimization_barrier((value,) + after)[0]


def three_parts(x):
    high = x.astype(BF16)
    rest = x - high.astype(F32)
    middle = rest.astype(BF16)
    low = (rest - middle.astype(F32)).astype(BF16)
    return high, middle, low


def two_parts(x):
    high = x.astype(BF16)
    return high, (x - high.astype(F32)).astype(BF16)


def merge_rows(stretches):
    rows = [("own", c, 0) for c in range(stretches - 1)]
    for c in range(stretches - 1):
        k = 0
        while (c >> k) & 1:
            rows.append(("merge", c, k))
            k += 1
    return rows


def head_rows(head, width):
    return slice(head * width, (head + 1) * width)


def exact_dot(x, ones):
    return sum(dot(part, ones) for part in three_parts(x))


def split_kernel(me_ref, *refs):
    half = len(refs) // 2
    for value_ref, part_ref in zip(refs[:half], refs[half:]):
        part_ref[...] = jnp.transpose(value_ref[...])


def fade_kernel(blocks, me_ref, decay_ref, own_ref, side_ref, *refs):
    far_refs, total_ref = refs[:-1], refs[-1]
    head_count, tokens = decay_ref.shape
    rows = tokens // blocks
    row = lax.broadcasted_iota(jnp.int32, (rows, rows), 0)
    col = lax.broadcasted_iota(jnp.int32, (rows, rows), 1)
    later = jnp.where(row > col, 1.0, 0.0).astype(BF16)
    me = me_ref[0]
    after = jnp.zeros((head_count, 1), F32)
    for block in reversed(range(blocks)):
        decay = decay_ref[:, block * rows : (block + 1) * rows]
        left = exact_dot(decay, later)
        fade = jnp.exp(left + after)
        after = after + left[:, 0:1] + decay[:, 0:1]
        own_index = me ^ block

        @pl.when(own_index == 0)
        def _():
            own_ref[...] = fade

        @pl.when(own_index == 1)
        def _():
            side_ref[...] = fade

        for i, far_ref in enumerate(far_refs):
            for j in range(2):

                @pl.when(own_index == 2 * (i + 1) + j)
                def _():
                    far_ref[j] = fade

    total_ref[...] = jnp.zeros_like(total_ref)
    total_ref[:head_count, :] = jnp.broadcast_to(after, (head_count, LANES))


def pack_kernel(*refs):
    side_ref, *got_refs, out_ref = refs
    out_ref[0] = side_ref[...]
    for i, got_ref in enumerate(got_refs):
        out_ref[i + 1] = got_ref[0]


def factors_kernel(
    levels, blocks, decay_ref, class_ref, table_ref, in_ref, out_ref,
    lift_ref, read_ref, cross_ref, merge_ref, score_ref, masked_ref, reader_ref, pair_ref,
):
    head_count, tokens = decay_ref.shape
    stretches = tokens // CH
    rows = tokens // blocks
    per_block = rows // CH
    local = read_ref.shape[0] - 1
    state_size = in_ref.shape[1]
    padded = table_ref.shape[0] // levels
    classes = table_ref.shape[1]
    row = lax.broadcasted_iota(jnp.int32, (rows, rows), 0)
    col = lax.broadcasted_iota(jnp.int32, (rows, rows), 1)
    inside = (row // CH == col // CH) & (row <= col)
    upto = jnp.where(inside, 1.0, 0.0).astype(BF16)
    within, starts = [], [jnp.zeros((head_count, 1), F32)]
    for g in range(blocks):
        within.append(exact_dot(decay_ref[:, g * rows : (g + 1) * rows], upto))
        for s in range(per_block):
            last = (s + 1) * CH
            starts.append(starts[-1] + within[-1][:, last - 1 : last])
    class_row = lax.broadcasted_iota(jnp.int32, (classes, rows), 0)
    lane = lax.broadcasted_iota(jnp.int32, (head_count, rows), 1) // CH
    token = lax.broadcasted_iota(jnp.int32, (rows, state_size), 0) // CH

    def by_stretch(columns):
        spread = jnp.broadcast_to(columns[0], (head_count, rows))
        for s in range(1, per_block):
            spread = jnp.where(lane == s, columns[s], spread)
        return spread

    for g in range(blocks):
        at = slice(g * rows, (g + 1) * rows)
        onehot = jnp.where(class_ref[:, at] == class_row, 1.0, 0.0).astype(BF16)
        weights = sum(dot(part, onehot) for part in three_parts(table_ref[...]))
        weight = lambda level: weights[level * padded : level * padded + head_count, :]
        lift_ref[g] = jnp.exp(-within[g])
        read_ref[0, g] = jnp.exp(within[g]) * weight(0)
        first = g * per_block
        for level in range(1, local + 1):
            begins, active = [], []
            for c in range(first, first + per_block):
                upper = (c >> (level - 1)) & 1
                begins.append(starts[c] - starts[(c >> (level - 1)) << (level - 1)])
                active.append(jnp.full((head_count, 1), float(upper), F32))
            factor = jnp.exp(within[g] + by_stretch(begins)) * weight(level)
            read_ref[level, g] = factor * by_stretch(active)
        far = jnp.exp(within[g] + by_stretch(starts[first : first + per_block]))
        for level in range(local + 1, levels):
            cross_ref[level - local - 1, g] = far * weight(level)
        own_in, own_out = in_ref[at, :], out_ref[at, :]
        scores = jnp.where(inside, dot_nt(own_in, own_out), 0.0)
        score_ref[g, 0], score_ref[g, 1] = two_parts(scores)
        for s in range(per_block):
            masked = jnp.where(token == s, own_in.astype(F32), 0.0).astype(BF16)
            masked_ref[g, :, s * state_size : (s + 1) * state_size] = masked
        turned = jnp.transpose(own_out.astype(F32))
        reader = turned.astype(BF16)
        reader_ref[g, :state_size, :] = reader
        reader_ref[g, state_size:, :] = reader
        pairs = max(per_block // 2, 1)
        place = lax.broadcasted_iota(jnp.int32, (state_size, rows), 1) // (2 * CH)
        for j in range(pairs):
            alone = jnp.where(place == j, turned, 0.0).astype(BF16)
            pair_ref[g, j * state_size : (j + 1) * state_size, :] = alone
    for i, (kind, c, k) in enumerate(merge_rows(stretches)):
        first = c if kind == "own" else c + 1 - 2**k
        merge_ref[i] = jnp.broadcast_to(jnp.exp(starts[c + 1] - starts[first]), (head_count, LANES))


def partial_state_kernel(count, *refs):
    value_refs, refs = refs[:count], refs[count:]
    fade_refs, (in_ref, keep_ref, send_ref, faded) = refs[:count], refs[count:]
    own_in = in_ref[...]
    for r in [*range(1, count, 2), *range(0, count, 2)]:
        fade = fade_refs[r][...].reshape(fade_refs[r].shape[-2:])
        head_count = fade.shape[0]
        width = value_refs[r].shape[0] // head_count
        for h in range(head_count):
            at = head_rows(h, width)
            faded[at, :] = (fade[h : h + 1, :] * value_refs[r][at, :].astype(F32)).astype(BF16)
        state = dot(faded[...], own_in)
        if r % 2 == 1:
            send_ref[r // 2] = state.astype(BF16)
        else:
            keep_ref[r // 2] = state


def fold_kernel(*refs):
    count = len(refs) // 3
    for keep_ref, got_ref, far_ref in zip(refs[:count], refs[count : 2 * count], refs[2 * count :]):
        far_ref[...] = (keep_ref[0] + got_ref[0].astype(F32)).astype(BF16)


def pack_state(sent_ref, state, total):
    channels = state.shape[0]
    sent_ref[:channels, :] = state.astype(BF16)
    high, middle, low = (part.astype(F32) for part in three_parts(total))
    lane = lax.broadcasted_iota(jnp.int32, total.shape, 1)
    parts = jnp.where(lane < LANES // 4, high, jnp.where(lane < LANES // 2, middle, low))
    sent_ref[channels:, :] = parts.astype(BF16)


def first_kernel(own_ref, core_ref, total_ref, *refs):
    *far_refs, running_ref, sent_ref = refs
    running = own_ref[0] + core_ref[0].astype(F32)
    for far_ref in far_refs:
        running = running + far_ref[...].astype(F32)
    running_ref[...] = running
    pack_state(sent_ref, running, total_ref[...])


def merge_kernel(
    bit, head_count, place_ref, running_ref, total_ref, offset_ref, got_ref,
    next_running_ref, next_total_ref, next_offset_ref, factor_ref, sent_ref,
):
    channels = running_ref.shape[0]
    width = channels // head_count
    place = place_ref[0]
    upper = place // 2**bit % 2 == 1
    total = total_ref[...]
    parts = got_ref[channels:, :].astype(F32)
    middle, low = LANES // 4, LANES // 2
    partner = parts[:, 0:1] + parts[:, middle : middle + 1] + parts[:, low : low + 1]
    partner = jnp.broadcast_to(partner, total.shape)
    fading = jnp.exp(jnp.where(upper, total, partner))
    for h in range(head_count):
        at = head_rows(h, width)
        got, running = got_ref[at, :].astype(F32), running_ref[at, :]
        lower, higher = jnp.where(upper, got, running), jnp.where(upper, running, got)
        next_running_ref[at, :] = fading[h : h + 1, :] * lower + higher
    joined = total + partner
    next_total_ref[...] = joined
    offset = jnp.where(upper, offset_ref[...] + partner, offset_ref[...])
    next_offset_ref[...] = offset
    next_upper = place // 2 ** (bit + 1) % 2 == 1
    factor_ref[...] = jnp.where(next_upper, jnp.exp(offset), 0.0)
    pack_state(sent_ref, next_running_ref[...], joined)


def local_kernel(near, me_ref, *refs):
    groups = refs[-1].shape[0]
    value_refs, refs = refs[:groups], refs[groups:]
    lift_ref, read_ref, merge_ref, score_ref, masked_ref, reader_ref, pair_ref = refs[:7]
    skip_ref, cross_ref, *refs = refs[7:]
    factor_refs, state_refs, refs = refs[:near], refs[near : 2 * near], refs[2 * near :]
    pre_ref, lifted, sums, operand, pairs_ref, nodes = refs
    channels, group_rows = value_refs[0].shape
    head_count = lift_ref.shape[1]
    width = channels // head_count
    me = me_ref[0]
    per_group = group_rows // CH
    stretches = groups * per_group
    state_size = reader_ref.shape[1] // 2
    place = {kind: i for i, kind in enumerate(merge_rows(stretches))}
    heads = [(h, head_rows(h, width)) for h in range(head_count)]
    for r, value_ref in enumerate(value_refs):
        g = me ^ r
        lift = lift_ref[g]
        for h, at in heads:
            lifted[at, :] = (lift[h : h + 1, :] * value_ref[at, :].astype(F32)).astype(BF16)
        direct = dot(lifted[...], score_ref[g, 0]) + dot(lifted[...], score_ref[g, 1])
        read = read_ref[0, g]
        terms = []
        for level, (state_ref, factor_ref) in enumerate(zip(state_refs, factor_refs)):
            gained = dot(state_ref[:channels, :], reader_ref[g, :state_size, :])
            scale = cross_ref[level, g] * factor_ref[:head_count, 0:1]
            terms.append((scale, gained))
        for h, at in heads:
            total = read[h : h + 1, :] * direct[at, :]
            total = total + skip_ref[h : h + 1, :] * value_ref[at, :].astype(F32)
            for scale, gained in terms:
                total = total + scale[h : h + 1, :] * gained[at, :]
            pre_ref[g, at, :] = total
        nodes[g] = dot(lifted[...], masked_ref[g])

    for g in range(groups):
        terms = []
        level = per_group.bit_length()
        while 2 ** (level - 1) < stretches:
            if (g * per_group >> (level - 1)) & 1:
                terms.append((read_ref[level, g], dot(operand[level - 1], reader_ref[g])))
            level += 1
        for s in range(per_group):
            c = g * per_group + s
            if c + 1 == stretches:
                break
            merges = [merge_ref[place["own", c, 0]]]
            k = 0
            while (c >> k) & 1:
                merges.append(merge_ref[place["merge", c, k]])
                k += 1
            for h, at in heads:
                node = nodes[g, at, s * state_size : (s + 1) * state_size]
                node = node * merges[0][h : h + 1, :]
                for i, merge in enumerate(merges[1:]):
                    node = node + merge[h : h + 1, :] * sums[i, at, :]
                sums[k, at, :] = node
                high, low = two_parts(node)
                if k == 0 and per_group > 1:
                    pairs_ref[at, s // 2 * state_size : (s // 2 + 1) * state_size] = high
                else:
                    operand[k, at, :state_size] = high
                    operand[k, at, state_size:] = low
            if 1 <= k < per_group.bit_length() - 1:
                scale = read_ref[k + 1, g]
                lane = lax.broadcasted_iota(jnp.int32, scale.shape, 1) // (CH << (k + 1))
                scale = jnp.where(lane == s >> (k + 1), scale, 0.0)
                terms.append((scale, dot(operand[k], reader_ref[g])))
        if per_group > 1:
            terms.append((read_ref[1, g], dot(pairs_ref[...], pair_ref[g])))
        for h, at in heads:
            total = pre_ref[g, at, :]
            for scale, gained in terms:
                total = total + scale[h : h + 1, :] * gained[at, :]
            pre_ref[g, at, :] = total


def finish_kernel(
    half, me_ref, pre_ref, reader_ref, cross_ref, factor_ref, state_ref, gain_ref, *refs
):
    keep_refs, send_ref = refs[:half], refs[half]
    groups, channels, _ = pre_ref.shape
    head_count = cross_ref.shape[2]
    width = channels // head_count
    state_size = reader_ref.shape[1] // 2
    me = me_ref[0]
    state = state_ref[:channels, :]
    for r in range(groups):
        g = me ^ r
        gained = dot(state, reader_ref[g, :state_size, :])
        scale = cross_ref[0, g] * factor_ref[:head_count, 0:1]
        for h in range(head_count):
            at = head_rows(h, width)
            total = pre_ref[g, at, :] + scale[h : h + 1, :] * gained[at, :]
            mean_square = jnp.sum(total * total, axis=0, keepdims=True) * (1.0 / width)
            normed = total * lax.rsqrt(mean_square + EPSILON) * gain_ref[at, 0:1]
            if r % 2 == 0:
                keep_refs[r // 2][at, :] = normed.astype(BF16)
            else:
                send_ref[r // 2, at, :] = normed.astype(BF16)


def project_kernel(place_ref, *refs):
    *refs, out_ref = refs
    rows = out_ref.shape[0]
    kept_refs, other_refs, refs = refs[:rows], refs[rows : 2 * rows], refs[2 * rows :]
    count = len(refs) // 2
    weights, partners = refs[:count], refs[count:]
    width = weights[0].shape[0]
    turn = place_ref[0] % count
    for i, (kept_ref, other_ref) in enumerate(zip(kept_refs, other_refs)):
        for j, (weight, partner) in enumerate(zip(weights, partners)):
            found = dot(weight[...], kept_ref[...]) + dot(partner[...], other_ref[0])
            at = pl.ds(pl.multiple_of((turn ^ j) * width, width), width)
            out_ref[i, at, :] = found.astype(out_ref.dtype)


def assemble_kernel(place_ref, *refs):
    out_ref = refs[-1]
    width = refs[0].shape[0]
    groups = out_ref.shape[1] // width
    each = (len(refs) - 1) // groups
    for p in range(groups):
        own_ref, *far_refs = refs[p * each : (p + 1) * each]
        total = own_ref[...]
        for far_ref in far_refs:
            total = total + far_ref[...].astype(F32)
        start = pl.multiple_of((place_ref[0] ^ p) * width, width)
        out_ref[:, pl.ds(start, width)] = jnp.transpose(total).astype(BF16)


def whole(shape):
    return pl.BlockSpec(shape, lambda *_: (0,) * len(shape))


def on_device(
    values,
    state_in,
    state_out,
    log_decay,
    level_class,
    level_table,
    skip_gain,
    norm_gain,
    out_weight,
):
    heads_size = lax.axis_size("head")
    ctx_size = lax.axis_size("ctx")
    ctx_bits = ctx_size.bit_length() - 1
    me = lax.axis_index("head")
    me1 = me.reshape(1).astype(jnp.int32)
    position = lax.axis_index("ctx")
    place1 = position.reshape(1).astype(jnp.int32)
    tokens = state_in.shape[0]
    rows_dev = values.shape[0]
    head_count = log_decay.shape[1]
    features = values.shape[1] // heads_size
    state_size = state_in.shape[1]
    columns = out_weight.shape[1]
    stretches = tokens // CH
    per_group = rows_dev // CH
    local = stretches.bit_length() - 1
    levels = level_table.shape[1]
    classes = level_table.shape[0]
    extra = -(-head_count // 16) * 16
    padded = -(-head_count // 8) * 8
    half = heads_size // 2
    near = ctx_bits - 1
    params = pltpu.CompilerParams(vmem_limit_bytes=VMEM_LIMIT)
    cheap = pl.CostEstimate(flops=0, bytes_accessed=0, transcendentals=0)
    smem = pl.BlockSpec(memory_space=pltpu.SMEM)
    vmem = pl.BlockSpec(memory_space=pltpu.VMEM)

    def kernel_call(body, name, out_shape, **kwargs):
        return pl.pallas_call(
            body, out_shape=out_shape, compiler_params=params, cost_estimate=cheap, name=name, **kwargs
        )

    def shape(dims, kind=BF16):
        return jax.ShapeDtypeStruct(dims, kind)

    def part(array, index):
        return pl.BlockSpec((1,) + array.shape[1:], lambda *_: (index,) + (0,) * (array.ndim - 1))

    def fenced(body, *operands):
        shapes = jax.eval_shape(body, *operands)
        zeros = lambda *_: jax.tree.map(lambda leaf: jnp.zeros(leaf.shape, leaf.dtype), shapes)
        return lax.cond(position < ctx_size, body, zeros, *operands)

    held, partners = {0: out_weight.T}, {}
    for bit in range(ctx_bits):
        held[2**bit] = swap(held[0], "ctx", 2**bit)

    decays = log_decay.T
    own_fade, side_fade, *far_fades, total = kernel_call(
        functools.partial(fade_kernel, heads_size),
        "fade",
        tuple(
            [shape((head_count, rows_dev), F32)] * 2
            + [shape((2, head_count, rows_dev), F32)] * (half - 1)
            + [shape((extra, LANES), F32)]
        ),
        in_specs=[smem, vmem],
    )(me1, decays)

    got_fades = []
    for i, far in enumerate(far_fades):
        got_fades.append(swap(tie(far, *got_fades), "head", 2 * (i + 1)))
    sides = kernel_call(
        pack_kernel,
        "pack_fades",
        shape((half, head_count, rows_dev), F32),
        grid=(1,),
        in_specs=[whole(side_fade.shape)] + [part(got, 1) for got in got_fades],
        out_specs=whole((half, head_count, rows_dev)),
    )(side_fade, *got_fades)
    sides = swap(sides, "head", 1)

    portions = kernel_call(
        split_kernel,
        "split_values",
        tuple([shape((features, rows_dev))] * heads_size),
        grid_spec=pltpu.PrefetchScalarGridSpec(
            num_scalar_prefetch=1,
            grid=(1,),
            in_specs=[
                pl.BlockSpec((rows_dev, features), lambda i, m, r=r: (0, m[0] ^ r))
                for r in range(heads_size)
            ],
            out_specs=[whole((features, rows_dev))] * heads_size,
        ),
    )(me1, *[values] * heads_size)
    value_head = swap(portions[2], "head", 2)

    fades, fade_specs = [], []
    for r in range(heads_size):
        if r == 0:
            fades.append(own_fade)
            fade_specs.append(whole(own_fade.shape))
        else:
            fades.append(sides if r % 2 else got_fades[r // 2 - 1])
            fade_specs.append(part(fades[-1], r // 2 if r % 2 else 0))
    keep, send = kernel_call(
        lambda me_ref, *refs: partial_state_kernel(heads_size, *refs),
        "partial_states",
        (shape((half, features, state_size), F32), shape((half, features, state_size))),
        grid_spec=pltpu.PrefetchScalarGridSpec(
            num_scalar_prefetch=1,
            grid=(1,),
            in_specs=[whole((features, rows_dev))] * heads_size
            + fade_specs
            + [pl.BlockSpec((rows_dev, state_size), lambda i, m: (m[0], 0))],
            out_specs=[whole((half, features, state_size))] * 2,
            scratch_shapes=[pltpu.VMEM((features, rows_dev), BF16)],
        ),
    )(me1, *portions, *fades, state_in)

    def core_sum(keep, send):
        got = swap(send, "head", 1)
        far = kernel_call(
            fold_kernel,
            "fold",
            tuple([shape((features, state_size))] * (half - 1)),
            in_specs=[part(keep, i) for i in range(1, half)] * 2,
            out_specs=tuple([whole((features, state_size))] * (half - 1)),
            grid=(1,),
        )(*[keep] * (half - 1), *[got] * (half - 1))
        return got, far

    core_states, far_states = fenced(core_sum, keep, send)

    merge_count = len(merge_rows(stretches))
    grouped = (heads_size, head_count, rows_dev)
    pair_rows = max(per_group // 2, 1) * state_size

    def step(bit, running, total, offset, got):
        return kernel_call(
            functools.partial(merge_kernel, bit, head_count),
            "merge",
            (
                shape((features, state_size), F32),
                shape((extra, LANES), F32),
                shape((extra, LANES), F32),
                shape((extra, LANES), F32),
                shape((features + extra, state_size)),
            ),
            in_specs=[smem] + [vmem] * 4,
        )(place1, running, total, offset, got)

    def near_chain(
        keep, core_states, far_states, total, decays, level_class, level_table, state_in, state_out, portion
    ):
        got_states, latest = [], []
        for i, far in enumerate(far_states):
            latest = [swap(tie(far, *latest), "head", 2 * (i + 1))]
            got_states += latest
        running, sent = kernel_call(
            first_kernel,
            "first_state",
            (shape((features, state_size), F32), shape((features + extra, state_size))),
            grid=(1,),
            in_specs=[part(keep, 0), part(core_states, 0), whole(total.shape)]
            + [whole((features, state_size))] * len(got_states),
            out_specs=(whole((features, state_size)), whole((features + extra, state_size))),
        )(keep, core_states, total, *got_states)
        moved, passed, after = {}, {}, []
        for r, array in portion.items():
            moved[r] = swap(tie(array, *after), "head", 1)
            after = [moved[r]]
        after = [running]
        for r, array in moved.items():
            passed[r] = swap(tie(array, *after), "head", r - 1)
            after = [passed[r]]
        table = jnp.transpose(level_table, (1, 2, 0))
        table = jnp.pad(table, ((0, 0), (0, padded - head_count), (0, 0)))
        tables = kernel_call(
            functools.partial(factors_kernel, levels, heads_size),
            "factors",
            (
                shape(grouped, F32),
                shape((local + 1,) + grouped, F32),
                shape((ctx_bits,) + grouped, F32),
                shape((merge_count, head_count, LANES), F32),
                shape((heads_size, 2, rows_dev, rows_dev)),
                shape((heads_size, rows_dev, per_group * state_size)),
                shape((heads_size, 2 * state_size, rows_dev)),
                shape((heads_size, pair_rows, rows_dev)),
            ),
        )(
            tie(decays, running),
            level_class.reshape(1, tokens),
            table.reshape(levels * padded, classes),
            state_in,
            state_out,
        )
        offset = jnp.zeros((extra, LANES), F32)
        factors = [jnp.broadcast_to((position % 2).astype(F32), (extra, LANES))]
        states = []
        for bit in range(near):
            got = swap(sent, "ctx", 2**bit)
            states.append(tie(got, tables[0]) if bit == 0 else got)
            running, total, offset, factor, sent = step(bit, running, total, offset, states[-1])
            factors.append(factor)
        return states, factors, sent, tables, passed

    states, factors, sent, tables, passed = fenced(
        near_chain, keep, core_states, tie(far_states, value_head), total, decays, level_class,
        level_table, state_in, state_out, {r: portions[r] for r in range(3, heads_size, 2)},
    )
    states, passed = list(states), dict(passed)
    passed[2] = value_head
    sent = tie(sent, *[held[2**bit] for bit in range(ctx_bits)])
    for r in range(4, heads_size, 2):
        passed[r] = swap(tie(portions[r], sent), "head", r)

    for r in range(2, ctx_size):
        low = r & -r
        if r not in held and low > 1:
            held[r] = swap(tie(held[r ^ low], sent), "ctx", low)
    for bit in range(2, ctx_bits):
        held[2**bit + 1] = swap(tie(held[2**bit], sent), "ctx", 1)
    for r in (0, 1):
        partners[r] = swap(tie(held[r], sent), "head", 1)

    skips = jnp.broadcast_to(skip_gain[:, None], (head_count, rows_dev))
    gains = norm_gain[:, None]

    def read_levels(sent, tables, factors, states, arrays, skips, gains):
        lift, read, cross, merge, scores, masked, readers, pairs = tables
        state = swap(sent, "ctx", 2**near)
        arrays = [arrays[0], swap(arrays[1], "head", 1)] + list(arrays[2:])
        pre = kernel_call(
            functools.partial(local_kernel, near),
            "local_levels",
            shape((heads_size, features, rows_dev), F32),
            in_specs=[smem] + [vmem] * (heads_size + 9 + 2 * near),
            scratch_shapes=[
                pltpu.VMEM((features, rows_dev), BF16),
                pltpu.VMEM((max(local, 1), features, state_size), F32),
                pltpu.VMEM((max(local, 1), features, 2 * state_size), BF16),
                pltpu.VMEM((features, pair_rows), BF16),
                pltpu.VMEM((heads_size, features, per_group * state_size), F32),
            ],
        )(
            me1, *arrays, lift, read, merge, scores, masked, readers, pairs, skips, cross,
            *factors[:near], *states,
        )
        return kernel_call(
            functools.partial(finish_kernel, half),
            "finish",
            tuple([shape((features, rows_dev))] * half + [shape((half, features, rows_dev))]),
            grid=(1,),
            in_specs=[
                smem,
                whole(pre.shape),
                whole(readers.shape),
                part(cross, near),
                whole((extra, LANES)),
                whole((features + extra, state_size)),
                whole((features, 1)),
            ],
            out_specs=[whole((features, rows_dev))] * half + [whole((half, features, rows_dev))],
        )(me1, pre, readers, cross, factors[near], state, gains)

    arrays = [portions[0], portions[1]] + [passed[r] for r in range(2, heads_size)]
    *kept, sides = fenced(read_levels, sent, tables, factors, states, arrays, skips, gains)

    early_blocks = set(held)
    done = [held[r] for r in held if r not in (0, 1)] + [kept[0]]
    held[3] = swap(tie(held[1], *done), "ctx", 2)
    for r in range(5, ctx_size, 2):
        if r not in held:
            held[r] = swap(tie(held[r ^ 1], *done), "ctx", 1)

    count = 1
    while count * columns % 128 and 2 * count <= ctx_size:
        count *= 2

    others = swap(sides, "head", 1)
    firsts = list(range(0, ctx_size, count))
    group_of = lambda first: range(first, first + count)

    def project(name, first, kept, others, blocks, partners, kind):
        rows = len(kept)
        return kernel_call(
            project_kernel,
            name,
            shape((rows, count * columns, rows_dev), kind),
            in_specs=[smem]
            + [whole((features, rows_dev))] * rows
            + [part(others, first + i) for i in range(rows)]
            + [whole((columns, features))] * (2 * count),
            out_specs=whole((rows, count * columns, rows_dev)),
            grid=(1,),
        )(place1, *kept, *[others] * rows, *blocks, *partners)

    def far_rows(first, kept, others, blocks, partners):
        return project(
            "project_far", 1, kept[1:], others,
            [blocks[r] for r in group_of(first)], [partners[r] for r in group_of(first)], BF16,
        )

    def own_rows(first, kept, others, blocks, partners):
        return project(
            "project_own", 0, kept[:1], others,
            [blocks[r] for r in group_of(first)], [partners[r] for r in group_of(first)], F32,
        )[0]

    def send_rows(far, *after):
        far = tie(far, *after)
        return [swap(far[i - 1], "head", 2 * i) for i in range(1, half)]

    def first_groups(kept, others, blocks, partners):
        more = {r: swap(blocks[r], "head", 1) for r in blocks if r not in partners}
        partners = {**partners, **more}
        fars = [far_rows(first, kept, others, blocks, partners) for first in early_groups]
        return fars[1:], send_rows(fars[0]), more

    def last_groups(kept, others, blocks, partners, early):
        partners, results, arrived = dict(partners), {}, []
        for first in late_groups:
            for r in group_of(first):
                if r not in partners:
                    partners[r] = swap(blocks[r], "head", 1)
            got = send_rows(far_rows(first, kept, others, blocks, partners), *arrived)
            results[first] = [own_rows(first, kept, others, blocks, partners)] + got
            arrived = got
        owns = [own_rows(first, kept, others, early, partners) for first in early_groups[1:]]
        return results, owns

    early_groups = [f for f in firsts if all(r in early_blocks for r in group_of(f))] or firsts[:1]
    late_groups = [f for f in firsts if f not in early_groups]
    early = {r: held[r] for f in early_groups for r in group_of(f)}
    late = {r: held[r] for f in late_groups for r in group_of(f)}
    fars, got, more = fenced(first_groups, kept, others, early, partners)
    partners = {**partners, **more}
    sent_groups = [got]
    for far in fars:
        sent_groups.append(send_rows(far, *sent_groups[-1]))
    own = own_rows(early_groups[0], [tie(kept[0], *fars)], others, early, partners)
    if late_groups:
        late[late_groups[0]] = tie(late[late_groups[0]], own)
    results, owns = fenced(last_groups, kept, others, late, partners, early)
    for first, own, got in zip(early_groups, [own] + owns, sent_groups):
        results[first] = [own] + got
    pieces = [piece for first in firsts for piece in results[first]]
    return kernel_call(
        assemble_kernel,
        "assemble",
        shape((rows_dev, ctx_size * columns)),
        in_specs=[smem] + [vmem] * len(pieces),
    )(place1 // count, *pieces)


def solution(mesh):
    return jax.shard_map(
        on_device,
        mesh=mesh,
        in_specs=(
            P(("ctx", "head"), None),
            P("ctx", None),
            P("ctx", None),
            P("ctx", "head"),
            P("ctx"),
            P(None, None, "head"),
            P("head"),
            P("head"),
            P("head", "ctx"),
        ),
        out_specs=P(("ctx", "head"), None),
        check_vma=False,
    )
```

```python
import functools

import jax
import jax.numpy as jnp
from jax import lax
from jax.experimental import pallas as pl
from jax.experimental.pallas import tpu as pltpu
from jax.sharding import PartitionSpec as P

CH = 64
EPSILON = 1e-05
LANES = 128
F32 = jnp.float32
BF16 = jnp.bfloat16
VMEM_LIMIT = 40 * 1024 * 1024


def dot(a, b):
    return lax.dot_general(a, b, (((1,), (0,)), ((), ())), preferred_element_type=F32)


def dot_nt(a, b):
    return lax.dot_general(a, b, (((1,), (1,)), ((), ())), preferred_element_type=F32)


def swap(value, axis, distance):
    pairs = [(source, source ^ distance) for source in range(lax.axis_size(axis))]
    return lax.ppermute(value, axis, pairs)


def tie(value, *after):
    return lax.optimization_barrier((value,) + after)[0]


def three_parts(x):
    high = x.astype(BF16)
    rest = x - high.astype(F32)
    middle = rest.astype(BF16)
    low = (rest - middle.astype(F32)).astype(BF16)
    return high, middle, low


def two_parts(x):
    high = x.astype(BF16)
    return high, (x - high.astype(F32)).astype(BF16)


def merge_rows(stretches):
    rows = [("own", c, 0) for c in range(stretches - 1)]
    for c in range(stretches - 1):
        k = 0
        while (c >> k) & 1:
            rows.append(("merge", c, k))
            k += 1
    return rows


def head_rows(head, width):
    return slice(head * width, (head + 1) * width)


def exact_dot(x, ones):
    return sum(dot(part, ones) for part in three_parts(x))


def split_kernel(me_ref, *refs):
    half = len(refs) // 2
    for value_ref, part_ref in zip(refs[:half], refs[half:]):
        part_ref[...] = jnp.transpose(value_ref[...])


def fade_kernel(blocks, me_ref, decay_ref, own_ref, side_ref, *refs):
    far_refs, total_ref = refs[:-1], refs[-1]
    head_count, tokens = decay_ref.shape
    rows = tokens // blocks
    row = lax.broadcasted_iota(jnp.int32, (rows, rows), 0)
    col = lax.broadcasted_iota(jnp.int32, (rows, rows), 1)
    later = jnp.where(row > col, 1.0, 0.0).astype(BF16)
    me = me_ref[0]
    after = jnp.zeros((head_count, 1), F32)
    for block in reversed(range(blocks)):
        decay = decay_ref[:, block * rows : (block + 1) * rows]
        left = exact_dot(decay, later)
        fade = jnp.exp(left + after)
        after = after + left[:, 0:1] + decay[:, 0:1]
        own_index = me ^ block

        @pl.when(own_index == 0)
        def _():
            own_ref[...] = fade

        @pl.when(own_index == 1)
        def _():
            side_ref[...] = fade

        for i, far_ref in enumerate(far_refs):
            for j in range(2):

                @pl.when(own_index == 2 * (i + 1) + j)
                def _():
                    far_ref[j] = fade

    total_ref[...] = jnp.zeros_like(total_ref)
    total_ref[:head_count, :] = jnp.broadcast_to(after, (head_count, LANES))


def pack_kernel(*refs):
    side_ref, *got_refs, out_ref = refs
    out_ref[0] = side_ref[...]
    for i, got_ref in enumerate(got_refs):
        out_ref[i + 1] = got_ref[0]


def factors_kernel(
    levels, blocks, decay_ref, class_ref, table_ref, in_ref, out_ref,
    lift_ref, read_ref, cross_ref, merge_ref, score_ref, masked_ref, reader_ref, pair_ref,
):
    head_count, tokens = decay_ref.shape
    stretches = tokens // CH
    rows = tokens // blocks
    per_block = rows // CH
    local = read_ref.shape[0] - 1
    state_size = in_ref.shape[1]
    padded = table_ref.shape[0] // levels
    classes = table_ref.shape[1]
    row = lax.broadcasted_iota(jnp.int32, (rows, rows), 0)
    col = lax.broadcasted_iota(jnp.int32, (rows, rows), 1)
    inside = (row // CH == col // CH) & (row <= col)
    upto = jnp.where(inside, 1.0, 0.0).astype(BF16)
    within, starts = [], [jnp.zeros((head_count, 1), F32)]
    for g in range(blocks):
        within.append(exact_dot(decay_ref[:, g * rows : (g + 1) * rows], upto))
        for s in range(per_block):
            last = (s + 1) * CH
            starts.append(starts[-1] + within[-1][:, last - 1 : last])
    class_row = lax.broadcasted_iota(jnp.int32, (classes, rows), 0)
    lane = lax.broadcasted_iota(jnp.int32, (head_count, rows), 1) // CH
    token = lax.broadcasted_iota(jnp.int32, (rows, state_size), 0) // CH

    def by_stretch(columns):
        spread = jnp.broadcast_to(columns[0], (head_count, rows))
        for s in range(1, per_block):
            spread = jnp.where(lane == s, columns[s], spread)
        return spread

    for g in range(blocks):
        at = slice(g * rows, (g + 1) * rows)
        onehot = jnp.where(class_ref[:, at] == class_row, 1.0, 0.0).astype(BF16)
        weights = sum(dot(part, onehot) for part in three_parts(table_ref[...]))
        weight = lambda level: weights[level * padded : level * padded + head_count, :]
        lift_ref[g] = jnp.exp(-within[g])
        read_ref[0, g] = jnp.exp(within[g]) * weight(0)
        first = g * per_block
        for level in range(1, local + 1):
            begins, active = [], []
            for c in range(first, first + per_block):
                upper = (c >> (level - 1)) & 1
                begins.append(starts[c] - starts[(c >> (level - 1)) << (level - 1)])
                active.append(jnp.full((head_count, 1), float(upper), F32))
            factor = jnp.exp(within[g] + by_stretch(begins)) * weight(level)
            read_ref[level, g] = factor * by_stretch(active)
        far = jnp.exp(within[g] + by_stretch(starts[first : first + per_block]))
        for level in range(local + 1, levels):
            cross_ref[level - local - 1, g] = far * weight(level)
        own_in, own_out = in_ref[at, :], out_ref[at, :]
        scores = jnp.where(inside, dot_nt(own_in, own_out), 0.0)
        score_ref[g, 0], score_ref[g, 1] = two_parts(scores)
        for s in range(per_block):
            masked = jnp.where(token == s, own_in.astype(F32), 0.0).astype(BF16)
            masked_ref[g, :, s * state_size : (s + 1) * state_size] = masked
        turned = jnp.transpose(own_out.astype(F32))
        reader = turned.astype(BF16)
        reader_ref[g, :state_size, :] = reader
        reader_ref[g, state_size:, :] = reader
        pairs = max(per_block // 2, 1)
        place = lax.broadcasted_iota(jnp.int32, (state_size, rows), 1) // (2 * CH)
        for j in range(pairs):
            alone = jnp.where(place == j, turned, 0.0).astype(BF16)
            pair_ref[g, j * state_size : (j + 1) * state_size, :] = alone
    for i, (kind, c, k) in enumerate(merge_rows(stretches)):
        first = c if kind == "own" else c + 1 - 2**k
        merge_ref[i] = jnp.broadcast_to(jnp.exp(starts[c + 1] - starts[first]), (head_count, LANES))


def load(refs, pieces, at):
    parts = [refs[i][at, first : first + count] for i, first, count in pieces]
    return parts[0] if len(parts) == 1 else jnp.concatenate(parts, axis=1)


def partial_state_kernel(pieces, *refs):
    count = len(pieces)
    arrays = sum(len(parts) for parts in pieces)
    value_refs, refs = refs[:arrays], refs[arrays:]
    fade_refs, (in_ref, keep_ref, send_ref, faded) = refs[:count], refs[count:]
    own_in = in_ref[...]
    for r in [*range(1, count, 2), *range(0, count, 2)]:
        fade = fade_refs[r][...].reshape(fade_refs[r].shape[-2:])
        head_count = fade.shape[0]
        width = value_refs[0].shape[0] // head_count
        for h in range(head_count):
            at = head_rows(h, width)
            value = load(value_refs, pieces[r], at).astype(F32)
            faded[at, :] = (fade[h : h + 1, :] * value).astype(BF16)
        state = dot(faded[...], own_in)
        if r % 2 == 1:
            send_ref[r // 2] = state.astype(BF16)
        else:
            keep_ref[r // 2] = state


def fold_kernel(*refs):
    count = len(refs) // 3
    for keep_ref, got_ref, far_ref in zip(refs[:count], refs[count : 2 * count], refs[2 * count :]):
        far_ref[...] = (keep_ref[0] + got_ref[0].astype(F32)).astype(BF16)


def pack_state(sent_ref, state, total):
    channels = state.shape[0]
    sent_ref[:channels, :] = state.astype(BF16)
    high, middle, low = (part.astype(F32) for part in three_parts(total))
    lane = lax.broadcasted_iota(jnp.int32, total.shape, 1)
    parts = jnp.where(lane < LANES // 4, high, jnp.where(lane < LANES // 2, middle, low))
    sent_ref[channels:, :] = parts.astype(BF16)


def first_kernel(own_ref, core_ref, total_ref, *refs):
    *far_refs, running_ref, sent_ref = refs
    running = own_ref[0] + core_ref[0].astype(F32)
    for far_ref in far_refs:
        running = running + far_ref[...].astype(F32)
    running_ref[...] = running
    pack_state(sent_ref, running, total_ref[...])


def merge_kernel(
    bit, head_count, place_ref, running_ref, total_ref, offset_ref, got_ref,
    next_running_ref, next_total_ref, next_offset_ref, factor_ref, sent_ref,
):
    channels = running_ref.shape[0]
    width = channels // head_count
    place = place_ref[0]
    upper = place // 2**bit % 2 == 1
    total = total_ref[...]
    parts = got_ref[channels:, :].astype(F32)
    middle, low = LANES // 4, LANES // 2
    partner = parts[:, 0:1] + parts[:, middle : middle + 1] + parts[:, low : low + 1]
    partner = jnp.broadcast_to(partner, total.shape)
    fading = jnp.exp(jnp.where(upper, total, partner))
    for h in range(head_count):
        at = head_rows(h, width)
        got, running = got_ref[at, :].astype(F32), running_ref[at, :]
        lower, higher = jnp.where(upper, got, running), jnp.where(upper, running, got)
        next_running_ref[at, :] = fading[h : h + 1, :] * lower + higher
    joined = total + partner
    next_total_ref[...] = joined
    offset = jnp.where(upper, offset_ref[...] + partner, offset_ref[...])
    next_offset_ref[...] = offset
    next_upper = place // 2 ** (bit + 1) % 2 == 1
    factor_ref[...] = jnp.where(next_upper, jnp.exp(offset), 0.0)
    pack_state(sent_ref, next_running_ref[...], joined)


def local_kernel(near, pieces, me_ref, *refs):
    groups = refs[-1].shape[0]
    arrays = 1 + max(i for parts in pieces for i, _, _ in parts)
    value_refs, refs = refs[:arrays], refs[arrays:]
    lift_ref, read_ref, merge_ref, score_ref, masked_ref, reader_ref, pair_ref = refs[:7]
    skip_ref, cross_ref, *refs = refs[7:]
    factor_refs, state_refs, refs = refs[:near], refs[near : 2 * near], refs[2 * near :]
    pre_ref, lifted, sums, operand, pairs_ref, nodes = refs
    channels, group_rows = value_refs[0].shape
    assert len(pieces) == groups
    head_count = lift_ref.shape[1]
    width = channels // head_count
    me = me_ref[0]
    per_group = group_rows // CH
    stretches = groups * per_group
    state_size = reader_ref.shape[1] // 2
    place = {kind: i for i, kind in enumerate(merge_rows(stretches))}
    heads = [(h, head_rows(h, width)) for h in range(head_count)]
    for r in range(groups):
        g = me ^ r
        lift = lift_ref[g]
        for h, at in heads:
            value = load(value_refs, pieces[r], at).astype(F32)
            lifted[at, :] = (lift[h : h + 1, :] * value).astype(BF16)
        direct = dot(lifted[...], score_ref[g, 0]) + dot(lifted[...], score_ref[g, 1])
        read = read_ref[0, g]
        terms = []
        for level, (state_ref, factor_ref) in enumerate(zip(state_refs, factor_refs)):
            gained = dot(state_ref[:channels, :], reader_ref[g, :state_size, :])
            scale = cross_ref[level, g] * factor_ref[:head_count, 0:1]
            terms.append((scale, gained))
        for h, at in heads:
            total = read[h : h + 1, :] * direct[at, :]
            total = total + skip_ref[h : h + 1, :] * load(value_refs, pieces[r], at).astype(F32)
            for scale, gained in terms:
                total = total + scale[h : h + 1, :] * gained[at, :]
            pre_ref[g, at, :] = total
        nodes[g] = dot(lifted[...], masked_ref[g])

    for g in range(groups):
        terms = []
        level = per_group.bit_length()
        while 2 ** (level - 1) < stretches:
            if (g * per_group >> (level - 1)) & 1:
                terms.append((read_ref[level, g], dot(operand[level - 1], reader_ref[g])))
            level += 1
        for s in range(per_group):
            c = g * per_group + s
            if c + 1 == stretches:
                break
            merges = [merge_ref[place["own", c, 0]]]
            k = 0
            while (c >> k) & 1:
                merges.append(merge_ref[place["merge", c, k]])
                k += 1
            for h, at in heads:
                node = nodes[g, at, s * state_size : (s + 1) * state_size]
                node = node * merges[0][h : h + 1, :]
                for i, merge in enumerate(merges[1:]):
                    node = node + merge[h : h + 1, :] * sums[i, at, :]
                sums[k, at, :] = node
                high, low = two_parts(node)
                if k == 0 and per_group > 1:
                    pairs_ref[at, s // 2 * state_size : (s // 2 + 1) * state_size] = high
                else:
                    operand[k, at, :state_size] = high
                    operand[k, at, state_size:] = low
            if 1 <= k < per_group.bit_length() - 1:
                scale = read_ref[k + 1, g]
                lane = lax.broadcasted_iota(jnp.int32, scale.shape, 1) // (CH << (k + 1))
                scale = jnp.where(lane == s >> (k + 1), scale, 0.0)
                terms.append((scale, dot(operand[k], reader_ref[g])))
        if per_group > 1:
            terms.append((read_ref[1, g], dot(pairs_ref[...], pair_ref[g])))
        for h, at in heads:
            total = pre_ref[g, at, :]
            for scale, gained in terms:
                total = total + scale[h : h + 1, :] * gained[at, :]
            pre_ref[g, at, :] = total


def finish_kernel(
    half, me_ref, pre_ref, reader_ref, cross_ref, factor_ref, state_ref, gain_ref, *refs
):
    keep_refs, send_ref = refs[:half], refs[half]
    groups, channels, _ = pre_ref.shape
    head_count = cross_ref.shape[2]
    width = channels // head_count
    state_size = reader_ref.shape[1] // 2
    me = me_ref[0]
    state = state_ref[:channels, :]
    for r in range(groups):
        g = me ^ r
        gained = dot(state, reader_ref[g, :state_size, :])
        scale = cross_ref[0, g] * factor_ref[:head_count, 0:1]
        for h in range(head_count):
            at = head_rows(h, width)
            total = pre_ref[g, at, :] + scale[h : h + 1, :] * gained[at, :]
            mean_square = jnp.sum(total * total, axis=0, keepdims=True) * (1.0 / width)
            normed = total * lax.rsqrt(mean_square + EPSILON) * gain_ref[at, 0:1]
            if r % 2 == 0:
                keep_refs[r // 2][at, :] = normed.astype(BF16)
            else:
                send_ref[r // 2, at, :] = normed.astype(BF16)


def project_kernel(place_ref, *refs):
    *refs, out_ref = refs
    rows = out_ref.shape[0]
    kept_refs, other_refs, refs = refs[:rows], refs[rows : 2 * rows], refs[2 * rows :]
    count = len(refs) // 2
    weights, partners = refs[:count], refs[count:]
    width = weights[0].shape[0]
    turn = place_ref[0] % count
    for i, (kept_ref, other_ref) in enumerate(zip(kept_refs, other_refs)):
        for j, (weight, partner) in enumerate(zip(weights, partners)):
            found = dot(weight[...], kept_ref[...]) + dot(partner[...], other_ref[0])
            at = pl.ds(pl.multiple_of((turn ^ j) * width, width), width)
            out_ref[i, at, :] = found.astype(out_ref.dtype)


def assemble_kernel(place_ref, *refs):
    out_ref = refs[-1]
    width = refs[0].shape[0]
    groups = out_ref.shape[1] // width
    each = (len(refs) - 1) // groups
    for p in range(groups):
        own_ref, *far_refs = refs[p * each : (p + 1) * each]
        total = own_ref[...]
        for far_ref in far_refs:
            total = total + far_ref[...].astype(F32)
        start = pl.multiple_of((place_ref[0] ^ p) * width, width)
        out_ref[:, pl.ds(start, width)] = jnp.transpose(total).astype(BF16)


def whole(shape):
    return pl.BlockSpec(shape, lambda *_: (0,) * len(shape))


def on_device(
    values,
    state_in,
    state_out,
    log_decay,
    level_class,
    level_table,
    skip_gain,
    norm_gain,
    out_weight,
):
    heads_size = lax.axis_size("head")
    ctx_size = lax.axis_size("ctx")
    ctx_bits = ctx_size.bit_length() - 1
    me = lax.axis_index("head")
    me1 = me.reshape(1).astype(jnp.int32)
    position = lax.axis_index("ctx")
    place1 = position.reshape(1).astype(jnp.int32)
    tokens = state_in.shape[0]
    rows_dev = values.shape[0]
    head_count = log_decay.shape[1]
    features = values.shape[1] // heads_size
    state_size = state_in.shape[1]
    columns = out_weight.shape[1]
    stretches = tokens // CH
    per_group = rows_dev // CH
    local = stretches.bit_length() - 1
    levels = level_table.shape[1]
    classes = level_table.shape[0]
    extra = -(-head_count // 16) * 16
    padded = -(-head_count // 8) * 8
    half = heads_size // 2
    near = ctx_bits - 1
    params = pltpu.CompilerParams(vmem_limit_bytes=VMEM_LIMIT)
    cheap = pl.CostEstimate(flops=0, bytes_accessed=0, transcendentals=0)
    smem = pl.BlockSpec(memory_space=pltpu.SMEM)
    vmem = pl.BlockSpec(memory_space=pltpu.VMEM)

    def kernel_call(body, name, out_shape, **kwargs):
        return pl.pallas_call(
            body, out_shape=out_shape, compiler_params=params, cost_estimate=cheap, name=name, **kwargs
        )

    def shape(dims, kind=BF16):
        return jax.ShapeDtypeStruct(dims, kind)

    def part(array, index):
        return pl.BlockSpec((1,) + array.shape[1:], lambda *_: (index,) + (0,) * (array.ndim - 1))

    def fenced(body, *operands):
        shapes = jax.eval_shape(body, *operands)
        zeros = lambda *_: jax.tree.map(lambda leaf: jnp.zeros(leaf.shape, leaf.dtype), shapes)
        return lax.cond(position < ctx_size, body, zeros, *operands)

    held, partners = {0: out_weight.T}, {}
    for bit in range(ctx_bits):
        held[2**bit] = swap(held[0], "ctx", 2**bit)

    decays = log_decay.T
    own_fade, side_fade, *far_fades, total = kernel_call(
        functools.partial(fade_kernel, heads_size),
        "fade",
        tuple(
            [shape((head_count, rows_dev), F32)] * 2
            + [shape((2, head_count, rows_dev), F32)] * (half - 1)
            + [shape((extra, LANES), F32)]
        ),
        in_specs=[smem, vmem],
    )(me1, decays)

    got_fades = []
    for i, far in enumerate(far_fades):
        got_fades.append(swap(tie(far, *got_fades), "head", 2 * (i + 1)))
    sides = kernel_call(
        pack_kernel,
        "pack_fades",
        shape((half, head_count, rows_dev), F32),
        grid=(1,),
        in_specs=[whole(side_fade.shape)] + [part(got, 1) for got in got_fades],
        out_specs=whole((half, head_count, rows_dev)),
    )(side_fade, *got_fades)
    sides = swap(sides, "head", 1)

    early = rows_dev // 2
    cuts = [(r, first, early) for r in (2,) for first in (0, early)]
    cuts = [(0, 0, rows_dev), (1, 0, rows_dev)] + cuts
    cuts += [(r, 0, rows_dev) for r in range(3, heads_size)]
    portions = kernel_call(
        split_kernel,
        "split_values",
        tuple(shape((features, count)) for _, _, count in cuts),
        grid_spec=pltpu.PrefetchScalarGridSpec(
            num_scalar_prefetch=1,
            grid=(1,),
            in_specs=[
                pl.BlockSpec((count, features), lambda i, m, r=r, at=first // count: (at, m[0] ^ r))
                for r, first, count in cuts
            ],
            out_specs=[whole((features, count)) for _, _, count in cuts],
        ),
    )(me1, *[values] * len(cuts))
    portion = {(r, first): array for (r, first, _), array in zip(cuts, portions)}
    value_head = swap(tie(portion[2, 0], *got_fades), "head", 2)

    pieces = [[] for _ in range(heads_size)]
    for i, (r, _, count) in enumerate(cuts):
        pieces[r].append((i, 0, count))
    fades, fade_specs = [], []
    for r in range(heads_size):
        if r == 0:
            fades.append(own_fade)
            fade_specs.append(whole(own_fade.shape))
        else:
            fades.append(sides if r % 2 else got_fades[r // 2 - 1])
            fade_specs.append(part(fades[-1], r // 2 if r % 2 else 0))
    keep, send = kernel_call(
        lambda me_ref, *refs: partial_state_kernel(pieces, *refs),
        "partial_states",
        (shape((half, features, state_size), F32), shape((half, features, state_size))),
        grid_spec=pltpu.PrefetchScalarGridSpec(
            num_scalar_prefetch=1,
            grid=(1,),
            in_specs=[whole(array.shape) for array in portions]
            + fade_specs
            + [pl.BlockSpec((rows_dev, state_size), lambda i, m: (m[0], 0))],
            out_specs=[whole((half, features, state_size))] * 2,
            scratch_shapes=[pltpu.VMEM((features, rows_dev), BF16)],
        ),
    )(me1, *portions, *fades, state_in)

    def core_sum(keep, send):
        got = swap(send, "head", 1)
        far = kernel_call(
            fold_kernel,
            "fold",
            tuple([shape((features, state_size))] * (half - 1)),
            in_specs=[part(keep, i) for i in range(1, half)] * 2,
            out_specs=tuple([whole((features, state_size))] * (half - 1)),
            grid=(1,),
        )(*[keep] * (half - 1), *[got] * (half - 1))
        return got, far

    core_states, far_states = fenced(core_sum, keep, send)

    merge_count = len(merge_rows(stretches))
    grouped = (heads_size, head_count, rows_dev)
    pair_rows = max(per_group // 2, 1) * state_size

    def step(bit, running, total, offset, got):
        return kernel_call(
            functools.partial(merge_kernel, bit, head_count),
            "merge",
            (
                shape((features, state_size), F32),
                shape((extra, LANES), F32),
                shape((extra, LANES), F32),
                shape((extra, LANES), F32),
                shape((features + extra, state_size)),
            ),
            in_specs=[smem] + [vmem] * 4,
        )(place1, running, total, offset, got)

    def chip_sum(
        keep, core_states, far_states, total, decays, level_class, level_table, state_in, state_out,
        second, crossing,
    ):
        got_states, latest = [], []
        for i, far in enumerate(far_states):
            latest = [swap(tie(far, *latest), "head", 2 * (i + 1))]
            got_states += latest
        moved, after = [], []
        for array in crossing:
            moved.append(swap(tie(array, *after), "head", 1))
            after = moved[-1:]
        if moved:
            moved[0] = jnp.concatenate([second, moved[0]], axis=1)
        table = jnp.transpose(level_table, (1, 2, 0))
        table = jnp.pad(table, ((0, 0), (0, padded - head_count), (0, 0)))
        tables = kernel_call(
            functools.partial(factors_kernel, levels, heads_size),
            "factors",
            (
                shape(grouped, F32),
                shape((local + 1,) + grouped, F32),
                shape((ctx_bits,) + grouped, F32),
                shape((merge_count, head_count, LANES), F32),
                shape((heads_size, 2, rows_dev, rows_dev)),
                shape((heads_size, rows_dev, per_group * state_size)),
                shape((heads_size, 2 * state_size, rows_dev)),
                shape((heads_size, pair_rows, rows_dev)),
            ),
        )(
            decays,
            level_class.reshape(1, tokens),
            table.reshape(levels * padded, classes),
            state_in,
            state_out,
        )
        got_states[-1] = tie(got_states[-1], tables[0], *moved)
        running, sent = kernel_call(
            first_kernel,
            "first_state",
            (shape((features, state_size), F32), shape((features + extra, state_size))),
            grid=(1,),
            in_specs=[part(keep, 0), part(core_states, 0), whole(total.shape)]
            + [whole((features, state_size))] * len(got_states),
            out_specs=(whole((features, state_size)), whole((features + extra, state_size))),
        )(keep, core_states, total, *got_states)
        return running, sent, tables, moved

    def near_steps(running, total, sent):
        offset = jnp.zeros((extra, LANES), F32)
        factors = [jnp.broadcast_to((position % 2).astype(F32), (extra, LANES))]
        states = []
        for bit in range(near):
            states.append(swap(sent, "ctx", 2**bit))
            running, total, offset, factor, sent = step(bit, running, total, offset, states[-1])
            factors.append(factor)
        return states, factors, sent

    running, sent, tables, moved = fenced(
        chip_sum, keep, core_states, tie(far_states, value_head), total, decays, level_class,
        level_table, state_in, state_out, portion[2, early],
        [portion[r, 0] for r in range(3, heads_size, 2)],
    )
    passed, after = {}, []
    for i, array in enumerate(moved):
        passed[2 * i + 3] = swap(tie(array, *after), "head", 2 * i + 2)
        after = [passed[2 * i + 3]]
    for r in range(4, heads_size, 2):
        passed[r] = swap(tie(portion[r, 0], *after), "head", r)
        after = [passed[r]]
    states, factors, sent = fenced(near_steps, running, total, sent)
    states = list(states)
    sent = tie(sent, *[held[2**bit] for bit in range(ctx_bits)])
    last_state = swap(sent, "ctx", 2**near)

    for r in range(2, ctx_size):
        low = r & -r
        if r not in held and low > 1:
            held[r] = swap(tie(held[r ^ low], sent), "ctx", low)
    for bit in range(2, ctx_bits):
        held[2**bit + 1] = swap(tie(held[2**bit], sent), "ctx", 1)
    for r in (0, 1):
        partners[r] = swap(tie(held[r], sent), "head", 1)

    skips = jnp.broadcast_to(skip_gain[:, None], (head_count, rows_dev))
    gains = norm_gain[:, None]

    lift, read, cross, merge, scores, masked, readers, pairs = tables
    arrays = [portion[0, 0], swap(tie(portion[1, 0], sent), "head", 1), value_head]
    pieces = [[(0, 0, rows_dev)], [(1, 0, rows_dev)], [(2, 0, early)]]
    for r in range(3, heads_size):
        first = rows_dev - early if r == 3 else 0
        if r == 3:
            pieces[2].append((len(arrays), 0, first))
        pieces.append([(len(arrays), first, rows_dev)])
        arrays.append(passed[r])
    pre = kernel_call(
        functools.partial(local_kernel, near, pieces),
        "local_levels",
        shape((heads_size, features, rows_dev), F32),
        in_specs=[smem] + [vmem] * (len(arrays) + 9 + 2 * near),
        scratch_shapes=[
            pltpu.VMEM((features, rows_dev), BF16),
            pltpu.VMEM((max(local, 1), features, state_size), F32),
            pltpu.VMEM((max(local, 1), features, 2 * state_size), BF16),
            pltpu.VMEM((features, pair_rows), BF16),
            pltpu.VMEM((heads_size, features, per_group * state_size), F32),
        ],
    )(
        me1, *arrays, lift, read, merge, scores, masked, readers, pairs, skips, cross,
        *factors[:near], *states,
    )
    *kept, sides = kernel_call(
        functools.partial(finish_kernel, half),
        "finish",
        tuple([shape((features, rows_dev))] * half + [shape((half, features, rows_dev))]),
        grid=(1,),
        in_specs=[
            smem,
            whole(pre.shape),
            whole(readers.shape),
            part(cross, near),
            whole((extra, LANES)),
            whole((features + extra, state_size)),
            whole((features, 1)),
        ],
        out_specs=[whole((features, rows_dev))] * half + [whole((half, features, rows_dev))],
    )(me1, pre, readers, cross, factors[near], last_state, gains)
    early_blocks = set(held)
    done = [held[r] for r in held if r not in (0, 1)] + [kept[0]]
    held[3] = swap(tie(held[1], *done), "ctx", 2)
    for r in range(5, ctx_size, 2):
        if r not in held:
            held[r] = swap(tie(held[r ^ 1], *done), "ctx", 1)

    count = 1
    while count * columns % 128 and 2 * count <= ctx_size:
        count *= 2

    others = swap(sides, "head", 1)
    firsts = list(range(0, ctx_size, count))
    group_of = lambda first: range(first, first + count)

    def project(name, first, kept, others, blocks, partners, kind):
        rows = len(kept)
        return kernel_call(
            project_kernel,
            name,
            shape((rows, count * columns, rows_dev), kind),
            in_specs=[smem]
            + [whole((features, rows_dev))] * rows
            + [part(others, first + i) for i in range(rows)]
            + [whole((columns, features))] * (2 * count),
            out_specs=whole((rows, count * columns, rows_dev)),
            grid=(1,),
        )(place1, *kept, *[others] * rows, *blocks, *partners)

    def far_rows(first, kept, others, blocks, partners):
        return project(
            "project_far", 1, kept[1:], others,
            [blocks[r] for r in group_of(first)], [partners[r] for r in group_of(first)], BF16,
        )

    def own_rows(first, kept, others, blocks, partners):
        return project(
            "project_own", 0, kept[:1], others,
            [blocks[r] for r in group_of(first)], [partners[r] for r in group_of(first)], F32,
        )[0]

    def send_rows(far, *after):
        far = tie(far, *after)
        return [swap(far[i - 1], "head", 2 * i) for i in range(1, half)]

    def first_groups(kept, others, blocks, partners):
        more = {r: swap(blocks[r], "head", 1) for r in blocks if r not in partners}
        partners = {**partners, **more}
        fars = [far_rows(first, kept, others, blocks, partners) for first in early_groups]
        return fars[1:], send_rows(fars[0]), more

    def last_groups(kept, others, blocks, partners, early):
        partners, results, arrived = dict(partners), {}, []
        for first in late_groups:
            for r in group_of(first):
                if r not in partners:
                    partners[r] = swap(blocks[r], "head", 1)
            got = send_rows(far_rows(first, kept, others, blocks, partners), *arrived)
            results[first] = [own_rows(first, kept, others, blocks, partners)] + got
            arrived = got
        owns = [own_rows(first, kept, others, early, partners) for first in early_groups[1:]]
        return results, owns

    early_groups = [f for f in firsts if all(r in early_blocks for r in group_of(f))] or firsts[:1]
    late_groups = [f for f in firsts if f not in early_groups]
    early = {r: held[r] for f in early_groups for r in group_of(f)}
    late = {r: held[r] for f in late_groups for r in group_of(f)}
    fars, got, more = fenced(first_groups, kept, others, early, partners)
    partners = {**partners, **more}
    sent_groups = [got]
    for far in fars:
        sent_groups.append(send_rows(far, *sent_groups[-1]))
    own = own_rows(early_groups[0], [tie(kept[0], *fars)], others, early, partners)
    if late_groups:
        late[late_groups[0]] = tie(late[late_groups[0]], own)
    results, owns = fenced(last_groups, kept, others, late, partners, early)
    for first, own, got in zip(early_groups, [own] + owns, sent_groups):
        results[first] = [own] + got
    pieces = [piece for first in firsts for piece in results[first]]
    return kernel_call(
        assemble_kernel,
        "assemble",
        shape((rows_dev, ctx_size * columns)),
        in_specs=[smem] + [vmem] * len(pieces),
    )(place1 // count, *pieces)


def solution(mesh):
    return jax.shard_map(
        on_device,
        mesh=mesh,
        in_specs=(
            P(("ctx", "head"), None),
            P("ctx", None),
            P("ctx", None),
            P("ctx", "head"),
            P("ctx"),
            P(None, None, "head"),
            P("head"),
            P("head"),
            P("head", "ctx"),
        ),
        out_specs=P(("ctx", "head"), None),
        check_vma=False,
    )
```

```python
import functools

import jax
import jax.numpy as jnp
from jax import lax
from jax.experimental import pallas as pl
from jax.experimental.pallas import tpu as pltpu
from jax.sharding import PartitionSpec as P

CH = 64
EPSILON = 1e-05
LANES = 128
F32 = jnp.float32
BF16 = jnp.bfloat16
VMEM_LIMIT = 40 * 1024 * 1024


def dot(a, b):
    return lax.dot_general(a, b, (((1,), (0,)), ((), ())), preferred_element_type=F32)


def dot_nt(a, b):
    return lax.dot_general(a, b, (((1,), (1,)), ((), ())), preferred_element_type=F32)


def swap(value, axis, distance):
    pairs = [(source, source ^ distance) for source in range(lax.axis_size(axis))]
    return lax.ppermute(value, axis, pairs)


def tie(value, *after):
    return lax.optimization_barrier((value,) + after)[0]


def three_parts(x):
    high = x.astype(BF16)
    rest = x - high.astype(F32)
    middle = rest.astype(BF16)
    low = (rest - middle.astype(F32)).astype(BF16)
    return high, middle, low


def two_parts(x):
    high = x.astype(BF16)
    return high, (x - high.astype(F32)).astype(BF16)


def merge_rows(stretches):
    rows = [("own", c, 0) for c in range(stretches - 1)]
    for c in range(stretches - 1):
        k = 0
        while (c >> k) & 1:
            rows.append(("merge", c, k))
            k += 1
    return rows


def head_rows(head, width):
    return slice(head * width, (head + 1) * width)


def exact_dot(x, ones):
    return sum(dot(part, ones) for part in three_parts(x))


def split_kernel(me_ref, *refs):
    half = len(refs) // 2
    for value_ref, part_ref in zip(refs[:half], refs[half:]):
        part_ref[...] = jnp.transpose(value_ref[...])


def fade_kernel(blocks, me_ref, decay_ref, own_ref, side_ref, *refs):
    far_refs, total_ref = refs[:-1], refs[-1]
    head_count, tokens = decay_ref.shape
    rows = tokens // blocks
    row = lax.broadcasted_iota(jnp.int32, (rows, rows), 0)
    col = lax.broadcasted_iota(jnp.int32, (rows, rows), 1)
    later = jnp.where(row > col, 1.0, 0.0).astype(BF16)
    me = me_ref[0]
    after = jnp.zeros((head_count, 1), F32)
    for block in reversed(range(blocks)):
        decay = decay_ref[:, block * rows : (block + 1) * rows]
        left = exact_dot(decay, later)
        fade = jnp.exp(left + after)
        after = after + left[:, 0:1] + decay[:, 0:1]
        own_index = me ^ block

        @pl.when(own_index == 0)
        def _():
            own_ref[...] = fade

        @pl.when(own_index == 1)
        def _():
            side_ref[...] = fade

        for i, far_ref in enumerate(far_refs):
            for j in range(2):

                @pl.when(own_index == 2 * (i + 1) + j)
                def _():
                    far_ref[j] = fade

    total_ref[...] = jnp.zeros_like(total_ref)
    total_ref[:head_count, :] = jnp.broadcast_to(after, (head_count, LANES))


def pack_kernel(*refs):
    side_ref, *got_refs, out_ref = refs
    out_ref[0] = side_ref[...]
    for i, got_ref in enumerate(got_refs):
        out_ref[i + 1] = got_ref[0]


def factors_kernel(
    levels, blocks, decay_ref, class_ref, table_ref, in_ref, out_ref,
    lift_ref, read_ref, cross_ref, merge_ref, score_ref, masked_ref, reader_ref, pair_ref,
):
    head_count, tokens = decay_ref.shape
    stretches = tokens // CH
    rows = tokens // blocks
    per_block = rows // CH
    local = read_ref.shape[0] - 1
    state_size = in_ref.shape[1]
    padded = table_ref.shape[0] // levels
    classes = table_ref.shape[1]
    row = lax.broadcasted_iota(jnp.int32, (rows, rows), 0)
    col = lax.broadcasted_iota(jnp.int32, (rows, rows), 1)
    inside = (row // CH == col // CH) & (row <= col)
    upto = jnp.where(inside, 1.0, 0.0).astype(BF16)
    within, starts = [], [jnp.zeros((head_count, 1), F32)]
    for g in range(blocks):
        within.append(exact_dot(decay_ref[:, g * rows : (g + 1) * rows], upto))
        for s in range(per_block):
            last = (s + 1) * CH
            starts.append(starts[-1] + within[-1][:, last - 1 : last])
    class_row = lax.broadcasted_iota(jnp.int32, (classes, rows), 0)
    lane = lax.broadcasted_iota(jnp.int32, (head_count, rows), 1) // CH
    token = lax.broadcasted_iota(jnp.int32, (rows, state_size), 0) // CH

    def by_stretch(columns):
        spread = jnp.broadcast_to(columns[0], (head_count, rows))
        for s in range(1, per_block):
            spread = jnp.where(lane == s, columns[s], spread)
        return spread

    for g in range(blocks):
        at = slice(g * rows, (g + 1) * rows)
        onehot = jnp.where(class_ref[:, at] == class_row, 1.0, 0.0).astype(BF16)
        weights = sum(dot(part, onehot) for part in three_parts(table_ref[...]))
        weight = lambda level: weights[level * padded : level * padded + head_count, :]
        lift_ref[g] = jnp.exp(-within[g])
        read_ref[0, g] = jnp.exp(within[g]) * weight(0)
        first = g * per_block
        for level in range(1, local + 1):
            begins, active = [], []
            for c in range(first, first + per_block):
                upper = (c >> (level - 1)) & 1
                begins.append(starts[c] - starts[(c >> (level - 1)) << (level - 1)])
                active.append(jnp.full((head_count, 1), float(upper), F32))
            factor = jnp.exp(within[g] + by_stretch(begins)) * weight(level)
            read_ref[level, g] = factor * by_stretch(active)
        far = jnp.exp(within[g] + by_stretch(starts[first : first + per_block]))
        for level in range(local + 1, levels):
            cross_ref[level - local - 1, g] = far * weight(level)
        own_in, own_out = in_ref[at, :], out_ref[at, :]
        scores = jnp.where(inside, dot_nt(own_in, own_out), 0.0)
        score_ref[g, 0], score_ref[g, 1] = two_parts(scores)
        for s in range(per_block):
            masked = jnp.where(token == s, own_in.astype(F32), 0.0).astype(BF16)
            masked_ref[g, :, s * state_size : (s + 1) * state_size] = masked
        turned = jnp.transpose(own_out.astype(F32))
        reader = turned.astype(BF16)
        reader_ref[g, :state_size, :] = reader
        reader_ref[g, state_size:, :] = reader
        pairs = max(per_block // 2, 1)
        place = lax.broadcasted_iota(jnp.int32, (state_size, rows), 1) // (2 * CH)
        for j in range(pairs):
            alone = jnp.where(place == j, turned, 0.0).astype(BF16)
            pair_ref[g, j * state_size : (j + 1) * state_size, :] = alone
    for i, (kind, c, k) in enumerate(merge_rows(stretches)):
        first = c if kind == "own" else c + 1 - 2**k
        merge_ref[i] = jnp.broadcast_to(jnp.exp(starts[c + 1] - starts[first]), (head_count, LANES))


def load(refs, pieces, at):
    parts = [refs[i][at, first : first + count] for i, first, count in pieces]
    return parts[0] if len(parts) == 1 else jnp.concatenate(parts, axis=1)


def partial_state_kernel(pieces, *refs):
    count = len(pieces)
    arrays = sum(len(parts) for parts in pieces)
    value_refs, refs = refs[:arrays], refs[arrays:]
    fade_refs, (in_ref, keep_ref, send_ref, faded) = refs[:count], refs[count:]
    own_in = in_ref[...]
    for r in [*range(1, count, 2), *range(0, count, 2)]:
        fade = fade_refs[r][...].reshape(fade_refs[r].shape[-2:])
        head_count = fade.shape[0]
        width = value_refs[0].shape[0] // head_count
        for h in range(head_count):
            at = head_rows(h, width)
            value = load(value_refs, pieces[r], at).astype(F32)
            faded[at, :] = (fade[h : h + 1, :] * value).astype(BF16)
        state = dot(faded[...], own_in)
        if r % 2 == 1:
            send_ref[r // 2] = state.astype(BF16)
        else:
            keep_ref[r // 2] = state


def fold_kernel(*refs):
    count = len(refs) // 3
    for keep_ref, got_ref, far_ref in zip(refs[:count], refs[count : 2 * count], refs[2 * count :]):
        far_ref[...] = (keep_ref[0] + got_ref[0].astype(F32)).astype(BF16)


def pack_state(sent_ref, state, total):
    channels = state.shape[0]
    sent_ref[:channels, :] = state.astype(BF16)
    high, middle, low = (part.astype(F32) for part in three_parts(total))
    lane = lax.broadcasted_iota(jnp.int32, total.shape, 1)
    parts = jnp.where(lane < LANES // 4, high, jnp.where(lane < LANES // 2, middle, low))
    sent_ref[channels:, :] = parts.astype(BF16)


def first_kernel(own_ref, core_ref, total_ref, *refs):
    *far_refs, running_ref, sent_ref = refs
    running = own_ref[0] + core_ref[0].astype(F32)
    for far_ref in far_refs:
        running = running + far_ref[...].astype(F32)
    running_ref[...] = running
    pack_state(sent_ref, running, total_ref[...])


def merge_kernel(
    bit, head_count, place_ref, running_ref, total_ref, offset_ref, got_ref,
    next_total_ref, next_offset_ref, factor_ref, sent_ref, next_running_ref,
):
    channels = running_ref.shape[0]
    width = channels // head_count
    place = place_ref[0]
    upper = place // 2**bit % 2 == 1
    total = total_ref[...]
    parts = got_ref[channels:, :].astype(F32)
    middle, low = LANES // 4, LANES // 2
    partner = parts[:, 0:1] + parts[:, middle : middle + 1] + parts[:, low : low + 1]
    partner = jnp.broadcast_to(partner, total.shape)
    fading = jnp.exp(jnp.where(upper, total, partner))
    for h in range(head_count):
        at = head_rows(h, width)
        got, running = got_ref[at, :].astype(F32), running_ref[at, :]
        lower, higher = jnp.where(upper, got, running), jnp.where(upper, running, got)
        next_running_ref[at, :] = fading[h : h + 1, :] * lower + higher
    joined = total + partner
    next_total_ref[...] = joined
    offset = jnp.where(upper, offset_ref[...] + partner, offset_ref[...])
    next_offset_ref[...] = offset
    next_upper = place // 2 ** (bit + 1) % 2 == 1
    factor_ref[...] = jnp.where(next_upper, jnp.exp(offset), 0.0)
    pack_state(sent_ref, next_running_ref[...], joined)


def local_kernel(near, pieces, me_ref, *refs):
    groups = refs[-1].shape[0]
    arrays = 1 + max(i for parts in pieces for i, _, _ in parts)
    value_refs, refs = refs[:arrays], refs[arrays:]
    lift_ref, read_ref, merge_ref, score_ref, masked_ref, reader_ref, pair_ref = refs[:7]
    skip_ref, cross_ref, *refs = refs[7:]
    factor_refs, state_refs, refs = refs[:near], refs[near : 2 * near], refs[2 * near :]
    pre_ref, lifted, sums, operand, pairs_ref, nodes = refs
    channels, group_rows = value_refs[0].shape
    assert len(pieces) == groups
    head_count = lift_ref.shape[1]
    width = channels // head_count
    me = me_ref[0]
    per_group = group_rows // CH
    stretches = groups * per_group
    state_size = reader_ref.shape[1] // 2
    place = {kind: i for i, kind in enumerate(merge_rows(stretches))}
    heads = [(h, head_rows(h, width)) for h in range(head_count)]
    for r in range(groups):
        g = me ^ r
        lift = lift_ref[g]
        for h, at in heads:
            value = load(value_refs, pieces[r], at).astype(F32)
            lifted[at, :] = (lift[h : h + 1, :] * value).astype(BF16)
        direct = dot(lifted[...], score_ref[g, 0]) + dot(lifted[...], score_ref[g, 1])
        read = read_ref[0, g]
        terms = []
        for level, (state_ref, factor_ref) in enumerate(zip(state_refs, factor_refs)):
            gained = dot(state_ref[:channels, :], reader_ref[g, :state_size, :])
            scale = cross_ref[level, g] * factor_ref[:head_count, 0:1]
            terms.append((scale, gained))
        for h, at in heads:
            total = read[h : h + 1, :] * direct[at, :]
            total = total + skip_ref[h : h + 1, :] * load(value_refs, pieces[r], at).astype(F32)
            for scale, gained in terms:
                total = total + scale[h : h + 1, :] * gained[at, :]
            pre_ref[g, at, :] = total
        nodes[g] = dot(lifted[...], masked_ref[g])

    for g in range(groups):
        terms = []
        level = per_group.bit_length()
        while 2 ** (level - 1) < stretches:
            if (g * per_group >> (level - 1)) & 1:
                terms.append((read_ref[level, g], dot(operand[level - 1], reader_ref[g])))
            level += 1
        for s in range(per_group):
            c = g * per_group + s
            if c + 1 == stretches:
                break
            merges = [merge_ref[place["own", c, 0]]]
            k = 0
            while (c >> k) & 1:
                merges.append(merge_ref[place["merge", c, k]])
                k += 1
            for h, at in heads:
                node = nodes[g, at, s * state_size : (s + 1) * state_size]
                node = node * merges[0][h : h + 1, :]
                for i, merge in enumerate(merges[1:]):
                    node = node + merge[h : h + 1, :] * sums[i, at, :]
                sums[k, at, :] = node
                high, low = two_parts(node)
                if k == 0 and per_group > 1:
                    pairs_ref[at, s // 2 * state_size : (s // 2 + 1) * state_size] = high
                else:
                    operand[k, at, :state_size] = high
                    operand[k, at, state_size:] = low
            if 1 <= k < per_group.bit_length() - 1:
                scale = read_ref[k + 1, g]
                lane = lax.broadcasted_iota(jnp.int32, scale.shape, 1) // (CH << (k + 1))
                scale = jnp.where(lane == s >> (k + 1), scale, 0.0)
                terms.append((scale, dot(operand[k], reader_ref[g])))
        if per_group > 1:
            terms.append((read_ref[1, g], dot(pairs_ref[...], pair_ref[g])))
        for h, at in heads:
            total = pre_ref[g, at, :]
            for scale, gained in terms:
                total = total + scale[h : h + 1, :] * gained[at, :]
            pre_ref[g, at, :] = total


def finish_kernel(
    half, me_ref, pre_ref, reader_ref, cross_ref, factor_ref, state_ref, gain_ref, *refs
):
    keep_refs, send_ref = refs[:half], refs[half]
    groups, channels, _ = pre_ref.shape
    head_count = cross_ref.shape[2]
    width = channels // head_count
    state_size = reader_ref.shape[1] // 2
    me = me_ref[0]
    state = state_ref[:channels, :]
    for r in range(groups):
        g = me ^ r
        gained = dot(state, reader_ref[g, :state_size, :])
        scale = cross_ref[0, g] * factor_ref[:head_count, 0:1]
        for h in range(head_count):
            at = head_rows(h, width)
            total = pre_ref[g, at, :] + scale[h : h + 1, :] * gained[at, :]
            mean_square = jnp.sum(total * total, axis=0, keepdims=True) * (1.0 / width)
            normed = total * lax.rsqrt(mean_square + EPSILON) * gain_ref[at, 0:1]
            if r % 2 == 0:
                keep_refs[r // 2][at, :] = normed.astype(BF16)
            else:
                send_ref[r // 2, at, :] = normed.astype(BF16)


def project_kernel(*refs):
    *refs, out_ref = refs
    rows = out_ref.shape[0]
    kept_refs, other_refs, refs = refs[:rows], refs[rows : 2 * rows], refs[2 * rows :]
    count = len(refs) // 2
    weights, partners = refs[:count], refs[count:]
    width = weights[0].shape[0]
    for i, (kept_ref, other_ref) in enumerate(zip(kept_refs, other_refs)):
        for j, (weight, partner) in enumerate(zip(weights, partners)):
            found = dot(weight[...], kept_ref[...]) + dot(partner[...], other_ref[0])
            out_ref[i, j * width : (j + 1) * width, :] = found.astype(out_ref.dtype)


def assemble_kernel(groups, place_ref, *refs):
    *refs, out_ref, columns_ref = refs
    each = len(refs) // len(groups)
    for g, group in enumerate(groups):
        own_ref, *far_refs = refs[g * each : (g + 1) * each]
        width = own_ref.shape[0] // len(group)
        for j, r in enumerate(group):
            rows = slice(j * width, (j + 1) * width)
            total = own_ref[rows, :]
            for far_ref in far_refs:
                total = total + far_ref[rows, :].astype(F32)
            start = pl.multiple_of((place_ref[0] ^ r) * width, width)
            columns_ref[pl.ds(start, width), :] = total
    for first in range(0, out_ref.shape[1], LANES):
        at = slice(first, first + LANES)
        out_ref[:, at] = jnp.transpose(columns_ref[at, :]).astype(BF16)


def whole(shape):
    return pl.BlockSpec(shape, lambda *_: (0,) * len(shape))


def on_device(
    values,
    state_in,
    state_out,
    log_decay,
    level_class,
    level_table,
    skip_gain,
    norm_gain,
    out_weight,
):
    heads_size = lax.axis_size("head")
    ctx_size = lax.axis_size("ctx")
    ctx_bits = ctx_size.bit_length() - 1
    me = lax.axis_index("head")
    me1 = me.reshape(1).astype(jnp.int32)
    position = lax.axis_index("ctx")
    place1 = position.reshape(1).astype(jnp.int32)
    tokens = state_in.shape[0]
    rows_dev = values.shape[0]
    head_count = log_decay.shape[1]
    features = values.shape[1] // heads_size
    state_size = state_in.shape[1]
    columns = out_weight.shape[1]
    stretches = tokens // CH
    per_group = rows_dev // CH
    local = stretches.bit_length() - 1
    levels = level_table.shape[1]
    classes = level_table.shape[0]
    extra = -(-head_count // 16) * 16
    padded = -(-head_count // 8) * 8
    half = heads_size // 2
    near = ctx_bits - 1
    params = pltpu.CompilerParams(vmem_limit_bytes=VMEM_LIMIT)
    cheap = pl.CostEstimate(flops=0, bytes_accessed=0, transcendentals=0)
    smem = pl.BlockSpec(memory_space=pltpu.SMEM)
    vmem = pl.BlockSpec(memory_space=pltpu.VMEM)

    def kernel_call(body, name, out_shape, **kwargs):
        return pl.pallas_call(
            body, out_shape=out_shape, compiler_params=params, cost_estimate=cheap, name=name, **kwargs
        )

    def shape(dims, kind=BF16):
        return jax.ShapeDtypeStruct(dims, kind)

    def part(array, index):
        return pl.BlockSpec((1,) + array.shape[1:], lambda *_: (index,) + (0,) * (array.ndim - 1))

    def fenced(body, *operands):
        shapes = jax.eval_shape(body, *operands)
        zeros = lambda *_: jax.tree.map(lambda leaf: jnp.zeros(leaf.shape, leaf.dtype), shapes)
        return lax.cond(position < ctx_size, body, zeros, *operands)

    held, partners = {0: out_weight.T}, {}
    for bit in range(ctx_bits):
        held[2**bit] = swap(held[0], "ctx", 2**bit)

    decays = log_decay.T
    own_fade, side_fade, *far_fades, total = kernel_call(
        functools.partial(fade_kernel, heads_size),
        "fade",
        tuple(
            [shape((head_count, rows_dev), F32)] * 2
            + [shape((2, head_count, rows_dev), F32)] * (half - 1)
            + [shape((extra, LANES), F32)]
        ),
        in_specs=[smem, vmem],
    )(me1, decays)

    got_fades = []
    for i, far in enumerate(far_fades):
        got_fades.append(swap(tie(far, *got_fades), "head", 2 * (i + 1)))
    sides = kernel_call(
        pack_kernel,
        "pack_fades",
        shape((half, head_count, rows_dev), F32),
        grid=(1,),
        in_specs=[whole(side_fade.shape)] + [part(got, 1) for got in got_fades],
        out_specs=whole((half, head_count, rows_dev)),
    )(side_fade, *got_fades)
    sides = swap(sides, "head", 1)

    early = rows_dev // 2
    cuts = [(r, first, early) for r in (2,) for first in (0, early)]
    cuts = [(0, 0, rows_dev), (1, 0, rows_dev)] + cuts
    cuts += [(r, 0, rows_dev) for r in range(3, heads_size)]
    portions = kernel_call(
        split_kernel,
        "split_values",
        tuple(shape((features, count)) for _, _, count in cuts),
        grid_spec=pltpu.PrefetchScalarGridSpec(
            num_scalar_prefetch=1,
            grid=(1,),
            in_specs=[
                pl.BlockSpec((count, features), lambda i, m, r=r, at=first // count: (at, m[0] ^ r))
                for r, first, count in cuts
            ],
            out_specs=[whole((features, count)) for _, _, count in cuts],
        ),
    )(me1, *[values] * len(cuts))
    portion = {(r, first): array for (r, first, _), array in zip(cuts, portions)}
    value_head = swap(tie(portion[2, 0], *got_fades), "head", 2)

    pieces = [[] for _ in range(heads_size)]
    for i, (r, _, count) in enumerate(cuts):
        pieces[r].append((i, 0, count))
    fades, fade_specs = [], []
    for r in range(heads_size):
        if r == 0:
            fades.append(own_fade)
            fade_specs.append(whole(own_fade.shape))
        else:
            fades.append(sides if r % 2 else got_fades[r // 2 - 1])
            fade_specs.append(part(fades[-1], r // 2 if r % 2 else 0))
    keep, send = kernel_call(
        lambda me_ref, *refs: partial_state_kernel(pieces, *refs),
        "partial_states",
        (shape((half, features, state_size), F32), shape((half, features, state_size))),
        grid_spec=pltpu.PrefetchScalarGridSpec(
            num_scalar_prefetch=1,
            grid=(1,),
            in_specs=[whole(array.shape) for array in portions]
            + fade_specs
            + [pl.BlockSpec((rows_dev, state_size), lambda i, m: (m[0], 0))],
            out_specs=[whole((half, features, state_size))] * 2,
            scratch_shapes=[pltpu.VMEM((features, rows_dev), BF16)],
        ),
    )(me1, *portions, *fades, state_in)

    def core_sum(keep, send):
        got = swap(send, "head", 1)
        far = kernel_call(
            fold_kernel,
            "fold",
            tuple([shape((features, state_size))] * (half - 1)),
            in_specs=[part(keep, i) for i in range(1, half)] * 2,
            out_specs=tuple([whole((features, state_size))] * (half - 1)),
            grid=(1,),
        )(*[keep] * (half - 1), *[got] * (half - 1))
        return got, far

    core_states, far_states = fenced(core_sum, keep, send)

    merge_count = len(merge_rows(stretches))
    grouped = (heads_size, head_count, rows_dev)
    pair_rows = max(per_group // 2, 1) * state_size

    def step(bit, running, total, offset, got):
        last = bit + 1 == near
        shapes = [shape((extra, LANES), F32)] * 3 + [shape((features + extra, state_size))]
        running_shape = shape((features, state_size), F32)
        results = kernel_call(
            functools.partial(merge_kernel, bit, head_count),
            "merge",
            tuple(shapes if last else shapes + [running_shape]),
            in_specs=[smem] + [vmem] * 4,
            scratch_shapes=[pltpu.VMEM((features, state_size), F32)] if last else [],
        )(place1, running, total, offset, got)
        return list(results) + [None] * last

    def chip_sum(
        keep, core_states, far_states, total, decays, level_class, level_table, state_in, state_out,
        second, crossing,
    ):
        got_states, latest = [], []
        for i, far in enumerate(far_states):
            latest = [swap(tie(far, *latest), "head", 2 * (i + 1))]
            got_states += latest
        moved, after = [], []
        for array in crossing:
            moved.append(swap(tie(array, *after), "head", 1))
            after = moved[-1:]
        if moved:
            moved[0] = jnp.concatenate([second, moved[0]], axis=1)
        table = jnp.transpose(level_table, (1, 2, 0))
        table = jnp.pad(table, ((0, 0), (0, padded - head_count), (0, 0)))
        tables = kernel_call(
            functools.partial(factors_kernel, levels, heads_size),
            "factors",
            (
                shape(grouped, F32),
                shape((local + 1,) + grouped, F32),
                shape((ctx_bits,) + grouped, F32),
                shape((merge_count, head_count, LANES), F32),
                shape((heads_size, 2, rows_dev, rows_dev)),
                shape((heads_size, rows_dev, per_group * state_size)),
                shape((heads_size, 2 * state_size, rows_dev)),
                shape((heads_size, pair_rows, rows_dev)),
            ),
        )(
            decays,
            level_class.reshape(1, tokens),
            table.reshape(levels * padded, classes),
            state_in,
            state_out,
        )
        got_states[-1] = tie(got_states[-1], tables[0], *moved)
        running, sent = kernel_call(
            first_kernel,
            "first_state",
            (shape((features, state_size), F32), shape((features + extra, state_size))),
            grid=(1,),
            in_specs=[part(keep, 0), part(core_states, 0), whole(total.shape)]
            + [whole((features, state_size))] * len(got_states),
            out_specs=(whole((features, state_size)), whole((features + extra, state_size))),
        )(keep, core_states, total, *got_states)
        return running, sent, tables, moved

    def near_steps(running, total, sent):
        offset = jnp.zeros((extra, LANES), F32)
        factors = [jnp.broadcast_to((position % 2).astype(F32), (extra, LANES))]
        states = []
        for bit in range(near):
            states.append(swap(sent, "ctx", 2**bit))
            total, offset, factor, sent, running = step(bit, running, total, offset, states[-1])
            factors.append(factor)
        return states, factors, sent

    running, sent, tables, moved = fenced(
        chip_sum, keep, core_states, tie(far_states, value_head), total, decays, level_class,
        level_table, state_in, state_out, portion[2, early],
        [portion[r, 0] for r in range(3, heads_size, 2)],
    )
    passed, after = {}, []
    for i, array in enumerate(moved):
        passed[2 * i + 3] = swap(tie(array, *after), "head", 2 * i + 2)
        after = [passed[2 * i + 3]]
    for r in range(4, heads_size, 2):
        passed[r] = swap(tie(portion[r, 0], *after), "head", r)
        after = [passed[r]]
    states, factors, sent = fenced(near_steps, running, total, sent)
    states = list(states)
    sent = tie(sent, *[held[2**bit] for bit in range(ctx_bits)])
    last_state = swap(sent, "ctx", 2**near)

    for r in range(2, ctx_size):
        low = r & -r
        if r not in held and low > 1:
            held[r] = swap(tie(held[r ^ low], sent), "ctx", low)
    for bit in range(2, ctx_bits):
        held[2**bit + 1] = swap(tie(held[2**bit], sent), "ctx", 1)
    for r in (0, 1):
        partners[r] = swap(tie(held[r], sent), "head", 1)

    skips = jnp.broadcast_to(skip_gain[:, None], (head_count, rows_dev))
    gains = norm_gain[:, None]

    lift, read, cross, merge, scores, masked, readers, pairs = tables
    arrays = [portion[0, 0], swap(tie(portion[1, 0], sent), "head", 1), value_head]
    pieces = [[(0, 0, rows_dev)], [(1, 0, rows_dev)], [(2, 0, early)]]
    for r in range(3, heads_size):
        first = rows_dev - early if r == 3 else 0
        if r == 3:
            pieces[2].append((len(arrays), 0, first))
        pieces.append([(len(arrays), first, rows_dev)])
        arrays.append(passed[r])
    pre = kernel_call(
        functools.partial(local_kernel, near, pieces),
        "local_levels",
        shape((heads_size, features, rows_dev), F32),
        in_specs=[smem] + [vmem] * (len(arrays) + 9 + 2 * near),
        scratch_shapes=[
            pltpu.VMEM((features, rows_dev), BF16),
            pltpu.VMEM((max(local, 1), features, state_size), F32),
            pltpu.VMEM((max(local, 1), features, 2 * state_size), BF16),
            pltpu.VMEM((features, pair_rows), BF16),
            pltpu.VMEM((heads_size, features, per_group * state_size), F32),
        ],
    )(
        me1, *arrays, lift, read, merge, scores, masked, readers, pairs, skips, cross,
        *factors[:near], *states,
    )
    *kept, sides = kernel_call(
        functools.partial(finish_kernel, half),
        "finish",
        tuple([shape((features, rows_dev))] * half + [shape((half, features, rows_dev))]),
        grid=(1,),
        in_specs=[
            smem,
            whole(pre.shape),
            whole(readers.shape),
            part(cross, near),
            whole((extra, LANES)),
            whole((features + extra, state_size)),
            whole((features, 1)),
        ],
        out_specs=[whole((features, rows_dev))] * half + [whole((half, features, rows_dev))],
    )(me1, pre, readers, cross, factors[near], last_state, gains)
    done = [held[r] for r in held if r not in (0, 1)] + [kept[0]]
    early_blocks = sorted(held)
    held[3] = swap(tie(held[1], *done), "ctx", 2)
    for r in range(5, ctx_size, 2):
        if r not in held:
            held[r] = swap(tie(held[r ^ 1], *done), "ctx", 1)

    order = sorted(early_blocks, key=lambda r: (r // 2 * 2 not in early_blocks or r ^ 1 not in early_blocks, r))
    order += [r for r in range(ctx_size) if r not in early_blocks]
    count = 2
    groups = [order[first : first + count] for first in range(0, ctx_size, count)]
    others = swap(sides, "head", 1)

    def project(name, first, kept, others, group, blocks, partners, kind):
        rows = len(kept)
        return kernel_call(
            project_kernel,
            name,
            shape((rows, count * columns, rows_dev), kind),
            in_specs=[whole((features, rows_dev))] * rows
            + [part(others, first + i) for i in range(rows)]
            + [whole((columns, features))] * (2 * count),
            out_specs=whole((rows, count * columns, rows_dev)),
            grid=(1,),
        )(*kept, *[others] * rows, *[blocks[r] for r in group], *[partners[r] for r in group])

    def far_rows(group, kept, others, blocks, partners):
        return project("project_far", 1, kept[1:], others, group, blocks, partners, BF16)

    def own_rows(group, kept, others, blocks, partners):
        return project("project_own", 0, kept[:1], others, group, blocks, partners, F32)[0]

    def send_rows(far, *after):
        far = tie(far, *after)
        return [swap(far[i - 1], "head", 2 * i) for i in range(1, half)]

    def with_partners(blocks, partners):
        more = {r: swap(blocks[r], "head", 1) for r in blocks if r not in partners}
        return {**partners, **more}, more

    def first_groups(kept, others, blocks, partners):
        partners, more = with_partners(blocks, partners)
        got = send_rows(far_rows(groups[0], kept, others, blocks, partners))
        return far_rows(groups[1], kept, others, blocks, partners), got, more

    def middle_group(index):
        def body(far, kept, others, blocks, partners):
            partners, more = with_partners(blocks, partners)
            return far_rows(groups[index], kept, others, blocks, partners), send_rows(far), more

        return body

    def last_group(kept, others, blocks, partners):
        partners, more = with_partners(blocks, partners)
        return far_rows(groups[-1], kept, others, blocks, partners), more

    def some(array, group):
        return {r: array[r] for r in group if r in array}

    arrived = []
    far, got, more = fenced(
        first_groups, kept, others, some(held, groups[0] + groups[1]), some(partners, groups[0] + groups[1])
    )
    arrived.append(got)
    partners.update(more)
    for index in range(2, len(groups) - 1):
        far, got, more = fenced(
            middle_group(index), far, kept, others, some(held, groups[index]), some(partners, groups[index])
        )
        arrived.append(got)
        partners.update(more)
    got = send_rows(far, *[held[r] for r in groups[-1]])
    arrived.append(got)
    ahead = own_rows(groups[0], [tie(kept[0], far)], others, held, partners)
    blocks = some(held, groups[-1])
    blocks[groups[-1][0]] = tie(blocks[groups[-1][0]], ahead)
    far, more = fenced(last_group, kept, others, blocks, some(partners, groups[-1]))
    partners.update(more)
    arrived.append(send_rows(far, *got))
    pieces = []
    for group, got in zip(groups, arrived):
        own = ahead if group == groups[0] else own_rows(group, kept, others, held, partners)
        pieces += [own] + got
    return kernel_call(
        functools.partial(assemble_kernel, groups),
        "assemble",
        shape((rows_dev, ctx_size * columns)),
        in_specs=[smem] + [vmem] * len(pieces),
        scratch_shapes=[pltpu.VMEM((ctx_size * columns, rows_dev), F32)],
    )(place1, *pieces)


def solution(mesh):
    return jax.shard_map(
        on_device,
        mesh=mesh,
        in_specs=(
            P(("ctx", "head"), None),
            P("ctx", None),
            P("ctx", None),
            P("ctx", "head"),
            P("ctx"),
            P(None, None, "head"),
            P("head"),
            P("head"),
            P("head", "ctx"),
        ),
        out_specs=P(("ctx", "head"), None),
        check_vma=False,
    )
```

```python
import functools

import jax
import jax.numpy as jnp
from jax import lax
from jax.experimental import pallas as pl
from jax.experimental.pallas import tpu as pltpu
from jax.sharding import PartitionSpec as P

CH = 64
EPSILON = 1e-05
LANES = 128
F32 = jnp.float32
BF16 = jnp.bfloat16
VMEM_LIMIT = 40 * 1024 * 1024


def dot(a, b):
    return lax.dot_general(a, b, (((1,), (0,)), ((), ())), preferred_element_type=F32)


def dot_nt(a, b):
    return lax.dot_general(a, b, (((1,), (1,)), ((), ())), preferred_element_type=F32)


def swap(value, axis, distance):
    pairs = [(source, source ^ distance) for source in range(lax.axis_size(axis))]
    return lax.ppermute(value, axis, pairs)


def tie(value, *after):
    return lax.optimization_barrier((value,) + after)[0]


def three_parts(x):
    high = x.astype(BF16)
    rest = x - high.astype(F32)
    middle = rest.astype(BF16)
    low = (rest - middle.astype(F32)).astype(BF16)
    return high, middle, low


def two_parts(x):
    high = x.astype(BF16)
    return high, (x - high.astype(F32)).astype(BF16)


def merge_rows(stretches):
    rows = [("own", c, 0) for c in range(stretches - 1)]
    for c in range(stretches - 1):
        k = 0
        while (c >> k) & 1:
            rows.append(("merge", c, k))
            k += 1
    return rows


def head_rows(head, width):
    return slice(head * width, (head + 1) * width)


def exact_dot(x, ones):
    return sum(dot(part, ones) for part in three_parts(x))


def split_kernel(me_ref, *refs):
    half = len(refs) // 2
    for value_ref, part_ref in zip(refs[:half], refs[half:]):
        part_ref[...] = jnp.transpose(value_ref[...])


def fade_kernel(blocks, me_ref, decay_ref, own_ref, side_ref, *refs):
    far_refs, total_ref = refs[:-1], refs[-1]
    head_count, tokens = decay_ref.shape
    rows = tokens // blocks
    row = lax.broadcasted_iota(jnp.int32, (rows, rows), 0)
    col = lax.broadcasted_iota(jnp.int32, (rows, rows), 1)
    later = jnp.where(row > col, 1.0, 0.0).astype(BF16)
    me = me_ref[0]
    after = jnp.zeros((head_count, 1), F32)
    for block in reversed(range(blocks)):
        decay = decay_ref[:, block * rows : (block + 1) * rows]
        left = exact_dot(decay, later)
        fade = jnp.exp(left + after)
        after = after + left[:, 0:1] + decay[:, 0:1]
        own_index = me ^ block

        @pl.when(own_index == 0)
        def _():
            own_ref[...] = fade

        @pl.when(own_index == 1)
        def _():
            side_ref[...] = fade

        for i, far_ref in enumerate(far_refs):
            for j in range(2):

                @pl.when(own_index == 2 * (i + 1) + j)
                def _():
                    far_ref[j] = fade

    total_ref[...] = jnp.zeros_like(total_ref)
    total_ref[:head_count, :] = jnp.broadcast_to(after, (head_count, LANES))


def pack_kernel(*refs):
    side_ref, *got_refs, out_ref = refs
    out_ref[0] = side_ref[...]
    for i, got_ref in enumerate(got_refs):
        out_ref[i + 1] = got_ref[0]


def factors_kernel(
    levels, blocks, decay_ref, class_ref, table_ref, in_ref, out_ref,
    lift_ref, read_ref, cross_ref, merge_ref, score_ref, masked_ref, reader_ref, pair_ref,
):
    head_count, tokens = decay_ref.shape
    stretches = tokens // CH
    rows = tokens // blocks
    per_block = rows // CH
    local = read_ref.shape[0] - 1
    state_size = in_ref.shape[1]
    padded = table_ref.shape[0] // levels
    classes = table_ref.shape[1]
    row = lax.broadcasted_iota(jnp.int32, (rows, rows), 0)
    col = lax.broadcasted_iota(jnp.int32, (rows, rows), 1)
    inside = (row // CH == col // CH) & (row <= col)
    upto = jnp.where(inside, 1.0, 0.0).astype(BF16)
    within, starts = [], [jnp.zeros((head_count, 1), F32)]
    for g in range(blocks):
        within.append(exact_dot(decay_ref[:, g * rows : (g + 1) * rows], upto))
        for s in range(per_block):
            last = (s + 1) * CH
            starts.append(starts[-1] + within[-1][:, last - 1 : last])
    class_row = lax.broadcasted_iota(jnp.int32, (classes, rows), 0)
    lane = lax.broadcasted_iota(jnp.int32, (head_count, rows), 1) // CH
    token = lax.broadcasted_iota(jnp.int32, (rows, state_size), 0) // CH

    def by_stretch(columns):
        spread = jnp.broadcast_to(columns[0], (head_count, rows))
        for s in range(1, per_block):
            spread = jnp.where(lane == s, columns[s], spread)
        return spread

    for g in range(blocks):
        at = slice(g * rows, (g + 1) * rows)
        onehot = jnp.where(class_ref[:, at] == class_row, 1.0, 0.0).astype(BF16)
        weights = sum(dot(part, onehot) for part in three_parts(table_ref[...]))
        weight = lambda level: weights[level * padded : level * padded + head_count, :]
        lift_ref[g] = jnp.exp(-within[g])
        read_ref[0, g] = jnp.exp(within[g]) * weight(0)
        first = g * per_block
        for level in range(1, local + 1):
            begins, active = [], []
            for c in range(first, first + per_block):
                upper = (c >> (level - 1)) & 1
                begins.append(starts[c] - starts[(c >> (level - 1)) << (level - 1)])
                active.append(jnp.full((head_count, 1), float(upper), F32))
            factor = jnp.exp(within[g] + by_stretch(begins)) * weight(level)
            read_ref[level, g] = factor * by_stretch(active)
        far = jnp.exp(within[g] + by_stretch(starts[first : first + per_block]))
        for level in range(local + 1, levels):
            cross_ref[level - local - 1, g] = far * weight(level)
        own_in, own_out = in_ref[at, :], out_ref[at, :]
        scores = jnp.where(inside, dot_nt(own_in, own_out), 0.0)
        score_ref[g, 0], score_ref[g, 1] = two_parts(scores)
        for s in range(per_block):
            masked = jnp.where(token == s, own_in.astype(F32), 0.0).astype(BF16)
            masked_ref[g, :, s * state_size : (s + 1) * state_size] = masked
        turned = jnp.transpose(own_out.astype(F32))
        reader = turned.astype(BF16)
        reader_ref[g, :state_size, :] = reader
        reader_ref[g, state_size:, :] = reader
        pairs = max(per_block // 2, 1)
        place = lax.broadcasted_iota(jnp.int32, (state_size, rows), 1) // (2 * CH)
        for j in range(pairs):
            alone = jnp.where(place == j, turned, 0.0).astype(BF16)
            pair_ref[g, j * state_size : (j + 1) * state_size, :] = alone
    for i, (kind, c, k) in enumerate(merge_rows(stretches)):
        first = c if kind == "own" else c + 1 - 2**k
        merge_ref[i] = jnp.broadcast_to(jnp.exp(starts[c + 1] - starts[first]), (head_count, LANES))


def load(refs, pieces, at):
    parts = [refs[i][at, first : first + count] for i, first, count in pieces]
    return parts[0] if len(parts) == 1 else jnp.concatenate(parts, axis=1)


def partial_state_kernel(pieces, *refs):
    count = len(pieces)
    arrays = sum(len(parts) for parts in pieces)
    value_refs, refs = refs[:arrays], refs[arrays:]
    fade_refs, (in_ref, keep_ref, send_ref, faded) = refs[:count], refs[count:]
    own_in = in_ref[...]
    for r in [*range(1, count, 2), *range(0, count, 2)]:
        fade = fade_refs[r][...].reshape(fade_refs[r].shape[-2:])
        head_count = fade.shape[0]
        width = value_refs[0].shape[0] // head_count
        for h in range(head_count):
            at = head_rows(h, width)
            value = load(value_refs, pieces[r], at).astype(F32)
            faded[at, :] = (fade[h : h + 1, :] * value).astype(BF16)
        state = dot(faded[...], own_in)
        if r % 2 == 1:
            send_ref[r // 2] = state.astype(BF16)
        else:
            keep_ref[r // 2] = state


def fold_kernel(*refs):
    count = len(refs) // 3
    for keep_ref, got_ref, far_ref in zip(refs[:count], refs[count : 2 * count], refs[2 * count :]):
        far_ref[...] = (keep_ref[0] + got_ref[0].astype(F32)).astype(BF16)


def pack_state(sent_ref, state, total):
    channels = state.shape[0]
    sent_ref[:channels, :] = state.astype(BF16)
    high, middle, low = (part.astype(F32) for part in three_parts(total))
    lane = lax.broadcasted_iota(jnp.int32, total.shape, 1)
    parts = jnp.where(lane < LANES // 4, high, jnp.where(lane < LANES // 2, middle, low))
    sent_ref[channels:, :] = parts.astype(BF16)


def first_kernel(own_ref, core_ref, total_ref, *refs):
    *far_refs, running_ref, sent_ref = refs
    running = own_ref[0] + core_ref[0].astype(F32)
    for far_ref in far_refs:
        running = running + far_ref[...].astype(F32)
    running_ref[...] = running
    pack_state(sent_ref, running, total_ref[...])


def merge_kernel(
    bit, head_count, place_ref, running_ref, total_ref, offset_ref, got_ref,
    next_total_ref, next_offset_ref, factor_ref, sent_ref, next_running_ref,
):
    channels = running_ref.shape[0]
    width = channels // head_count
    place = place_ref[0]
    upper = place // 2**bit % 2 == 1
    total = total_ref[...]
    parts = got_ref[channels:, :].astype(F32)
    middle, low = LANES // 4, LANES // 2
    partner = parts[:, 0:1] + parts[:, middle : middle + 1] + parts[:, low : low + 1]
    partner = jnp.broadcast_to(partner, total.shape)
    fading = jnp.exp(jnp.where(upper, total, partner))
    for h in range(head_count):
        at = head_rows(h, width)
        got, running = got_ref[at, :].astype(F32), running_ref[at, :]
        lower, higher = jnp.where(upper, got, running), jnp.where(upper, running, got)
        next_running_ref[at, :] = fading[h : h + 1, :] * lower + higher
    joined = total + partner
    next_total_ref[...] = joined
    offset = jnp.where(upper, offset_ref[...] + partner, offset_ref[...])
    next_offset_ref[...] = offset
    next_upper = place // 2 ** (bit + 1) % 2 == 1
    factor_ref[...] = jnp.where(next_upper, jnp.exp(offset), 0.0)
    pack_state(sent_ref, next_running_ref[...], joined)


def local_kernel(near, pieces, me_ref, *refs):
    groups = refs[-1].shape[0]
    arrays = 1 + max(i for parts in pieces for i, _, _ in parts)
    value_refs, refs = refs[:arrays], refs[arrays:]
    lift_ref, read_ref, merge_ref, score_ref, masked_ref, reader_ref, pair_ref = refs[:7]
    skip_ref, cross_ref, *refs = refs[7:]
    factor_refs, state_refs, refs = refs[:near], refs[near : 2 * near], refs[2 * near :]
    pre_ref, lifted, sums, operand, pairs_ref, nodes = refs
    channels, group_rows = value_refs[0].shape
    assert len(pieces) == groups
    head_count = lift_ref.shape[1]
    width = channels // head_count
    me = me_ref[0]
    per_group = group_rows // CH
    stretches = groups * per_group
    state_size = reader_ref.shape[1] // 2
    place = {kind: i for i, kind in enumerate(merge_rows(stretches))}
    heads = [(h, head_rows(h, width)) for h in range(head_count)]
    for r in range(groups):
        g = me ^ r
        lift = lift_ref[g]
        for h, at in heads:
            value = load(value_refs, pieces[r], at).astype(F32)
            lifted[at, :] = (lift[h : h + 1, :] * value).astype(BF16)
        direct = dot(lifted[...], score_ref[g, 0]) + dot(lifted[...], score_ref[g, 1])
        read = read_ref[0, g]
        terms = []
        for level, (state_ref, factor_ref) in enumerate(zip(state_refs, factor_refs)):
            gained = dot(state_ref[:channels, :], reader_ref[g, :state_size, :])
            scale = cross_ref[level, g] * factor_ref[:head_count, 0:1]
            terms.append((scale, gained))
        for h, at in heads:
            total = read[h : h + 1, :] * direct[at, :]
            total = total + skip_ref[h : h + 1, :] * load(value_refs, pieces[r], at).astype(F32)
            for scale, gained in terms:
                total = total + scale[h : h + 1, :] * gained[at, :]
            pre_ref[g, at, :] = total
        nodes[g] = dot(lifted[...], masked_ref[g])

    for g in range(groups):
        terms = []
        level = per_group.bit_length()
        while 2 ** (level - 1) < stretches:
            if (g * per_group >> (level - 1)) & 1:
                terms.append((read_ref[level, g], dot(operand[level - 1], reader_ref[g])))
            level += 1
        for s in range(per_group):
            c = g * per_group + s
            if c + 1 == stretches:
                break
            merges = [merge_ref[place["own", c, 0]]]
            k = 0
            while (c >> k) & 1:
                merges.append(merge_ref[place["merge", c, k]])
                k += 1
            for h, at in heads:
                node = nodes[g, at, s * state_size : (s + 1) * state_size]
                node = node * merges[0][h : h + 1, :]
                for i, merge in enumerate(merges[1:]):
                    node = node + merge[h : h + 1, :] * sums[i, at, :]
                sums[k, at, :] = node
                high, low = two_parts(node)
                if k == 0 and per_group > 1:
                    pairs_ref[at, s // 2 * state_size : (s // 2 + 1) * state_size] = high
                else:
                    operand[k, at, :state_size] = high
                    operand[k, at, state_size:] = low
            if 1 <= k < per_group.bit_length() - 1:
                scale = read_ref[k + 1, g]
                lane = lax.broadcasted_iota(jnp.int32, scale.shape, 1) // (CH << (k + 1))
                scale = jnp.where(lane == s >> (k + 1), scale, 0.0)
                terms.append((scale, dot(operand[k], reader_ref[g])))
        if per_group > 1:
            terms.append((read_ref[1, g], dot(pairs_ref[...], pair_ref[g])))
        for h, at in heads:
            total = pre_ref[g, at, :]
            for scale, gained in terms:
                total = total + scale[h : h + 1, :] * gained[at, :]
            pre_ref[g, at, :] = total


def finish_kernel(
    half, me_ref, pre_ref, reader_ref, cross_ref, factor_ref, state_ref, gain_ref, *refs
):
    keep_refs, send_refs = refs[:half], refs[half:]
    groups, channels, _ = pre_ref.shape
    head_count = cross_ref.shape[2]
    width = channels // head_count
    state_size = reader_ref.shape[1] // 2
    me = me_ref[0]
    state = state_ref[:channels, :]
    for r in range(groups):
        g = me ^ r
        gained = dot(state, reader_ref[g, :state_size, :])
        scale = cross_ref[0, g] * factor_ref[:head_count, 0:1]
        for h in range(head_count):
            at = head_rows(h, width)
            total = pre_ref[g, at, :] + scale[h : h + 1, :] * gained[at, :]
            mean_square = jnp.sum(total * total, axis=0, keepdims=True) * (1.0 / width)
            normed = total * lax.rsqrt(mean_square + EPSILON) * gain_ref[at, 0:1]
            if r % 2 == 0:
                keep_refs[r // 2][at, :] = normed.astype(BF16)
            else:
                send_refs[r // 2][at, :] = normed.astype(BF16)


def project_kernel(*refs):
    *refs, out_ref = refs
    rows = out_ref.shape[0]
    kept_refs, other_refs, refs = refs[:rows], refs[rows : 2 * rows], refs[2 * rows :]
    count = len(refs) // 2
    weights, partners = refs[:count], refs[count:]
    width = weights[0].shape[0]
    for i, (kept_ref, other_ref) in enumerate(zip(kept_refs, other_refs)):
        for j, (weight, partner) in enumerate(zip(weights, partners)):
            found = dot(weight[...], kept_ref[...]) + dot(partner[...], other_ref[...])
            out_ref[i, j * width : (j + 1) * width, :] = found.astype(out_ref.dtype)


def assemble_kernel(groups, place_ref, *refs):
    *refs, out_ref, columns_ref = refs
    each = len(refs) // len(groups)
    for g, group in enumerate(groups):
        own_ref, *far_refs = refs[g * each : (g + 1) * each]
        width = own_ref.shape[0] // len(group)
        for j, r in enumerate(group):
            rows = slice(j * width, (j + 1) * width)
            total = own_ref[rows, :]
            for far_ref in far_refs:
                total = total + far_ref[rows, :].astype(F32)
            start = pl.multiple_of((place_ref[0] ^ r) * width, width)
            columns_ref[pl.ds(start, width), :] = total
    for first in range(0, out_ref.shape[1], LANES):
        at = slice(first, first + LANES)
        out_ref[:, at] = jnp.transpose(columns_ref[at, :]).astype(BF16)


def whole(shape):
    return pl.BlockSpec(shape, lambda *_: (0,) * len(shape))


def on_device(
    values,
    state_in,
    state_out,
    log_decay,
    level_class,
    level_table,
    skip_gain,
    norm_gain,
    out_weight,
):
    heads_size = lax.axis_size("head")
    ctx_size = lax.axis_size("ctx")
    ctx_bits = ctx_size.bit_length() - 1
    me = lax.axis_index("head")
    me1 = me.reshape(1).astype(jnp.int32)
    position = lax.axis_index("ctx")
    place1 = position.reshape(1).astype(jnp.int32)
    tokens = state_in.shape[0]
    rows_dev = values.shape[0]
    head_count = log_decay.shape[1]
    features = values.shape[1] // heads_size
    state_size = state_in.shape[1]
    columns = out_weight.shape[1]
    stretches = tokens // CH
    per_group = rows_dev // CH
    local = stretches.bit_length() - 1
    levels = level_table.shape[1]
    classes = level_table.shape[0]
    extra = -(-head_count // 16) * 16
    padded = -(-head_count // 8) * 8
    half = heads_size // 2
    near = ctx_bits - 1
    params = pltpu.CompilerParams(vmem_limit_bytes=VMEM_LIMIT)
    cheap = pl.CostEstimate(flops=0, bytes_accessed=0, transcendentals=0)
    smem = pl.BlockSpec(memory_space=pltpu.SMEM)
    vmem = pl.BlockSpec(memory_space=pltpu.VMEM)

    def kernel_call(body, name, out_shape, **kwargs):
        return pl.pallas_call(
            body, out_shape=out_shape, compiler_params=params, cost_estimate=cheap, name=name, **kwargs
        )

    def shape(dims, kind=BF16):
        return jax.ShapeDtypeStruct(dims, kind)

    def part(array, index):
        return pl.BlockSpec((1,) + array.shape[1:], lambda *_: (index,) + (0,) * (array.ndim - 1))

    def fenced(body, *operands):
        shapes = jax.eval_shape(body, *operands)
        zeros = lambda *_: jax.tree.map(lambda leaf: jnp.zeros(leaf.shape, leaf.dtype), shapes)
        return lax.cond(position < ctx_size, body, zeros, *operands)

    held, partners = {0: out_weight.T}, {}
    for bit in range(ctx_bits):
        held[2**bit] = swap(held[0], "ctx", 2**bit)

    decays = log_decay.T
    own_fade, side_fade, *far_fades, total = kernel_call(
        functools.partial(fade_kernel, heads_size),
        "fade",
        tuple(
            [shape((head_count, rows_dev), F32)] * 2
            + [shape((2, head_count, rows_dev), F32)] * (half - 1)
            + [shape((extra, LANES), F32)]
        ),
        in_specs=[smem, vmem],
    )(me1, decays)

    got_fades = []
    for i, far in enumerate(far_fades):
        got_fades.append(swap(tie(far, *got_fades), "head", 2 * (i + 1)))
    sides = kernel_call(
        pack_kernel,
        "pack_fades",
        shape((half, head_count, rows_dev), F32),
        grid=(1,),
        in_specs=[whole(side_fade.shape)] + [part(got, 1) for got in got_fades],
        out_specs=whole((half, head_count, rows_dev)),
    )(side_fade, *got_fades)
    sides = swap(sides, "head", 1)

    early = rows_dev // 2
    cuts = [(r, first, early) for r in (2,) for first in (0, early)]
    cuts = [(0, 0, rows_dev), (1, 0, rows_dev)] + cuts
    cuts += [(r, 0, rows_dev) for r in range(3, heads_size)]
    portions = kernel_call(
        split_kernel,
        "split_values",
        tuple(shape((features, count)) for _, _, count in cuts),
        grid_spec=pltpu.PrefetchScalarGridSpec(
            num_scalar_prefetch=1,
            grid=(1,),
            in_specs=[
                pl.BlockSpec((count, features), lambda i, m, r=r, at=first // count: (at, m[0] ^ r))
                for r, first, count in cuts
            ],
            out_specs=[whole((features, count)) for _, _, count in cuts],
        ),
    )(me1, *[values] * len(cuts))
    portion = {(r, first): array for (r, first, _), array in zip(cuts, portions)}
    value_head = swap(tie(portion[2, 0], *got_fades), "head", 2)

    pieces = [[] for _ in range(heads_size)]
    for i, (r, _, count) in enumerate(cuts):
        pieces[r].append((i, 0, count))
    fades, fade_specs = [], []
    for r in range(heads_size):
        if r == 0:
            fades.append(own_fade)
            fade_specs.append(whole(own_fade.shape))
        else:
            fades.append(sides if r % 2 else got_fades[r // 2 - 1])
            fade_specs.append(part(fades[-1], r // 2 if r % 2 else 0))
    keep, send = kernel_call(
        lambda me_ref, *refs: partial_state_kernel(pieces, *refs),
        "partial_states",
        (shape((half, features, state_size), F32), shape((half, features, state_size))),
        grid_spec=pltpu.PrefetchScalarGridSpec(
            num_scalar_prefetch=1,
            grid=(1,),
            in_specs=[whole(array.shape) for array in portions]
            + fade_specs
            + [pl.BlockSpec((rows_dev, state_size), lambda i, m: (m[0], 0))],
            out_specs=[whole((half, features, state_size))] * 2,
            scratch_shapes=[pltpu.VMEM((features, rows_dev), BF16)],
        ),
    )(me1, *portions, *fades, state_in)

    def core_sum(keep, send):
        got = swap(send, "head", 1)
        far = kernel_call(
            fold_kernel,
            "fold",
            tuple([shape((features, state_size))] * (half - 1)),
            in_specs=[part(keep, i) for i in range(1, half)] * 2,
            out_specs=tuple([whole((features, state_size))] * (half - 1)),
            grid=(1,),
        )(*[keep] * (half - 1), *[got] * (half - 1))
        return got, far

    core_states, far_states = fenced(core_sum, keep, send)

    merge_count = len(merge_rows(stretches))
    grouped = (heads_size, head_count, rows_dev)
    pair_rows = max(per_group // 2, 1) * state_size

    def step(bit, running, total, offset, got):
        last = bit + 1 == near
        shapes = [shape((extra, LANES), F32)] * 3 + [shape((features + extra, state_size))]
        running_shape = shape((features, state_size), F32)
        results = kernel_call(
            functools.partial(merge_kernel, bit, head_count),
            "merge",
            tuple(shapes if last else shapes + [running_shape]),
            in_specs=[smem] + [vmem] * 4,
            scratch_shapes=[pltpu.VMEM((features, state_size), F32)] if last else [],
        )(place1, running, total, offset, got)
        return list(results) + [None] * last

    def chip_sum(
        keep, core_states, far_states, total, decays, level_class, level_table, state_in, state_out,
        second, crossing,
    ):
        got_states, latest = [], []
        for i, far in enumerate(far_states):
            latest = [swap(tie(far, *latest), "head", 2 * (i + 1))]
            got_states += latest
        moved, after = [], []
        for array in crossing:
            moved.append(swap(tie(array, *after), "head", 1))
            after = moved[-1:]
        if moved:
            moved[0] = jnp.concatenate([second, moved[0]], axis=1)
        table = jnp.transpose(level_table, (1, 2, 0))
        table = jnp.pad(table, ((0, 0), (0, padded - head_count), (0, 0)))
        tables = kernel_call(
            functools.partial(factors_kernel, levels, heads_size),
            "factors",
            (
                shape(grouped, F32),
                shape((local + 1,) + grouped, F32),
                shape((ctx_bits,) + grouped, F32),
                shape((merge_count, head_count, LANES), F32),
                shape((heads_size, 2, rows_dev, rows_dev)),
                shape((heads_size, rows_dev, per_group * state_size)),
                shape((heads_size, 2 * state_size, rows_dev)),
                shape((heads_size, pair_rows, rows_dev)),
            ),
        )(
            decays,
            level_class.reshape(1, tokens),
            table.reshape(levels * padded, classes),
            state_in,
            state_out,
        )
        got_states[-1] = tie(got_states[-1], tables[0], *moved)
        running, sent = kernel_call(
            first_kernel,
            "first_state",
            (shape((features, state_size), F32), shape((features + extra, state_size))),
            grid=(1,),
            in_specs=[part(keep, 0), part(core_states, 0), whole(total.shape)]
            + [whole((features, state_size))] * len(got_states),
            out_specs=(whole((features, state_size)), whole((features + extra, state_size))),
        )(keep, core_states, total, *got_states)
        return running, sent, tables, moved

    def near_steps(running, total, sent, beside):
        beside = swap(beside, "head", 1)
        offset = jnp.zeros((extra, LANES), F32)
        factors = [jnp.broadcast_to((position % 2).astype(F32), (extra, LANES))]
        states = []
        for bit in range(near):
            states.append(swap(sent, "ctx", 2**bit))
            total, offset, factor, sent, running = step(bit, running, total, offset, states[-1])
            factors.append(factor)
        return states, factors, sent, beside

    running, sent, tables, moved = fenced(
        chip_sum, keep, core_states, tie(far_states, value_head), total, decays, level_class,
        level_table, state_in, state_out, portion[2, early],
        [portion[r, 0] for r in range(3, heads_size, 2)],
    )
    passed, after = {}, []
    for i, array in enumerate(moved):
        passed[2 * i + 3] = swap(tie(array, *after), "head", 2 * i + 2)
        after = [passed[2 * i + 3]]
    for r in range(4, heads_size, 2):
        passed[r] = swap(tie(portion[r, 0], *after), "head", r)
        after = [passed[r]]
    sent = tie(sent, held[1])
    states, factors, sent, beside = fenced(near_steps, running, total, sent, portion[1, 0])
    states = list(states)
    sent = tie(sent, *[held[2**bit] for bit in range(ctx_bits)])
    last_state = swap(sent, "ctx", 2**near)

    for r in range(2, ctx_size):
        low = r & -r
        if r not in held and low > 1:
            held[r] = swap(tie(held[r ^ low], sent), "ctx", low)
    for bit in range(2, ctx_bits):
        held[2**bit + 1] = swap(tie(held[2**bit], sent), "ctx", 1)
    partners[0] = swap(tie(held[0], sent), "head", 1)

    skips = jnp.broadcast_to(skip_gain[:, None], (head_count, rows_dev))
    gains = norm_gain[:, None]

    lift, read, cross, merge, scores, masked, readers, pairs = tables
    arrays = [portion[0, 0], beside, value_head]
    pieces = [[(0, 0, rows_dev)], [(1, 0, rows_dev)], [(2, 0, early)]]
    for r in range(3, heads_size):
        first = rows_dev - early if r == 3 else 0
        if r == 3:
            pieces[2].append((len(arrays), 0, first))
        pieces.append([(len(arrays), first, rows_dev)])
        arrays.append(passed[r])
    pre = kernel_call(
        functools.partial(local_kernel, near, pieces),
        "local_levels",
        shape((heads_size, features, rows_dev), F32),
        in_specs=[smem] + [vmem] * (len(arrays) + 9 + 2 * near),
        scratch_shapes=[
            pltpu.VMEM((features, rows_dev), BF16),
            pltpu.VMEM((max(local, 1), features, state_size), F32),
            pltpu.VMEM((max(local, 1), features, 2 * state_size), BF16),
            pltpu.VMEM((features, pair_rows), BF16),
            pltpu.VMEM((heads_size, features, per_group * state_size), F32),
        ],
    )(
        me1, *arrays, lift, read, merge, scores, masked, readers, pairs, skips, cross,
        *factors[:near], *states,
    )
    normed = kernel_call(
        functools.partial(finish_kernel, half),
        "finish",
        tuple([shape((features, rows_dev))] * heads_size),
        grid=(1,),
        in_specs=[
            smem,
            whole(pre.shape),
            whole(readers.shape),
            part(cross, near),
            whole((extra, LANES)),
            whole((features + extra, state_size)),
            whole((features, 1)),
        ],
        out_specs=[whole((features, rows_dev))] * heads_size,
    )(me1, pre, readers, cross, factors[near], last_state, gains)
    kept, sides = normed[:half], normed[half:]
    early_blocks = sorted(held)
    order = sorted(early_blocks, key=lambda r: (r // 2 * 2 not in early_blocks or r ^ 1 not in early_blocks, r))
    order += [r for r in range(ctx_size) if r not in early_blocks]
    count = 2
    groups = [order[first : first + count] for first in range(0, ctx_size, count)]
    others = [swap(side, "head", 1) for side in sides[1:]]

    def project(name, kept, others, group, blocks, partners, kind):
        rows = len(kept)
        return kernel_call(
            project_kernel,
            name,
            shape((rows, count * columns, rows_dev), kind),
            in_specs=[vmem] * (2 * rows + 2 * count),
        )(*kept, *others, *[blocks[r] for r in group], *[partners[r] for r in group])

    def far_rows(group, kept, others, blocks, partners):
        return project("project_far", kept[1:], others, group, blocks, partners, BF16)

    def own_rows(group, kept, others, blocks, partners):
        return project("project_own", kept[:1], others, group, blocks, partners, F32)[0]

    def send_rows(far, *after):
        far = tie(far, *after)
        return [swap(far[i - 1], "head", 2 * i) for i in range(1, half)]

    def with_partners(blocks, partners):
        more = {r: swap(blocks[r], "head", 1) for r in blocks if r not in partners}
        return {**partners, **more}, more

    def group_of(index):
        def body(kept, others, blocks, partners):
            partners, more = with_partners(blocks, partners)
            return far_rows(groups[index], kept, others, blocks, partners), more

        return body

    def some(array, group):
        return {r: array[r] for r in group if r in array}

    arrived, owns = [], {}
    for index, group in enumerate(groups):
        last = index + 1 == len(groups)
        blocks = some(held, group)
        if last:
            owns[0] = own_rows(groups[0], [tie(kept[0], far)], [own_other], held, partners)
            blocks[group[0]] = tie(blocks[group[0]], owns[0])
        far, more = fenced(group_of(index), kept, others, blocks, some(partners, group))
        partners.update(more)
        after = list(arrived[-1]) if arrived else []
        if index + 2 == len(groups):
            after += [held[r] for r in groups[-1]]
        arrived.append(send_rows(far, *after))
        if index == 0:
            ready = [held[r] for r in held if r not in (0, 1)] + [far]
            held[3] = swap(tie(held[1], *ready), "ctx", 2)
            for r in range(5, ctx_size, 2):
                if r not in held:
                    held[r] = swap(tie(held[r ^ 1], *ready), "ctx", 1)
            own_other = swap(tie(sides[0], far), "head", 1)
    pieces = []
    for index, (group, got) in enumerate(zip(groups, arrived)):
        if index not in owns:
            owns[index] = own_rows(group, kept, [own_other], held, partners)
        pieces += [owns[index]] + got
    return kernel_call(
        functools.partial(assemble_kernel, groups),
        "assemble",
        shape((rows_dev, ctx_size * columns)),
        in_specs=[smem] + [vmem] * len(pieces),
        scratch_shapes=[pltpu.VMEM((ctx_size * columns, rows_dev), F32)],
    )(place1, *pieces)


def solution(mesh):
    return jax.shard_map(
        on_device,
        mesh=mesh,
        in_specs=(
            P(("ctx", "head"), None),
            P("ctx", None),
            P("ctx", None),
            P("ctx", "head"),
            P("ctx"),
            P(None, None, "head"),
            P("head"),
            P("head"),
            P("head", "ctx"),
        ),
        out_specs=P(("ctx", "head"), None),
        check_vma=False,
    )
```

```python
import functools

import jax
import jax.numpy as jnp
from jax import lax
from jax.experimental import pallas as pl
from jax.experimental.pallas import tpu as pltpu
from jax.sharding import PartitionSpec as P

CH = 64
EPSILON = 1e-05
LANES = 128
F32 = jnp.float32
BF16 = jnp.bfloat16
VMEM_LIMIT = 40 * 1024 * 1024


def dot(a, b):
    return lax.dot_general(a, b, (((1,), (0,)), ((), ())), preferred_element_type=F32)


def dot_nt(a, b):
    return lax.dot_general(a, b, (((1,), (1,)), ((), ())), preferred_element_type=F32)


def swap(value, axis, distance):
    pairs = [(source, source ^ distance) for source in range(lax.axis_size(axis))]
    return lax.ppermute(value, axis, pairs)


def tie(value, *after):
    return lax.optimization_barrier((value,) + after)[0]


def three_parts(x):
    high = x.astype(BF16)
    rest = x - high.astype(F32)
    middle = rest.astype(BF16)
    low = (rest - middle.astype(F32)).astype(BF16)
    return high, middle, low


def two_parts(x):
    high = x.astype(BF16)
    return high, (x - high.astype(F32)).astype(BF16)


def merge_rows(stretches):
    rows = [("own", c, 0) for c in range(stretches - 1)]
    for c in range(stretches - 1):
        k = 0
        while (c >> k) & 1:
            rows.append(("merge", c, k))
            k += 1
    return rows


def head_rows(head, width):
    return slice(head * width, (head + 1) * width)


def exact_dot(x, ones):
    return sum(dot(part, ones) for part in three_parts(x))


def split_kernel(me_ref, *refs):
    half = len(refs) // 2
    for value_ref, part_ref in zip(refs[:half], refs[half:]):
        part_ref[...] = jnp.transpose(value_ref[...])


def fade_kernel(blocks, me_ref, decay_ref, own_ref, side_ref, *refs):
    far_refs, total_ref = refs[:-1], refs[-1]
    head_count, tokens = decay_ref.shape
    rows = tokens // blocks
    row = lax.broadcasted_iota(jnp.int32, (rows, rows), 0)
    col = lax.broadcasted_iota(jnp.int32, (rows, rows), 1)
    later = jnp.where(row > col, 1.0, 0.0).astype(BF16)
    me = me_ref[0]
    after = jnp.zeros((head_count, 1), F32)
    for block in reversed(range(blocks)):
        decay = decay_ref[:, block * rows : (block + 1) * rows]
        left = exact_dot(decay, later)
        fade = jnp.exp(left + after)
        after = after + left[:, 0:1] + decay[:, 0:1]
        own_index = me ^ block

        @pl.when(own_index == 0)
        def _():
            own_ref[...] = fade

        @pl.when(own_index == 1)
        def _():
            side_ref[...] = fade

        for i, far_ref in enumerate(far_refs):
            for j in range(2):

                @pl.when(own_index == 2 * (i + 1) + j)
                def _():
                    far_ref[j] = fade

    total_ref[...] = jnp.zeros_like(total_ref)
    total_ref[:head_count, :] = jnp.broadcast_to(after, (head_count, LANES))


def pack_kernel(*refs):
    side_ref, *got_refs, out_ref = refs
    out_ref[0] = side_ref[...]
    for i, got_ref in enumerate(got_refs):
        out_ref[i + 1] = got_ref[0]


def factors_kernel(
    levels, blocks, decay_ref, class_ref, table_ref, in_ref, out_ref,
    lift_ref, read_ref, cross_ref, merge_ref, score_ref, masked_ref, reader_ref, pair_ref,
):
    head_count, tokens = decay_ref.shape
    stretches = tokens // CH
    rows = tokens // blocks
    per_block = rows // CH
    local = read_ref.shape[0] - 1
    state_size = in_ref.shape[1]
    padded = table_ref.shape[0] // levels
    classes = table_ref.shape[1]
    row = lax.broadcasted_iota(jnp.int32, (rows, rows), 0)
    col = lax.broadcasted_iota(jnp.int32, (rows, rows), 1)
    inside = (row // CH == col // CH) & (row <= col)
    upto = jnp.where(inside, 1.0, 0.0).astype(BF16)
    within, starts = [], [jnp.zeros((head_count, 1), F32)]
    for g in range(blocks):
        within.append(exact_dot(decay_ref[:, g * rows : (g + 1) * rows], upto))
        for s in range(per_block):
            last = (s + 1) * CH
            starts.append(starts[-1] + within[-1][:, last - 1 : last])
    class_row = lax.broadcasted_iota(jnp.int32, (classes, rows), 0)
    lane = lax.broadcasted_iota(jnp.int32, (head_count, rows), 1) // CH
    token = lax.broadcasted_iota(jnp.int32, (rows, state_size), 0) // CH

    def by_stretch(columns):
        spread = jnp.broadcast_to(columns[0], (head_count, rows))
        for s in range(1, per_block):
            spread = jnp.where(lane == s, columns[s], spread)
        return spread

    for g in range(blocks):
        at = slice(g * rows, (g + 1) * rows)
        onehot = jnp.where(class_ref[:, at] == class_row, 1.0, 0.0).astype(BF16)
        weights = sum(dot(part, onehot) for part in three_parts(table_ref[...]))
        weight = lambda level: weights[level * padded : level * padded + head_count, :]
        lift_ref[g] = jnp.exp(-within[g])
        read_ref[0, g] = jnp.exp(within[g]) * weight(0)
        first = g * per_block
        for level in range(1, local + 1):
            begins, active = [], []
            for c in range(first, first + per_block):
                upper = (c >> (level - 1)) & 1
                begins.append(starts[c] - starts[(c >> (level - 1)) << (level - 1)])
                active.append(jnp.full((head_count, 1), float(upper), F32))
            factor = jnp.exp(within[g] + by_stretch(begins)) * weight(level)
            read_ref[level, g] = factor * by_stretch(active)
        far = jnp.exp(within[g] + by_stretch(starts[first : first + per_block]))
        for level in range(local + 1, levels):
            cross_ref[level - local - 1, g] = far * weight(level)
        own_in, own_out = in_ref[at, :], out_ref[at, :]
        scores = jnp.where(inside, dot_nt(own_in, own_out), 0.0)
        score_ref[g, 0], score_ref[g, 1] = two_parts(scores)
        for s in range(per_block):
            masked = jnp.where(token == s, own_in.astype(F32), 0.0).astype(BF16)
            masked_ref[g, :, s * state_size : (s + 1) * state_size] = masked
        turned = jnp.transpose(own_out.astype(F32))
        reader = turned.astype(BF16)
        reader_ref[g, :state_size, :] = reader
        reader_ref[g, state_size:, :] = reader
        pairs = max(per_block // 2, 1)
        place = lax.broadcasted_iota(jnp.int32, (state_size, rows), 1) // (2 * CH)
        for j in range(pairs):
            alone = jnp.where(place == j, turned, 0.0).astype(BF16)
            pair_ref[g, j * state_size : (j + 1) * state_size, :] = alone
    for i, (kind, c, k) in enumerate(merge_rows(stretches)):
        first = c if kind == "own" else c + 1 - 2**k
        merge_ref[i] = jnp.broadcast_to(jnp.exp(starts[c + 1] - starts[first]), (head_count, LANES))


def load(refs, pieces, at):
    parts = [refs[i][at, first : first + count] for i, first, count in pieces]
    return parts[0] if len(parts) == 1 else jnp.concatenate(parts, axis=1)


def partial_state_kernel(pieces, *refs):
    count = len(pieces)
    arrays = sum(len(parts) for parts in pieces)
    value_refs, refs = refs[:arrays], refs[arrays:]
    fade_refs, (in_ref, keep_ref, send_ref, faded) = refs[:count], refs[count:]
    own_in = in_ref[...]
    for r in [*range(1, count, 2), *range(0, count, 2)]:
        fade = fade_refs[r][...].reshape(fade_refs[r].shape[-2:])
        head_count = fade.shape[0]
        width = value_refs[0].shape[0] // head_count
        for h in range(head_count):
            at = head_rows(h, width)
            value = load(value_refs, pieces[r], at).astype(F32)
            faded[at, :] = (fade[h : h + 1, :] * value).astype(BF16)
        state = dot(faded[...], own_in)
        if r % 2 == 1:
            send_ref[r // 2] = state.astype(BF16)
        else:
            keep_ref[r // 2] = state


def fold_kernel(*refs):
    count = len(refs) // 3
    for keep_ref, got_ref, far_ref in zip(refs[:count], refs[count : 2 * count], refs[2 * count :]):
        far_ref[...] = (keep_ref[0] + got_ref[0].astype(F32)).astype(BF16)


def pack_state(sent_ref, state, total):
    channels = state.shape[0]
    sent_ref[:channels, :] = state.astype(BF16)
    high, middle, low = (part.astype(F32) for part in three_parts(total))
    lane = lax.broadcasted_iota(jnp.int32, total.shape, 1)
    parts = jnp.where(lane < LANES // 4, high, jnp.where(lane < LANES // 2, middle, low))
    sent_ref[channels:, :] = parts.astype(BF16)


def first_kernel(own_ref, core_ref, total_ref, *refs):
    *far_refs, running_ref, sent_ref = refs
    running = own_ref[0] + core_ref[0].astype(F32)
    for far_ref in far_refs:
        running = running + far_ref[...].astype(F32)
    running_ref[...] = running
    pack_state(sent_ref, running, total_ref[...])


def merge_kernel(
    bit, head_count, place_ref, running_ref, total_ref, offset_ref, got_ref,
    next_total_ref, next_offset_ref, factor_ref, sent_ref, next_running_ref,
):
    channels = running_ref.shape[0]
    width = channels // head_count
    place = place_ref[0]
    upper = place // 2**bit % 2 == 1
    total = total_ref[...]
    parts = got_ref[channels:, :].astype(F32)
    middle, low = LANES // 4, LANES // 2
    partner = parts[:, 0:1] + parts[:, middle : middle + 1] + parts[:, low : low + 1]
    partner = jnp.broadcast_to(partner, total.shape)
    fading = jnp.exp(jnp.where(upper, total, partner))
    for h in range(head_count):
        at = head_rows(h, width)
        got, running = got_ref[at, :].astype(F32), running_ref[at, :]
        lower, higher = jnp.where(upper, got, running), jnp.where(upper, running, got)
        next_running_ref[at, :] = fading[h : h + 1, :] * lower + higher
    joined = total + partner
    next_total_ref[...] = joined
    offset = jnp.where(upper, offset_ref[...] + partner, offset_ref[...])
    next_offset_ref[...] = offset
    next_upper = place // 2 ** (bit + 1) % 2 == 1
    factor_ref[...] = jnp.where(next_upper, jnp.exp(offset), 0.0)
    pack_state(sent_ref, next_running_ref[...], joined)


def local_kernel(near, pieces, me_ref, *refs):
    groups = refs[-1].shape[0]
    arrays = 1 + max(i for parts in pieces for i, _, _ in parts)
    value_refs, refs = refs[:arrays], refs[arrays:]
    lift_ref, read_ref, merge_ref, score_ref, masked_ref, reader_ref, pair_ref = refs[:7]
    skip_ref, cross_ref, *refs = refs[7:]
    factor_refs, state_refs, refs = refs[:near], refs[near : 2 * near], refs[2 * near :]
    pre_ref, lifted, sums, operand, pairs_ref, nodes = refs
    channels, group_rows = value_refs[0].shape
    assert len(pieces) == groups
    head_count = lift_ref.shape[1]
    width = channels // head_count
    me = me_ref[0]
    per_group = group_rows // CH
    stretches = groups * per_group
    state_size = reader_ref.shape[1] // 2
    place = {kind: i for i, kind in enumerate(merge_rows(stretches))}
    heads = [(h, head_rows(h, width)) for h in range(head_count)]
    for r in range(groups):
        g = me ^ r
        lift = lift_ref[g]
        for h, at in heads:
            value = load(value_refs, pieces[r], at).astype(F32)
            lifted[at, :] = (lift[h : h + 1, :] * value).astype(BF16)
        direct = dot(lifted[...], score_ref[g, 0]) + dot(lifted[...], score_ref[g, 1])
        read = read_ref[0, g]
        terms = []
        for level, (state_ref, factor_ref) in enumerate(zip(state_refs, factor_refs)):
            gained = dot(state_ref[:channels, :], reader_ref[g, :state_size, :])
            scale = cross_ref[level, g] * factor_ref[:head_count, 0:1]
            terms.append((scale, gained))
        for h, at in heads:
            total = read[h : h + 1, :] * direct[at, :]
            total = total + skip_ref[h : h + 1, :] * load(value_refs, pieces[r], at).astype(F32)
            for scale, gained in terms:
                total = total + scale[h : h + 1, :] * gained[at, :]
            pre_ref[g, at, :] = total
        nodes[g] = dot(lifted[...], masked_ref[g])

    for g in range(groups):
        terms = []
        level = per_group.bit_length()
        while 2 ** (level - 1) < stretches:
            if (g * per_group >> (level - 1)) & 1:
                terms.append((read_ref[level, g], dot(operand[level - 1], reader_ref[g])))
            level += 1
        for s in range(per_group):
            c = g * per_group + s
            if c + 1 == stretches:
                break
            merges = [merge_ref[place["own", c, 0]]]
            k = 0
            while (c >> k) & 1:
                merges.append(merge_ref[place["merge", c, k]])
                k += 1
            for h, at in heads:
                node = nodes[g, at, s * state_size : (s + 1) * state_size]
                node = node * merges[0][h : h + 1, :]
                for i, merge in enumerate(merges[1:]):
                    node = node + merge[h : h + 1, :] * sums[i, at, :]
                sums[k, at, :] = node
                high, low = two_parts(node)
                if k == 0 and per_group > 1:
                    pairs_ref[at, s // 2 * state_size : (s // 2 + 1) * state_size] = high
                else:
                    operand[k, at, :state_size] = high
                    operand[k, at, state_size:] = low
            if 1 <= k < per_group.bit_length() - 1:
                scale = read_ref[k + 1, g]
                lane = lax.broadcasted_iota(jnp.int32, scale.shape, 1) // (CH << (k + 1))
                scale = jnp.where(lane == s >> (k + 1), scale, 0.0)
                terms.append((scale, dot(operand[k], reader_ref[g])))
        if per_group > 1:
            terms.append((read_ref[1, g], dot(pairs_ref[...], pair_ref[g])))
        for h, at in heads:
            total = pre_ref[g, at, :]
            for scale, gained in terms:
                total = total + scale[h : h + 1, :] * gained[at, :]
            pre_ref[g, at, :] = total


def finish_kernel(
    half, me_ref, pre_ref, reader_ref, cross_ref, factor_ref, state_ref, gain_ref, *refs
):
    keep_refs, send_ref = refs[:half], refs[half]
    groups, channels, _ = pre_ref.shape
    head_count = cross_ref.shape[2]
    width = channels // head_count
    state_size = reader_ref.shape[1] // 2
    me = me_ref[0]
    state = state_ref[:channels, :]
    for r in range(groups):
        g = me ^ r
        gained = dot(state, reader_ref[g, :state_size, :])
        scale = cross_ref[0, g] * factor_ref[:head_count, 0:1]
        for h in range(head_count):
            at = head_rows(h, width)
            total = pre_ref[g, at, :] + scale[h : h + 1, :] * gained[at, :]
            mean_square = jnp.sum(total * total, axis=0, keepdims=True) * (1.0 / width)
            normed = total * lax.rsqrt(mean_square + EPSILON) * gain_ref[at, 0:1]
            if r % 2 == 0:
                keep_refs[r // 2][at, :] = normed.astype(BF16)
            else:
                send_ref[r // 2, at, :] = normed.astype(BF16)


def project_kernel(*refs):
    *refs, out_ref = refs
    rows = out_ref.shape[0]
    kept_refs, other_refs, refs = refs[:rows], refs[rows : 2 * rows], refs[2 * rows :]
    count = len(refs) // 2
    weights, partners = refs[:count], refs[count:]
    width = weights[0].shape[0]
    for i, (kept_ref, other_ref) in enumerate(zip(kept_refs, other_refs)):
        for j, (weight, partner) in enumerate(zip(weights, partners)):
            found = dot(weight[...], kept_ref[...]) + dot(partner[...], other_ref[0])
            out_ref[i, j * width : (j + 1) * width, :] = found.astype(out_ref.dtype)


def assemble_kernel(groups, place_ref, *refs):
    *refs, out_ref, columns_ref = refs
    each = len(refs) // len(groups)
    for g, group in enumerate(groups):
        own_ref, *far_refs = refs[g * each : (g + 1) * each]
        width = own_ref.shape[0] // len(group)
        for j, r in enumerate(group):
            rows = slice(j * width, (j + 1) * width)
            total = own_ref[rows, :]
            for far_ref in far_refs:
                total = total + far_ref[rows, :].astype(F32)
            start = pl.multiple_of((place_ref[0] ^ r) * width, width)
            columns_ref[pl.ds(start, width), :] = total
    for first in range(0, out_ref.shape[1], LANES):
        at = slice(first, first + LANES)
        out_ref[:, at] = jnp.transpose(columns_ref[at, :]).astype(BF16)


def whole(shape):
    return pl.BlockSpec(shape, lambda *_: (0,) * len(shape))


def on_device(
    values,
    state_in,
    state_out,
    log_decay,
    level_class,
    level_table,
    skip_gain,
    norm_gain,
    out_weight,
):
    heads_size = lax.axis_size("head")
    ctx_size = lax.axis_size("ctx")
    ctx_bits = ctx_size.bit_length() - 1
    me = lax.axis_index("head")
    me1 = me.reshape(1).astype(jnp.int32)
    position = lax.axis_index("ctx")
    place1 = position.reshape(1).astype(jnp.int32)
    tokens = state_in.shape[0]
    rows_dev = values.shape[0]
    head_count = log_decay.shape[1]
    features = values.shape[1] // heads_size
    state_size = state_in.shape[1]
    columns = out_weight.shape[1]
    stretches = tokens // CH
    per_group = rows_dev // CH
    local = stretches.bit_length() - 1
    levels = level_table.shape[1]
    classes = level_table.shape[0]
    extra = -(-head_count // 16) * 16
    padded = -(-head_count // 8) * 8
    half = heads_size // 2
    near = ctx_bits - 1
    params = pltpu.CompilerParams(vmem_limit_bytes=VMEM_LIMIT)
    cheap = pl.CostEstimate(flops=0, bytes_accessed=0, transcendentals=0)
    smem = pl.BlockSpec(memory_space=pltpu.SMEM)
    vmem = pl.BlockSpec(memory_space=pltpu.VMEM)

    def kernel_call(body, name, out_shape, **kwargs):
        return pl.pallas_call(
            body, out_shape=out_shape, compiler_params=params, cost_estimate=cheap, name=name, **kwargs
        )

    def shape(dims, kind=BF16):
        return jax.ShapeDtypeStruct(dims, kind)

    def part(array, index):
        return pl.BlockSpec((1,) + array.shape[1:], lambda *_: (index,) + (0,) * (array.ndim - 1))

    def fenced(body, *operands):
        shapes = jax.eval_shape(body, *operands)
        zeros = lambda *_: jax.tree.map(lambda leaf: jnp.zeros(leaf.shape, leaf.dtype), shapes)
        return lax.cond(position < ctx_size, body, zeros, *operands)

    held, partners = {0: out_weight.T}, {}
    for bit in range(ctx_bits):
        held[2**bit] = swap(held[0], "ctx", 2**bit)

    decays = log_decay.T
    own_fade, side_fade, *far_fades, total = kernel_call(
        functools.partial(fade_kernel, heads_size),
        "fade",
        tuple(
            [shape((head_count, rows_dev), F32)] * 2
            + [shape((2, head_count, rows_dev), F32)] * (half - 1)
            + [shape((extra, LANES), F32)]
        ),
        in_specs=[smem, vmem],
    )(me1, decays)

    got_fades = []
    for i, far in enumerate(far_fades):
        got_fades.append(swap(tie(far, *got_fades), "head", 2 * (i + 1)))
    sides = kernel_call(
        pack_kernel,
        "pack_fades",
        shape((half, head_count, rows_dev), F32),
        grid=(1,),
        in_specs=[whole(side_fade.shape)] + [part(got, 1) for got in got_fades],
        out_specs=whole((half, head_count, rows_dev)),
    )(side_fade, *got_fades)
    sides = swap(sides, "head", 1)

    early = rows_dev // 2
    cuts = [(r, first, early) for r in (2,) for first in (0, early)]
    cuts = [(0, 0, rows_dev), (1, 0, rows_dev)] + cuts
    cuts += [(r, 0, rows_dev) for r in range(3, heads_size)]
    portions = kernel_call(
        split_kernel,
        "split_values",
        tuple(shape((features, count)) for _, _, count in cuts),
        grid_spec=pltpu.PrefetchScalarGridSpec(
            num_scalar_prefetch=1,
            grid=(1,),
            in_specs=[
                pl.BlockSpec((count, features), lambda i, m, r=r, at=first // count: (at, m[0] ^ r))
                for r, first, count in cuts
            ],
            out_specs=[whole((features, count)) for _, _, count in cuts],
        ),
    )(me1, *[values] * len(cuts))
    portion = {(r, first): array for (r, first, _), array in zip(cuts, portions)}
    value_head = swap(tie(portion[2, 0], *got_fades), "head", 2)

    pieces = [[] for _ in range(heads_size)]
    for i, (r, _, count) in enumerate(cuts):
        pieces[r].append((i, 0, count))
    fades, fade_specs = [], []
    for r in range(heads_size):
        if r == 0:
            fades.append(own_fade)
            fade_specs.append(whole(own_fade.shape))
        else:
            fades.append(sides if r % 2 else got_fades[r // 2 - 1])
            fade_specs.append(part(fades[-1], r // 2 if r % 2 else 0))
    keep, send = kernel_call(
        lambda me_ref, *refs: partial_state_kernel(pieces, *refs),
        "partial_states",
        (shape((half, features, state_size), F32), shape((half, features, state_size))),
        grid_spec=pltpu.PrefetchScalarGridSpec(
            num_scalar_prefetch=1,
            grid=(1,),
            in_specs=[whole(array.shape) for array in portions]
            + fade_specs
            + [pl.BlockSpec((rows_dev, state_size), lambda i, m: (m[0], 0))],
            out_specs=[whole((half, features, state_size))] * 2,
            scratch_shapes=[pltpu.VMEM((features, rows_dev), BF16)],
        ),
    )(me1, *portions, *fades, state_in)

    def core_sum(keep, send):
        got = swap(send, "head", 1)
        far = kernel_call(
            fold_kernel,
            "fold",
            tuple([shape((features, state_size))] * (half - 1)),
            in_specs=[part(keep, i) for i in range(1, half)] * 2,
            out_specs=tuple([whole((features, state_size))] * (half - 1)),
            grid=(1,),
        )(*[keep] * (half - 1), *[got] * (half - 1))
        return got, far

    core_states, far_states = fenced(core_sum, keep, send)

    merge_count = len(merge_rows(stretches))
    grouped = (heads_size, head_count, rows_dev)
    pair_rows = max(per_group // 2, 1) * state_size

    def step(bit, running, total, offset, got):
        last = bit + 1 == near
        shapes = [shape((extra, LANES), F32)] * 3 + [shape((features + extra, state_size))]
        running_shape = shape((features, state_size), F32)
        results = kernel_call(
            functools.partial(merge_kernel, bit, head_count),
            "merge",
            tuple(shapes if last else shapes + [running_shape]),
            in_specs=[smem] + [vmem] * 4,
            scratch_shapes=[pltpu.VMEM((features, state_size), F32)] if last else [],
        )(place1, running, total, offset, got)
        return list(results) + [None] * last

    def chip_sum(
        keep, core_states, far_states, total, decays, level_class, level_table, state_in, state_out,
        second, crossing,
    ):
        got_states, latest = [], []
        for i, far in enumerate(far_states):
            latest = [swap(tie(far, *latest), "head", 2 * (i + 1))]
            got_states += latest
        moved, after = [], []
        for array in crossing:
            moved.append(swap(tie(array, *after), "head", 1))
            after = moved[-1:]
        if moved:
            moved[0] = jnp.concatenate([second, moved[0]], axis=1)
        table = jnp.transpose(level_table, (1, 2, 0))
        table = jnp.pad(table, ((0, 0), (0, padded - head_count), (0, 0)))
        tables = kernel_call(
            functools.partial(factors_kernel, levels, heads_size),
            "factors",
            (
                shape(grouped, F32),
                shape((local + 1,) + grouped, F32),
                shape((ctx_bits,) + grouped, F32),
                shape((merge_count, head_count, LANES), F32),
                shape((heads_size, 2, rows_dev, rows_dev)),
                shape((heads_size, rows_dev, per_group * state_size)),
                shape((heads_size, 2 * state_size, rows_dev)),
                shape((heads_size, pair_rows, rows_dev)),
            ),
        )(
            decays,
            level_class.reshape(1, tokens),
            table.reshape(levels * padded, classes),
            state_in,
            state_out,
        )
        got_states[-1] = tie(got_states[-1], tables[0], *moved)
        running, sent = kernel_call(
            first_kernel,
            "first_state",
            (shape((features, state_size), F32), shape((features + extra, state_size))),
            grid=(1,),
            in_specs=[part(keep, 0), part(core_states, 0), whole(total.shape)]
            + [whole((features, state_size))] * len(got_states),
            out_specs=(whole((features, state_size)), whole((features + extra, state_size))),
        )(keep, core_states, total, *got_states)
        return running, sent, tables, moved

    def near_steps(running, total, sent):
        offset = jnp.zeros((extra, LANES), F32)
        factors = [jnp.broadcast_to((position % 2).astype(F32), (extra, LANES))]
        states = []
        for bit in range(near):
            states.append(swap(sent, "ctx", 2**bit))
            total, offset, factor, sent, running = step(bit, running, total, offset, states[-1])
            factors.append(factor)
        return states, factors, sent

    running, sent, tables, moved = fenced(
        chip_sum, keep, core_states, tie(far_states, value_head), total, decays, level_class,
        level_table, state_in, state_out, portion[2, early],
        [portion[r, 0] for r in range(3, heads_size, 2)],
    )
    passed, after = {}, []
    for i, array in enumerate(moved):
        passed[2 * i + 3] = swap(tie(array, *after), "head", 2 * i + 2)
        after = [passed[2 * i + 3]]
    for r in range(4, heads_size, 2):
        passed[r] = swap(tie(portion[r, 0], *after), "head", r)
        after = [passed[r]]
    states, factors, sent = fenced(near_steps, running, total, sent)
    states = list(states)
    sent = tie(sent, *[held[2**bit] for bit in range(ctx_bits)])
    last_state = swap(sent, "ctx", 2**near)

    for r in range(2, ctx_size):
        low = r & -r
        if r not in held and low > 1:
            held[r] = swap(tie(held[r ^ low], sent), "ctx", low)
    for bit in range(2, ctx_bits):
        held[2**bit + 1] = swap(tie(held[2**bit], sent), "ctx", 1)
    for r in (0, 1):
        partners[r] = swap(tie(held[r], sent), "head", 1)

    skips = jnp.broadcast_to(skip_gain[:, None], (head_count, rows_dev))
    gains = norm_gain[:, None]

    lift, read, cross, merge, scores, masked, readers, pairs = tables
    arrays = [portion[0, 0], swap(tie(portion[1, 0], sent), "head", 1), value_head]
    pieces = [[(0, 0, rows_dev)], [(1, 0, rows_dev)], [(2, 0, early)]]
    for r in range(3, heads_size):
        first = rows_dev - early if r == 3 else 0
        if r == 3:
            pieces[2].append((len(arrays), 0, first))
        pieces.append([(len(arrays), first, rows_dev)])
        arrays.append(passed[r])
    pre = kernel_call(
        functools.partial(local_kernel, near, pieces),
        "local_levels",
        shape((heads_size, features, rows_dev), F32),
        in_specs=[smem] + [vmem] * (len(arrays) + 9 + 2 * near),
        scratch_shapes=[
            pltpu.VMEM((features, rows_dev), BF16),
            pltpu.VMEM((max(local, 1), features, state_size), F32),
            pltpu.VMEM((max(local, 1), features, 2 * state_size), BF16),
            pltpu.VMEM((features, pair_rows), BF16),
            pltpu.VMEM((heads_size, features, per_group * state_size), F32),
        ],
    )(
        me1, *arrays, lift, read, merge, scores, masked, readers, pairs, skips, cross,
        *factors[:near], *states,
    )
    *kept, sides = kernel_call(
        functools.partial(finish_kernel, half),
        "finish",
        tuple([shape((features, rows_dev))] * half + [shape((half, features, rows_dev))]),
        grid=(1,),
        in_specs=[
            smem,
            whole(pre.shape),
            whole(readers.shape),
            part(cross, near),
            whole((extra, LANES)),
            whole((features + extra, state_size)),
            whole((features, 1)),
        ],
        out_specs=[whole((features, rows_dev))] * half + [whole((half, features, rows_dev))],
    )(me1, pre, readers, cross, factors[near], last_state, gains)
    done = [held[r] for r in held if r not in (0, 1)] + [kept[0]]
    early_blocks = sorted(held)
    held[3] = swap(tie(held[1], *done), "ctx", 2)
    for r in range(5, ctx_size, 2):
        if r not in held:
            held[r] = swap(tie(held[r ^ 1], *done), "ctx", 1)

    order = sorted(early_blocks, key=lambda r: (r // 2 * 2 not in early_blocks or r ^ 1 not in early_blocks, r))
    order += [r for r in range(ctx_size) if r not in early_blocks]
    count = 2
    groups = [order[first : first + count] for first in range(0, ctx_size, count)]
    others = swap(sides, "head", 1)

    def project(name, first, kept, others, group, blocks, partners, kind):
        rows = len(kept)
        return kernel_call(
            project_kernel,
            name,
            shape((rows, count * columns, rows_dev), kind),
            in_specs=[whole((features, rows_dev))] * rows
            + [part(others, first + i) for i in range(rows)]
            + [whole((columns, features))] * (2 * count),
            out_specs=whole((rows, count * columns, rows_dev)),
            grid=(1,),
        )(*kept, *[others] * rows, *[blocks[r] for r in group], *[partners[r] for r in group])

    def far_rows(group, kept, others, blocks, partners):
        return project("project_far", 1, kept[1:], others, group, blocks, partners, BF16)

    def own_rows(group, kept, others, blocks, partners):
        return project("project_own", 0, kept[:1], others, group, blocks, partners, F32)[0]

    def send_rows(far, *after):
        far = tie(far, *after)
        return [swap(far[i - 1], "head", 2 * i) for i in range(1, half)]

    def with_partners(blocks, partners):
        more = {r: swap(blocks[r], "head", 1) for r in blocks if r not in partners}
        return {**partners, **more}, more

    def first_groups(kept, others, blocks, partners):
        partners, more = with_partners(blocks, partners)
        got = send_rows(far_rows(groups[0], kept, others, blocks, partners))
        far = far_rows(groups[1], kept, others, blocks, partners)
        return far, got, more, own_rows(groups[0], [tie(kept[0], far)], others, blocks, partners)

    def middle_group(index):
        def body(far, kept, others, blocks, partners):
            known = partners
            partners, more = with_partners({r: blocks[r] for r in groups[index]}, partners)
            next_far = far_rows(groups[index], kept, others, blocks, partners)
            own = own_rows(groups[index - 1], [tie(kept[0], next_far)], others, blocks, known)
            return next_far, send_rows(far), more, own

        return body

    def last_group(kept, others, blocks, partners):
        partners, more = with_partners(blocks, partners)
        return far_rows(groups[-1], kept, others, blocks, partners), more

    def some(array, group):
        return {r: array[r] for r in group if r in array}

    arrived = []
    far, got, more, own = fenced(
        first_groups, kept, others, some(held, groups[0] + groups[1]), some(partners, groups[0] + groups[1])
    )
    arrived.append(got)
    owns = [own]
    partners.update(more)
    for index in range(2, len(groups) - 1):
        both = groups[index - 1] + groups[index]
        far, got, more, own = fenced(
            middle_group(index), far, kept, others, some(held, both), some(partners, both)
        )
        arrived.append(got)
        owns.append(own)
        partners.update(more)
    got = send_rows(far, *[held[r] for r in groups[-1]])
    arrived.append(got)
    far, more = fenced(last_group, kept, others, some(held, groups[-1]), some(partners, groups[-1]))
    partners.update(more)
    arrived.append(send_rows(far, *got))
    pieces = []
    for index, (group, got) in enumerate(zip(groups, arrived)):
        if index == len(owns):
            owns.append(own_rows(group, kept, others, held, partners))
        pieces += [owns[index]] + got
    return kernel_call(
        functools.partial(assemble_kernel, groups),
        "assemble",
        shape((rows_dev, ctx_size * columns)),
        in_specs=[smem] + [vmem] * len(pieces),
        scratch_shapes=[pltpu.VMEM((ctx_size * columns, rows_dev), F32)],
    )(place1, *pieces)


def solution(mesh):
    return jax.shard_map(
        on_device,
        mesh=mesh,
        in_specs=(
            P(("ctx", "head"), None),
            P("ctx", None),
            P("ctx", None),
            P("ctx", "head"),
            P("ctx"),
            P(None, None, "head"),
            P("head"),
            P("head"),
            P("head", "ctx"),
        ),
        out_specs=P(("ctx", "head"), None),
        check_vma=False,
    )
```

```python
import functools

import jax
import jax.numpy as jnp
from jax import lax
from jax.experimental import pallas as pl
from jax.experimental.pallas import tpu as pltpu
from jax.sharding import PartitionSpec as P

CH = 64
EPSILON = 1e-05
LANES = 128
F32 = jnp.float32
BF16 = jnp.bfloat16
MIB = 1024 * 1024


def dot(a, b):
    return lax.dot_general(a, b, (((1,), (0,)), ((), ())), preferred_element_type=F32)


def dot_nt(a, b):
    return lax.dot_general(a, b, (((1,), (1,)), ((), ())), preferred_element_type=F32)


def swap(value, axis, distance):
    pairs = [(source, source ^ distance) for source in range(lax.axis_size(axis))]
    return lax.ppermute(value, axis, pairs)


def tie(value, *after):
    return lax.optimization_barrier((value,) + after)[0]


def three_parts(x):
    high = x.astype(BF16)
    rest = x - high.astype(F32)
    middle = rest.astype(BF16)
    low = (rest - middle.astype(F32)).astype(BF16)
    return high, middle, low


def two_parts(x):
    high = x.astype(BF16)
    return high, (x - high.astype(F32)).astype(BF16)


def merge_rows(stretches):
    rows = [("own", c, 0) for c in range(stretches - 1)]
    for c in range(stretches - 1):
        k = 0
        while (c >> k) & 1:
            rows.append(("merge", c, k))
            k += 1
    return rows


def head_rows(head, width):
    return slice(head * width, (head + 1) * width)


def exact_dot(x, ones):
    return sum(dot(part, ones) for part in three_parts(x))


def split_kernel(me_ref, *refs):
    half = len(refs) // 2
    for value_ref, part_ref in zip(refs[:half], refs[half:]):
        part_ref[...] = jnp.transpose(value_ref[...])


def fade_kernel(blocks, me_ref, decay_ref, own_ref, side_ref, *refs):
    far_refs, total_ref = refs[:-1], refs[-1]
    head_count, tokens = decay_ref.shape
    rows = tokens // blocks
    row = lax.broadcasted_iota(jnp.int32, (rows, rows), 0)
    col = lax.broadcasted_iota(jnp.int32, (rows, rows), 1)
    later = jnp.where(row > col, 1.0, 0.0).astype(BF16)
    me = me_ref[0]
    after = jnp.zeros((head_count, 1), F32)
    for block in reversed(range(blocks)):
        decay = decay_ref[:, block * rows : (block + 1) * rows]
        left = exact_dot(decay, later)
        fade = jnp.exp(left + after)
        after = after + left[:, 0:1] + decay[:, 0:1]
        own_index = me ^ block

        @pl.when(own_index == 0)
        def _():
            own_ref[...] = fade

        @pl.when(own_index == 1)
        def _():
            side_ref[...] = fade

        for i, far_ref in enumerate(far_refs):
            for j in range(2):

                @pl.when(own_index == 2 * (i + 1) + j)
                def _():
                    far_ref[j] = fade

    total_ref[...] = jnp.zeros_like(total_ref)
    total_ref[:head_count, :] = jnp.broadcast_to(after, (head_count, LANES))


def pack_kernel(*refs):
    side_ref, *got_refs, out_ref = refs
    out_ref[0] = side_ref[...]
    for i, got_ref in enumerate(got_refs):
        out_ref[i + 1] = got_ref[0]


def factors_kernel(
    levels, blocks, decay_ref, class_ref, table_ref, in_ref, out_ref,
    lift_ref, read_ref, cross_ref, merge_ref, score_ref, masked_ref, reader_ref, pair_ref,
):
    head_count, tokens = decay_ref.shape
    stretches = tokens // CH
    rows = tokens // blocks
    per_block = rows // CH
    local = read_ref.shape[0] - 1
    state_size = in_ref.shape[1]
    padded = table_ref.shape[0] // levels
    classes = table_ref.shape[1]
    row = lax.broadcasted_iota(jnp.int32, (rows, rows), 0)
    col = lax.broadcasted_iota(jnp.int32, (rows, rows), 1)
    inside = (row // CH == col // CH) & (row <= col)
    upto = jnp.where(inside, 1.0, 0.0).astype(BF16)
    within, starts = [], [jnp.zeros((head_count, 1), F32)]
    for g in range(blocks):
        within.append(exact_dot(decay_ref[:, g * rows : (g + 1) * rows], upto))
        for s in range(per_block):
            last = (s + 1) * CH
            starts.append(starts[-1] + within[-1][:, last - 1 : last])
    class_row = lax.broadcasted_iota(jnp.int32, (classes, rows), 0)
    lane = lax.broadcasted_iota(jnp.int32, (head_count, rows), 1) // CH
    token = lax.broadcasted_iota(jnp.int32, (rows, state_size), 0) // CH

    def by_stretch(columns):
        spread = jnp.broadcast_to(columns[0], (head_count, rows))
        for s in range(1, per_block):
            spread = jnp.where(lane == s, columns[s], spread)
        return spread

    for g in range(blocks):
        at = slice(g * rows, (g + 1) * rows)
        onehot = jnp.where(class_ref[:, at] == class_row, 1.0, 0.0).astype(BF16)
        weights = sum(dot(part, onehot) for part in three_parts(table_ref[...]))
        weight = lambda level: weights[level * padded : level * padded + head_count, :]
        lift_ref[g] = jnp.exp(-within[g])
        read_ref[0, g] = jnp.exp(within[g]) * weight(0)
        first = g * per_block
        for level in range(1, local + 1):
            begins, active = [], []
            for c in range(first, first + per_block):
                upper = (c >> (level - 1)) & 1
                begins.append(starts[c] - starts[(c >> (level - 1)) << (level - 1)])
                active.append(jnp.full((head_count, 1), float(upper), F32))
            factor = jnp.exp(within[g] + by_stretch(begins)) * weight(level)
            read_ref[level, g] = factor * by_stretch(active)
        far = jnp.exp(within[g] + by_stretch(starts[first : first + per_block]))
        for level in range(local + 1, levels):
            cross_ref[level - local - 1, g] = far * weight(level)
        own_in, own_out = in_ref[at, :], out_ref[at, :]
        scores = jnp.where(inside, dot_nt(own_in, own_out), 0.0)
        score_ref[g, 0], score_ref[g, 1] = two_parts(scores)
        for s in range(per_block):
            masked = jnp.where(token == s, own_in.astype(F32), 0.0).astype(BF16)
            masked_ref[g, :, s * state_size : (s + 1) * state_size] = masked
        turned = jnp.transpose(own_out.astype(F32))
        reader = turned.astype(BF16)
        reader_ref[g, :state_size, :] = reader
        reader_ref[g, state_size:, :] = reader
        pairs = max(per_block // 2, 1)
        place = lax.broadcasted_iota(jnp.int32, (state_size, rows), 1) // (2 * CH)
        for j in range(pairs):
            alone = jnp.where(place == j, turned, 0.0).astype(BF16)
            pair_ref[g, j * state_size : (j + 1) * state_size, :] = alone
    for i, (kind, c, k) in enumerate(merge_rows(stretches)):
        first = c if kind == "own" else c + 1 - 2**k
        merge_ref[i] = jnp.broadcast_to(jnp.exp(starts[c + 1] - starts[first]), (head_count, LANES))


def load(refs, pieces, at):
    parts = [refs[i][at, first : first + count] for i, first, count in pieces]
    return parts[0] if len(parts) == 1 else jnp.concatenate(parts, axis=1)


def partial_state_kernel(pieces, *refs):
    count = len(pieces)
    arrays = sum(len(parts) for parts in pieces)
    value_refs, refs = refs[:arrays], refs[arrays:]
    fade_refs, (in_ref, keep_ref, send_ref, faded) = refs[:count], refs[count:]
    own_in = in_ref[...]
    for r in [*range(1, count, 2), *range(0, count, 2)]:
        fade = fade_refs[r][...].reshape(fade_refs[r].shape[-2:])
        head_count = fade.shape[0]
        width = value_refs[0].shape[0] // head_count
        for h in range(head_count):
            at = head_rows(h, width)
            value = load(value_refs, pieces[r], at).astype(F32)
            faded[at, :] = (fade[h : h + 1, :] * value).astype(BF16)
        state = dot(faded[...], own_in)
        if r % 2 == 1:
            send_ref[r // 2] = state.astype(BF16)
        else:
            keep_ref[r // 2] = state


def fold_kernel(*refs):
    count = len(refs) // 3
    for keep_ref, got_ref, far_ref in zip(refs[:count], refs[count : 2 * count], refs[2 * count :]):
        far_ref[...] = (keep_ref[0] + got_ref[0].astype(F32)).astype(BF16)


def pack_state(sent_ref, state, total):
    channels = state.shape[0]
    sent_ref[:channels, :] = state.astype(BF16)
    high, middle, low = (part.astype(F32) for part in three_parts(total))
    lane = lax.broadcasted_iota(jnp.int32, total.shape, 1)
    parts = jnp.where(lane < LANES // 4, high, jnp.where(lane < LANES // 2, middle, low))
    sent_ref[channels:, :] = parts.astype(BF16)


def first_kernel(own_ref, core_ref, total_ref, *refs):
    *far_refs, running_ref, sent_ref = refs
    running = own_ref[0] + core_ref[0].astype(F32)
    for far_ref in far_refs:
        running = running + far_ref[...].astype(F32)
    running_ref[...] = running
    pack_state(sent_ref, running, total_ref[...])


def merge_kernel(
    bit, head_count, place_ref, running_ref, total_ref, offset_ref, got_ref,
    next_total_ref, next_offset_ref, factor_ref, sent_ref, next_running_ref,
):
    channels = running_ref.shape[0]
    width = channels // head_count
    place = place_ref[0]
    upper = place // 2**bit % 2 == 1
    total = total_ref[...]
    parts = got_ref[channels:, :].astype(F32)
    middle, low = LANES // 4, LANES // 2
    partner = parts[:, 0:1] + parts[:, middle : middle + 1] + parts[:, low : low + 1]
    partner = jnp.broadcast_to(partner, total.shape)
    fading = jnp.exp(jnp.where(upper, total, partner))
    for h in range(head_count):
        at = head_rows(h, width)
        got, running = got_ref[at, :].astype(F32), running_ref[at, :]
        lower, higher = jnp.where(upper, got, running), jnp.where(upper, running, got)
        next_running_ref[at, :] = fading[h : h + 1, :] * lower + higher
    joined = total + partner
    next_total_ref[...] = joined
    offset = jnp.where(upper, offset_ref[...] + partner, offset_ref[...])
    next_offset_ref[...] = offset
    next_upper = place // 2 ** (bit + 1) % 2 == 1
    factor_ref[...] = jnp.where(next_upper, jnp.exp(offset), 0.0)
    pack_state(sent_ref, next_running_ref[...], joined)


def local_kernel(near, pieces, me_ref, *refs):
    groups = refs[-1].shape[0]
    arrays = 1 + max(i for parts in pieces for i, _, _ in parts)
    value_refs, refs = refs[:arrays], refs[arrays:]
    lift_ref, read_ref, merge_ref, score_ref, masked_ref, reader_ref, pair_ref = refs[:7]
    skip_ref, cross_ref, *refs = refs[7:]
    factor_refs, state_refs, refs = refs[:near], refs[near : 2 * near], refs[2 * near :]
    pre_ref, lifted, sums, operand, pairs_ref, nodes = refs
    channels, group_rows = value_refs[0].shape
    assert len(pieces) == groups
    head_count = lift_ref.shape[1]
    width = channels // head_count
    me = me_ref[0]
    per_group = group_rows // CH
    stretches = groups * per_group
    state_size = reader_ref.shape[1] // 2
    place = {kind: i for i, kind in enumerate(merge_rows(stretches))}
    heads = [(h, head_rows(h, width)) for h in range(head_count)]
    for r in range(groups):
        g = me ^ r
        lift = lift_ref[g]
        for h, at in heads:
            value = load(value_refs, pieces[r], at).astype(F32)
            lifted[at, :] = (lift[h : h + 1, :] * value).astype(BF16)
        direct = dot(lifted[...], score_ref[g, 0]) + dot(lifted[...], score_ref[g, 1])
        read = read_ref[0, g]
        terms = []
        for level, (state_ref, factor_ref) in enumerate(zip(state_refs, factor_refs)):
            gained = dot(state_ref[:channels, :], reader_ref[g, :state_size, :])
            scale = cross_ref[level, g] * factor_ref[:head_count, 0:1]
            terms.append((scale, gained))
        for h, at in heads:
            total = read[h : h + 1, :] * direct[at, :]
            total = total + skip_ref[h : h + 1, :] * load(value_refs, pieces[r], at).astype(F32)
            for scale, gained in terms:
                total = total + scale[h : h + 1, :] * gained[at, :]
            pre_ref[g, at, :] = total
        nodes[g] = dot(lifted[...], masked_ref[g])

    for g in range(groups):
        terms = []
        level = per_group.bit_length()
        while 2 ** (level - 1) < stretches:
            if (g * per_group >> (level - 1)) & 1:
                terms.append((read_ref[level, g], dot(operand[level - 1], reader_ref[g])))
            level += 1
        for s in range(per_group):
            c = g * per_group + s
            if c + 1 == stretches:
                break
            merges = [merge_ref[place["own", c, 0]]]
            k = 0
            while (c >> k) & 1:
                merges.append(merge_ref[place["merge", c, k]])
                k += 1
            for h, at in heads:
                node = nodes[g, at, s * state_size : (s + 1) * state_size]
                node = node * merges[0][h : h + 1, :]
                for i, merge in enumerate(merges[1:]):
                    node = node + merge[h : h + 1, :] * sums[i, at, :]
                sums[k, at, :] = node
                high, low = two_parts(node)
                if k == 0 and per_group > 1:
                    pairs_ref[at, s // 2 * state_size : (s // 2 + 1) * state_size] = high
                else:
                    operand[k, at, :state_size] = high
                    operand[k, at, state_size:] = low
            if 1 <= k < per_group.bit_length() - 1:
                scale = read_ref[k + 1, g]
                lane = lax.broadcasted_iota(jnp.int32, scale.shape, 1) // (CH << (k + 1))
                scale = jnp.where(lane == s >> (k + 1), scale, 0.0)
                terms.append((scale, dot(operand[k], reader_ref[g])))
        if per_group > 1:
            terms.append((read_ref[1, g], dot(pairs_ref[...], pair_ref[g])))
        for h, at in heads:
            total = pre_ref[g, at, :]
            for scale, gained in terms:
                total = total + scale[h : h + 1, :] * gained[at, :]
            pre_ref[g, at, :] = total


def finish_kernel(
    half, me_ref, pre_ref, reader_ref, cross_ref, factor_ref, state_ref, gain_ref, *refs
):
    keep_refs, send_ref = refs[:half], refs[half]
    groups, channels, _ = pre_ref.shape
    head_count = cross_ref.shape[2]
    width = channels // head_count
    state_size = reader_ref.shape[1] // 2
    me = me_ref[0]
    state = state_ref[:channels, :]
    for r in range(groups):
        g = me ^ r
        gained = dot(state, reader_ref[g, :state_size, :])
        scale = cross_ref[0, g] * factor_ref[:head_count, 0:1]
        for h in range(head_count):
            at = head_rows(h, width)
            total = pre_ref[g, at, :] + scale[h : h + 1, :] * gained[at, :]
            mean_square = jnp.sum(total * total, axis=0, keepdims=True) * (1.0 / width)
            normed = total * lax.rsqrt(mean_square + EPSILON) * gain_ref[at, 0:1]
            if r % 2 == 0:
                keep_refs[r // 2][at, :] = normed.astype(BF16)
            else:
                send_ref[r // 2, at, :] = normed.astype(BF16)


def project_kernel(*refs):
    *refs, out_ref = refs
    rows = out_ref.shape[0]
    kept_refs, other_refs, refs = refs[:rows], refs[rows : 2 * rows], refs[2 * rows :]
    count = len(refs) // 2
    weights, partners = refs[:count], refs[count:]
    width = weights[0].shape[0]
    for i, (kept_ref, other_ref) in enumerate(zip(kept_refs, other_refs)):
        for j, (weight, partner) in enumerate(zip(weights, partners)):
            found = dot(weight[...], kept_ref[...]) + dot(partner[...], other_ref[0])
            out_ref[i, j * width : (j + 1) * width, :] = found.astype(out_ref.dtype)


def assemble_kernel(groups, place_ref, *refs):
    *refs, out_ref, columns_ref = refs
    each = len(refs) // len(groups)
    for g, group in enumerate(groups):
        own_ref, *far_refs = refs[g * each : (g + 1) * each]
        width = own_ref.shape[0] // len(group)
        for j, r in enumerate(group):
            rows = slice(j * width, (j + 1) * width)
            total = own_ref[rows, :]
            for far_ref in far_refs:
                total = total + far_ref[rows, :].astype(F32)
            start = pl.multiple_of((place_ref[0] ^ r) * width, width)
            columns_ref[pl.ds(start, width), :] = total
    for first in range(0, out_ref.shape[1], LANES):
        at = slice(first, first + LANES)
        out_ref[:, at] = jnp.transpose(columns_ref[at, :]).astype(BF16)


def whole(shape):
    return pl.BlockSpec(shape, lambda *_: (0,) * len(shape))


def on_device(
    values,
    state_in,
    state_out,
    log_decay,
    level_class,
    level_table,
    skip_gain,
    norm_gain,
    out_weight,
):
    heads_size = lax.axis_size("head")
    ctx_size = lax.axis_size("ctx")
    ctx_bits = ctx_size.bit_length() - 1
    me = lax.axis_index("head")
    me1 = me.reshape(1).astype(jnp.int32)
    position = lax.axis_index("ctx")
    place1 = position.reshape(1).astype(jnp.int32)
    tokens = state_in.shape[0]
    rows_dev = values.shape[0]
    head_count = log_decay.shape[1]
    features = values.shape[1] // heads_size
    state_size = state_in.shape[1]
    columns = out_weight.shape[1]
    stretches = tokens // CH
    per_group = rows_dev // CH
    local = stretches.bit_length() - 1
    levels = level_table.shape[1]
    classes = level_table.shape[0]
    extra = -(-head_count // 16) * 16
    padded = -(-head_count // 8) * 8
    half = heads_size // 2
    near = ctx_bits - 1
    cheap = pl.CostEstimate(flops=0, bytes_accessed=0, transcendentals=0)
    smem = pl.BlockSpec(memory_space=pltpu.SMEM)
    vmem = pl.BlockSpec(memory_space=pltpu.VMEM)

    def kernel_call(body, name, out_shape, mib=16, **kwargs):
        params = pltpu.CompilerParams(vmem_limit_bytes=mib * MIB)
        return pl.pallas_call(
            body, out_shape=out_shape, compiler_params=params, cost_estimate=cheap, name=name, **kwargs
        )

    def shape(dims, kind=BF16):
        return jax.ShapeDtypeStruct(dims, kind)

    def part(array, index):
        return pl.BlockSpec((1,) + array.shape[1:], lambda *_: (index,) + (0,) * (array.ndim - 1))

    def fenced(body, *operands):
        shapes = jax.eval_shape(body, *operands)
        zeros = lambda *_: jax.tree.map(lambda leaf: jnp.zeros(leaf.shape, leaf.dtype), shapes)
        return lax.cond(position < ctx_size, body, zeros, *operands)

    held, partners = {0: out_weight.T}, {}
    for bit in range(ctx_bits):
        held[2**bit] = swap(held[0], "ctx", 2**bit)

    decays = log_decay.T
    own_fade, side_fade, *far_fades, total = kernel_call(
        functools.partial(fade_kernel, heads_size),
        "fade",
        tuple(
            [shape((head_count, rows_dev), F32)] * 2
            + [shape((2, head_count, rows_dev), F32)] * (half - 1)
            + [shape((extra, LANES), F32)]
        ),
        in_specs=[smem, vmem],
    )(me1, decays)

    got_fades = []
    for i, far in enumerate(far_fades):
        got_fades.append(swap(tie(far, *got_fades), "head", 2 * (i + 1)))
    sides = kernel_call(
        pack_kernel,
        "pack_fades",
        shape((half, head_count, rows_dev), F32),
        grid=(1,),
        in_specs=[whole(side_fade.shape)] + [part(got, 1) for got in got_fades],
        out_specs=whole((half, head_count, rows_dev)),
    )(side_fade, *got_fades)
    sides = swap(sides, "head", 1)

    early = rows_dev // 2
    cuts = [(r, first, early) for r in (2,) for first in (0, early)]
    cuts = [(0, 0, rows_dev), (1, 0, rows_dev)] + cuts
    cuts += [(r, 0, rows_dev) for r in range(3, heads_size)]
    portions = kernel_call(
        split_kernel,
        "split_values",
        tuple(shape((features, count)) for _, _, count in cuts),
        grid_spec=pltpu.PrefetchScalarGridSpec(
            num_scalar_prefetch=1,
            grid=(1,),
            in_specs=[
                pl.BlockSpec((count, features), lambda i, m, r=r, at=first // count: (at, m[0] ^ r))
                for r, first, count in cuts
            ],
            out_specs=[whole((features, count)) for _, _, count in cuts],
        ),
    )(me1, *[values] * len(cuts))
    portion = {(r, first): array for (r, first, _), array in zip(cuts, portions)}
    value_head = swap(tie(portion[2, 0], *got_fades), "head", 2)

    pieces = [[] for _ in range(heads_size)]
    for i, (r, _, count) in enumerate(cuts):
        pieces[r].append((i, 0, count))
    fades, fade_specs = [], []
    for r in range(heads_size):
        if r == 0:
            fades.append(own_fade)
            fade_specs.append(whole(own_fade.shape))
        else:
            fades.append(sides if r % 2 else got_fades[r // 2 - 1])
            fade_specs.append(part(fades[-1], r // 2 if r % 2 else 0))
    keep, send = kernel_call(
        lambda me_ref, *refs: partial_state_kernel(pieces, *refs),
        "partial_states",
        (shape((half, features, state_size), F32), shape((half, features, state_size))),
        grid_spec=pltpu.PrefetchScalarGridSpec(
            num_scalar_prefetch=1,
            grid=(1,),
            in_specs=[whole(array.shape) for array in portions]
            + fade_specs
            + [pl.BlockSpec((rows_dev, state_size), lambda i, m: (m[0], 0))],
            out_specs=[whole((half, features, state_size))] * 2,
            scratch_shapes=[pltpu.VMEM((features, rows_dev), BF16)],
        ),
    )(me1, *portions, *fades, state_in)

    def core_sum(keep, send):
        got = swap(send, "head", 1)
        far = kernel_call(
            fold_kernel,
            "fold",
            tuple([shape((features, state_size))] * (half - 1)),
            in_specs=[part(keep, i) for i in range(1, half)] * 2,
            out_specs=tuple([whole((features, state_size))] * (half - 1)),
            grid=(1,),
        )(*[keep] * (half - 1), *[got] * (half - 1))
        return got, far

    core_states, far_states = fenced(core_sum, keep, send)

    merge_count = len(merge_rows(stretches))
    grouped = (heads_size, head_count, rows_dev)
    pair_rows = max(per_group // 2, 1) * state_size

    def step(bit, running, total, offset, got):
        last = bit + 1 == near
        shapes = [shape((extra, LANES), F32)] * 3 + [shape((features + extra, state_size))]
        running_shape = shape((features, state_size), F32)
        results = kernel_call(
            functools.partial(merge_kernel, bit, head_count),
            "merge",
            tuple(shapes if last else shapes + [running_shape]),
            in_specs=[smem] + [vmem] * 4,
            scratch_shapes=[pltpu.VMEM((features, state_size), F32)] if last else [],
        )(place1, running, total, offset, got)
        return list(results) + [None] * last

    def chip_sum(
        keep, core_states, far_states, total, decays, level_class, level_table, state_in, state_out,
        second, crossing,
    ):
        got_states, latest = [], []
        for i, far in enumerate(far_states):
            latest = [swap(tie(far, *latest), "head", 2 * (i + 1))]
            got_states += latest
        moved, after = [], []
        for array in crossing:
            moved.append(swap(tie(array, *after), "head", 1))
            after = moved[-1:]
        if moved:
            moved[0] = jnp.concatenate([second, moved[0]], axis=1)
        table = jnp.transpose(level_table, (1, 2, 0))
        table = jnp.pad(table, ((0, 0), (0, padded - head_count), (0, 0)))
        tables = kernel_call(
            functools.partial(factors_kernel, levels, heads_size),
            "factors",
            (
                shape(grouped, F32),
                shape((local + 1,) + grouped, F32),
                shape((ctx_bits,) + grouped, F32),
                shape((merge_count, head_count, LANES), F32),
                shape((heads_size, 2, rows_dev, rows_dev)),
                shape((heads_size, rows_dev, per_group * state_size)),
                shape((heads_size, 2 * state_size, rows_dev)),
                shape((heads_size, pair_rows, rows_dev)),
            ),
        )(
            decays,
            level_class.reshape(1, tokens),
            table.reshape(levels * padded, classes),
            state_in,
            state_out,
        )
        got_states[-1] = tie(got_states[-1], tables[0], *moved)
        running, sent = kernel_call(
            first_kernel,
            "first_state",
            (shape((features, state_size), F32), shape((features + extra, state_size))),
            grid=(1,),
            in_specs=[part(keep, 0), part(core_states, 0), whole(total.shape)]
            + [whole((features, state_size))] * len(got_states),
            out_specs=(whole((features, state_size)), whole((features + extra, state_size))),
        )(keep, core_states, total, *got_states)
        return running, sent, tables, moved

    def near_steps(running, total, sent):
        offset = jnp.zeros((extra, LANES), F32)
        factors = [jnp.broadcast_to((position % 2).astype(F32), (extra, LANES))]
        states = []
        for bit in range(near):
            states.append(swap(sent, "ctx", 2**bit))
            total, offset, factor, sent, running = step(bit, running, total, offset, states[-1])
            factors.append(factor)
        return states, factors, sent

    running, sent, tables, moved = fenced(
        chip_sum, keep, core_states, tie(far_states, value_head), total, decays, level_class,
        level_table, state_in, state_out, portion[2, early],
        [portion[r, 0] for r in range(3, heads_size, 2)],
    )
    passed, after = {}, []
    for i, array in enumerate(moved):
        passed[2 * i + 3] = swap(tie(array, *after), "head", 2 * i + 2)
        after = [passed[2 * i + 3]]
    for r in range(4, heads_size, 2):
        passed[r] = swap(tie(portion[r, 0], *after), "head", r)
        after = [passed[r]]
    states, factors, sent = fenced(near_steps, running, total, sent)
    states = list(states)
    sent = tie(sent, *[held[2**bit] for bit in range(ctx_bits)])
    last_state = swap(sent, "ctx", 2**near)

    for r in range(2, ctx_size):
        low = r & -r
        if r not in held and low > 1:
            held[r] = swap(tie(held[r ^ low], sent), "ctx", low)
    for bit in range(2, ctx_bits):
        held[2**bit + 1] = swap(tie(held[2**bit], sent), "ctx", 1)
    for r in (0, 1):
        partners[r] = swap(tie(held[r], sent), "head", 1)

    skips = jnp.broadcast_to(skip_gain[:, None], (head_count, rows_dev))
    gains = norm_gain[:, None]

    lift, read, cross, merge, scores, masked, readers, pairs = tables
    arrays = [portion[0, 0], swap(tie(portion[1, 0], sent), "head", 1), value_head]
    pieces = [[(0, 0, rows_dev)], [(1, 0, rows_dev)], [(2, 0, early)]]
    for r in range(3, heads_size):
        first = rows_dev - early if r == 3 else 0
        if r == 3:
            pieces[2].append((len(arrays), 0, first))
        pieces.append([(len(arrays), first, rows_dev)])
        arrays.append(passed[r])
    pre = kernel_call(
        functools.partial(local_kernel, near, pieces),
        "local_levels",
        shape((heads_size, features, rows_dev), F32),
        40,
        in_specs=[smem] + [vmem] * (len(arrays) + 9 + 2 * near),
        scratch_shapes=[
            pltpu.VMEM((features, rows_dev), BF16),
            pltpu.VMEM((max(local, 1), features, state_size), F32),
            pltpu.VMEM((max(local, 1), features, 2 * state_size), BF16),
            pltpu.VMEM((features, pair_rows), BF16),
            pltpu.VMEM((heads_size, features, per_group * state_size), F32),
        ],
    )(
        me1, *arrays, lift, read, merge, scores, masked, readers, pairs, skips, cross,
        *factors[:near], *states,
    )
    *kept, sides = kernel_call(
        functools.partial(finish_kernel, half),
        "finish",
        tuple([shape((features, rows_dev))] * half + [shape((half, features, rows_dev))]),
        28,
        grid=(1,),
        in_specs=[
            smem,
            whole(pre.shape),
            whole(readers.shape),
            part(cross, near),
            whole((extra, LANES)),
            whole((features + extra, state_size)),
            whole((features, 1)),
        ],
        out_specs=[whole((features, rows_dev))] * half + [whole((half, features, rows_dev))],
    )(me1, pre, readers, cross, factors[near], last_state, gains)
    done = [held[r] for r in held if r not in (0, 1)] + [kept[0]]
    early_blocks = sorted(held)
    held[3] = swap(tie(held[1], *done), "ctx", 2)
    for r in range(5, ctx_size, 2):
        if r not in held:
            held[r] = swap(tie(held[r ^ 1], *done), "ctx", 1)

    order = sorted(early_blocks, key=lambda r: (r // 2 * 2 not in early_blocks or r ^ 1 not in early_blocks, r))
    order += [r for r in range(ctx_size) if r not in early_blocks]
    count = 2
    groups = [order[first : first + count] for first in range(0, ctx_size, count)]
    others = swap(sides, "head", 1)

    def project(name, first, kept, others, group, blocks, partners, kind):
        rows = len(kept)
        return kernel_call(
            project_kernel,
            name,
            shape((rows, count * columns, rows_dev), kind),
            in_specs=[whole((features, rows_dev))] * rows
            + [part(others, first + i) for i in range(rows)]
            + [whole((columns, features))] * (2 * count),
            out_specs=whole((rows, count * columns, rows_dev)),
            grid=(1,),
        )(*kept, *[others] * rows, *[blocks[r] for r in group], *[partners[r] for r in group])

    def far_rows(group, kept, others, blocks, partners):
        return project("project_far", 1, kept[1:], others, group, blocks, partners, BF16)

    def own_rows(group, kept, others, blocks, partners):
        return project("project_own", 0, kept[:1], others, group, blocks, partners, F32)[0]

    def send_rows(far, *after):
        far = tie(far, *after)
        return [swap(far[i - 1], "head", 2 * i) for i in range(1, half)]

    def with_partners(blocks, partners):
        more = {r: swap(blocks[r], "head", 1) for r in blocks if r not in partners}
        return {**partners, **more}, more

    def first_groups(kept, others, blocks, partners):
        partners, more = with_partners(blocks, partners)
        got = send_rows(far_rows(groups[0], kept, others, blocks, partners))
        far = far_rows(groups[1], kept, others, blocks, partners)
        return far, got, more, own_rows(groups[0], [tie(kept[0], far)], others, blocks, partners)

    def middle_group(index):
        def body(far, kept, others, blocks, partners):
            known = partners
            partners, more = with_partners({r: blocks[r] for r in groups[index]}, partners)
            next_far = far_rows(groups[index], kept, others, blocks, partners)
            own = own_rows(groups[index - 1], [tie(kept[0], next_far)], others, blocks, known)
            return next_far, send_rows(far), more, own

        return body

    def last_group(kept, others, blocks, partners):
        partners, more = with_partners(blocks, partners)
        return far_rows(groups[-1], kept, others, blocks, partners), more

    def some(array, group):
        return {r: array[r] for r in group if r in array}

    arrived = []
    far, got, more, own = fenced(
        first_groups, kept, others, some(held, groups[0] + groups[1]), some(partners, groups[0] + groups[1])
    )
    arrived.append(got)
    owns = [own]
    partners.update(more)
    for index in range(2, len(groups) - 1):
        both = groups[index - 1] + groups[index]
        far, got, more, own = fenced(
            middle_group(index), far, kept, others, some(held, both), some(partners, both)
        )
        arrived.append(got)
        owns.append(own)
        partners.update(more)
    got = send_rows(far, *[held[r] for r in groups[-1]])
    arrived.append(got)
    far, more = fenced(last_group, kept, others, some(held, groups[-1]), some(partners, groups[-1]))
    partners.update(more)
    arrived.append(send_rows(far, *got))
    pieces = []
    for index, (group, got) in enumerate(zip(groups, arrived)):
        if index == len(owns):
            owns.append(own_rows(group, kept, others, held, partners))
        pieces += [owns[index]] + got
    return kernel_call(
        functools.partial(assemble_kernel, groups),
        "assemble",
        shape((rows_dev, ctx_size * columns)),
        in_specs=[smem] + [vmem] * len(pieces),
        scratch_shapes=[pltpu.VMEM((ctx_size * columns, rows_dev), F32)],
    )(place1, *pieces)


def solution(mesh):
    return jax.shard_map(
        on_device,
        mesh=mesh,
        in_specs=(
            P(("ctx", "head"), None),
            P("ctx", None),
            P("ctx", None),
            P("ctx", "head"),
            P("ctx"),
            P(None, None, "head"),
            P("head"),
            P("head"),
            P("head", "ctx"),
        ),
        out_specs=P(("ctx", "head"), None),
        check_vma=False,
    )
```

```python
import functools

import jax
import jax.numpy as jnp
from jax import lax
from jax.experimental import pallas as pl
from jax.experimental.pallas import tpu as pltpu
from jax.sharding import PartitionSpec as P

CH = 64
EPSILON = 1e-05
LANES = 128
F32 = jnp.float32
BF16 = jnp.bfloat16
MIB = 1024 * 1024


def dot(a, b):
    return lax.dot_general(a, b, (((1,), (0,)), ((), ())), preferred_element_type=F32)


def dot_nt(a, b):
    return lax.dot_general(a, b, (((1,), (1,)), ((), ())), preferred_element_type=F32)


def swap(value, axis, distance):
    pairs = [(source, source ^ distance) for source in range(lax.axis_size(axis))]
    return lax.ppermute(value, axis, pairs)


def tie(value, *after):
    return lax.optimization_barrier((value,) + after)[0]


def three_parts(x):
    high = x.astype(BF16)
    rest = x - high.astype(F32)
    middle = rest.astype(BF16)
    low = (rest - middle.astype(F32)).astype(BF16)
    return high, middle, low


def two_parts(x):
    high = x.astype(BF16)
    return high, (x - high.astype(F32)).astype(BF16)


def merge_rows(stretches):
    rows = [("own", c, 0) for c in range(stretches - 1)]
    for c in range(stretches - 1):
        k = 0
        while (c >> k) & 1:
            rows.append(("merge", c, k))
            k += 1
    return rows


def head_rows(head, width):
    return slice(head * width, (head + 1) * width)


def exact_dot(x, ones):
    return sum(dot(part, ones) for part in three_parts(x))


def split_kernel(me_ref, *refs):
    half = len(refs) // 2
    for value_ref, part_ref in zip(refs[:half], refs[half:]):
        part_ref[...] = jnp.transpose(value_ref[...])


def fade_kernel(blocks, me_ref, decay_ref, own_ref, side_ref, *refs):
    far_refs, total_ref = refs[:-1], refs[-1]
    head_count, tokens = decay_ref.shape
    rows = tokens // blocks
    row = lax.broadcasted_iota(jnp.int32, (rows, rows), 0)
    col = lax.broadcasted_iota(jnp.int32, (rows, rows), 1)
    later = jnp.where(row > col, 1.0, 0.0).astype(BF16)
    me = me_ref[0]
    after = jnp.zeros((head_count, 1), F32)
    for block in reversed(range(blocks)):
        decay = decay_ref[:, block * rows : (block + 1) * rows]
        left = exact_dot(decay, later)
        fade = jnp.exp(left + after)
        after = after + left[:, 0:1] + decay[:, 0:1]
        own_index = me ^ block

        @pl.when(own_index == 0)
        def _():
            own_ref[...] = fade

        @pl.when(own_index == 1)
        def _():
            side_ref[...] = fade

        for i, far_ref in enumerate(far_refs):
            for j in range(2):

                @pl.when(own_index == 2 * (i + 1) + j)
                def _():
                    far_ref[j] = fade

    total_ref[...] = jnp.zeros_like(total_ref)
    total_ref[:head_count, :] = jnp.broadcast_to(after, (head_count, LANES))


def pack_kernel(*refs):
    side_ref, *got_refs, out_ref = refs
    out_ref[0] = side_ref[...]
    for i, got_ref in enumerate(got_refs):
        out_ref[i + 1] = got_ref[0]


def factors_kernel(
    levels, blocks, decay_ref, class_ref, table_ref, in_ref, out_ref,
    lift_ref, read_ref, cross_ref, merge_ref, score_ref, masked_ref, reader_ref, pair_ref,
):
    head_count, tokens = decay_ref.shape
    stretches = tokens // CH
    rows = tokens // blocks
    per_block = rows // CH
    local = read_ref.shape[0] - 1
    state_size = in_ref.shape[1]
    padded = table_ref.shape[0] // levels
    classes = table_ref.shape[1]
    row = lax.broadcasted_iota(jnp.int32, (rows, rows), 0)
    col = lax.broadcasted_iota(jnp.int32, (rows, rows), 1)
    inside = (row // CH == col // CH) & (row <= col)
    upto = jnp.where(inside, 1.0, 0.0).astype(BF16)
    within, starts = [], [jnp.zeros((head_count, 1), F32)]
    for g in range(blocks):
        within.append(exact_dot(decay_ref[:, g * rows : (g + 1) * rows], upto))
        for s in range(per_block):
            last = (s + 1) * CH
            starts.append(starts[-1] + within[-1][:, last - 1 : last])
    class_row = lax.broadcasted_iota(jnp.int32, (classes, rows), 0)
    lane = lax.broadcasted_iota(jnp.int32, (head_count, rows), 1) // CH
    token = lax.broadcasted_iota(jnp.int32, (rows, state_size), 0) // CH

    def by_stretch(columns):
        spread = jnp.broadcast_to(columns[0], (head_count, rows))
        for s in range(1, per_block):
            spread = jnp.where(lane == s, columns[s], spread)
        return spread

    for g in range(blocks):
        at = slice(g * rows, (g + 1) * rows)
        onehot = jnp.where(class_ref[:, at] == class_row, 1.0, 0.0).astype(BF16)
        weights = sum(dot(part, onehot) for part in three_parts(table_ref[...]))
        weight = lambda level: weights[level * padded : level * padded + head_count, :]
        lift_ref[g] = jnp.exp(-within[g])
        read_ref[0, g] = jnp.exp(within[g]) * weight(0)
        first = g * per_block
        for level in range(1, local + 1):
            begins, active = [], []
            for c in range(first, first + per_block):
                upper = (c >> (level - 1)) & 1
                begins.append(starts[c] - starts[(c >> (level - 1)) << (level - 1)])
                active.append(jnp.full((head_count, 1), float(upper), F32))
            factor = jnp.exp(within[g] + by_stretch(begins)) * weight(level)
            read_ref[level, g] = factor * by_stretch(active)
        far = jnp.exp(within[g] + by_stretch(starts[first : first + per_block]))
        for level in range(local + 1, levels):
            cross_ref[level - local - 1, g] = far * weight(level)
        own_in, own_out = in_ref[at, :], out_ref[at, :]
        scores = jnp.where(inside, dot_nt(own_in, own_out), 0.0)
        score_ref[g, 0], score_ref[g, 1] = two_parts(scores)
        for s in range(per_block):
            masked = jnp.where(token == s, own_in.astype(F32), 0.0).astype(BF16)
            masked_ref[g, :, s * state_size : (s + 1) * state_size] = masked
        turned = jnp.transpose(own_out.astype(F32))
        reader = turned.astype(BF16)
        reader_ref[g, :state_size, :] = reader
        reader_ref[g, state_size:, :] = reader
        pairs = max(per_block // 2, 1)
        place = lax.broadcasted_iota(jnp.int32, (state_size, rows), 1) // (2 * CH)
        for j in range(pairs):
            alone = jnp.where(place == j, turned, 0.0).astype(BF16)
            pair_ref[g, j * state_size : (j + 1) * state_size, :] = alone
    for i, (kind, c, k) in enumerate(merge_rows(stretches)):
        first = c if kind == "own" else c + 1 - 2**k
        merge_ref[i] = jnp.broadcast_to(jnp.exp(starts[c + 1] - starts[first]), (head_count, LANES))


def load(refs, pieces, at):
    parts = [refs[i][at, first : first + count] for i, first, count in pieces]
    return parts[0] if len(parts) == 1 else jnp.concatenate(parts, axis=1)


def partial_state_kernel(pieces, *refs):
    count = len(pieces)
    arrays = sum(len(parts) for parts in pieces)
    value_refs, refs = refs[:arrays], refs[arrays:]
    fade_refs, (in_ref, keep_ref, send_ref, faded) = refs[:count], refs[count:]
    own_in = in_ref[...]
    for r in [*range(1, count, 2), *range(0, count, 2)]:
        fade = fade_refs[r][...].reshape(fade_refs[r].shape[-2:])
        head_count = fade.shape[0]
        width = value_refs[0].shape[0] // head_count
        for h in range(head_count):
            at = head_rows(h, width)
            value = load(value_refs, pieces[r], at).astype(F32)
            faded[at, :] = (fade[h : h + 1, :] * value).astype(BF16)
        state = dot(faded[...], own_in)
        if r % 2 == 1:
            send_ref[r // 2] = state.astype(BF16)
        else:
            keep_ref[r // 2] = state


def fold_kernel(*refs):
    count = len(refs) // 3
    for keep_ref, got_ref, far_ref in zip(refs[:count], refs[count : 2 * count], refs[2 * count :]):
        far_ref[...] = (keep_ref[0] + got_ref[0].astype(F32)).astype(BF16)


def pack_state(sent_ref, state, total):
    channels = state.shape[0]
    sent_ref[:channels, :] = state.astype(BF16)
    high, middle, low = (part.astype(F32) for part in three_parts(total))
    lane = lax.broadcasted_iota(jnp.int32, total.shape, 1)
    parts = jnp.where(lane < LANES // 4, high, jnp.where(lane < LANES // 2, middle, low))
    sent_ref[channels:, :] = parts.astype(BF16)


def first_kernel(own_ref, core_ref, total_ref, *refs):
    *far_refs, running_ref, sent_ref = refs
    running = own_ref[0] + core_ref[0].astype(F32)
    for far_ref in far_refs:
        running = running + far_ref[...].astype(F32)
    running_ref[...] = running
    pack_state(sent_ref, running, total_ref[...])


def merge_kernel(
    bit, head_count, place_ref, running_ref, total_ref, offset_ref, got_ref,
    next_total_ref, next_offset_ref, factor_ref, sent_ref, next_running_ref,
):
    channels = running_ref.shape[0]
    width = channels // head_count
    place = place_ref[0]
    upper = place // 2**bit % 2 == 1
    total = total_ref[...]
    parts = got_ref[channels:, :].astype(F32)
    middle, low = LANES // 4, LANES // 2
    partner = parts[:, 0:1] + parts[:, middle : middle + 1] + parts[:, low : low + 1]
    partner = jnp.broadcast_to(partner, total.shape)
    fading = jnp.exp(jnp.where(upper, total, partner))
    for h in range(head_count):
        at = head_rows(h, width)
        got, running = got_ref[at, :].astype(F32), running_ref[at, :]
        lower, higher = jnp.where(upper, got, running), jnp.where(upper, running, got)
        next_running_ref[at, :] = fading[h : h + 1, :] * lower + higher
    joined = total + partner
    next_total_ref[...] = joined
    offset = jnp.where(upper, offset_ref[...] + partner, offset_ref[...])
    next_offset_ref[...] = offset
    next_upper = place // 2 ** (bit + 1) % 2 == 1
    factor_ref[...] = jnp.where(next_upper, jnp.exp(offset), 0.0)
    pack_state(sent_ref, next_running_ref[...], joined)


def local_kernel(near, pieces, me_ref, *refs):
    groups = refs[-1].shape[0]
    arrays = 1 + max(i for parts in pieces for i, _, _ in parts)
    value_refs, refs = refs[:arrays], refs[arrays:]
    lift_ref, read_ref, merge_ref, score_ref, masked_ref, reader_ref, pair_ref = refs[:7]
    skip_ref, cross_ref, *refs = refs[7:]
    factor_refs, state_refs, refs = refs[:near], refs[near : 2 * near], refs[2 * near :]
    pre_ref, lifted, sums, operand, pairs_ref, nodes = refs
    channels, group_rows = value_refs[0].shape
    assert len(pieces) == groups
    head_count = lift_ref.shape[1]
    width = channels // head_count
    me = me_ref[0]
    per_group = group_rows // CH
    stretches = groups * per_group
    state_size = reader_ref.shape[1] // 2
    place = {kind: i for i, kind in enumerate(merge_rows(stretches))}
    heads = [(h, head_rows(h, width)) for h in range(head_count)]
    for r in range(groups):
        g = me ^ r
        lift = lift_ref[g]
        for h, at in heads:
            value = load(value_refs, pieces[r], at).astype(F32)
            lifted[at, :] = (lift[h : h + 1, :] * value).astype(BF16)
        direct = dot(lifted[...], score_ref[g, 0]) + dot(lifted[...], score_ref[g, 1])
        read = read_ref[0, g]
        terms = []
        for level, (state_ref, factor_ref) in enumerate(zip(state_refs, factor_refs)):
            gained = dot(state_ref[:channels, :], reader_ref[g, :state_size, :])
            scale = cross_ref[level, g] * factor_ref[:head_count, 0:1]
            terms.append((scale, gained))
        for h, at in heads:
            total = read[h : h + 1, :] * direct[at, :]
            total = total + skip_ref[h : h + 1, :] * load(value_refs, pieces[r], at).astype(F32)
            for scale, gained in terms:
                total = total + scale[h : h + 1, :] * gained[at, :]
            pre_ref[g, at, :] = total
        nodes[g] = dot(lifted[...], masked_ref[g])

    for g in range(groups):
        terms = []
        level = per_group.bit_length()
        while 2 ** (level - 1) < stretches:
            if (g * per_group >> (level - 1)) & 1:
                terms.append((read_ref[level, g], dot(operand[level - 1], reader_ref[g])))
            level += 1
        for s in range(per_group):
            c = g * per_group + s
            if c + 1 == stretches:
                break
            merges = [merge_ref[place["own", c, 0]]]
            k = 0
            while (c >> k) & 1:
                merges.append(merge_ref[place["merge", c, k]])
                k += 1
            for h, at in heads:
                node = nodes[g, at, s * state_size : (s + 1) * state_size]
                node = node * merges[0][h : h + 1, :]
                for i, merge in enumerate(merges[1:]):
                    node = node + merge[h : h + 1, :] * sums[i, at, :]
                sums[k, at, :] = node
                high, low = two_parts(node)
                if k == 0 and per_group > 1:
                    pairs_ref[at, s // 2 * state_size : (s // 2 + 1) * state_size] = high
                else:
                    operand[k, at, :state_size] = high
                    operand[k, at, state_size:] = low
            if 1 <= k < per_group.bit_length() - 1:
                scale = read_ref[k + 1, g]
                lane = lax.broadcasted_iota(jnp.int32, scale.shape, 1) // (CH << (k + 1))
                scale = jnp.where(lane == s >> (k + 1), scale, 0.0)
                terms.append((scale, dot(operand[k], reader_ref[g])))
        if per_group > 1:
            terms.append((read_ref[1, g], dot(pairs_ref[...], pair_ref[g])))
        for h, at in heads:
            total = pre_ref[g, at, :]
            for scale, gained in terms:
                total = total + scale[h : h + 1, :] * gained[at, :]
            pre_ref[g, at, :] = total


def finish_kernel(
    half, me_ref, pre_ref, reader_ref, cross_ref, factor_ref, state_ref, gain_ref, *refs
):
    keep_refs, send_ref = refs[:half], refs[half]
    groups, channels, _ = pre_ref.shape
    head_count = cross_ref.shape[2]
    width = channels // head_count
    state_size = reader_ref.shape[1] // 2
    me = me_ref[0]
    state = state_ref[:channels, :]
    for r in range(groups):
        g = me ^ r
        gained = dot(state, reader_ref[g, :state_size, :])
        scale = cross_ref[0, g] * factor_ref[:head_count, 0:1]
        for h in range(head_count):
            at = head_rows(h, width)
            total = pre_ref[g, at, :] + scale[h : h + 1, :] * gained[at, :]
            mean_square = jnp.sum(total * total, axis=0, keepdims=True) * (1.0 / width)
            normed = total * lax.rsqrt(mean_square + EPSILON) * gain_ref[at, 0:1]
            if r % 2 == 0:
                keep_refs[r // 2][at, :] = normed.astype(BF16)
            else:
                send_ref[r // 2, at, :] = normed.astype(BF16)


def project_kernel(*refs):
    *refs, out_ref = refs
    rows = out_ref.shape[0]
    kept_refs, other_refs, refs = refs[:rows], refs[rows : 2 * rows], refs[2 * rows :]
    count = len(refs) // 2
    weights, partners = refs[:count], refs[count:]
    width = weights[0].shape[0]
    for i, (kept_ref, other_ref) in enumerate(zip(kept_refs, other_refs)):
        for j, (weight, partner) in enumerate(zip(weights, partners)):
            found = dot(weight[...], kept_ref[...]) + dot(partner[...], other_ref[0])
            out_ref[i, j * width : (j + 1) * width, :] = found.astype(out_ref.dtype)


def assemble_kernel(groups, place_ref, *refs):
    *refs, out_ref, columns_ref = refs
    each = len(refs) // len(groups)
    for g, group in enumerate(groups):
        own_ref, *far_refs = refs[g * each : (g + 1) * each]
        width = own_ref.shape[0] // len(group)
        for j, r in enumerate(group):
            rows = slice(j * width, (j + 1) * width)
            total = own_ref[rows, :]
            for far_ref in far_refs:
                total = total + far_ref[rows, :].astype(F32)
            start = pl.multiple_of((place_ref[0] ^ r) * width, width)
            columns_ref[pl.ds(start, width), :] = total
    for first in range(0, out_ref.shape[1], LANES):
        at = slice(first, first + LANES)
        out_ref[:, at] = jnp.transpose(columns_ref[at, :]).astype(BF16)


def whole(shape):
    return pl.BlockSpec(shape, lambda *_: (0,) * len(shape))


def on_device(
    values,
    state_in,
    state_out,
    log_decay,
    level_class,
    level_table,
    skip_gain,
    norm_gain,
    out_weight,
):
    heads_size = lax.axis_size("head")
    ctx_size = lax.axis_size("ctx")
    ctx_bits = ctx_size.bit_length() - 1
    me = lax.axis_index("head")
    me1 = me.reshape(1).astype(jnp.int32)
    position = lax.axis_index("ctx")
    place1 = position.reshape(1).astype(jnp.int32)
    tokens = state_in.shape[0]
    rows_dev = values.shape[0]
    head_count = log_decay.shape[1]
    features = values.shape[1] // heads_size
    state_size = state_in.shape[1]
    columns = out_weight.shape[1]
    stretches = tokens // CH
    per_group = rows_dev // CH
    local = stretches.bit_length() - 1
    levels = level_table.shape[1]
    classes = level_table.shape[0]
    extra = -(-head_count // 16) * 16
    padded = -(-head_count // 8) * 8
    half = heads_size // 2
    near = ctx_bits - 1
    cheap = pl.CostEstimate(flops=0, bytes_accessed=0, transcendentals=0)
    smem = pl.BlockSpec(memory_space=pltpu.SMEM)
    vmem = pl.BlockSpec(memory_space=pltpu.VMEM)

    def kernel_call(body, name, out_shape, mib=16, **kwargs):
        params = pltpu.CompilerParams(vmem_limit_bytes=mib * MIB)
        return pl.pallas_call(
            body, out_shape=out_shape, compiler_params=params, cost_estimate=cheap, name=name, **kwargs
        )

    def shape(dims, kind=BF16):
        return jax.ShapeDtypeStruct(dims, kind)

    def part(array, index):
        return pl.BlockSpec((1,) + array.shape[1:], lambda *_: (index,) + (0,) * (array.ndim - 1))

    def fenced(body, *operands):
        shapes = jax.eval_shape(body, *operands)
        zeros = lambda *_: jax.tree.map(lambda leaf: jnp.zeros(leaf.shape, leaf.dtype), shapes)
        return lax.cond(position < ctx_size, body, zeros, *operands)

    held, partners = {0: out_weight.T}, {}
    for bit in range(ctx_bits):
        held[2**bit] = swap(held[0], "ctx", 2**bit)

    decays = log_decay.T
    own_fade, side_fade, *far_fades, total = kernel_call(
        functools.partial(fade_kernel, heads_size),
        "fade",
        tuple(
            [shape((head_count, rows_dev), F32)] * 2
            + [shape((2, head_count, rows_dev), F32)] * (half - 1)
            + [shape((extra, LANES), F32)]
        ),
        in_specs=[smem, vmem],
    )(me1, decays)

    got_fades = []
    for i, far in enumerate(far_fades):
        got_fades.append(swap(tie(far, *got_fades), "head", 2 * (i + 1)))
    sides = kernel_call(
        pack_kernel,
        "pack_fades",
        shape((half, head_count, rows_dev), F32),
        grid=(1,),
        in_specs=[whole(side_fade.shape)] + [part(got, 1) for got in got_fades],
        out_specs=whole((half, head_count, rows_dev)),
    )(side_fade, *got_fades)
    sides = swap(sides, "head", 1)

    early = rows_dev // 2
    cuts = [(r, first, early) for r in (2,) for first in (0, early)]
    cuts = [(0, 0, rows_dev), (1, 0, rows_dev)] + cuts
    cuts += [(r, 0, rows_dev) for r in range(3, heads_size)]
    portions = kernel_call(
        split_kernel,
        "split_values",
        tuple(shape((features, count)) for _, _, count in cuts),
        grid_spec=pltpu.PrefetchScalarGridSpec(
            num_scalar_prefetch=1,
            grid=(1,),
            in_specs=[
                pl.BlockSpec((count, features), lambda i, m, r=r, at=first // count: (at, m[0] ^ r))
                for r, first, count in cuts
            ],
            out_specs=[whole((features, count)) for _, _, count in cuts],
        ),
    )(me1, *[values] * len(cuts))
    portion = {(r, first): array for (r, first, _), array in zip(cuts, portions)}
    value_head = swap(tie(portion[2, 0], *got_fades), "head", 2)

    pieces = [[] for _ in range(heads_size)]
    for i, (r, _, count) in enumerate(cuts):
        pieces[r].append((i, 0, count))
    fades, fade_specs = [], []
    for r in range(heads_size):
        if r == 0:
            fades.append(own_fade)
            fade_specs.append(whole(own_fade.shape))
        else:
            fades.append(sides if r % 2 else got_fades[r // 2 - 1])
            fade_specs.append(part(fades[-1], r // 2 if r % 2 else 0))
    keep, send = kernel_call(
        lambda me_ref, *refs: partial_state_kernel(pieces, *refs),
        "partial_states",
        (shape((half, features, state_size), F32), shape((half, features, state_size))),
        grid_spec=pltpu.PrefetchScalarGridSpec(
            num_scalar_prefetch=1,
            grid=(1,),
            in_specs=[whole(array.shape) for array in portions]
            + fade_specs
            + [pl.BlockSpec((rows_dev, state_size), lambda i, m: (m[0], 0))],
            out_specs=[whole((half, features, state_size))] * 2,
            scratch_shapes=[pltpu.VMEM((features, rows_dev), BF16)],
        ),
    )(me1, *portions, *fades, state_in)

    def core_sum(keep, send):
        got = swap(send, "head", 1)
        far = kernel_call(
            fold_kernel,
            "fold",
            tuple([shape((features, state_size))] * (half - 1)),
            in_specs=[part(keep, i) for i in range(1, half)] * 2,
            out_specs=tuple([whole((features, state_size))] * (half - 1)),
            grid=(1,),
        )(*[keep] * (half - 1), *[got] * (half - 1))
        return got, far

    core_states, far_states = fenced(core_sum, keep, send)

    merge_count = len(merge_rows(stretches))
    grouped = (heads_size, head_count, rows_dev)
    pair_rows = max(per_group // 2, 1) * state_size

    def step(bit, running, total, offset, got):
        last = bit + 1 == near
        shapes = [shape((extra, LANES), F32)] * 3 + [shape((features + extra, state_size))]
        running_shape = shape((features, state_size), F32)
        results = kernel_call(
            functools.partial(merge_kernel, bit, head_count),
            "merge",
            tuple(shapes if last else shapes + [running_shape]),
            in_specs=[smem] + [vmem] * 4,
            scratch_shapes=[pltpu.VMEM((features, state_size), F32)] if last else [],
        )(place1, running, total, offset, got)
        return list(results) + [None] * last

    def chip_sum(
        keep, core_states, far_states, total, decays, level_class, level_table, state_in, state_out,
        second, crossing,
    ):
        got_states, latest = [], []
        for i, far in enumerate(far_states):
            latest = [swap(tie(far, *latest), "head", 2 * (i + 1))]
            got_states += latest
        moved, after = [], []
        for array in crossing:
            moved.append(swap(tie(array, *after), "head", 1))
            after = moved[-1:]
        if moved:
            moved[0] = jnp.concatenate([second, moved[0]], axis=1)
        table = jnp.transpose(level_table, (1, 2, 0))
        table = jnp.pad(table, ((0, 0), (0, padded - head_count), (0, 0)))
        tables = kernel_call(
            functools.partial(factors_kernel, levels, heads_size),
            "factors",
            (
                shape(grouped, F32),
                shape((local + 1,) + grouped, F32),
                shape((ctx_bits,) + grouped, F32),
                shape((merge_count, head_count, LANES), F32),
                shape((heads_size, 2, rows_dev, rows_dev)),
                shape((heads_size, rows_dev, per_group * state_size)),
                shape((heads_size, 2 * state_size, rows_dev)),
                shape((heads_size, pair_rows, rows_dev)),
            ),
        )(
            decays,
            level_class.reshape(1, tokens),
            table.reshape(levels * padded, classes),
            state_in,
            state_out,
        )
        got_states[-1] = tie(got_states[-1], tables[0], *moved)
        running, sent = kernel_call(
            first_kernel,
            "first_state",
            (shape((features, state_size), F32), shape((features + extra, state_size))),
            grid=(1,),
            in_specs=[part(keep, 0), part(core_states, 0), whole(total.shape)]
            + [whole((features, state_size))] * len(got_states),
            out_specs=(whole((features, state_size)), whole((features + extra, state_size))),
        )(keep, core_states, total, *got_states)
        return running, sent, tables, moved

    def near_steps(running, total, sent):
        offset = jnp.zeros((extra, LANES), F32)
        factors = [jnp.broadcast_to((position % 2).astype(F32), (extra, LANES))]
        states = []
        for bit in range(near):
            states.append(swap(sent, "ctx", 2**bit))
            total, offset, factor, sent, running = step(bit, running, total, offset, states[-1])
            factors.append(factor)
        return states, factors, sent

    running, sent, tables, moved = fenced(
        chip_sum, keep, core_states, tie(far_states, value_head), total, decays, level_class,
        level_table, state_in, state_out, portion[2, early],
        [portion[r, 0] for r in range(3, heads_size, 2)],
    )
    passed, after = {}, []
    for i, array in enumerate(moved):
        passed[2 * i + 3] = swap(tie(array, *after), "head", 2 * i + 2)
        after = [passed[2 * i + 3]]
    for r in range(4, heads_size, 2):
        passed[r] = swap(tie(portion[r, 0], *after), "head", r)
        after = [passed[r]]
    states, factors, sent = fenced(near_steps, running, total, sent)
    states = list(states)
    sent = tie(sent, *[held[2**bit] for bit in range(ctx_bits)])
    last_state = swap(sent, "ctx", 2**near)

    for r in range(2, ctx_size):
        low = r & -r
        if r not in held and low > 1:
            held[r] = swap(tie(held[r ^ low], sent), "ctx", low)
    for bit in range(2, ctx_bits):
        held[2**bit + 1] = swap(tie(held[2**bit], sent), "ctx", 1)
    for r in (0, 1):
        partners[r] = swap(tie(held[r], sent), "head", 1)

    skips = jnp.broadcast_to(skip_gain[:, None], (head_count, rows_dev))
    gains = norm_gain[:, None]

    lift, read, cross, merge, scores, masked, readers, pairs = tables
    arrays = [portion[0, 0], swap(tie(portion[1, 0], sent), "head", 1), value_head]
    pieces = [[(0, 0, rows_dev)], [(1, 0, rows_dev)], [(2, 0, early)]]
    for r in range(3, heads_size):
        first = rows_dev - early if r == 3 else 0
        if r == 3:
            pieces[2].append((len(arrays), 0, first))
        pieces.append([(len(arrays), first, rows_dev)])
        arrays.append(passed[r])
    pre = kernel_call(
        functools.partial(local_kernel, near, pieces),
        "local_levels",
        shape((heads_size, features, rows_dev), F32),
        40,
        in_specs=[smem] + [vmem] * (len(arrays) + 9 + 2 * near),
        scratch_shapes=[
            pltpu.VMEM((features, rows_dev), BF16),
            pltpu.VMEM((max(local, 1), features, state_size), F32),
            pltpu.VMEM((max(local, 1), features, 2 * state_size), BF16),
            pltpu.VMEM((features, pair_rows), BF16),
            pltpu.VMEM((heads_size, features, per_group * state_size), F32),
        ],
    )(
        me1, *arrays, lift, read, merge, scores, masked, readers, pairs, skips, cross,
        *factors[:near], *states,
    )
    *kept, sides = kernel_call(
        functools.partial(finish_kernel, half),
        "finish",
        tuple([shape((features, rows_dev))] * half + [shape((half, features, rows_dev))]),
        28,
        grid=(1,),
        in_specs=[
            smem,
            whole(pre.shape),
            whole(readers.shape),
            part(cross, near),
            whole((extra, LANES)),
            whole((features + extra, state_size)),
            whole((features, 1)),
        ],
        out_specs=[whole((features, rows_dev))] * half + [whole((half, features, rows_dev))],
    )(me1, pre, readers, cross, factors[near], last_state, gains)
    done = [held[r] for r in held if r not in (0, 1)] + [kept[0]]
    early_blocks = sorted(held)
    held[3] = swap(tie(held[1], *done), "ctx", 2)
    for r in range(5, ctx_size, 2):
        if r not in held:
            held[r] = swap(tie(held[r ^ 1], *done), "ctx", 1)

    order = sorted(early_blocks, key=lambda r: (r // 2 * 2 not in early_blocks or r ^ 1 not in early_blocks, r))
    order += [r for r in range(ctx_size) if r not in early_blocks]
    count = 2
    groups = [order[first : first + count] for first in range(0, ctx_size, count)]
    others = swap(sides, "head", 1)

    def project(name, first, kept, others, group, blocks, partners, kind):
        rows = len(kept)
        return kernel_call(
            project_kernel,
            name,
            shape((rows, count * columns, rows_dev), kind),
            in_specs=[whole((features, rows_dev))] * rows
            + [part(others, first + i) for i in range(rows)]
            + [whole((columns, features))] * (2 * count),
            out_specs=whole((rows, count * columns, rows_dev)),
            grid=(1,),
        )(*kept, *[others] * rows, *[blocks[r] for r in group], *[partners[r] for r in group])

    def far_rows(group, kept, others, blocks, partners):
        return project("project_far", 1, kept[1:], others, group, blocks, partners, BF16)

    def own_rows(group, kept, others, blocks, partners):
        return project("project_own", 0, kept[:1], others, group, blocks, partners, F32)[0]

    def send_rows(far, *after):
        far = tie(far, *after)
        return [swap(far[i - 1], "head", 2 * i) for i in range(1, half)]

    def with_partners(blocks, partners):
        more = {r: swap(blocks[r], "head", 1) for r in blocks if r not in partners}
        return {**partners, **more}, more

    def first_groups(kept, others, blocks, partners):
        partners, more = with_partners(blocks, partners)
        got = send_rows(far_rows(groups[0], kept, others, blocks, partners))
        far = far_rows(groups[1], kept, others, blocks, partners)
        return far, got, more, own_rows(groups[0], [tie(kept[0], far)], others, blocks, partners)

    def middle_group(index):
        def body(far, kept, others, blocks, partners):
            partners, more = with_partners(blocks, partners)
            return far_rows(groups[index], kept, others, blocks, partners), send_rows(far), more

        return body

    def last_group(kept, others, blocks, partners):
        partners, more = with_partners(blocks, partners)
        return far_rows(groups[-1], kept, others, blocks, partners), more

    def some(array, group):
        return {r: array[r] for r in group if r in array}

    arrived = []
    far, got, more, own = fenced(
        first_groups, kept, others, some(held, groups[0] + groups[1]), some(partners, groups[0] + groups[1])
    )
    arrived.append(got)
    owns = [own]
    partners.update(more)
    for index in range(2, len(groups) - 1):
        far, got, more = fenced(
            middle_group(index), far, kept, others, some(held, groups[index]), some(partners, groups[index])
        )
        arrived.append(got)
        partners.update(more)
    got = send_rows(far, *[held[r] for r in groups[-1]])
    arrived.append(got)
    far, more = fenced(last_group, kept, others, some(held, groups[-1]), some(partners, groups[-1]))
    partners.update(more)
    arrived.append(send_rows(far, *got))
    pieces = []
    for index, (group, got) in enumerate(zip(groups, arrived)):
        if index == len(owns):
            owns.append(own_rows(group, kept, others, held, partners))
        pieces += [owns[index]] + got
    return kernel_call(
        functools.partial(assemble_kernel, groups),
        "assemble",
        shape((rows_dev, ctx_size * columns)),
        in_specs=[smem] + [vmem] * len(pieces),
        scratch_shapes=[pltpu.VMEM((ctx_size * columns, rows_dev), F32)],
    )(place1, *pieces)


def solution(mesh):
    return jax.shard_map(
        on_device,
        mesh=mesh,
        in_specs=(
            P(("ctx", "head"), None),
            P("ctx", None),
            P("ctx", None),
            P("ctx", "head"),
            P("ctx"),
            P(None, None, "head"),
            P("head"),
            P("head"),
            P("head", "ctx"),
        ),
        out_specs=P(("ctx", "head"), None),
        check_vma=False,
    )
```

```python
import functools

import jax
import jax.numpy as jnp
from jax import lax
from jax.experimental import pallas as pl
from jax.experimental.pallas import tpu as pltpu
from jax.sharding import PartitionSpec as P

CH = 64
EPSILON = 1e-05
LANES = 128
F32 = jnp.float32
BF16 = jnp.bfloat16
MIB = 1024 * 1024


def dot(a, b):
    return lax.dot_general(a, b, (((1,), (0,)), ((), ())), preferred_element_type=F32)


def dot_nt(a, b):
    return lax.dot_general(a, b, (((1,), (1,)), ((), ())), preferred_element_type=F32)


def swap(value, axis, distance):
    pairs = [(source, source ^ distance) for source in range(lax.axis_size(axis))]
    return lax.ppermute(value, axis, pairs)


def tie(value, *after):
    return lax.optimization_barrier((value,) + after)[0]


def three_parts(x):
    high = x.astype(BF16)
    rest = x - high.astype(F32)
    middle = rest.astype(BF16)
    low = (rest - middle.astype(F32)).astype(BF16)
    return high, middle, low


def two_parts(x):
    high = x.astype(BF16)
    return high, (x - high.astype(F32)).astype(BF16)


def merge_rows(stretches):
    rows = [("own", c, 0) for c in range(stretches - 1)]
    for c in range(stretches - 1):
        k = 0
        while (c >> k) & 1:
            rows.append(("merge", c, k))
            k += 1
    return rows


def head_rows(head, width):
    return slice(head * width, (head + 1) * width)


def exact_dot(x, ones):
    return sum(dot(part, ones) for part in three_parts(x))


def split_kernel(me_ref, *refs):
    half = len(refs) // 2
    for value_ref, part_ref in zip(refs[:half], refs[half:]):
        part_ref[...] = jnp.transpose(value_ref[...])


def fade_kernel(blocks, me_ref, decay_ref, own_ref, side_ref, *refs):
    far_refs, total_ref = refs[:-1], refs[-1]
    head_count, tokens = decay_ref.shape
    rows = tokens // blocks
    row = lax.broadcasted_iota(jnp.int32, (rows, rows), 0)
    col = lax.broadcasted_iota(jnp.int32, (rows, rows), 1)
    later = jnp.where(row > col, 1.0, 0.0).astype(BF16)
    me = me_ref[0]
    after = jnp.zeros((head_count, 1), F32)
    for block in reversed(range(blocks)):
        decay = decay_ref[:, block * rows : (block + 1) * rows]
        left = exact_dot(decay, later)
        fade = jnp.exp(left + after)
        after = after + left[:, 0:1] + decay[:, 0:1]
        own_index = me ^ block

        @pl.when(own_index == 0)
        def _():
            own_ref[...] = fade

        @pl.when(own_index == 1)
        def _():
            side_ref[...] = fade

        for i, far_ref in enumerate(far_refs):
            for j in range(2):

                @pl.when(own_index == 2 * (i + 1) + j)
                def _():
                    far_ref[j] = fade

    total_ref[...] = jnp.zeros_like(total_ref)
    total_ref[:head_count, :] = jnp.broadcast_to(after, (head_count, LANES))


def pack_kernel(*refs):
    side_ref, *got_refs, out_ref = refs
    out_ref[0] = side_ref[...]
    for i, got_ref in enumerate(got_refs):
        out_ref[i + 1] = got_ref[0]


def factors_kernel(
    levels, blocks, decay_ref, class_ref, table_ref, in_ref, out_ref,
    lift_ref, read_ref, cross_ref, merge_ref, score_ref, masked_ref, reader_ref, pair_ref,
):
    head_count, tokens = decay_ref.shape
    stretches = tokens // CH
    rows = tokens // blocks
    per_block = rows // CH
    local = read_ref.shape[0] - 1
    state_size = in_ref.shape[1]
    padded = table_ref.shape[0] // levels
    classes = table_ref.shape[1]
    row = lax.broadcasted_iota(jnp.int32, (rows, rows), 0)
    col = lax.broadcasted_iota(jnp.int32, (rows, rows), 1)
    inside = (row // CH == col // CH) & (row <= col)
    upto = jnp.where(inside, 1.0, 0.0).astype(BF16)
    within, starts = [], [jnp.zeros((head_count, 1), F32)]
    for g in range(blocks):
        within.append(exact_dot(decay_ref[:, g * rows : (g + 1) * rows], upto))
        for s in range(per_block):
            last = (s + 1) * CH
            starts.append(starts[-1] + within[-1][:, last - 1 : last])
    class_row = lax.broadcasted_iota(jnp.int32, (classes, rows), 0)
    lane = lax.broadcasted_iota(jnp.int32, (head_count, rows), 1) // CH
    token = lax.broadcasted_iota(jnp.int32, (rows, state_size), 0) // CH

    def by_stretch(columns):
        spread = jnp.broadcast_to(columns[0], (head_count, rows))
        for s in range(1, per_block):
            spread = jnp.where(lane == s, columns[s], spread)
        return spread

    for g in range(blocks):
        at = slice(g * rows, (g + 1) * rows)
        onehot = jnp.where(class_ref[:, at] == class_row, 1.0, 0.0).astype(BF16)
        weights = sum(dot(part, onehot) for part in three_parts(table_ref[...]))
        weight = lambda level: weights[level * padded : level * padded + head_count, :]
        lift_ref[g] = jnp.exp(-within[g])
        read_ref[0, g] = jnp.exp(within[g]) * weight(0)
        first = g * per_block
        for level in range(1, local + 1):
            begins, active = [], []
            for c in range(first, first + per_block):
                upper = (c >> (level - 1)) & 1
                begins.append(starts[c] - starts[(c >> (level - 1)) << (level - 1)])
                active.append(jnp.full((head_count, 1), float(upper), F32))
            factor = jnp.exp(within[g] + by_stretch(begins)) * weight(level)
            read_ref[level, g] = factor * by_stretch(active)
        far = jnp.exp(within[g] + by_stretch(starts[first : first + per_block]))
        for level in range(local + 1, levels):
            cross_ref[level - local - 1, g] = far * weight(level)
        own_in, own_out = in_ref[at, :], out_ref[at, :]
        scores = jnp.where(inside, dot_nt(own_in, own_out), 0.0)
        score_ref[g, 0], score_ref[g, 1] = two_parts(scores)
        for s in range(per_block):
            masked = jnp.where(token == s, own_in.astype(F32), 0.0).astype(BF16)
            masked_ref[g, :, s * state_size : (s + 1) * state_size] = masked
        turned = jnp.transpose(own_out.astype(F32))
        reader = turned.astype(BF16)
        reader_ref[g, :state_size, :] = reader
        reader_ref[g, state_size:, :] = reader
        pairs = max(per_block // 2, 1)
        place = lax.broadcasted_iota(jnp.int32, (state_size, rows), 1) // (2 * CH)
        for j in range(pairs):
            alone = jnp.where(place == j, turned, 0.0).astype(BF16)
            pair_ref[g, j * state_size : (j + 1) * state_size, :] = alone
    for i, (kind, c, k) in enumerate(merge_rows(stretches)):
        first = c if kind == "own" else c + 1 - 2**k
        merge_ref[i] = jnp.broadcast_to(jnp.exp(starts[c + 1] - starts[first]), (head_count, LANES))


def load(refs, pieces, at):
    parts = [refs[i][at, first : first + count] for i, first, count in pieces]
    return parts[0] if len(parts) == 1 else jnp.concatenate(parts, axis=1)


def partial_state_kernel(pieces, *refs):
    count = len(pieces)
    arrays = sum(len(parts) for parts in pieces)
    value_refs, refs = refs[:arrays], refs[arrays:]
    fade_refs, (in_ref, keep_ref, send_ref, faded) = refs[:count], refs[count:]
    own_in = in_ref[...]
    for r in [*range(1, count, 2), *range(0, count, 2)]:
        fade = fade_refs[r][...].reshape(fade_refs[r].shape[-2:])
        head_count = fade.shape[0]
        width = value_refs[0].shape[0] // head_count
        for h in range(head_count):
            at = head_rows(h, width)
            value = load(value_refs, pieces[r], at).astype(F32)
            faded[at, :] = (fade[h : h + 1, :] * value).astype(BF16)
        state = dot(faded[...], own_in)
        if r % 2 == 1:
            send_ref[r // 2] = state.astype(BF16)
        else:
            keep_ref[r // 2] = state


def fold_kernel(*refs):
    count = len(refs) // 3
    for keep_ref, got_ref, far_ref in zip(refs[:count], refs[count : 2 * count], refs[2 * count :]):
        far_ref[...] = (keep_ref[0] + got_ref[0].astype(F32)).astype(BF16)


def pack_state(sent_ref, state, total):
    channels = state.shape[0]
    sent_ref[:channels, :] = state.astype(BF16)
    high, middle, low = (part.astype(F32) for part in three_parts(total))
    lane = lax.broadcasted_iota(jnp.int32, total.shape, 1)
    parts = jnp.where(lane < LANES // 4, high, jnp.where(lane < LANES // 2, middle, low))
    sent_ref[channels:, :] = parts.astype(BF16)


def first_kernel(own_ref, core_ref, total_ref, *refs):
    *far_refs, running_ref, sent_ref = refs
    running = own_ref[0] + core_ref[0].astype(F32)
    for far_ref in far_refs:
        running = running + far_ref[...].astype(F32)
    running_ref[...] = running
    pack_state(sent_ref, running, total_ref[...])


def merge_kernel(
    bit, head_count, place_ref, running_ref, total_ref, offset_ref, got_ref,
    next_total_ref, next_offset_ref, factor_ref, sent_ref, next_running_ref,
):
    channels = running_ref.shape[0]
    width = channels // head_count
    place = place_ref[0]
    upper = place // 2**bit % 2 == 1
    total = total_ref[...]
    parts = got_ref[channels:, :].astype(F32)
    middle, low = LANES // 4, LANES // 2
    partner = parts[:, 0:1] + parts[:, middle : middle + 1] + parts[:, low : low + 1]
    partner = jnp.broadcast_to(partner, total.shape)
    fading = jnp.exp(jnp.where(upper, total, partner))
    for h in range(head_count):
        at = head_rows(h, width)
        got, running = got_ref[at, :].astype(F32), running_ref[at, :]
        lower, higher = jnp.where(upper, got, running), jnp.where(upper, running, got)
        next_running_ref[at, :] = fading[h : h + 1, :] * lower + higher
    joined = total + partner
    next_total_ref[...] = joined
    offset = jnp.where(upper, offset_ref[...] + partner, offset_ref[...])
    next_offset_ref[...] = offset
    next_upper = place // 2 ** (bit + 1) % 2 == 1
    factor_ref[...] = jnp.where(next_upper, jnp.exp(offset), 0.0)
    pack_state(sent_ref, next_running_ref[...], joined)


def local_kernel(near, pieces, me_ref, *refs):
    groups = refs[-1].shape[0]
    arrays = 1 + max(i for parts in pieces for i, _, _ in parts)
    value_refs, refs = refs[:arrays], refs[arrays:]
    lift_ref, read_ref, merge_ref, score_ref, masked_ref, reader_ref, pair_ref = refs[:7]
    skip_ref, cross_ref, *refs = refs[7:]
    factor_refs, state_refs, refs = refs[:near], refs[near : 2 * near], refs[2 * near :]
    pre_ref, lifted, sums, operand, pairs_ref, nodes = refs
    channels, group_rows = value_refs[0].shape
    assert len(pieces) == groups
    head_count = lift_ref.shape[1]
    width = channels // head_count
    me = me_ref[0]
    per_group = group_rows // CH
    stretches = groups * per_group
    state_size = reader_ref.shape[1] // 2
    place = {kind: i for i, kind in enumerate(merge_rows(stretches))}
    heads = [(h, head_rows(h, width)) for h in range(head_count)]
    for r in range(groups):
        g = me ^ r
        lift = lift_ref[g]
        for h, at in heads:
            value = load(value_refs, pieces[r], at).astype(F32)
            lifted[at, :] = (lift[h : h + 1, :] * value).astype(BF16)
        direct = dot(lifted[...], score_ref[g, 0]) + dot(lifted[...], score_ref[g, 1])
        read = read_ref[0, g]
        terms = []
        for level, (state_ref, factor_ref) in enumerate(zip(state_refs, factor_refs)):
            gained = dot(state_ref[:channels, :], reader_ref[g, :state_size, :])
            scale = cross_ref[level, g] * factor_ref[:head_count, 0:1]
            terms.append((scale, gained))
        for h, at in heads:
            total = read[h : h + 1, :] * direct[at, :]
            total = total + skip_ref[h : h + 1, :] * load(value_refs, pieces[r], at).astype(F32)
            for scale, gained in terms:
                total = total + scale[h : h + 1, :] * gained[at, :]
            pre_ref[g, at, :] = total
        nodes[g] = dot(lifted[...], masked_ref[g])

    for g in range(groups):
        terms = []
        level = per_group.bit_length()
        while 2 ** (level - 1) < stretches:
            if (g * per_group >> (level - 1)) & 1:
                terms.append((read_ref[level, g], dot(operand[level - 1], reader_ref[g])))
            level += 1
        for s in range(per_group):
            c = g * per_group + s
            if c + 1 == stretches:
                break
            merges = [merge_ref[place["own", c, 0]]]
            k = 0
            while (c >> k) & 1:
                merges.append(merge_ref[place["merge", c, k]])
                k += 1
            for h, at in heads:
                node = nodes[g, at, s * state_size : (s + 1) * state_size]
                node = node * merges[0][h : h + 1, :]
                for i, merge in enumerate(merges[1:]):
                    node = node + merge[h : h + 1, :] * sums[i, at, :]
                sums[k, at, :] = node
                high, low = two_parts(node)
                if k == 0 and per_group > 1:
                    pairs_ref[at, s // 2 * state_size : (s // 2 + 1) * state_size] = high
                else:
                    operand[k, at, :state_size] = high
                    operand[k, at, state_size:] = low
            if 1 <= k < per_group.bit_length() - 1:
                scale = read_ref[k + 1, g]
                lane = lax.broadcasted_iota(jnp.int32, scale.shape, 1) // (CH << (k + 1))
                scale = jnp.where(lane == s >> (k + 1), scale, 0.0)
                terms.append((scale, dot(operand[k], reader_ref[g])))
        if per_group > 1:
            terms.append((read_ref[1, g], dot(pairs_ref[...], pair_ref[g])))
        for h, at in heads:
            total = pre_ref[g, at, :]
            for scale, gained in terms:
                total = total + scale[h : h + 1, :] * gained[at, :]
            pre_ref[g, at, :] = total


def finish_kernel(
    half, me_ref, pre_ref, reader_ref, cross_ref, factor_ref, state_ref, gain_ref, *refs
):
    keep_refs, send_ref = refs[:half], refs[half]
    groups, channels, _ = pre_ref.shape
    head_count = cross_ref.shape[2]
    width = channels // head_count
    state_size = reader_ref.shape[1] // 2
    me = me_ref[0]
    state = state_ref[:channels, :]
    for r in range(groups):
        g = me ^ r
        gained = dot(state, reader_ref[g, :state_size, :])
        scale = cross_ref[0, g] * factor_ref[:head_count, 0:1]
        for h in range(head_count):
            at = head_rows(h, width)
            total = pre_ref[g, at, :] + scale[h : h + 1, :] * gained[at, :]
            mean_square = jnp.sum(total * total, axis=0, keepdims=True) * (1.0 / width)
            normed = total * lax.rsqrt(mean_square + EPSILON) * gain_ref[at, 0:1]
            if r % 2 == 0:
                keep_refs[r // 2][at, :] = normed.astype(BF16)
            else:
                send_ref[r // 2, at, :] = normed.astype(BF16)


def project_kernel(*refs):
    *refs, out_ref = refs
    rows = out_ref.shape[0]
    kept_refs, other_refs, refs = refs[:rows], refs[rows : 2 * rows], refs[2 * rows :]
    count = len(refs) // 2
    weights, partners = refs[:count], refs[count:]
    width = weights[0].shape[0]
    for i, (kept_ref, other_ref) in enumerate(zip(kept_refs, other_refs)):
        for j, (weight, partner) in enumerate(zip(weights, partners)):
            found = dot(weight[...], kept_ref[...]) + dot(partner[...], other_ref[0])
            out_ref[i, j * width : (j + 1) * width, :] = found.astype(out_ref.dtype)


def assemble_kernel(groups, place_ref, *refs):
    *refs, out_ref, columns_ref = refs
    each = len(refs) // len(groups)
    for g, group in enumerate(groups):
        own_ref, *far_refs = refs[g * each : (g + 1) * each]
        width = own_ref.shape[0] // len(group)
        for j, r in enumerate(group):
            rows = slice(j * width, (j + 1) * width)
            total = own_ref[rows, :]
            for far_ref in far_refs:
                total = total + far_ref[rows, :].astype(F32)
            start = pl.multiple_of((place_ref[0] ^ r) * width, width)
            columns_ref[pl.ds(start, width), :] = total.astype(BF16)
    for first in range(0, out_ref.shape[1], LANES):
        at = slice(first, first + LANES)
        out_ref[:, at] = jnp.transpose(columns_ref[at, :])


def whole(shape):
    return pl.BlockSpec(shape, lambda *_: (0,) * len(shape))


def on_device(
    values,
    state_in,
    state_out,
    log_decay,
    level_class,
    level_table,
    skip_gain,
    norm_gain,
    out_weight,
):
    heads_size = lax.axis_size("head")
    ctx_size = lax.axis_size("ctx")
    ctx_bits = ctx_size.bit_length() - 1
    me = lax.axis_index("head")
    me1 = me.reshape(1).astype(jnp.int32)
    position = lax.axis_index("ctx")
    place1 = position.reshape(1).astype(jnp.int32)
    tokens = state_in.shape[0]
    rows_dev = values.shape[0]
    head_count = log_decay.shape[1]
    features = values.shape[1] // heads_size
    state_size = state_in.shape[1]
    columns = out_weight.shape[1]
    stretches = tokens // CH
    per_group = rows_dev // CH
    local = stretches.bit_length() - 1
    levels = level_table.shape[1]
    classes = level_table.shape[0]
    extra = -(-head_count // 16) * 16
    padded = -(-head_count // 8) * 8
    half = heads_size // 2
    near = ctx_bits - 1
    cheap = pl.CostEstimate(flops=0, bytes_accessed=0, transcendentals=0)
    smem = pl.BlockSpec(memory_space=pltpu.SMEM)
    vmem = pl.BlockSpec(memory_space=pltpu.VMEM)

    def kernel_call(body, name, out_shape, mib=16, **kwargs):
        params = pltpu.CompilerParams(vmem_limit_bytes=mib * MIB)
        return pl.pallas_call(
            body, out_shape=out_shape, compiler_params=params, cost_estimate=cheap, name=name, **kwargs
        )

    def shape(dims, kind=BF16):
        return jax.ShapeDtypeStruct(dims, kind)

    def part(array, index):
        return pl.BlockSpec((1,) + array.shape[1:], lambda *_: (index,) + (0,) * (array.ndim - 1))

    def fenced(body, *operands):
        shapes = jax.eval_shape(body, *operands)
        zeros = lambda *_: jax.tree.map(lambda leaf: jnp.zeros(leaf.shape, leaf.dtype), shapes)
        return lax.cond(position < ctx_size, body, zeros, *operands)

    held, partners = {0: out_weight.T}, {}
    for bit in range(ctx_bits):
        held[2**bit] = swap(held[0], "ctx", 2**bit)

    decays = log_decay.T
    own_fade, side_fade, *far_fades, total = kernel_call(
        functools.partial(fade_kernel, heads_size),
        "fade",
        tuple(
            [shape((head_count, rows_dev), F32)] * 2
            + [shape((2, head_count, rows_dev), F32)] * (half - 1)
            + [shape((extra, LANES), F32)]
        ),
        in_specs=[smem, vmem],
    )(me1, decays)

    got_fades = []
    for i, far in enumerate(far_fades):
        got_fades.append(swap(tie(far, *got_fades), "head", 2 * (i + 1)))
    sides = kernel_call(
        pack_kernel,
        "pack_fades",
        shape((half, head_count, rows_dev), F32),
        grid=(1,),
        in_specs=[whole(side_fade.shape)] + [part(got, 1) for got in got_fades],
        out_specs=whole((half, head_count, rows_dev)),
    )(side_fade, *got_fades)
    sides = swap(sides, "head", 1)

    early = rows_dev // 2
    cuts = [(r, first, early) for r in (2,) for first in (0, early)]
    cuts = [(0, 0, rows_dev), (1, 0, rows_dev)] + cuts
    cuts += [(r, 0, rows_dev) for r in range(3, heads_size)]
    portions = kernel_call(
        split_kernel,
        "split_values",
        tuple(shape((features, count)) for _, _, count in cuts),
        grid_spec=pltpu.PrefetchScalarGridSpec(
            num_scalar_prefetch=1,
            grid=(1,),
            in_specs=[
                pl.BlockSpec((count, features), lambda i, m, r=r, at=first // count: (at, m[0] ^ r))
                for r, first, count in cuts
            ],
            out_specs=[whole((features, count)) for _, _, count in cuts],
        ),
    )(me1, *[values] * len(cuts))
    portion = {(r, first): array for (r, first, _), array in zip(cuts, portions)}
    value_head = swap(tie(portion[2, 0], *got_fades), "head", 2)

    pieces = [[] for _ in range(heads_size)]
    for i, (r, _, count) in enumerate(cuts):
        pieces[r].append((i, 0, count))
    fades, fade_specs = [], []
    for r in range(heads_size):
        if r == 0:
            fades.append(own_fade)
            fade_specs.append(whole(own_fade.shape))
        else:
            fades.append(sides if r % 2 else got_fades[r // 2 - 1])
            fade_specs.append(part(fades[-1], r // 2 if r % 2 else 0))
    keep, send = kernel_call(
        lambda me_ref, *refs: partial_state_kernel(pieces, *refs),
        "partial_states",
        (shape((half, features, state_size), F32), shape((half, features, state_size))),
        grid_spec=pltpu.PrefetchScalarGridSpec(
            num_scalar_prefetch=1,
            grid=(1,),
            in_specs=[whole(array.shape) for array in portions]
            + fade_specs
            + [pl.BlockSpec((rows_dev, state_size), lambda i, m: (m[0], 0))],
            out_specs=[whole((half, features, state_size))] * 2,
            scratch_shapes=[pltpu.VMEM((features, rows_dev), BF16)],
        ),
    )(me1, *portions, *fades, state_in)

    def core_sum(keep, send):
        got = swap(send, "head", 1)
        far = kernel_call(
            fold_kernel,
            "fold",
            tuple([shape((features, state_size))] * (half - 1)),
            in_specs=[part(keep, i) for i in range(1, half)] * 2,
            out_specs=tuple([whole((features, state_size))] * (half - 1)),
            grid=(1,),
        )(*[keep] * (half - 1), *[got] * (half - 1))
        return got, far

    core_states, far_states = fenced(core_sum, keep, send)

    merge_count = len(merge_rows(stretches))
    grouped = (heads_size, head_count, rows_dev)
    pair_rows = max(per_group // 2, 1) * state_size

    def step(bit, running, total, offset, got):
        last = bit + 1 == near
        shapes = [shape((extra, LANES), F32)] * 3 + [shape((features + extra, state_size))]
        running_shape = shape((features, state_size), F32)
        results = kernel_call(
            functools.partial(merge_kernel, bit, head_count),
            "merge",
            tuple(shapes if last else shapes + [running_shape]),
            in_specs=[smem] + [vmem] * 4,
            scratch_shapes=[pltpu.VMEM((features, state_size), F32)] if last else [],
        )(place1, running, total, offset, got)
        return list(results) + [None] * last

    def chip_sum(
        keep, core_states, far_states, total, decays, level_class, level_table, state_in, state_out,
        second, crossing,
    ):
        got_states, latest = [], []
        for i, far in enumerate(far_states):
            latest = [swap(tie(far, *latest), "head", 2 * (i + 1))]
            got_states += latest
        moved, after = [], []
        for array in crossing:
            moved.append(swap(tie(array, *after), "head", 1))
            after = moved[-1:]
        if moved:
            moved[0] = jnp.concatenate([second, moved[0]], axis=1)
        table = jnp.transpose(level_table, (1, 2, 0))
        table = jnp.pad(table, ((0, 0), (0, padded - head_count), (0, 0)))
        tables = kernel_call(
            functools.partial(factors_kernel, levels, heads_size),
            "factors",
            (
                shape(grouped, F32),
                shape((local + 1,) + grouped, F32),
                shape((ctx_bits,) + grouped, F32),
                shape((merge_count, head_count, LANES), F32),
                shape((heads_size, 2, rows_dev, rows_dev)),
                shape((heads_size, rows_dev, per_group * state_size)),
                shape((heads_size, 2 * state_size, rows_dev)),
                shape((heads_size, pair_rows, rows_dev)),
            ),
        )(
            decays,
            level_class.reshape(1, tokens),
            table.reshape(levels * padded, classes),
            state_in,
            state_out,
        )
        got_states[-1] = tie(got_states[-1], tables[0], *moved)
        running, sent = kernel_call(
            first_kernel,
            "first_state",
            (shape((features, state_size), F32), shape((features + extra, state_size))),
            grid=(1,),
            in_specs=[part(keep, 0), part(core_states, 0), whole(total.shape)]
            + [whole((features, state_size))] * len(got_states),
            out_specs=(whole((features, state_size)), whole((features + extra, state_size))),
        )(keep, core_states, total, *got_states)
        return running, sent, tables, moved

    def near_steps(running, total, sent):
        offset = jnp.zeros((extra, LANES), F32)
        factors = [jnp.broadcast_to((position % 2).astype(F32), (extra, LANES))]
        states = []
        for bit in range(near):
            states.append(swap(sent, "ctx", 2**bit))
            total, offset, factor, sent, running = step(bit, running, total, offset, states[-1])
            factors.append(factor)
        return states, factors, sent

    running, sent, tables, moved = fenced(
        chip_sum, keep, core_states, tie(far_states, value_head), total, decays, level_class,
        level_table, state_in, state_out, portion[2, early],
        [portion[r, 0] for r in range(3, heads_size, 2)],
    )
    passed, after = {}, []
    for i, array in enumerate(moved):
        passed[2 * i + 3] = swap(tie(array, *after), "head", 2 * i + 2)
        after = [passed[2 * i + 3]]
    for r in range(4, heads_size, 2):
        passed[r] = swap(tie(portion[r, 0], *after), "head", r)
        after = [passed[r]]
    states, factors, sent = fenced(near_steps, running, total, sent)
    states = list(states)
    sent = tie(sent, *[held[2**bit] for bit in range(ctx_bits)])
    upwards = [(source, source + 2**near) for source in range(ctx_size - 2**near)]
    last_state = lax.ppermute(sent, "ctx", upwards)

    for r in range(2, ctx_size):
        low = r & -r
        if r not in held and low > 1:
            held[r] = swap(tie(held[r ^ low], sent), "ctx", low)
    for bit in range(2, ctx_bits):
        held[2**bit + 1] = swap(tie(held[2**bit], sent), "ctx", 1)
    for r in (0, 1):
        partners[r] = swap(tie(held[r], sent), "head", 1)

    skips = jnp.broadcast_to(skip_gain[:, None], (head_count, rows_dev))
    gains = norm_gain[:, None]

    lift, read, cross, merge, scores, masked, readers, pairs = tables
    arrays = [portion[0, 0], swap(tie(portion[1, 0], sent), "head", 1), value_head]
    pieces = [[(0, 0, rows_dev)], [(1, 0, rows_dev)], [(2, 0, early)]]
    for r in range(3, heads_size):
        first = rows_dev - early if r == 3 else 0
        if r == 3:
            pieces[2].append((len(arrays), 0, first))
        pieces.append([(len(arrays), first, rows_dev)])
        arrays.append(passed[r])
    pre = kernel_call(
        functools.partial(local_kernel, near, pieces),
        "local_levels",
        shape((heads_size, features, rows_dev), F32),
        40,
        in_specs=[smem] + [vmem] * (len(arrays) + 9 + 2 * near),
        scratch_shapes=[
            pltpu.VMEM((features, rows_dev), BF16),
            pltpu.VMEM((max(local, 1), features, state_size), F32),
            pltpu.VMEM((max(local, 1), features, 2 * state_size), BF16),
            pltpu.VMEM((features, pair_rows), BF16),
            pltpu.VMEM((heads_size, features, per_group * state_size), F32),
        ],
    )(
        me1, *arrays, lift, read, merge, scores, masked, readers, pairs, skips, cross,
        *factors[:near], *states,
    )
    *kept, sides = kernel_call(
        functools.partial(finish_kernel, half),
        "finish",
        tuple([shape((features, rows_dev))] * half + [shape((half, features, rows_dev))]),
        28,
        grid=(1,),
        in_specs=[
            smem,
            whole(pre.shape),
            whole(readers.shape),
            part(cross, near),
            whole((extra, LANES)),
            whole((features + extra, state_size)),
            whole((features, 1)),
        ],
        out_specs=[whole((features, rows_dev))] * half + [whole((half, features, rows_dev))],
    )(me1, pre, readers, cross, factors[near], last_state, gains)
    done = [held[r] for r in held if r not in (0, 1)] + [kept[0]]
    early_blocks = sorted(held)
    held[3] = swap(tie(held[1], *done), "ctx", 2)
    for r in range(5, ctx_size, 2):
        if r not in held:
            held[r] = swap(tie(held[r ^ 1], *done), "ctx", 1)

    order = sorted(early_blocks, key=lambda r: (r // 2 * 2 not in early_blocks or r ^ 1 not in early_blocks, r))
    order += [r for r in range(ctx_size) if r not in early_blocks]
    count = 2
    groups = [order[first : first + count] for first in range(0, ctx_size, count)]
    others = swap(sides, "head", 1)

    def project(name, first, kept, others, group, blocks, partners, kind):
        rows = len(kept)
        return kernel_call(
            project_kernel,
            name,
            shape((rows, count * columns, rows_dev), kind),
            in_specs=[whole((features, rows_dev))] * rows
            + [part(others, first + i) for i in range(rows)]
            + [whole((columns, features))] * (2 * count),
            out_specs=whole((rows, count * columns, rows_dev)),
            grid=(1,),
        )(*kept, *[others] * rows, *[blocks[r] for r in group], *[partners[r] for r in group])

    def far_rows(group, kept, others, blocks, partners):
        return project("project_far", 1, kept[1:], others, group, blocks, partners, BF16)

    def own_rows(group, kept, others, blocks, partners):
        return project("project_own", 0, kept[:1], others, group, blocks, partners, F32)[0]

    def send_rows(far, *after):
        far = tie(far, *after)
        return [swap(far[i - 1], "head", 2 * i) for i in range(1, half)]

    def with_partners(blocks, partners):
        more = {r: swap(blocks[r], "head", 1) for r in blocks if r not in partners}
        return {**partners, **more}, more

    def first_groups(kept, others, blocks, partners):
        partners, more = with_partners(blocks, partners)
        got = send_rows(far_rows(groups[0], kept, others, blocks, partners))
        far = far_rows(groups[1], kept, others, blocks, partners)
        return far, got, more, own_rows(groups[0], [tie(kept[0], far)], others, blocks, partners)

    def middle_group(index):
        def body(far, kept, others, blocks, partners):
            partners, more = with_partners(blocks, partners)
            return far_rows(groups[index], kept, others, blocks, partners), send_rows(far), more

        return body

    def last_group(kept, others, blocks, partners):
        partners, more = with_partners(blocks, partners)
        return far_rows(groups[-1], kept, others, blocks, partners), more

    def some(array, group):
        return {r: array[r] for r in group if r in array}

    arrived = []
    far, got, more, own = fenced(
        first_groups, kept, others, some(held, groups[0] + groups[1]), some(partners, groups[0] + groups[1])
    )
    arrived.append(got)
    owns = [own]
    partners.update(more)
    for index in range(2, len(groups) - 1):
        far, got, more = fenced(
            middle_group(index), far, kept, others, some(held, groups[index]), some(partners, groups[index])
        )
        arrived.append(got)
        partners.update(more)
    got = send_rows(far, *[held[r] for r in groups[-1]])
    arrived.append(got)
    far, more = fenced(last_group, kept, others, some(held, groups[-1]), some(partners, groups[-1]))
    partners.update(more)
    arrived.append(send_rows(far, *got))
    pieces = []
    for index, (group, got) in enumerate(zip(groups, arrived)):
        if index == len(owns):
            owns.append(own_rows(group, kept, others, held, partners))
        pieces += [owns[index]] + got
    return kernel_call(
        functools.partial(assemble_kernel, groups),
        "assemble",
        shape((rows_dev, ctx_size * columns)),
        in_specs=[smem] + [vmem] * len(pieces),
        scratch_shapes=[pltpu.VMEM((ctx_size * columns, rows_dev), BF16)],
    )(place1, *pieces)


def solution(mesh):
    return jax.shard_map(
        on_device,
        mesh=mesh,
        in_specs=(
            P(("ctx", "head"), None),
            P("ctx", None),
            P("ctx", None),
            P("ctx", "head"),
            P("ctx"),
            P(None, None, "head"),
            P("head"),
            P("head"),
            P("head", "ctx"),
        ),
        out_specs=P(("ctx", "head"), None),
        check_vma=False,
    )
```
